32 devices in a mesh: ctx: 8 (over y, x, core), fsdp: 4 (over z).
Axes of the slice: x: 2, y: 2, z: 4, core: 2. Of those that a mesh axis runs over, the one named last changes fastest.
Arguments:
- tokens: bfloat16 [4, 2048, 2048], P('fsdp', 'ctx'), may hold values from -6 to 6
- doc_ids: int32 [4, 2048], P('fsdp'), may hold values from 0 to 2, as said below
- block_pairs: int32 [8], replicated, may hold values from 0 to 7, each once
- ln1_gain: bfloat16 [2048], P('fsdp'), may hold values from 0.099609375 to 1.8984375
- ln1_bias: bfloat16 [2048], P('fsdp'), may hold values from -1.5 to 1.5
- w_qkv: bfloat16 [2048, 6144], P('fsdp'), may hold values from -0.125 to 0.125
- b_qkv: bfloat16 [6144], P('fsdp'), may hold values from -1.5 to 1.5
- w_out: bfloat16 [2048, 2048], P('fsdp'), may hold values from -1 to 1
- ln2_gain: bfloat16 [2048], P('fsdp'), may hold values from 0.099609375 to 1.8984375
- ln2_bias: bfloat16 [2048], P('fsdp'), may hold values from -1.5 to 1.5
- w_gate: bfloat16 [2048, 5632], P('fsdp'), may hold values from -0.125 to 0.125
- w_up: bfloat16 [2048, 5632], P('fsdp'), may hold values from -0.125 to 0.125
- w_down: bfloat16 [5632, 2048], P('fsdp'), may hold values from -0.078125 to 0.078125
- cotangent: bfloat16 [4, 2048, 2048], P('fsdp', 'ctx'), may hold values from -6 to 6
Outputs:
- layer_out: bfloat16 [4, 2048, 2048], P('fsdp', 'ctx')
- grad_tokens: float32 [4, 2048, 2048], P('fsdp', 'ctx')
- grad_ln1_gain: float32 [2048], P('fsdp')
- grad_ln1_bias: float32 [2048], P('fsdp')
- grad_w_qkv: float32 [2048, 6144], P('fsdp')
- grad_b_qkv: float32 [6144], P('fsdp')
- grad_w_out: float32 [2048, 2048], P('fsdp')
- grad_ln2_gain: float32 [2048], P('fsdp')
- grad_ln2_bias: float32 [2048], P('fsdp')
- grad_w_gate: float32 [2048, 5632], P('fsdp')
- grad_w_up: float32 [2048, 5632], P('fsdp')
- grad_w_down: float32 [5632, 2048], P('fsdp')
The draws below stay inside these ranges and needn't reach their ends.
Inputs may be any that keep to these rules, and one draw needn't show every extreme that they name: In each pack doc_ids never falls, starts at 0 and names three documents; one of them covers the first or the last half of the pack's places. Each value once; ctx device c holds in its first 128 rows the block of places block_pairs[c] and in its last ones block 15 - block_pairs[c], blocks of 128 places.
All inputs are finite; a program needn't handle non-finite values.
Results may differ from the reference program's by a relative error of at most 0.02.
Values may be sent and summed in bfloat16 or wider, within the bound.
A program may use at most 704 MiB of HBM per device.

```python
import jax
import jax.numpy as jnp
from jax import lax

D = 2048
HEADS = 32
HEAD = 64
ROT = 16
FF = 5632
TOK_DEV = 256
SEQ_LEN = 2048
PACKS = 4
PAIRS = 8


def draw_doc_ids(key, part):
    key = jax.random.fold_in(key, 7)

    def one_pack(pack_key):
        sub_keys = jax.random.split(pack_key, 3)
        long_len = jax.random.randint(sub_keys[0], (), SEQ_LEN // 2 + 1, 3 * SEQ_LEN // 4 + 1)
        rest_len = SEQ_LEN - long_len
        cut_len = jax.random.randint(sub_keys[1], (), 1, rest_len)
        long_first = jax.random.randint(sub_keys[2], (), 0, 2)
        places = jnp.arange(SEQ_LEN, dtype=jnp.int32)
        first_end = jnp.where(long_first == 1, long_len, cut_len)
        second_end = jnp.where(long_first == 1, long_len + cut_len, rest_len)
        return (places >= first_end).astype(jnp.int32) + (places >= second_end).astype(jnp.int32)
    return jax.vmap(one_pack)(jax.random.split(key, PACKS))


def shard_levels(key, dims, pieces, smallest, high):
    gain = 1.0
    for dim, blocks in pieces:
        heights = jax.random.uniform(jax.random.fold_in(jax.random.fold_in(key, 6), dim), (blocks,), jnp.float32, smallest / len(pieces), high / len(pieces))
        gain = gain * jnp.repeat(jnp.exp(heights), dims[dim] // blocks).reshape((-1,) + (1,) * (len(dims) - 1 - dim))
    return gain


def centred(key, extent, spread, most, cuts=(), kind=jnp.bfloat16):
    factor_of = shard_levels(key, extent, cuts, -0.22, 0.18) if cuts else 1.0
    result = jax.random.normal(key, extent, jnp.float32) * spread * factor_of
    return jnp.minimum(jnp.maximum(result, -most), most).astype(kind)


def setup_inputs(seed: int = 0) -> dict:
    arg_keys = jax.random.split(jax.random.key(seed), 15)
    return {
        "tokens": centred(arg_keys[0], (PACKS, SEQ_LEN, D), 1.0, 6.0, ((0, 4), (1, 8))),
        "doc_ids": draw_doc_ids(jax.random.fold_in(arg_keys[14], 71), 0),
        "block_pairs": jax.random.permutation(arg_keys[2], PAIRS).astype(jnp.int32),
        "ln1_gain": jnp.clip(1.0 + 0.18 * jax.random.normal(arg_keys[3], (D,), jnp.float32), 0.099609375, 1.8984375).astype(jnp.bfloat16),
        "ln1_bias": centred(arg_keys[4], (D,), 0.3, 1.5, ((0, 4),)),
        "w_qkv": centred(arg_keys[5], (D, 3 * D), D ** -0.5, 0.125, ((0, 4),)),
        "b_qkv": centred(arg_keys[6], (3 * D,), 0.3, 1.5, ((0, 4),)),
        "w_out": centred(arg_keys[7], (D, D), (D // 64) ** -0.5, 1.0, ((0, 4),)),
        "ln2_gain": jnp.clip(1.0 + 0.18 * jax.random.normal(arg_keys[8], (D,), jnp.float32), 0.099609375, 1.8984375).astype(jnp.bfloat16),
        "ln2_bias": centred(arg_keys[9], (D,), 0.3, 1.5, ((0, 4),)),
        "w_gate": centred(arg_keys[10], (D, FF), D ** -0.5, 0.125, ((0, 4),)),
        "w_up": centred(arg_keys[11], (D, FF), D ** -0.5, 0.125, ((0, 4),)),
        "w_down": centred(arg_keys[12], (FF, D), FF ** -0.5, 0.078125, ((0, 4),)),
        "cotangent": centred(arg_keys[13], (PACKS, SEQ_LEN, D), 1.0, 6.0, ((0, 4), (1, 8))),
    }


@jax.custom_vjp
def low(v):
    return lax.optimization_barrier(v.astype(jnp.bfloat16)).astype(jnp.float32)

@jax.custom_vjp
def low_back(v):
    return v

def low_keep(v):
    return (low(v), None)

def low_pass(kept, grad):
    return (grad,)

def back_keep(v):
    return (v, None)

def back_low(kept, grad):
    return (low(grad),)
low.defvjp(low_keep, low_pass)
low_back.defvjp(back_keep, back_low)
NORM_EPSILON = 1e-05
ROTARY_BASE = 10000.0
MASKED_SCORE = -1e+30
HIGHEST = lax.Precision.HIGHEST

def row_places(block_pairs):
    row_ids = jnp.arange(SEQ_LEN, dtype=jnp.int32)
    half_rows = TOK_DEV // 2
    owners = row_ids // TOK_DEV
    second = row_ids // half_rows % 2
    first_block = jnp.take(block_pairs, owners).astype(jnp.int32)
    blocks = jnp.where(second == 0, first_block, 2 * PAIRS - 1 - first_block)
    return (blocks * half_rows + row_ids % half_rows).astype(jnp.int32)

def layer_norm(values, gain_row, shift_row):
    centered = values - lax.optimization_barrier(jnp.mean(values, -1, keepdims=True))
    inverse = lax.rsqrt(lax.optimization_barrier(jnp.mean(centered * centered, -1, keepdims=True)) + NORM_EPSILON)
    return centered * inverse * gain_row + shift_row

def rotate(heads_in, angles):
    half_rot = ROT // 2
    cosine = jnp.cos(angles)[:, None, :]
    sine_row = jnp.sin(angles)[:, None, :]
    front_half = heads_in[..., :half_rot]
    behind = heads_in[..., half_rot:ROT]
    return jnp.concatenate([front_half * cosine - behind * sine_row, behind * cosine + front_half * sine_row, heads_in[..., ROT:]], -1)

def pack_layer(tokens_in, places, row_docs, angles, params):
    gain_one, shift_one, w_qkv, b_qkv, w_out, gain_two, shift_two, w_gate, w_up, w_down = params
    normed = low(layer_norm(tokens_in, gain_one, shift_one))
    projected = low_back(jnp.dot(normed, w_qkv, precision=HIGHEST) + b_qkv)
    split_heads = projected.reshape(SEQ_LEN, 3, HEADS, HEAD)
    queries = low(rotate(split_heads[:, 0], angles))
    key_rows = low(rotate(split_heads[:, 1], angles))
    value_rows = low(split_heads[:, 2])
    block_rows = min(512, SEQ_LEN)
    block_count = SEQ_LEN // block_rows

    def attend(block_args):
        query_block, query_places, query_docs = block_args
        raw_scores = low_back(jnp.einsum('qhd,khd->hqk', query_block, key_rows, precision=HIGHEST))
        allowed = (query_places[:, None] >= places[None, :]) & (query_docs[:, None] == row_docs[None, :])
        scores = jnp.where(allowed[None], raw_scores * HEAD ** (-0.5), MASKED_SCORE)
        soft_weights = low(jax.nn.softmax(scores, axis=-1))
        return jnp.einsum('hqk,khd->qhd', soft_weights, value_rows, precision=HIGHEST)
    attended = lax.map(jax.checkpoint(attend), (queries.reshape(block_count, block_rows, HEADS, HEAD), places.reshape(block_count, block_rows), row_docs.reshape(block_count, block_rows)))
    mixed_heads = low_back(low(attended.reshape(SEQ_LEN, D)))
    residual = tokens_in + low_back(jnp.dot(mixed_heads, w_out, precision=HIGHEST))
    normed_two = low(layer_norm(residual, gain_two, shift_two))
    gate_value = low_back(jnp.dot(normed_two, w_gate, precision=HIGHEST))
    up_value = low_back(jnp.dot(normed_two, w_up, precision=HIGHEST))
    hidden = low(jax.nn.silu(gate_value) * up_value)
    return residual + jnp.dot(hidden, w_down, precision=HIGHEST)

def reference(tokens, doc_ids, block_pairs, ln1_gain, ln1_bias, w_qkv, b_qkv, w_out, ln2_gain, ln2_bias, w_gate, w_up, w_down, cotangent):
    places = row_places(block_pairs)
    inverse_freq = ROTARY_BASE ** (-jnp.arange(ROT // 2, dtype=jnp.float32) * 2.0 / ROT)
    angles = places.astype(jnp.float32)[:, None] * inverse_freq[None, :]
    params = tuple((weight.astype(jnp.float32) for weight in (ln1_gain, ln1_bias, w_qkv, b_qkv, w_out, ln2_gain, ln2_bias, w_gate, w_up, w_down)))

    def forward(tokens_all, params_all):

        def one_pack(pack_args):
            tokens_in, docs_in = pack_args
            return pack_layer(tokens_in, places, jnp.take(docs_in, places), angles, params_all)
        return lax.map(jax.checkpoint(one_pack), (tokens_all, doc_ids))
    layer_out, pullback = jax.vjp(forward, tokens.astype(jnp.float32), params)
    grad_tokens, gradients = pullback(cotangent.astype(jnp.float32))
    return (layer_out.astype(jnp.bfloat16), grad_tokens, gradients[0], gradients[1], gradients[2], gradients[3], gradients[4], gradients[5], gradients[6], gradients[7], gradients[8], gradients[9])
```

```python
import jax
import jax.numpy as jnp
from jax import lax
from jax.sharding import PartitionSpec as P

HEAD = 64
ROT = 16


NORM_EPSILON = 1e-05
ROTARY_BASE = 10000.0
MASKED_SCORE = -1e30


def norm_rows(values, gain_row, shift_row):
    centered = values - jnp.mean(values, -1, keepdims=True)
    inverse = lax.rsqrt(jnp.mean(centered * centered, -1, keepdims=True) + NORM_EPSILON)
    unit_rows = centered * inverse
    return (unit_rows * gain_row + shift_row, unit_rows, inverse)


def norm_back(grad_rows, unit_rows, inverse, gain_row):
    scaled = grad_rows * gain_row
    return inverse * (
        scaled
        - jnp.mean(scaled, -1, keepdims=True)
        - unit_rows * jnp.mean(scaled * unit_rows, -1, keepdims=True)
    )


def row_places(row_ids, block_pairs, rows_here, axis_size):
    half_rows = rows_here // 2
    owners = row_ids // rows_here
    second = row_ids // half_rows % 2
    matches = owners[:, None] == jnp.arange(axis_size, dtype=jnp.int32)[None, :]
    first_block = jnp.sum(jnp.where(matches, block_pairs[None, :], 0), 1)
    blocks = jnp.where(second == 0, first_block, 2 * axis_size - 1 - first_block)
    return blocks * half_rows + row_ids % half_rows


def rotate(heads_in, angles, turn_sign):
    half_rot = ROT // 2
    cosine = jnp.cos(angles)[:, None, :]
    sine_row = turn_sign * jnp.sin(angles)[:, None, :]
    front_half = heads_in[..., :half_rot]
    behind = heads_in[..., half_rot:ROT]
    return jnp.concatenate(
        [
            front_half * cosine - behind * sine_row,
            behind * cosine + front_half * sine_row,
            heads_in[..., ROT:],
        ],
        -1,
    )


def inner(left_side, right_side):
    return lax.dot_general(
        left_side, right_side, (((0,), (0,)), ((), ())), preferred_element_type=jnp.float32
    )


def times_transposed(left_side, right_side):
    return lax.dot_general(
        left_side, right_side, (((1,), (1,)), ((), ())), preferred_element_type=jnp.float32
    )


def times(left_side, right_side):
    return jnp.dot(left_side, right_side, preferred_element_type=jnp.float32)


def attend(queries, keys, values, allowed):
    score_scale = HEAD ** (-0.5)

    def one_head(args):
        query, key, value = args
        scores = jnp.where(allowed, times_transposed(query, key) * score_scale, MASKED_SCORE)
        row_max = jnp.max(scores, -1, keepdims=True)
        exps = jnp.where(allowed, jnp.exp(scores - row_max), 0.0)
        total = jnp.sum(exps, -1, keepdims=True)
        weights = (exps / total).astype(jnp.bfloat16)
        return times(weights, value), row_max + jnp.log(total)

    return lax.map(one_head, (queries, keys, values))


def attend_back(queries, keys, values, grad_mixed, log_total, delta, allowed):
    score_scale = HEAD ** (-0.5)

    def one_head(args):
        query, key, value, grad, total, row_delta = args
        scores = times_transposed(query, key) * score_scale
        weights = jnp.where(allowed, jnp.exp(scores - total), 0.0)
        grad_value = inner(weights.astype(jnp.bfloat16), grad)
        grad_soft = times_transposed(grad, value)
        grad_raw = (weights * (grad_soft - row_delta) * score_scale).astype(jnp.bfloat16)
        return times(grad_raw, key), inner(grad_raw, query), grad_value

    return lax.map(one_head, (queries, keys, values, grad_mixed, log_total, delta))


def body(
    tokens,
    doc_ids,
    block_pairs,
    ln1_gain,
    ln1_bias,
    w_qkv,
    b_qkv,
    w_out,
    ln2_gain,
    ln2_bias,
    w_gate,
    w_up,
    w_down,
    cotangent,
):
    rows_here = tokens.shape[1]
    width = tokens.shape[2]
    head_count = width // HEAD
    ctx_size = lax.axis_size("ctx")
    fsdp_size = lax.axis_size("fsdp")
    seq_rows = rows_here * ctx_size
    position = lax.axis_index("ctx")
    part = lax.axis_index("fsdp")
    heads_here = head_count // ctx_size
    cols = width // ctx_size
    shard_rows = w_qkv.shape[0]
    hidden_shard = w_down.shape[0]
    strip = hidden_shard // ctx_size

    key_places = row_places(jnp.arange(seq_rows, dtype=jnp.int32), block_pairs, rows_here, ctx_size)
    key_docs = jnp.take(doc_ids[0], key_places)
    allowed = (key_places[:, None] >= key_places[None, :]) & (key_docs[:, None] == key_docs[None, :])
    inverse_freq = ROTARY_BASE ** (-jnp.arange(ROT // 2, dtype=jnp.float32) * 2.0 / ROT)
    angles = key_places.astype(jnp.float32)[:, None] * inverse_freq[None, :]

    small = lax.all_gather(
        jnp.concatenate([ln1_gain, ln1_bias, ln2_gain, ln2_bias, b_qkv]), "fsdp", axis=0
    ).astype(jnp.float32)
    gain_one, shift_one, gain_two, shift_two = (
        small[:, i * shard_rows : (i + 1) * shard_rows].reshape(1, width) for i in range(4)
    )
    bias_full = small[:, 4 * shard_rows :].reshape(3, ctx_size, cols)
    bias_here = lax.dynamic_index_in_dim(bias_full, position, 1, keepdims=False).reshape(3 * cols)

    qkv_strip = lax.dynamic_index_in_dim(
        w_qkv.reshape(shard_rows, 3, ctx_size, cols), position, 2, keepdims=False
    ).reshape(shard_rows, 3 * cols)
    gate_strip, up_strip = (
        lax.dynamic_index_in_dim(
            w.reshape(shard_rows, fsdp_size, ctx_size, strip), position, 2, keepdims=False
        ).reshape(shard_rows, fsdp_size * strip)
        for w in (w_gate, w_up)
    )
    down_strip = lax.dynamic_slice_in_dim(w_down, position * strip, strip, 0)
    out_piece = shard_rows // ctx_size
    out_strip = lax.dynamic_slice_in_dim(w_out, position * out_piece, out_piece, 0)

    tokens_in = tokens[0].astype(jnp.float32)
    normed, unit_one, inverse_one = norm_rows(tokens_in, gain_one, shift_one)
    normed_all = lax.all_gather(normed.astype(jnp.bfloat16), "ctx", axis=0, tiled=True)
    qkv_here = lax.all_gather(qkv_strip, "fsdp", axis=0, tiled=True)
    projected = times(normed_all, qkv_here) + bias_here
    split_heads = projected.reshape(seq_rows, 3, heads_here, HEAD)
    queries, keys, values = (
        jnp.transpose(rows.astype(jnp.bfloat16), (1, 0, 2))
        for rows in (
            rotate(split_heads[:, 0], angles, 1.0),
            rotate(split_heads[:, 1], angles, 1.0),
            split_heads[:, 2],
        )
    )
    attended, log_total = attend(queries, keys, values, allowed)
    mixed_here = (
        jnp.transpose(attended, (1, 0, 2)).reshape(seq_rows, cols).astype(jnp.bfloat16)
    )
    mixed_rows = lax.all_to_all(mixed_here, "ctx", split_axis=0, concat_axis=1, tiled=True)
    out_full = lax.all_gather(out_strip, ("fsdp", "ctx"), axis=0, tiled=True)
    residual = tokens_in + times(mixed_rows, out_full)
    normed_two, unit_two, inverse_two = norm_rows(residual, gain_two, shift_two)
    normed_two_all = lax.all_gather(normed_two.astype(jnp.bfloat16), "ctx", axis=0, tiled=True)
    gate_here = lax.all_gather(gate_strip, "fsdp", axis=0, tiled=True)
    up_here = lax.all_gather(up_strip, "fsdp", axis=0, tiled=True)
    down_here = lax.all_gather(down_strip, "fsdp", axis=0, tiled=True)
    gate_value = times(normed_two_all, gate_here)
    up_value = times(normed_two_all, up_here)
    sigmoid_gate = jax.nn.sigmoid(gate_value)
    silu_gate = gate_value * sigmoid_gate
    hidden = (silu_gate * up_value).astype(jnp.bfloat16)
    layer_out = residual + lax.psum_scatter(
        times(hidden, down_here).astype(jnp.bfloat16), "ctx", scatter_dimension=0, tiled=True
    ).astype(jnp.float32)

    grad_out = cotangent[0]
    grad_out_all = lax.all_gather(grad_out, "ctx", axis=0, tiled=True)
    grad_hidden = times_transposed(grad_out_all, down_here)
    grad_gate = (
        grad_hidden * up_value * sigmoid_gate * (1.0 + gate_value * (1.0 - sigmoid_gate))
    ).astype(jnp.bfloat16)
    grad_up = (grad_hidden * silu_gate).astype(jnp.bfloat16)
    grad_normed_two = lax.psum_scatter(
        (times_transposed(grad_gate, gate_here) + times_transposed(grad_up, up_here)).astype(
            jnp.bfloat16
        ),
        "ctx",
        scatter_dimension=0,
        tiled=True,
    ).astype(jnp.float32)
    grad_residual = grad_out.astype(jnp.float32) + norm_back(
        grad_normed_two, unit_two, inverse_two, gain_two
    )
    grad_branch = grad_residual.astype(jnp.bfloat16)
    grad_mixed_rows = times_transposed(grad_branch, out_full).astype(jnp.bfloat16)
    grad_mixed = lax.all_to_all(grad_mixed_rows, "ctx", split_axis=1, concat_axis=0, tiled=True)
    grad_mixed = jnp.transpose(grad_mixed.reshape(seq_rows, heads_here, HEAD), (1, 0, 2))
    delta = jnp.sum(grad_mixed.astype(jnp.float32) * attended, -1, keepdims=True)
    grad_queries, grad_keys, grad_values = (
        jnp.transpose(grad, (1, 0, 2))
        for grad in attend_back(queries, keys, values, grad_mixed, log_total, delta, allowed)
    )
    grad_projected = (
        jnp.stack(
            [rotate(grad_queries, angles, -1.0), rotate(grad_keys, angles, -1.0), grad_values], 1
        )
        .reshape(seq_rows, 3 * cols)
        .astype(jnp.bfloat16)
    )
    grad_normed = lax.psum_scatter(
        times_transposed(grad_projected, qkv_here).astype(jnp.bfloat16),
        "ctx",
        scatter_dimension=0,
        tiled=True,
    ).astype(jnp.float32)
    grad_tokens = grad_residual + norm_back(grad_normed, unit_one, inverse_one, gain_one)

    def reduced(grad, axes):
        return lax.psum_scatter(
            grad.astype(jnp.bfloat16), axes, scatter_dimension=0, tiled=True
        )

    def spread(piece):
        return lax.all_gather(piece, "ctx", axis=0)

    grad_down_w = spread(reduced(inner(hidden, grad_out_all), "fsdp"))
    grad_gate_w = spread(reduced(inner(normed_two_all, grad_gate), "fsdp"))
    grad_up_w = spread(reduced(inner(normed_two_all, grad_up), "fsdp"))
    grad_out_w = spread(reduced(inner(mixed_rows, grad_branch), ("fsdp", "ctx")))
    grad_qkv_w = spread(reduced(inner(normed_all, grad_projected), "fsdp"))

    grad_bias = jnp.sum(grad_projected.astype(jnp.float32), 0).reshape(3, 1, cols)
    grad_bias = lax.dynamic_update_slice(
        jnp.zeros((3, ctx_size, cols), jnp.float32), grad_bias, (0, position, 0)
    )
    sums = jnp.concatenate(
        [
            jnp.sum(grad_normed * unit_one, 0),
            jnp.sum(grad_normed, 0),
            jnp.sum(grad_normed_two * unit_two, 0),
            jnp.sum(grad_normed_two, 0),
            grad_bias.reshape(3 * width),
        ]
    )
    sums = lax.psum(sums, ("fsdp", "ctx"))
    norm_sums = lax.dynamic_slice_in_dim(
        sums[: 4 * width].reshape(4, width), part * shard_rows, shard_rows, 1
    )
    bias_sums = lax.dynamic_slice_in_dim(
        sums[4 * width :], part * b_qkv.shape[0], b_qkv.shape[0], 0
    )
    float32 = jnp.float32
    return (
        layer_out.astype(jnp.bfloat16)[None],
        grad_tokens[None],
        norm_sums[0],
        norm_sums[1],
        jnp.transpose(grad_qkv_w.reshape(ctx_size, shard_rows, 3, cols), (1, 2, 0, 3))
        .reshape(w_qkv.shape)
        .astype(float32),
        bias_sums,
        grad_out_w.reshape(w_out.shape).astype(float32),
        norm_sums[2],
        norm_sums[3],
        jnp.transpose(grad_gate_w.reshape(ctx_size, shard_rows, fsdp_size, strip), (1, 2, 0, 3))
        .reshape(w_gate.shape)
        .astype(float32),
        jnp.transpose(grad_up_w.reshape(ctx_size, shard_rows, fsdp_size, strip), (1, 2, 0, 3))
        .reshape(w_up.shape)
        .astype(float32),
        grad_down_w.reshape(w_down.shape).astype(float32),
    )


def solution(mesh):
    placed = (
        P("fsdp", "ctx", None),
        P("fsdp", None),
        P(),
        P("fsdp"),
        P("fsdp"),
        P("fsdp", None),
        P("fsdp"),
        P("fsdp", None),
        P("fsdp"),
        P("fsdp"),
        P("fsdp", None),
        P("fsdp", None),
        P("fsdp", None),
        P("fsdp", "ctx", None),
    )
    return jax.shard_map(
        body,
        mesh=mesh,
        in_specs=placed,
        out_specs=(
            P("fsdp", "ctx", None),
            P("fsdp", "ctx", None),
            P("fsdp"),
            P("fsdp"),
            P("fsdp", None),
            P("fsdp"),
            P("fsdp", None),
            P("fsdp"),
            P("fsdp"),
            P("fsdp", None),
            P("fsdp", None),
            P("fsdp", None),
        ),
        check_vma=False,
    )
```

```python
import functools

import jax
import jax.numpy as jnp
from jax import lax
from jax.experimental import pallas as pl
from jax.experimental.pallas import tpu as pltpu
from jax.sharding import PartitionSpec as P

HEAD = 64
ROT = 16


NORM_EPSILON = 1e-05
ROTARY_BASE = 10000.0
MASKED_SCORE = -1e30


MESH_IDS = pl.DeviceIdType.MESH


def bit_of(index, bit):
    return index // (1 << bit) % 2


def flipped(index, mask, bits):
    result = index
    for bit in range(bits):
        if mask >> bit & 1:
            result = result + (1 - 2 * bit_of(index, bit)) * (1 << bit)
    return result


def greet(partners):
    barrier = pltpu.get_barrier_semaphore()
    for partner in partners:
        pl.semaphore_signal(barrier, inc=1, device_id={"ctx": partner}, device_id_type=MESH_IDS)
    pl.semaphore_wait(barrier, len(partners))


def half_orders(bits):
    chip_bits = list(range(1, bits))
    return [chip_bits, chip_bits[1:] + chip_bits[:1]]


def gather_plan(bits):
    steps = []
    for order in half_orders(bits):
        held = [0]
        plan = []
        for bit in order:
            plan.append((bit, list(held)))
            held = held + [mask | 1 << bit for mask in held]
        steps.append((plan, held))
    return steps


def column_half(ref, half):
    width = ref.shape[-1] // 2
    return ref.at[..., pl.ds(half * width, width)]


def row_half(ref, half):
    rows = ref.shape[-2] // 2
    if len(ref.shape) == 2:
        return ref.at[pl.ds(half * rows, rows)]
    return ref.at[..., pl.ds(half * rows, rows), :]


def stacked_rows(ref, block, half):
    return row_half(ref.at[block], half)


def stacked_columns(ref, block, half):
    return column_half(ref.at[block], half)


def middle_columns(ref, block, half):
    return column_half(ref.at[:, block], half)


def block_view(ref, block):
    return ref.at[block]


def column_view(ref, block, width):
    return ref.at[:, pl.ds(pl.multiple_of(block * width, width), width)]


def gather_run(bits, take, put, source, out, send_sem, recv_sem, core_send, core_recv, local_sem):
    me = lax.axis_index("ctx")
    steps = gather_plan(bits)
    finals = []
    for half in range(2):
        copy = pltpu.make_async_copy(take(source, half), put(out, me, half), local_sem.at[half])
        copy.start()
        finals.append(copy.wait)

    def push(half, mask, bit, send, recv, index):
        block = flipped(me, mask, bits)
        copy = pltpu.make_async_remote_copy(
            src_ref=take(source, half) if mask == 0 else put(out, block, half),
            dst_ref=put(out, block, half),
            send_sem=send.at[half, index],
            recv_sem=recv.at[half, index],
            device_id={"ctx": flipped(me, 1 << bit, bits)},
            device_id_type=MESH_IDS,
        )
        copy.start()
        return copy

    arriving = {}
    for phase in range(bits):
        for half in range(2):
            plan, held = steps[half]
            if phase > 0:
                for copy in arriving[half]:
                    copy.wait_recv()
            if phase < bits - 1:
                bit, masks = plan[phase]
                arriving[half] = [
                    push(half, mask, bit, send_sem, recv_sem, (1 << phase) - 1 + number)
                    for number, mask in enumerate(masks)
                ]
                finals += [copy.wait_send for copy in arriving[half]]
            fresh = held[:1] if phase == 0 else held[1 << (phase - 1) : 1 << phase]
            for mask in fresh:
                copy = push(half, mask, 0, core_send, core_recv, held.index(mask))
                finals.append(copy.wait)
            yield
    for wait in finals:
        wait()


def gather_op(x, size, take=row_half, put=stacked_rows, out_shape=None):
    bits = size.bit_length() - 1
    steps = size // 2 - 1
    dma = pltpu.SemaphoreType.DMA
    return dict(
        run=functools.partial(gather_run, bits, take, put),
        inputs=[x],
        in_space=pl.ANY,
        outs=[jax.ShapeDtypeStruct(out_shape or (size,) + x.shape, x.dtype)],
        out_space=pl.ANY,
        scratch=[dma((2, steps)), dma((2, steps)), dma((2, steps + 1)), dma((2, steps + 1)), dma((2,))],
        far=False,
        moved=2 * size * x.size * 2,
    )


def add_into(target, first, second, rows, step):
    @pl.loop(0, rows // step)
    def _(i):
        at = pl.ds(pl.multiple_of(i * step, step), step)
        target[at] = (first[at].astype(jnp.float32) + second[at].astype(jnp.float32)).astype(
            target.dtype
        )


def scatter_plan(bits):
    plans = []
    for order in half_orders(bits):
        kept = [mask << 1 for mask in range(1 << (bits - 1))]
        plan = []
        for bit in order:
            plan.append((bit, [mask for mask in kept if mask >> bit & 1]))
            kept = [mask for mask in kept if not mask >> bit & 1]
        plans.append(plan)
    return plans


def farthest_first(masks):
    return sorted(masks, key=lambda mask: -bin(mask).count("1"))


def scatter_run(bits, step, part_ref, out_ref, core_buf, chip_buf, core_send, core_recv, send_sem, recv_sem):
    me = lax.axis_index("ctx")
    rows = part_ref.shape[1]
    width = part_ref.shape[2] // 2
    plans = scatter_plan(bits)
    chip_masks = farthest_first([mask << 1 for mask in range(1 << (bits - 1))])
    finals = []
    core_copies = {}
    for mask in chip_masks:
        copy = pltpu.make_async_remote_copy(
            src_ref=part_ref.at[flipped(me, mask | 1, bits)],
            dst_ref=core_buf.at[mask >> 1],
            send_sem=core_send.at[mask >> 1],
            recv_sem=core_recv.at[mask >> 1],
            device_id={"ctx": flipped(me, 1, bits)},
            device_id_type=MESH_IDS,
        )
        copy.start()
        core_copies[mask] = copy
        finals.append(copy.wait_send)
    arriving = {}

    def columns(half):
        return pl.ds(half * width, width)

    def send(half, phase, bit, mask):
        slot = plans[half][phase][1].index(mask)
        copy = pltpu.make_async_remote_copy(
            src_ref=part_ref.at[flipped(me, mask, bits), :, columns(half)],
            dst_ref=chip_buf.at[half, phase, slot],
            send_sem=send_sem.at[half, phase, slot],
            recv_sem=recv_sem.at[half, phase, slot],
            device_id={"ctx": flipped(me, 1 << bit, bits)},
            device_id_type=MESH_IDS,
        )
        copy.start()
        finals.append(copy.wait_send)
        arriving[half, phase, mask & ~(1 << bit)] = (copy, slot)

    yield
    for mask in chip_masks:
        core_copies[mask].wait_recv()
        here = part_ref.at[flipped(me, mask, bits)]
        add_into(here, here, core_buf.at[mask >> 1], rows, step)
        for half in range(2):
            bit, masks = plans[half][0]
            if mask in masks:
                send(half, 0, bit, mask)
    yield
    phases = bits - 1
    for phase in range(1, phases + 1):
        for half in range(2):
            last_bit, last_masks = plans[half][phase - 1]
            kept = farthest_first([mask & ~(1 << last_bit) for mask in last_masks])
            for mask in kept:
                copy, slot = arriving[half, phase - 1, mask]
                copy.wait_recv()
                here = part_ref.at[flipped(me, mask, bits), :, columns(half)]
                buf = chip_buf.at[half, phase - 1, slot]
                if phase < phases:
                    add_into(here, here, buf, rows, step)
                    bit, masks = plans[half][phase]
                    if mask in masks:
                        send(half, phase, bit, mask)
                else:
                    add_into(out_ref.at[:, columns(half)], here, buf, rows, step)
        yield
    for wait in finals:
        wait()


def scatter_op(part, size):
    bits = size.bit_length() - 1
    chips = size // 2
    rows, width = part.shape[1:]
    dma = pltpu.SemaphoreType.DMA
    return dict(
        run=functools.partial(scatter_run, bits, 32),
        inputs=[part],
        in_space=pltpu.VMEM,
        outs=[jax.ShapeDtypeStruct((rows, width), jnp.float32)],
        out_space=pltpu.VMEM,
        scratch=[
            pltpu.VMEM((chips, rows, width), part.dtype),
            pltpu.VMEM((2, bits - 1, chips // 2, rows, width // 2), part.dtype),
            dma((chips,)),
            dma((chips,)),
            dma((2, bits - 1, chips // 2)),
            dma((2, bits - 1, chips // 2)),
        ],
        far=False,
        moved=4 * part.size,
    )


def exchange_run(size, take, put, source, out, send_sem, recv_sem, local_sem):
    me = lax.axis_index("ctx")
    local = pltpu.make_async_copy(take(source, me), put(out, me), local_sem)
    local.start()
    copies = []
    for step in range(1, size):
        other = lax.rem(me + step, size)
        copy = pltpu.make_async_remote_copy(
            src_ref=take(source, other),
            dst_ref=put(out, me),
            send_sem=send_sem.at[step - 1],
            recv_sem=recv_sem.at[step - 1],
            device_id={"ctx": other},
            device_id_type=MESH_IDS,
        )
        copy.start()
        copies.append(copy)
    yield
    local.wait()
    for copy in copies:
        copy.wait()


def exchange_op(x, size, out_shape, take, put):
    dma = pltpu.SemaphoreType.DMA
    return dict(
        run=functools.partial(exchange_run, size, take, put),
        inputs=[x],
        in_space=pl.ANY,
        outs=[jax.ShapeDtypeStruct(out_shape, x.dtype)],
        out_space=pl.ANY,
        scratch=[dma((size - 1,)), dma((size - 1,)), dma],
        far=True,
        moved=4 * x.size,
    )


def plane_kernel(size, parts, *refs):
    bits = size.bit_length() - 1
    me = lax.axis_index("ctx")
    if any(far for _, _, _, _, far in parts):
        greet([lax.rem(me + step, size) for step in range(1, size)])
    else:
        greet([flipped(me, 1 << bit, bits) for bit in range(bits)])
    ins = sum(part[1] for part in parts)
    outs = sum(part[2] for part in parts)
    groups = [list(refs[:ins]), list(refs[ins : ins + outs]), list(refs[ins + outs :])]
    running = []
    for run, *counts, far in parts:
        own = []
        for group, count in zip(groups, counts):
            own += group[:count]
            del group[:count]
        running.append(run(*own))
    while running:
        running = [turn_of for turn_of in running if next(turn_of, 1) is None]


def plane(size, collective_id, *ops):
    parts = [
        (op["run"], len(op["inputs"]), len(op["outs"]), len(op["scratch"]), op["far"]) for op in ops
    ]
    results = pl.pallas_call(
        functools.partial(plane_kernel, size, parts),
        out_shape=[out for op in ops for out in op["outs"]],
        in_specs=[pl.BlockSpec(memory_space=op["in_space"]) for op in ops for _ in op["inputs"]],
        out_specs=[pl.BlockSpec(memory_space=op["out_space"]) for op in ops for _ in op["outs"]],
        scratch_shapes=[scratch for op in ops for scratch in op["scratch"]],
        compiler_params=pltpu.CompilerParams(
            collective_id=collective_id, has_side_effects=True, vmem_limit_bytes=60 << 20
        ),
        cost_estimate=pl.CostEstimate(
            flops=0, bytes_accessed=sum(op["moved"] for op in ops), transcendentals=0
        ),
    )(*[x for op in ops for x in op["inputs"]])
    return results if len(results) > 1 else results[0]


def plane_groups(size, collective_id, *ops):
    groups = []
    room = 0
    for op in ops:
        need = 0 if op["in_space"] == pl.ANY else op["moved"] * 5 // 4
        if not groups or need > room:
            groups.append([])
            room = 52 << 20
        groups[-1].append(op)
        room -= need
    results = []
    for i, group in enumerate(groups):
        got = plane(size, collective_id + i, *group)
        results += got if isinstance(got, (list, tuple)) else [got]
    return results


def unpack_kernel(segments, count, source, out):
    strip = source.shape[2] // segments
    pieces = []
    for segment in range(segments):
        for owner in range(count):
            pieces.append(source[owner, :, segment * strip : (segment + 1) * strip])
    out[...] = jnp.concatenate(pieces, 1).astype(jnp.float32)


def unpack_columns(gathered, segments):
    count, rows, width = gathered.shape
    step = 64
    return pl.pallas_call(
        functools.partial(unpack_kernel, segments, count),
        grid=(rows // step,),
        in_specs=[pl.BlockSpec((count, step, width), lambda i: (0, i, 0))],
        out_specs=pl.BlockSpec((step, count * width), lambda i: (i, 0)),
        out_shape=jax.ShapeDtypeStruct((rows, count * width), jnp.float32),
        compiler_params=pltpu.CompilerParams(vmem_limit_bytes=32 << 20),
        cost_estimate=pl.CostEstimate(
            flops=0, bytes_accessed=6 * gathered.size, transcendentals=0
        ),
    )(gathered)


def norm_rows(values, gain_row, shift_row):
    centered = values - jnp.mean(values, -1, keepdims=True)
    inverse = lax.rsqrt(jnp.mean(centered * centered, -1, keepdims=True) + NORM_EPSILON)
    unit_rows = centered * inverse
    return (unit_rows * gain_row + shift_row, unit_rows, inverse)


def norm_back(grad_rows, unit_rows, inverse, gain_row):
    scaled = grad_rows * gain_row
    return inverse * (
        scaled
        - jnp.mean(scaled, -1, keepdims=True)
        - unit_rows * jnp.mean(scaled * unit_rows, -1, keepdims=True)
    )


def turn(rows, cosine, sine_low, sine_high, width):
    repeat = width // 128
    wide = [jnp.concatenate([table] * repeat, 1) for table in (cosine, sine_low, sine_high)]
    return (
        rows * wide[0]
        + pltpu.roll(rows, width - ROT // 2, 1) * wide[1]
        + pltpu.roll(rows, ROT // 2, 1) * wide[2]
    )


def head_stack(features_first, heads):
    owner = lax.broadcasted_iota(jnp.int32, features_first.shape, 0) // HEAD
    zero = jnp.zeros_like(features_first)
    return jnp.concatenate([jnp.where(owner == h, features_first, zero) for h in range(heads)], 1)


def row_stack(rows, heads):
    owner = lax.broadcasted_iota(jnp.int32, rows.shape, 1) // HEAD
    zero = jnp.zeros_like(rows)
    return jnp.concatenate([jnp.where(owner == h, rows, zero) for h in range(heads)], 0)


def allowed_pairs(query_tile, key_tile, tile, heads, starts):
    query_place = query_tile * tile + lax.broadcasted_iota(jnp.int32, (1, tile), 1)
    query_place = jnp.concatenate([query_place] * heads, 1)
    first_key = jnp.concatenate([starts] * heads, 1)
    key_place = key_tile * tile + lax.broadcasted_iota(jnp.int32, (tile, 1), 0)
    return (key_place <= query_place) & (key_place >= first_key)


def transposed(rows):
    return jnp.transpose(rows.astype(jnp.float32)).astype(rows.dtype)


def attend_kernel(
    block,
    heads,
    order,
    lowest,
    projected,
    starts,
    cosine,
    sine_low,
    sine_high,
    qkv,
    attended,
    mixed,
    log_total,
    value_t,
    summed,
    top,
    total,
):
    cols = heads * HEAD
    seq = projected.shape[0]
    tile = 2 * block

    @pl.loop(0, seq // block)
    def _(p):
        at = pl.ds(pl.multiple_of(p * block, block), block)
        rows = projected[pl.ds(pl.multiple_of(order[p] * block, block), block)]
        tables = (cosine[at], sine_low[at], sine_high[at])
        query = turn(rows[:, :cols], *tables, cols) * HEAD ** (-0.5)
        key = turn(rows[:, cols : 2 * cols], *tables, cols)
        value = rows[:, 2 * cols :]
        qkv[at, :cols] = query.astype(jnp.bfloat16)
        qkv[at, cols : 2 * cols] = key.astype(jnp.bfloat16)
        qkv[at, 2 * cols :] = value.astype(jnp.bfloat16)
        value_t[:, at] = jnp.transpose(value).astype(jnp.bfloat16)

    @pl.loop(0, seq // tile)
    def _(i):
        at = pl.ds(pl.multiple_of(i * tile, tile), tile)
        query_t = head_stack(transposed(qkv[at, :cols]), heads)
        first_keys = starts[:, at]
        top[...] = jnp.full(top.shape, MASKED_SCORE, jnp.float32)
        total[...] = jnp.zeros_like(total)
        summed[...] = jnp.zeros_like(summed)

        @pl.loop(lowest[i], i + 1)
        def _(j):
            keys_at = pl.ds(pl.multiple_of(j * tile, tile), tile)
            scores = jnp.dot(
                qkv[keys_at, cols : 2 * cols], query_t, preferred_element_type=jnp.float32
            )
            scores = jnp.where(
                allowed_pairs(i, j, tile, heads, first_keys), scores, MASKED_SCORE
            )
            old_top = top[...]
            new_top = jnp.maximum(old_top, jnp.max(scores, 0, keepdims=True))
            exps = jnp.exp(scores - new_top)
            fade = jnp.exp(old_top - new_top)
            total[...] = total[...] * fade + jnp.sum(exps, 0, keepdims=True)
            top[...] = new_top
            low = exps.astype(jnp.bfloat16)
            for h in range(heads):
                own = slice(h * tile, (h + 1) * tile)
                features = slice(h * HEAD, (h + 1) * HEAD)
                summed[features] = summed[features] * fade[:, own] + jnp.dot(
                    value_t[features, keys_at], low[:, own], preferred_element_type=jnp.float32
                )

        log_total[i] = top[...] + jnp.log(total[...])
        scale = 1.0 / total[...]
        for h in range(heads):
            features = slice(h * HEAD, (h + 1) * HEAD)
            summed[features] = summed[features] * scale[:, h * tile : (h + 1) * tile]
        rows = jnp.transpose(summed[...])
        attended[at] = rows
        for part in range(2):
            place = pl.ds(pl.multiple_of(order[2 * i + part] * block, block), block)
            mixed[place] = rows[part * block : (part + 1) * block].astype(jnp.bfloat16)


def attend(projected, order, lowest, starts, tables, heads):
    seq, wide = projected.shape
    cols = wide // 3
    block = seq // order.shape[0]
    tile = 2 * block
    vmem = pl.BlockSpec(memory_space=pltpu.VMEM)
    smem = pl.BlockSpec(memory_space=pltpu.SMEM)
    return pl.pallas_call(
        functools.partial(attend_kernel, block, heads),
        in_specs=[smem, smem] + [vmem] * 5,
        out_specs=[vmem] * 4,
        out_shape=[
            jax.ShapeDtypeStruct((seq, wide), jnp.bfloat16),
            jax.ShapeDtypeStruct((seq, cols), jnp.float32),
            jax.ShapeDtypeStruct((seq, cols), jnp.bfloat16),
            jax.ShapeDtypeStruct((seq // tile, 1, heads * tile), jnp.float32),
        ],
        scratch_shapes=[
            pltpu.VMEM((cols, seq), jnp.bfloat16),
            pltpu.VMEM((cols, tile), jnp.float32),
            pltpu.VMEM((1, heads * tile), jnp.float32),
            pltpu.VMEM((1, heads * tile), jnp.float32),
        ],
        compiler_params=pltpu.CompilerParams(vmem_limit_bytes=48 << 20),
        cost_estimate=pl.CostEstimate(
            flops=4 * seq * seq * cols, bytes_accessed=12 * seq * cols, transcendentals=0
        ),
    )(order, lowest, projected, starts, *tables)


def attend_back_kernel(
    block,
    heads,
    order,
    lowest,
    qkv,
    grad_mixed,
    attended,
    log_total,
    starts,
    cosine,
    sine_low,
    sine_high,
    out,
    sums,
    key_t,
    grad_rows,
    grad_key,
    grad_value,
    grad_query,
):
    cols = heads * HEAD
    seq = qkv.shape[0]
    tile = 2 * block

    @pl.loop(0, seq // block)
    def _(p):
        at = pl.ds(pl.multiple_of(p * block, block), block)
        key_t[:, at] = transposed(qkv[at, cols : 2 * cols])
        grad_rows[at] = grad_mixed[pl.ds(pl.multiple_of(order[p] * block, block), block)]
        grad_key[at] = jnp.zeros((block, cols), jnp.float32)
        grad_value[at] = jnp.zeros((block, cols), jnp.float32)

    sums[...] = jnp.zeros_like(sums)

    def finish(p, columns, rows):
        low = rows.astype(jnp.bfloat16)
        out[pl.ds(pl.multiple_of(order[p] * block, block), block), columns] = low
        sums[:, columns] += jnp.sum(low.astype(jnp.float32), 0, keepdims=True)

    def turned_back(p, rows):
        at = pl.ds(pl.multiple_of(p * block, block), block)
        return turn(rows, cosine[at], -sine_low[at], -sine_high[at], cols)

    @pl.loop(0, seq // tile)
    def _(i):
        at = pl.ds(pl.multiple_of(i * tile, tile), tile)
        query = qkv[at, :cols]
        grad = grad_rows[at]
        query_t = head_stack(transposed(query), heads)
        query_rows = row_stack(query, heads)
        grad_t = head_stack(transposed(grad), heads)
        grads = row_stack(grad, heads)
        products = jnp.transpose(grad.astype(jnp.float32) * attended[at])
        delta = jnp.concatenate(
            [
                jnp.sum(products[h * HEAD : (h + 1) * HEAD], 0, keepdims=True)
                for h in range(heads)
            ],
            1,
        )
        logs = log_total[i]
        first_keys = starts[:, at]
        grad_query[...] = jnp.zeros_like(grad_query)

        @pl.loop(lowest[i], i + 1)
        def _(j):
            keys_at = pl.ds(pl.multiple_of(j * tile, tile), tile)
            scores = jnp.dot(
                qkv[keys_at, cols : 2 * cols], query_t, preferred_element_type=jnp.float32
            )
            weights = jnp.where(
                allowed_pairs(i, j, tile, heads, first_keys), jnp.exp(scores - logs), 0.0
            )
            grad_soft = jnp.dot(
                qkv[keys_at, 2 * cols :], grad_t, preferred_element_type=jnp.float32
            )
            grad_value[keys_at] += jnp.dot(
                weights.astype(jnp.bfloat16), grads, preferred_element_type=jnp.float32
            )
            grad_scores = (weights * (grad_soft - delta)).astype(jnp.bfloat16)
            grad_key[keys_at] += jnp.dot(
                grad_scores, query_rows, preferred_element_type=jnp.float32
            )
            for h in range(heads):
                features = slice(h * HEAD, (h + 1) * HEAD)
                grad_query[features] += jnp.dot(
                    key_t[features, keys_at],
                    grad_scores[:, h * tile : (h + 1) * tile],
                    preferred_element_type=jnp.float32,
                )

        rows = jnp.transpose(grad_query[...]) * HEAD ** (-0.5)
        for part in range(2):
            p = 2 * i + part
            finish(p, slice(0, cols), turned_back(p, rows[part * block : (part + 1) * block]))

    @pl.loop(0, seq // block)
    def _(p):
        at = pl.ds(pl.multiple_of(p * block, block), block)
        finish(p, slice(cols, 2 * cols), turned_back(p, grad_key[at]))
        finish(p, slice(2 * cols, 3 * cols), grad_value[at])


def attend_back(qkv, grad_mixed, attended, log_total, order, lowest, starts, tables, heads):
    seq, wide = qkv.shape
    cols = wide // 3
    block = seq // order.shape[0]
    tile = 2 * block
    vmem = pl.BlockSpec(memory_space=pltpu.VMEM)
    smem = pl.BlockSpec(memory_space=pltpu.SMEM)
    return pl.pallas_call(
        functools.partial(attend_back_kernel, block, heads),
        in_specs=[smem, smem] + [vmem] * 8,
        out_specs=[vmem] * 2,
        out_shape=[
            jax.ShapeDtypeStruct((seq, wide), jnp.bfloat16),
            jax.ShapeDtypeStruct((1, wide), jnp.float32),
        ],
        scratch_shapes=[
            pltpu.VMEM((cols, seq), jnp.bfloat16),
            pltpu.VMEM((seq, cols), jnp.bfloat16),
            pltpu.VMEM((seq, cols), jnp.float32),
            pltpu.VMEM((seq, cols), jnp.float32),
            pltpu.VMEM((cols, tile), jnp.float32),
        ],
        compiler_params=pltpu.CompilerParams(vmem_limit_bytes=48 << 20),
        cost_estimate=pl.CostEstimate(
            flops=10 * seq * seq * cols, bytes_accessed=20 * seq * cols, transcendentals=0
        ),
    )(order, lowest, qkv, grad_mixed, attended, log_total, starts, *tables)


def rotary_tables(seq):
    lane = jnp.arange(128, dtype=jnp.int32)[None, :] % HEAD
    half_rot = ROT // 2
    freq = ROTARY_BASE ** (-(lane % half_rot).astype(jnp.float32) * 2.0 / ROT)
    angles = jnp.arange(seq, dtype=jnp.int32).astype(jnp.float32)[:, None] * freq
    sine = jnp.sin(angles)
    return (
        jnp.where(lane < ROT, jnp.cos(angles), 1.0),
        jnp.where(lane < half_rot, -sine, 0.0),
        jnp.where((lane >= half_rot) & (lane < ROT), sine, 0.0),
    )


def place_order(block_pairs, axis_size):
    device_blocks = jnp.stack([block_pairs, 2 * axis_size - 1 - block_pairs], 1).reshape(-1)
    places = jnp.arange(2 * axis_size, dtype=jnp.int32)
    return jnp.sum(
        jnp.where(device_blocks[None, :] == places[:, None], places[None, :], 0), 1
    ).astype(jnp.int32)


def document_starts(docs):
    first = jnp.sum((docs < 1).astype(jnp.int32))
    second = jnp.sum((docs < 2).astype(jnp.int32))
    return jnp.where(docs == 0, 0, jnp.where(docs == 1, first, second))


def inner(left_side, right_side):
    return lax.dot_general(
        left_side, right_side, (((0,), (0,)), ((), ())), preferred_element_type=jnp.float32
    )


def times_transposed(left_side, right_side):
    return lax.dot_general(
        left_side, right_side, (((1,), (1,)), ((), ())), preferred_element_type=jnp.float32
    )


def times(left_side, right_side):
    return jnp.dot(left_side, right_side, preferred_element_type=jnp.float32)


def after(value, *earlier):
    return lax.optimization_barrier((value,) + earlier)[0]


def body(
    tokens,
    doc_ids,
    block_pairs,
    ln1_gain,
    ln1_bias,
    w_qkv,
    b_qkv,
    w_out,
    ln2_gain,
    ln2_bias,
    w_gate,
    w_up,
    w_down,
    cotangent,
):
    rows_here = tokens.shape[1]
    width = tokens.shape[2]
    head_count = width // HEAD
    ctx_size = lax.axis_size("ctx")
    fsdp_size = lax.axis_size("fsdp")
    seq_rows = rows_here * ctx_size
    position = lax.axis_index("ctx")
    heads_here = head_count // ctx_size
    cols = width // ctx_size
    shard_rows = w_qkv.shape[0]
    hidden_shard = w_down.shape[0]
    strip = hidden_shard // ctx_size

    tile = 2 * (rows_here // 2)
    order = place_order(block_pairs, ctx_size)
    starts = document_starts(doc_ids[0])
    lowest = starts[::tile] // tile
    starts = starts[None]
    tables = rotary_tables(seq_rows)

    small = lax.all_gather(
        jnp.concatenate([ln1_gain, ln1_bias, ln2_gain, ln2_bias, b_qkv]), "fsdp", axis=0
    ).astype(jnp.float32)
    gain_one, shift_one, gain_two, shift_two = (
        small[:, i * shard_rows : (i + 1) * shard_rows].reshape(1, width) for i in range(4)
    )
    bias_full = small[:, 4 * shard_rows :].reshape(3, ctx_size, cols)
    bias_here = lax.dynamic_index_in_dim(bias_full, position, 1, keepdims=False).reshape(3 * cols)

    def strips(w, count, size):
        stride = w.shape[1] // count
        return [
            lax.dynamic_slice_in_dim(w, i * stride + position * size, size, 1)
            for i in range(count)
        ]

    qkv_strip = jnp.concatenate(strips(w_qkv, 3, cols), 1)
    both_strip = jnp.concatenate(
        strips(w_gate, fsdp_size, strip) + strips(w_up, fsdp_size, strip), 1
    )
    down_strip = lax.dynamic_slice_in_dim(w_down, position * strip, strip, 0)
    out_piece = shard_rows // ctx_size
    out_strip = lax.dynamic_slice_in_dim(w_out, position * out_piece, out_piece, 0)
    hidden_here = fsdp_size * strip

    out_here = lax.all_gather(out_strip, "fsdp", axis=0)
    qkv_here = lax.all_gather(qkv_strip, "fsdp", axis=0, tiled=True)
    both_here = lax.all_gather(both_strip, "fsdp", axis=0, tiled=True)
    down_here = lax.all_gather(down_strip, "fsdp", axis=0, tiled=True)

    grad_out = cotangent[0]
    tokens_all, grad_out_all = plane(
        ctx_size, 1, gather_op(tokens[0], ctx_size), gather_op(grad_out, ctx_size)
    )
    tokens_all = tokens_all.reshape(seq_rows, width)
    grad_out_all = grad_out_all.reshape(seq_rows, width)
    tokens_in = tokens[0].astype(jnp.float32)
    normed, unit_one, inverse_one = norm_rows(tokens_in, gain_one, shift_one)
    normed_all = norm_rows(tokens_all.astype(jnp.float32), gain_one, shift_one)[0].astype(
        jnp.bfloat16
    )
    projected = times(normed_all, qkv_here) + bias_here
    qkv_rows, attended, mixed_here, log_total = attend(
        projected, order, lowest, starts, tables, heads_here
    )
    mixed_here = mixed_here.reshape(ctx_size, rows_here, cols)
    to_columns = functools.partial(column_view, width=cols)
    mixed_rows, out_full = plane(
        ctx_size,
        2,
        exchange_op(mixed_here, ctx_size, (rows_here, width), block_view, to_columns),
        gather_op(
            out_here,
            ctx_size,
            column_half,
            middle_columns,
            (fsdp_size, ctx_size, out_piece, width),
        ),
    )
    out_full = out_full.reshape(width, width)
    residual = tokens_in + times(mixed_rows, out_full)
    normed_two, unit_two, inverse_two = norm_rows(residual, gain_two, shift_two)
    normed_two_all = plane(ctx_size, 3, gather_op(normed_two.astype(jnp.bfloat16), ctx_size))
    normed_two_all = normed_two_all.reshape(seq_rows, width)
    both_value = times(normed_two_all, both_here)
    gate_value = both_value[:, :hidden_here]
    up_value = both_value[:, hidden_here:]
    sigmoid_gate = jax.nn.sigmoid(gate_value)
    silu_gate = gate_value * sigmoid_gate
    hidden = (silu_gate * up_value).astype(jnp.bfloat16)

    def blocks(rows):
        return rows.astype(jnp.bfloat16).reshape(ctx_size, rows_here, width)

    grad_down_w = inner(hidden, grad_out_all).astype(jnp.bfloat16)
    grad_hidden = times_transposed(after(grad_out_all, grad_down_w), down_here)
    grad_gate = grad_hidden * up_value * sigmoid_gate * (1.0 + gate_value * (1.0 - sigmoid_gate))
    grad_up = grad_hidden * silu_gate
    grad_both = jnp.concatenate([grad_gate, grad_up], 1).astype(jnp.bfloat16)
    grad_both_w = inner(normed_two_all, grad_both).astype(jnp.bfloat16)
    grad_normed_two = plane(
        ctx_size,
        4,
        scatter_op(blocks(times_transposed(after(grad_both, grad_both_w), both_here)), ctx_size),
    )
    grad_residual = grad_out.astype(jnp.float32) + norm_back(
        grad_normed_two, unit_two, inverse_two, gain_two
    )
    grad_branch = grad_residual.astype(jnp.bfloat16)
    grad_mixed_rows = times_transposed(grad_branch, out_full).astype(jnp.bfloat16)
    grad_mixed = plane(
        ctx_size,
        5,
        exchange_op(
            grad_mixed_rows, ctx_size, (ctx_size, rows_here, cols), to_columns, block_view
        ),
    )
    grad_projected, grad_bias = attend_back(
        qkv_rows,
        grad_mixed.reshape(seq_rows, cols),
        attended,
        log_total,
        order,
        lowest,
        starts,
        tables,
        heads_here,
    )
    grad_qkv_w = inner(normed_all, grad_projected).astype(jnp.bfloat16)
    mixed_blocks = jnp.transpose(
        mixed_rows.reshape(rows_here, fsdp_size, ctx_size, out_piece), (0, 2, 1, 3)
    ).reshape(rows_here, width)
    grad_normed, grad_out_w = plane_groups(
        ctx_size,
        6,
        scatter_op(
            blocks(times_transposed(after(grad_projected, grad_qkv_w), qkv_here)), ctx_size
        ),
        scatter_op(
            inner(mixed_blocks, after(grad_branch, grad_qkv_w))
            .astype(jnp.bfloat16)
            .reshape(ctx_size, fsdp_size * out_piece, width),
            ctx_size,
        ),
    )
    grad_tokens = grad_residual + norm_back(grad_normed, unit_one, inverse_one, gain_one)

    def reduced(grad):
        return lax.psum_scatter(
            grad.astype(jnp.bfloat16), "fsdp", scatter_dimension=0, tiled=True
        )

    grad_down_w = reduced(grad_down_w)
    grad_both_w = reduced(grad_both_w)
    grad_qkv_w = reduced(grad_qkv_w)
    norm_sums = jnp.stack(
        [
            jnp.sum(grad_normed * unit_one, 0),
            jnp.sum(grad_normed, 0),
            jnp.sum(grad_normed_two * unit_two, 0),
            jnp.sum(grad_normed_two, 0),
        ]
    )
    norm_sums = jnp.transpose(norm_sums.reshape(4, fsdp_size, shard_rows), (1, 0, 2)).reshape(
        fsdp_size, 1, 4 * shard_rows
    )
    bias_sums = lax.dynamic_update_slice(
        jnp.zeros((3, ctx_size, cols), jnp.float32),
        grad_bias.reshape(3, 1, cols),
        (0, position, 0),
    ).reshape(fsdp_size, 1, 3 * width // fsdp_size)
    padded = [
        jnp.pad(rows, ((0, 0), (0, extra), (0, width - rows.shape[2])))
        for rows, extra in ((norm_sums, 0), (bias_sums, 14))
    ]
    grad_out_w = jnp.concatenate(
        [grad_out_w.reshape(fsdp_size, out_piece, width)] + padded, 1
    )
    grad_out_w = reduced(grad_out_w.reshape(fsdp_size * (out_piece + 16), width))
    layer_part, grad_down_w, grad_both_w = plane_groups(
        ctx_size,
        8,
        scatter_op(blocks(times(after(hidden, grad_normed), down_here)), ctx_size),
        gather_op(grad_down_w, ctx_size, column_half, stacked_columns),
        gather_op(grad_both_w, ctx_size),
    )
    layer_out = residual + layer_part
    grad_out_w, grad_qkv_w = plane(
        ctx_size,
        10,
        gather_op(after(grad_out_w, grad_down_w), ctx_size, column_half, stacked_columns),
        gather_op(grad_qkv_w, ctx_size),
    )
    sums = jnp.sum(grad_out_w[:, out_piece : out_piece + 2].astype(jnp.float32), 0)
    norm_sums = sums[0, : 4 * shard_rows].reshape(4, shard_rows)
    bias_sums = sums[1, : b_qkv.shape[0]]
    grad_out_w = grad_out_w[:, :out_piece]
    float32 = jnp.float32
    return (
        layer_out.astype(jnp.bfloat16)[None],
        grad_tokens[None],
        norm_sums[0],
        norm_sums[1],
        unpack_columns(grad_qkv_w, 3),
        bias_sums,
        grad_out_w.reshape(w_out.shape).astype(float32),
        norm_sums[2],
        norm_sums[3],
        unpack_columns(grad_both_w[:, :, :hidden_here], fsdp_size),
        unpack_columns(grad_both_w[:, :, hidden_here:], fsdp_size),
        grad_down_w.reshape(w_down.shape).astype(float32),
    )


def solution(mesh):
    placed = (
        P("fsdp", "ctx", None),
        P("fsdp", None),
        P(),
        P("fsdp"),
        P("fsdp"),
        P("fsdp", None),
        P("fsdp"),
        P("fsdp", None),
        P("fsdp"),
        P("fsdp"),
        P("fsdp", None),
        P("fsdp", None),
        P("fsdp", None),
        P("fsdp", "ctx", None),
    )
    return jax.shard_map(
        body,
        mesh=mesh,
        in_specs=placed,
        out_specs=(
            P("fsdp", "ctx", None),
            P("fsdp", "ctx", None),
            P("fsdp"),
            P("fsdp"),
            P("fsdp", None),
            P("fsdp"),
            P("fsdp", None),
            P("fsdp"),
            P("fsdp"),
            P("fsdp", None),
            P("fsdp", None),
            P("fsdp", None),
        ),
        check_vma=False,
    )
```

```python
import functools

import jax
import jax.numpy as jnp
from jax import lax
from jax.experimental import pallas as pl
from jax.experimental.pallas import tpu as pltpu
from jax.sharding import PartitionSpec as P

HEAD = 64
ROT = 16


NORM_EPSILON = 1e-05
ROTARY_BASE = 10000.0
MASKED_SCORE = -1e30


MESH_IDS = pl.DeviceIdType.MESH


def bit_of(index, bit):
    return index // (1 << bit) % 2


def flipped(index, mask, bits):
    result = index
    for bit in range(bits):
        if mask >> bit & 1:
            result = result + (1 - 2 * bit_of(index, bit)) * (1 << bit)
    return result


def greet(partners, along_z=()):
    barrier = pltpu.get_barrier_semaphore()
    for axis, others in (("ctx", partners), ("fsdp", along_z)):
        for other in others:
            pl.semaphore_signal(barrier, inc=1, device_id={axis: other}, device_id_type=MESH_IDS)
    pl.semaphore_wait(barrier, len(partners) + len(along_z))


def half_orders(bits):
    chip_bits = list(range(1, bits))
    return [chip_bits, chip_bits[1:] + chip_bits[:1]]


def gather_plan(bits):
    steps = []
    for order in half_orders(bits):
        held = [0]
        plan = []
        for bit in order:
            plan.append((bit, list(held)))
            held = held + [mask | 1 << bit for mask in held]
        steps.append((plan, held))
    return steps


def column_half(ref, half):
    width = ref.shape[-1] // 2
    return ref.at[..., pl.ds(half * width, width)]


def row_half(ref, half):
    rows = ref.shape[-2] // 2
    if len(ref.shape) == 2:
        return ref.at[pl.ds(half * rows, rows)]
    return ref.at[..., pl.ds(half * rows, rows), :]


def stacked_rows(ref, block, half):
    return row_half(ref.at[block], half)


def stacked_columns(ref, block, half):
    return column_half(ref.at[block], half)


def middle_columns(ref, block, half):
    return column_half(ref.at[:, block], half)


def block_view(ref, block):
    return ref.at[block]


def column_view(ref, block, width):
    return ref.at[:, pl.ds(pl.multiple_of(block * width, width), width)]


def gather_run(
    bits, take, put, relative, source, out, send_sem, recv_sem, core_send, core_recv, local_sem
):
    me = lax.axis_index("ctx")
    steps = gather_plan(bits)
    finals = []
    for half in range(2):
        own = put(out, 0 if relative else me, half)
        copy = pltpu.make_async_copy(take(source, half), own, local_sem.at[half])
        copy.start()
        finals.append(copy.wait)

    def push(half, mask, bit, send, recv, index):
        block = mask if relative else flipped(me, mask, bits)
        there = mask | 1 << bit if relative else block
        copy = pltpu.make_async_remote_copy(
            src_ref=take(source, half) if mask == 0 else put(out, block, half),
            dst_ref=put(out, there, half),
            send_sem=send.at[half, index],
            recv_sem=recv.at[half, index],
            device_id={"ctx": flipped(me, 1 << bit, bits)},
            device_id_type=MESH_IDS,
        )
        copy.start()
        return copy

    arriving = {}
    for phase in range(bits):
        for half in range(2):
            plan, held = steps[half]
            if phase > 0:
                for copy in arriving[half]:
                    copy.wait_recv()
            if phase < bits - 1:
                bit, masks = plan[phase]
                arriving[half] = [
                    push(half, mask, bit, send_sem, recv_sem, (1 << phase) - 1 + number)
                    for number, mask in enumerate(masks)
                ]
                finals += [copy.wait_send for copy in arriving[half]]
            fresh = held[:1] if phase == 0 else held[1 << (phase - 1) : 1 << phase]
            for mask in fresh:
                copy = push(half, mask, 0, core_send, core_recv, held.index(mask))
                finals.append(copy.wait)
            yield
    for wait in finals:
        wait()


def gather_op(x, size, take=row_half, put=stacked_rows, out_shape=None, relative=False):
    bits = size.bit_length() - 1
    steps = size // 2 - 1
    dma = pltpu.SemaphoreType.DMA
    return dict(
        run=functools.partial(gather_run, bits, take, put, relative),
        inputs=[x],
        in_space=pl.ANY,
        outs=[jax.ShapeDtypeStruct(out_shape or (size,) + x.shape, x.dtype)],
        out_space=pl.ANY,
        scratch=[dma((2, steps)), dma((2, steps)), dma((2, steps + 1)), dma((2, steps + 1)), dma((2,))],
        moved=2 * size * x.size * 2,
    )


def add_into(target, first, second, rows, step):
    @pl.loop(0, rows // step)
    def _(i):
        at = pl.ds(pl.multiple_of(i * step, step), step)
        target[at] = (first[at].astype(jnp.float32) + second[at].astype(jnp.float32)).astype(
            target.dtype
        )


def scatter_plan(bits):
    plans = []
    for order in half_orders(bits):
        kept = [mask << 1 for mask in range(1 << (bits - 1))]
        plan = []
        for bit in order:
            plan.append((bit, [mask for mask in kept if mask >> bit & 1]))
            kept = [mask for mask in kept if not mask >> bit & 1]
        plans.append(plan)
    return plans


def farthest_first(masks):
    return sorted(masks, key=lambda mask: -bin(mask).count("1"))


def scatter_run(bits, step, part_ref, out_ref, core_buf, chip_buf, core_send, core_recv, send_sem, recv_sem):
    me = lax.axis_index("ctx")
    rows = part_ref.shape[1]
    width = part_ref.shape[2] // 2
    plans = scatter_plan(bits)
    chip_masks = farthest_first([mask << 1 for mask in range(1 << (bits - 1))])
    finals = []
    core_copies = {}
    for mask in chip_masks:
        copy = pltpu.make_async_remote_copy(
            src_ref=part_ref.at[flipped(me, mask | 1, bits)],
            dst_ref=core_buf.at[mask >> 1],
            send_sem=core_send.at[mask >> 1],
            recv_sem=core_recv.at[mask >> 1],
            device_id={"ctx": flipped(me, 1, bits)},
            device_id_type=MESH_IDS,
        )
        copy.start()
        core_copies[mask] = copy
        finals.append(copy.wait_send)
    arriving = {}

    def columns(half):
        return pl.ds(half * width, width)

    def send(half, phase, bit, mask):
        slot = plans[half][phase][1].index(mask)
        copy = pltpu.make_async_remote_copy(
            src_ref=part_ref.at[flipped(me, mask, bits), :, columns(half)],
            dst_ref=chip_buf.at[half, phase, slot],
            send_sem=send_sem.at[half, phase, slot],
            recv_sem=recv_sem.at[half, phase, slot],
            device_id={"ctx": flipped(me, 1 << bit, bits)},
            device_id_type=MESH_IDS,
        )
        copy.start()
        finals.append(copy.wait_send)
        arriving[half, phase, mask & ~(1 << bit)] = (copy, slot)

    yield
    for mask in chip_masks:
        core_copies[mask].wait_recv()
        here = part_ref.at[flipped(me, mask, bits)]
        add_into(here, here, core_buf.at[mask >> 1], rows, step)
        for half in range(2):
            bit, masks = plans[half][0]
            if mask in masks:
                send(half, 0, bit, mask)
    yield
    phases = bits - 1
    for phase in range(1, phases + 1):
        for half in range(2):
            last_bit, last_masks = plans[half][phase - 1]
            kept = farthest_first([mask & ~(1 << last_bit) for mask in last_masks])
            for mask in kept:
                copy, slot = arriving[half, phase - 1, mask]
                copy.wait_recv()
                here = part_ref.at[flipped(me, mask, bits), :, columns(half)]
                buf = chip_buf.at[half, phase - 1, slot]
                if phase < phases:
                    add_into(here, here, buf, rows, step)
                    bit, masks = plans[half][phase]
                    if mask in masks:
                        send(half, phase, bit, mask)
                else:
                    add_into(out_ref.at[:, columns(half)], here, buf, rows, step)
        yield
    for wait in finals:
        wait()


def scatter_op(part, size):
    bits = size.bit_length() - 1
    chips = size // 2
    rows, width = part.shape[1:]
    dma = pltpu.SemaphoreType.DMA
    return dict(
        run=functools.partial(scatter_run, bits, 32),
        inputs=[part],
        in_space=pltpu.VMEM,
        outs=[jax.ShapeDtypeStruct((rows, width), jnp.float32)],
        out_space=pltpu.VMEM,
        scratch=[
            pltpu.VMEM((chips, rows, width), part.dtype),
            pltpu.VMEM((2, bits - 1, chips // 2, rows, width // 2), part.dtype),
            dma((chips,)),
            dma((chips,)),
            dma((2, bits - 1, chips // 2)),
            dma((2, bits - 1, chips // 2)),
        ],
        moved=4 * part.size,
    )


def exchange_run(size, take, put, source, out, send_sem, recv_sem, local_sem):
    me = lax.axis_index("ctx")
    local = pltpu.make_async_copy(take(source, me), put(out, me), local_sem)
    local.start()
    copies = []
    for step in range(1, size):
        other = lax.rem(me + step, size)
        copy = pltpu.make_async_remote_copy(
            src_ref=take(source, other),
            dst_ref=put(out, me),
            send_sem=send_sem.at[step - 1],
            recv_sem=recv_sem.at[step - 1],
            device_id={"ctx": other},
            device_id_type=MESH_IDS,
        )
        copy.start()
        copies.append(copy)
    yield
    local.wait()
    for copy in copies:
        copy.wait()


def exchange_op(x, size, out_shape, take, put):
    dma = pltpu.SemaphoreType.DMA
    return dict(
        run=functools.partial(exchange_run, size, take, put),
        inputs=[x],
        in_space=pl.ANY,
        outs=[jax.ShapeDtypeStruct(out_shape, x.dtype)],
        out_space=pl.ANY,
        scratch=[dma((size - 1,)), dma((size - 1,)), dma],
        far=True,
        moved=4 * x.size,
    )


def z_gather_run(size, source, out, send_sem, recv_sem, local_sem):
    me = lax.axis_index("fsdp")
    local = pltpu.make_async_copy(source, out.at[me], local_sem)
    local.start()
    copies = []
    for step in range(1, size):
        copy = pltpu.make_async_remote_copy(
            src_ref=source,
            dst_ref=out.at[me],
            send_sem=send_sem.at[step - 1],
            recv_sem=recv_sem.at[step - 1],
            device_id={"fsdp": lax.rem(me + step, size)},
            device_id_type=MESH_IDS,
        )
        copy.start()
        copies.append(copy)
    for _ in range(4):
        yield
    local.wait()
    for copy in copies:
        copy.wait()


def z_gather_op(x, size):
    dma = pltpu.SemaphoreType.DMA
    return dict(
        run=functools.partial(z_gather_run, size),
        inputs=[x],
        in_space=pl.ANY,
        outs=[jax.ShapeDtypeStruct((size,) + x.shape, x.dtype)],
        out_space=pl.ANY,
        scratch=[dma((size - 1,)), dma((size - 1,)), dma],
        z=size,
        moved=2 * size * x.size,
    )


def z_scatter_run(size, source, out, buf, send_sem, recv_sem):
    me = lax.axis_index("fsdp")
    copies = []
    for step in range(1, size):
        other = lax.rem(me + step, size)
        copy = pltpu.make_async_remote_copy(
            src_ref=source.at[other],
            dst_ref=buf.at[step - 1],
            send_sem=send_sem.at[step - 1],
            recv_sem=recv_sem.at[step - 1],
            device_id={"fsdp": other},
            device_id_type=MESH_IDS,
        )
        copy.start()
        copies.append(copy)
    for _ in range(4):
        yield
    total = source[me].astype(jnp.float32)
    for step, copy in enumerate(copies):
        copy.wait()
        total += buf[step].astype(jnp.float32)
    out[...] = total.astype(out.dtype)


def z_scatter_op(x, size):
    dma = pltpu.SemaphoreType.DMA
    return dict(
        run=functools.partial(z_scatter_run, size),
        inputs=[x],
        in_space=pltpu.VMEM,
        outs=[jax.ShapeDtypeStruct(x.shape[1:], x.dtype)],
        out_space=pltpu.VMEM,
        scratch=[
            pltpu.VMEM((size - 1,) + x.shape[1:], x.dtype),
            dma((size - 1,)),
            dma((size - 1,)),
        ],
        z=size,
        moved=4 * x.size,
    )


def z_sum_gather_run(bits, size, source, out, low, buf, send_sem, recv_sem, *sems):
    yield from z_scatter_run(size, source, low, buf, send_sem, recv_sem)
    yield from gather_run(bits, column_half, stacked_columns, False, low, out, *sems)


def z_sum_gather_op(x, z_size, size):
    summed = z_scatter_op(x, z_size)
    (shape,) = summed["outs"]
    gather = gather_op(shape, size)
    return dict(
        run=functools.partial(z_sum_gather_run, size.bit_length() - 1, z_size),
        inputs=[x],
        in_space=pltpu.VMEM,
        outs=gather["outs"],
        out_space=pl.ANY,
        scratch=[pltpu.VMEM(shape.shape, shape.dtype)] + summed["scratch"] + gather["scratch"],
        z=z_size,
        moved=summed["moved"] + gather["moved"],
    )


def project_run(
    cols,
    tokens,
    weights,
    gain,
    shift,
    bias,
    cosine,
    sine_low,
    sine_high,
    qkv,
    normed,
    tokens_buf,
    normed_buf,
    weights_buf,
    load_sem,
    store_sem,
    weights_sem,
):
    size, rows = tokens.shape[:2]

    def load(block):
        slot = block % 2
        return pltpu.make_async_copy(tokens.at[block], tokens_buf.at[slot], load_sem.at[slot])

    def store(block):
        slot = block % 2
        return pltpu.make_async_copy(normed_buf.at[slot], normed.at[block], store_sem.at[slot])

    load_weights = pltpu.make_async_copy(weights, weights_buf, weights_sem)
    load(0).start()
    load_weights.start()
    yield
    for block in range(size):
        if block + 1 < size:
            load(block + 1).start()
        load(block).wait()
        at = pl.ds(block * rows, rows)
        values = tokens_buf[block % 2].astype(jnp.float32)
        centered = values - jnp.mean(values, -1, keepdims=True)
        inverse = lax.rsqrt(jnp.mean(centered * centered, -1, keepdims=True) + NORM_EPSILON)
        low = (centered * inverse * gain[...] + shift[...]).astype(jnp.bfloat16)
        if block >= 2:
            store(block - 2).wait()
        normed_buf[block % 2] = low
        store(block).start()
        if block == 0:
            load_weights.wait()
        projected = jnp.dot(low, weights_buf[...], preferred_element_type=jnp.float32)
        projected += bias[...]
        tables = (cosine[at], sine_low[at], sine_high[at])
        query = turn(projected[:, :cols], *tables, cols) * HEAD ** (-0.5)
        qkv[block, :, :cols] = query.astype(jnp.bfloat16)
        key = turn(projected[:, cols : 2 * cols], *tables, cols)
        qkv[block, :, cols : 2 * cols] = key.astype(jnp.bfloat16)
        qkv[block, :, 2 * cols :] = projected[:, 2 * cols :].astype(jnp.bfloat16)
        yield
    store(size - 2).wait()
    store(size - 1).wait()


def project_op(tokens, weights, gain, shift, bias, tables):
    size, rows, width = tokens.shape
    wide = weights.shape[1]
    low = jnp.bfloat16
    dma = pltpu.SemaphoreType.DMA
    return dict(
        run=functools.partial(project_run, wide // 3),
        inputs=[tokens, weights, gain, shift, bias, *tables],
        in_spaces=[pl.ANY] * 2 + [pltpu.VMEM] * 6,
        outs=[
            jax.ShapeDtypeStruct((size, rows, wide), low),
            jax.ShapeDtypeStruct((size, rows, width), low),
        ],
        out_spaces=[pltpu.VMEM, pl.ANY],
        scratch=[
            pltpu.VMEM((2, rows, width), low),
            pltpu.VMEM((2, rows, width), low),
            pltpu.VMEM(weights.shape, low),
            dma((2,)),
            dma((2,)),
            dma,
        ],
        moved=4 * tokens.size,
    )


def plane_kernel(size, parts, far, z_size, *refs):
    bits = size.bit_length() - 1
    me = lax.axis_index("ctx")
    my_z = lax.axis_index("fsdp")
    partners = [flipped(me, 1 << bit, bits) for bit in range(bits)]
    if far:
        partners = [lax.rem(me + step, size) for step in range(1, size)]
    greet(partners, [lax.rem(my_z + step, z_size) for step in range(1, z_size)])
    ins = sum(part[1] for part in parts)
    outs = sum(part[2] for part in parts)
    groups = [list(refs[:ins]), list(refs[ins : ins + outs]), list(refs[ins + outs :])]
    running = []
    for run, *counts in parts:
        own = []
        for group, count in zip(groups, counts):
            own += group[:count]
            del group[:count]
        running.append(run(*own))
    while running:
        running = [turn_of for turn_of in running if next(turn_of, 1) is None]


def spaces(op, side):
    arrays = op["inputs"] if side == "in" else op["outs"]
    return op.get(side + "_spaces") or [op[side + "_space"]] * len(arrays)


def plane(size, collective_id, *ops):
    parts = [(op["run"], len(op["inputs"]), len(op["outs"]), len(op["scratch"])) for op in ops]
    far = any(op.get("far") for op in ops)
    z_size = max(op.get("z", 1) for op in ops)
    results = pl.pallas_call(
        functools.partial(plane_kernel, size, parts, far, z_size),
        out_shape=[out for op in ops for out in op["outs"]],
        in_specs=[pl.BlockSpec(memory_space=space) for op in ops for space in spaces(op, "in")],
        out_specs=[pl.BlockSpec(memory_space=space) for op in ops for space in spaces(op, "out")],
        scratch_shapes=[scratch for op in ops for scratch in op["scratch"]],
        compiler_params=pltpu.CompilerParams(
            collective_id=collective_id, has_side_effects=True, vmem_limit_bytes=60 << 20
        ),
        cost_estimate=pl.CostEstimate(
            flops=0, bytes_accessed=sum(op["moved"] for op in ops), transcendentals=0
        ),
    )(*[x for op in ops for x in op["inputs"]])
    return results if len(results) > 1 else results[0]


def plane_groups(size, collective_id, *ops):
    groups = []
    room = 0
    for op in ops:
        need = 0 if op.get("in_space") == pl.ANY else op["moved"] * 5 // 4
        if not groups or need > room:
            groups.append([])
            room = 52 << 20
        groups[-1].append(op)
        room -= need
    results = []
    for i, group in enumerate(groups):
        got = plane(size, collective_id + i, *group)
        results += got if isinstance(got, (list, tuple)) else [got]
    return results


def swapped(tile):
    return tile % 2 + 2 * (tile // 4 % 2) + 4 * (tile // 2 % 2)


def tile_put(ref, mask, half):
    return row_half(ref.at[mask if half == 0 else swapped(mask)], half)


def tile_partner(me, bit):
    return {"ctx": flipped(me, 1 << bit, 3)}


def tile_copy(source, target, half, bit, me, send_sem, recv_sem):
    rows = source.shape[0] // 2
    at = pl.ds(half * rows, rows)
    return pltpu.make_async_remote_copy(
        src_ref=source.at[at],
        dst_ref=target.at[at],
        send_sem=send_sem.at[half],
        recv_sem=recv_sem.at[half],
        device_id=tile_partner(me, bit),
        device_id_type=MESH_IDS,
    )


def core_copy(source, target, me, send_sem, recv_sem):
    return pltpu.make_async_remote_copy(
        src_ref=source,
        dst_ref=target,
        send_sem=send_sem,
        recv_sem=recv_sem,
        device_id=tile_partner(me, 0),
        device_id_type=MESH_IDS,
    )


class TileGather:
    def __init__(self, tiles, send_sem, recv_sem, core_send, core_recv):
        me = lax.axis_index("ctx")
        self.hops = {
            target: [
                tile_copy(
                    tiles.at[source],
                    tiles.at[target],
                    half,
                    (first, 3 - first)[half],
                    me,
                    send_sem.at[target // 2 - 1],
                    recv_sem.at[target // 2 - 1],
                )
                for half in range(2)
            ]
            for source, target, first in ((0, 2, 1), (0, 4, 2), (2, 6, 2))
        }
        self.cores = [
            core_copy(tiles.at[2 * i], tiles.at[2 * i + 1], me, core_send.at[i], core_recv.at[i])
            for i in range(4)
        ]

    def before(self, tile):
        if tile == 0:
            for copy in self.hops[2]:
                copy.start()
            self.cores[0].start()
        elif tile % 2 == 1:
            self.cores[tile // 2].wait_recv()
            if tile == 1:
                for copy in self.hops[4]:
                    copy.start()
        else:
            for copy in self.hops[tile]:
                copy.wait_recv()
            if tile == 2:
                for copy in self.hops[6]:
                    copy.start()
            self.cores[tile // 2].start()

    def finish(self):
        for copies in self.hops.values():
            for copy in copies:
                copy.wait_send()
        for copy in self.cores:
            copy.wait_send()


def gather_sems():
    dma = pltpu.SemaphoreType.DMA
    return [dma((3, 2)), dma((3, 2)), dma((4,)), dma((4,))]


class TileScatter:
    def __init__(self, parts, core_buf, chip_buf, send_sem, recv_sem, core_send, core_recv):
        me = lax.axis_index("ctx")
        self.parts, self.core_buf, self.chip_buf = parts, core_buf, chip_buf
        self.hops = {
            source: [
                tile_copy(
                    parts.at[source],
                    chip_buf.at[source // 2 - 1],
                    half,
                    (first, 3 - first)[half],
                    me,
                    send_sem.at[source // 2 - 1],
                    recv_sem.at[source // 2 - 1],
                )
                for half in range(2)
            ]
            for source, first in ((6, 1), (4, 2), (2, 1))
        }
        self.cores = [
            core_copy(parts.at[2 * i + 1], core_buf.at[i], me, core_send.at[i], core_recv.at[i])
            for i in range(4)
        ]

    def add(self, tile, buf):
        here = self.parts.at[tile]
        add_into(here, here, buf, here.shape[0], 32)

    def after(self, tile):
        if tile % 2 == 1:
            self.cores[tile // 2].start()
            return
        self.cores[tile // 2].wait_recv()
        self.add(tile, self.core_buf.at[tile // 2])
        if tile == 6 or tile == 2:
            for copy in self.hops[tile]:
                copy.start()
        if tile == 2:
            self.pass_on()

    def pass_on(self):
        for copy in self.hops[6]:
            copy.wait_recv()
        self.add(4, self.chip_buf.at[2])
        for copy in self.hops[4]:
            copy.start()

    def finish(self, out):
        for tile in (2, 4):
            for copy in self.hops[tile]:
                copy.wait_recv()
        rows = out.shape[0]

        @pl.loop(0, rows // 32)
        def _(i):
            at = pl.ds(pl.multiple_of(i * 32, 32), 32)
            out[at] = (
                self.parts[0, at].astype(jnp.float32)
                + self.chip_buf[0, at].astype(jnp.float32)
                + self.chip_buf[1, at].astype(jnp.float32)
            )

        for copies in self.hops.values():
            for copy in copies:
                copy.wait_send()
        for copy in self.cores:
            copy.wait_send()


def scatter_scratch(rows, width):
    return [
        pltpu.VMEM((8, rows, width), jnp.bfloat16),
        pltpu.VMEM((4, rows, width), jnp.bfloat16),
        pltpu.VMEM((3, rows, width), jnp.bfloat16),
    ] + gather_sems()


def produce_run(produce, count, *refs):
    inputs, (out, *scratch) = refs[:count], refs[count:]
    me = lax.axis_index("ctx")
    scatter = TileScatter(*scratch)
    for tile in range(7, -1, -1):
        scatter.parts[tile] = produce(inputs, tile, me).astype(jnp.bfloat16)
        scatter.after(tile)
        yield
    scatter.finish(out)


def produce_op(produce, rows, width, *inputs):
    return dict(
        run=functools.partial(produce_run, produce, len(inputs)),
        inputs=list(inputs),
        in_space=pltpu.VMEM,
        outs=[jax.ShapeDtypeStruct((rows, width), jnp.float32)],
        out_space=pltpu.VMEM,
        scratch=scatter_scratch(rows, width),
        moved=32 * rows * width,
    )


def tile_rows(ref, tile, me):
    half = ref.shape[1] // 2
    return jnp.concatenate(
        [ref[flipped(me, tile, 3), :half], ref[flipped(me, swapped(tile), 3), half:]], 0
    )


def product_of_rows(refs, tile, me):
    return times_transposed(tile_rows(refs[0], tile, me), refs[1][...])


def product_of_tiles(refs, tile, me):
    return jnp.dot(refs[0][tile], refs[1][...], preferred_element_type=jnp.float32)


def product_of_columns(refs, tile, me):
    return jnp.dot(
        tile_rows(refs[0], tile, me), refs[1][...], preferred_element_type=jnp.float32
    )


def unpack_both_kernel(segments, count, source, gate, up):
    hidden_size = source.shape[2] // 2
    main = hidden_size // 128 * 128
    strip = hidden_size // segments
    for out, first, last in ((gate, 0, 2 * main), (up, main, main + hidden_size)):
        owners = [
            jnp.concatenate(
                [
                    source[owner, :, first : first + main],
                    source[owner, :, last : last + hidden_size - main],
                ],
                1,
            )
            for owner in range(count)
        ]
        out[...] = jnp.concatenate(
            [
                rows[:, segment * strip : (segment + 1) * strip]
                for segment in range(segments)
                for rows in owners
            ],
            1,
        ).astype(jnp.float32)


def unpack_both(gathered, segments):
    count, rows, width = gathered.shape
    step = 64
    block = pl.BlockSpec((step, count * width // 2), lambda i: (i, 0))
    return pl.pallas_call(
        functools.partial(unpack_both_kernel, segments, count),
        grid=(rows // step,),
        in_specs=[pl.BlockSpec((count, step, width), lambda i: (0, i, 0))],
        out_specs=[block, block],
        out_shape=[jax.ShapeDtypeStruct((rows, count * width // 2), jnp.float32)] * 2,
        compiler_params=pltpu.CompilerParams(vmem_limit_bytes=32 << 20),
        cost_estimate=pl.CostEstimate(
            flops=0, bytes_accessed=6 * gathered.size, transcendentals=0
        ),
    )(gathered)


def greet_near(size):
    me = lax.axis_index("ctx")
    bits = size.bit_length() - 1
    greet([flipped(me, 1 << bit, bits) for bit in range(bits)])


def forward_kernel(
    hidden_size,
    normed,
    weights,
    grads,
    normed_t,
    values,
    hidden,
    grad_down,
    tiles,
    weights_buf,
    grads_buf,
    turned,
    values_buf,
    hidden_t,
    load_sem,
    out_sem,
    *sems,
):
    greet_near(8)
    own = pltpu.make_async_copy(normed, tiles.at[0], load_sem.at[0])
    load = pltpu.make_async_copy(weights, weights_buf, load_sem.at[1])
    own.start()
    load.start()
    pltpu.make_async_copy(grads, grads_buf, load_sem.at[2]).start()
    own.wait()
    gather = TileGather(tiles, *sems)
    rows = tiles.shape[1]
    main = hidden_size // 128 * 128

    def write_out(tile, slot):
        at = pl.ds(pl.multiple_of(tile * rows, rows), rows)
        return [
            pltpu.make_async_copy(values_buf.at[slot], values.at[tile], out_sem.at[0, slot]),
            pltpu.make_async_copy(turned.at[slot], normed_t.at[:, at], out_sem.at[1, slot]),
        ]

    @pl.loop(0, 8)
    def _(t):
        for tile in range(8):

            @pl.when(t == tile)
            def _():
                gather.before(tile)
                if tile == 0:
                    load.wait()

        slot = t % 2

        @pl.when(t >= 2)
        def _():
            for copy in write_out(t - 2, slot):
                copy.wait()

        here = tiles[t]
        value = jnp.dot(here, weights_buf[...], preferred_element_type=jnp.float32)
        values_buf[slot] = value
        gate, up = value[:, :main], value[:, main : 2 * main]
        front = gate * jax.nn.sigmoid(gate) * up
        last = value[:, 2 * main :]
        behind = last * jax.nn.sigmoid(last) * pltpu.roll(last, 64, 1)
        both = jnp.concatenate([front, behind], 1)
        hidden[t] = both[:, :hidden_size].astype(jnp.bfloat16)
        at = pl.ds(pl.multiple_of(t * rows, rows), rows)
        hidden_t[:, at] = jnp.transpose(both)[:hidden_size].astype(jnp.bfloat16)
        turned[slot] = jnp.transpose(here)
        for copy in write_out(t, slot):
            copy.start()

    pltpu.make_async_copy(grads, grads_buf, load_sem.at[2]).wait()
    width = grads_buf.shape[2]
    step = 256

    @pl.loop(0, width // step)
    def _(i):
        at = pl.ds(pl.multiple_of(i * step, step), step)
        grad_down[:, at] = jnp.dot(
            hidden_t[...],
            grads_buf[:, :, at].reshape(8 * rows, step),
            preferred_element_type=jnp.float32,
        ).astype(jnp.bfloat16)

    for tile in (6, 7):
        for copy in write_out(tile, tile % 2):
            copy.wait()
    gather.finish()


def forward_mlp(normed, weights, grads, hidden_size, collective_id):
    rows, width = normed.shape
    wide = weights.shape[1]
    any_space = pl.BlockSpec(memory_space=pl.ANY)
    vmem = pl.BlockSpec(memory_space=pltpu.VMEM)
    low = jnp.bfloat16
    dma = pltpu.SemaphoreType.DMA
    return pl.pallas_call(
        functools.partial(forward_kernel, hidden_size),
        in_specs=[any_space] * 3,
        out_specs=[any_space, any_space, vmem, vmem],
        out_shape=[
            jax.ShapeDtypeStruct((width, 8 * rows), low),
            jax.ShapeDtypeStruct((8, rows, wide), jnp.float32),
            jax.ShapeDtypeStruct((8, rows, hidden_size), low),
            jax.ShapeDtypeStruct((hidden_size, width), low),
        ],
        scratch_shapes=[
            pltpu.VMEM((8, rows, width), low),
            pltpu.VMEM(weights.shape, low),
            pltpu.VMEM((8, rows, width), low),
            pltpu.VMEM((2, width, rows), low),
            pltpu.VMEM((2, rows, wide), jnp.float32),
            pltpu.VMEM((hidden_size, 8 * rows), low),
            dma((3,)),
            dma((2, 2)),
        ]
        + gather_sems(),
        compiler_params=pltpu.CompilerParams(
            collective_id=collective_id, has_side_effects=True, vmem_limit_bytes=60 << 20
        ),
        cost_estimate=pl.CostEstimate(
            flops=16 * rows * width * (wide + hidden_size),
            bytes_accessed=64 * rows * width,
            transcendentals=0,
        ),
    )(normed, weights, grads)


def backward_kernel(
    hidden_size,
    grads,
    values,
    weights,
    down,
    normed_t,
    grad_normed,
    grad_both_w,
    grads_buf,
    values_buf,
    weights_buf,
    down_buf,
    normed_buf,
    grad_both,
    out_buf,
    load_sem,
    tile_sem,
    out_sem,
    *scatter_refs,
):
    greet_near(8)
    scatter = TileScatter(*scatter_refs)
    rows = grads_buf.shape[1]
    main = hidden_size // 128 * 128
    load_weights = pltpu.make_async_copy(weights, weights_buf, load_sem.at[0])
    load_down = pltpu.make_async_copy(down, down_buf, load_sem.at[1])

    def load_tile(tile, slot):
        return [
            pltpu.make_async_copy(grads.at[tile], grads_buf.at[slot], tile_sem.at[0, slot]),
            pltpu.make_async_copy(values.at[tile], values_buf.at[slot], tile_sem.at[1, slot]),
        ]

    def load_chunk(i):
        at = pl.ds(pl.multiple_of(i * rows, rows), rows)
        return pltpu.make_async_copy(normed_t.at[at], normed_buf.at[i % 2], tile_sem.at[2, i % 2])

    load_down.start()
    for copy in load_tile(7, 1):
        copy.start()
    load_weights.start()
    load_chunk(0).start()

    @pl.loop(0, 8)
    def _(u):
        t = 7 - u
        slot = t % 2

        @pl.when(u < 7)
        def _():
            for copy in load_tile(t - 1, 1 - slot):
                copy.start()

        @pl.when(u == 0)
        def _():
            load_down.wait()

        for copy in load_tile(t, slot):
            copy.wait()
        grad_hidden = lax.dot_general(
            grads_buf[slot],
            down_buf[...],
            (((1,), (1,)), ((), ())),
            preferred_element_type=jnp.float32,
        )
        value = values_buf[slot]
        gate, up, above = value[:, :main], value[:, main : 2 * main], grad_hidden[:, :main]
        sigmoid = jax.nn.sigmoid(gate)
        grad_both[t, :, :main] = (
            above * up * sigmoid * (1.0 + gate * (1.0 - sigmoid))
        ).astype(jnp.bfloat16)
        grad_both[t, :, main : 2 * main] = (above * (gate * sigmoid)).astype(jnp.bfloat16)
        last = value[:, 2 * main :]
        above = grad_hidden[:, main:]
        above = jnp.concatenate([above, jnp.zeros_like(above)], 1)
        sigmoid = jax.nn.sigmoid(last)
        to_gate = above * pltpu.roll(last, 64, 1) * sigmoid * (1.0 + last * (1.0 - sigmoid))
        to_up = pltpu.roll(above * (last * sigmoid), 64, 1)
        lane = lax.broadcasted_iota(jnp.int32, last.shape, 1)
        grad_both[t, :, 2 * main :] = jnp.where(lane < 64, to_gate, to_up).astype(jnp.bfloat16)

        @pl.when(u == 0)
        def _():
            load_weights.wait()

        scatter.parts[t] = lax.dot_general(
            grad_both[t],
            weights_buf[...],
            (((1,), (1,)), ((), ())),
            preferred_element_type=jnp.float32,
        ).astype(jnp.bfloat16)
        for tile in range(8):

            @pl.when(t == tile)
            def _():
                scatter.after(tile)

    chunks = normed_t.shape[0] // rows

    def store_chunk(i):
        at = pl.ds(pl.multiple_of(i * rows, rows), rows)
        return pltpu.make_async_copy(out_buf.at[i % 2], grad_both_w.at[at], out_sem.at[i % 2])

    @pl.loop(0, chunks)
    def _(i):
        @pl.when(i < chunks - 1)
        def _():
            load_chunk(i + 1).start()

        load_chunk(i).wait()

        @pl.when(i >= 2)
        def _():
            store_chunk(i - 2).wait()

        out_buf[i % 2] = jnp.dot(
            normed_buf[i % 2],
            grad_both[...].reshape(8 * rows, grad_both.shape[2]),
            preferred_element_type=jnp.float32,
        ).astype(jnp.bfloat16)
        store_chunk(i).start()

    store_chunk(chunks - 2).wait()
    store_chunk(chunks - 1).wait()
    scatter.finish(grad_normed)


def backward_mlp(grads, values, weights, down, normed_t, collective_id):
    size, rows, width = grads.shape
    hidden_size = down.shape[0]
    wide = weights.shape[1]
    any_space = pl.BlockSpec(memory_space=pl.ANY)
    vmem = pl.BlockSpec(memory_space=pltpu.VMEM)
    low = jnp.bfloat16
    dma = pltpu.SemaphoreType.DMA
    return pl.pallas_call(
        functools.partial(backward_kernel, hidden_size),
        in_specs=[any_space] * 5,
        out_specs=[vmem, any_space],
        out_shape=[
            jax.ShapeDtypeStruct((rows, width), jnp.float32),
            jax.ShapeDtypeStruct((width, wide), low),
        ],
        scratch_shapes=[
            pltpu.VMEM((2, rows, width), low),
            pltpu.VMEM((2, rows, wide), jnp.float32),
            pltpu.VMEM(weights.shape, low),
            pltpu.VMEM(down.shape, low),
            pltpu.VMEM((2, rows, 8 * rows), low),
            pltpu.VMEM((8, rows, wide), low),
            pltpu.VMEM((2, rows, wide), low),
            dma((2,)),
            dma((3, 2)),
            dma((2,)),
        ]
        + scatter_scratch(rows, width),
        compiler_params=pltpu.CompilerParams(
            collective_id=collective_id, has_side_effects=True, vmem_limit_bytes=60 << 20
        ),
        cost_estimate=pl.CostEstimate(
            flops=16 * rows * width * (2 * wide + hidden_size),
            bytes_accessed=64 * rows * width,
            transcendentals=0,
        ),
    )(grads, values, weights, down, normed_t)


def unpack_kernel(segments, count, source, out):
    strip = source.shape[2] // segments
    pieces = []
    for segment in range(segments):
        for owner in range(count):
            pieces.append(source[owner, :, segment * strip : (segment + 1) * strip])
    out[...] = jnp.concatenate(pieces, 1).astype(jnp.float32)


def unpack_columns(gathered, segments):
    count, rows, width = gathered.shape
    step = 64
    return pl.pallas_call(
        functools.partial(unpack_kernel, segments, count),
        grid=(rows // step,),
        in_specs=[pl.BlockSpec((count, step, width), lambda i: (0, i, 0))],
        out_specs=pl.BlockSpec((step, count * width), lambda i: (i, 0)),
        out_shape=jax.ShapeDtypeStruct((rows, count * width), jnp.float32),
        compiler_params=pltpu.CompilerParams(vmem_limit_bytes=32 << 20),
        cost_estimate=pl.CostEstimate(
            flops=0, bytes_accessed=6 * gathered.size, transcendentals=0
        ),
    )(gathered)


def norm_rows(values, gain_row, shift_row):
    centered = values - jnp.mean(values, -1, keepdims=True)
    inverse = lax.rsqrt(jnp.mean(centered * centered, -1, keepdims=True) + NORM_EPSILON)
    unit_rows = centered * inverse
    return (unit_rows * gain_row + shift_row, unit_rows, inverse)


def norm_back(grad_rows, unit_rows, inverse, gain_row):
    scaled = grad_rows * gain_row
    return inverse * (
        scaled
        - jnp.mean(scaled, -1, keepdims=True)
        - unit_rows * jnp.mean(scaled * unit_rows, -1, keepdims=True)
    )


def turn(rows, cosine, sine_low, sine_high, width):
    repeat = width // 128
    wide = [jnp.concatenate([table] * repeat, 1) for table in (cosine, sine_low, sine_high)]
    return (
        rows * wide[0]
        + pltpu.roll(rows, width - ROT // 2, 1) * wide[1]
        + pltpu.roll(rows, ROT // 2, 1) * wide[2]
    )


def head_stack(features_first, heads):
    owner = lax.broadcasted_iota(jnp.int32, features_first.shape, 0) // HEAD
    zero = jnp.zeros_like(features_first)
    return jnp.concatenate([jnp.where(owner == h, features_first, zero) for h in range(heads)], 1)


def row_stack(rows, heads):
    owner = lax.broadcasted_iota(jnp.int32, rows.shape, 1) // HEAD
    zero = jnp.zeros_like(rows)
    return jnp.concatenate([jnp.where(owner == h, rows, zero) for h in range(heads)], 0)


def allowed_pairs(query_tile, key_tile, tile, heads, starts):
    query_place = query_tile * tile + lax.broadcasted_iota(jnp.int32, (1, tile), 1)
    query_place = jnp.concatenate([query_place] * heads, 1)
    first_key = jnp.concatenate([starts] * heads, 1)
    key_place = key_tile * tile + lax.broadcasted_iota(jnp.int32, (tile, 1), 0)
    return (key_place <= query_place) & (key_place >= first_key)


def transposed(rows):
    return jnp.transpose(rows.astype(jnp.float32)).astype(rows.dtype)


def attend_kernel(
    block,
    heads,
    order,
    lowest,
    projected,
    starts,
    qkv,
    attended,
    mixed,
    log_total,
    value_t,
    summed,
    top,
    total,
):
    cols = heads * HEAD
    seq = projected.shape[0]
    tile = 2 * block

    @pl.loop(0, seq // block)
    def _(p):
        at = pl.ds(pl.multiple_of(p * block, block), block)
        rows = projected[pl.ds(pl.multiple_of(order[p] * block, block), block)]
        qkv[at] = rows
        value_t[:, at] = transposed(rows[:, 2 * cols :])

    @pl.loop(0, seq // tile)
    def _(i):
        at = pl.ds(pl.multiple_of(i * tile, tile), tile)
        query_t = head_stack(transposed(qkv[at, :cols]), heads)
        first_keys = starts[:, at]
        top[...] = jnp.full(top.shape, MASKED_SCORE, jnp.float32)
        total[...] = jnp.zeros_like(total)
        summed[...] = jnp.zeros_like(summed)

        @pl.loop(lowest[i], i + 1)
        def _(j):
            keys_at = pl.ds(pl.multiple_of(j * tile, tile), tile)
            scores = jnp.dot(
                qkv[keys_at, cols : 2 * cols], query_t, preferred_element_type=jnp.float32
            )
            scores = jnp.where(
                allowed_pairs(i, j, tile, heads, first_keys), scores, MASKED_SCORE
            )
            old_top = top[...]
            new_top = jnp.maximum(old_top, jnp.max(scores, 0, keepdims=True))
            exps = jnp.exp(scores - new_top)
            fade = jnp.exp(old_top - new_top)
            total[...] = total[...] * fade + jnp.sum(exps, 0, keepdims=True)
            top[...] = new_top
            low = exps.astype(jnp.bfloat16)
            for h in range(heads):
                own = slice(h * tile, (h + 1) * tile)
                features = slice(h * HEAD, (h + 1) * HEAD)
                summed[features] = summed[features] * fade[:, own] + jnp.dot(
                    value_t[features, keys_at], low[:, own], preferred_element_type=jnp.float32
                )

        log_total[i] = top[...] + jnp.log(total[...])
        scale = 1.0 / total[...]
        for h in range(heads):
            features = slice(h * HEAD, (h + 1) * HEAD)
            summed[features] = summed[features] * scale[:, h * tile : (h + 1) * tile]
        rows = jnp.transpose(summed[...])
        attended[at] = rows
        for part in range(2):
            place = pl.ds(pl.multiple_of(order[2 * i + part] * block, block), block)
            mixed[place] = rows[part * block : (part + 1) * block].astype(jnp.bfloat16)


def attend(projected, order, lowest, starts, heads):
    seq, wide = projected.shape
    cols = wide // 3
    block = seq // order.shape[0]
    tile = 2 * block
    vmem = pl.BlockSpec(memory_space=pltpu.VMEM)
    smem = pl.BlockSpec(memory_space=pltpu.SMEM)
    return pl.pallas_call(
        functools.partial(attend_kernel, block, heads),
        in_specs=[smem, smem] + [vmem] * 2,
        out_specs=[vmem] * 4,
        out_shape=[
            jax.ShapeDtypeStruct((seq, wide), jnp.bfloat16),
            jax.ShapeDtypeStruct((seq, cols), jnp.float32),
            jax.ShapeDtypeStruct((seq, cols), jnp.bfloat16),
            jax.ShapeDtypeStruct((seq // tile, 1, heads * tile), jnp.float32),
        ],
        scratch_shapes=[
            pltpu.VMEM((cols, seq), jnp.bfloat16),
            pltpu.VMEM((cols, tile), jnp.float32),
            pltpu.VMEM((1, heads * tile), jnp.float32),
            pltpu.VMEM((1, heads * tile), jnp.float32),
        ],
        compiler_params=pltpu.CompilerParams(vmem_limit_bytes=48 << 20),
        cost_estimate=pl.CostEstimate(
            flops=4 * seq * seq * cols, bytes_accessed=12 * seq * cols, transcendentals=0
        ),
    )(order, lowest, projected, starts)


def attend_back_kernel(
    block,
    heads,
    order,
    lowest,
    qkv,
    grad_mixed,
    attended,
    log_total,
    starts,
    cosine,
    sine_low,
    sine_high,
    out,
    sums,
    key_t,
    grad_rows,
    grad_key,
    grad_value,
    grad_query,
):
    cols = heads * HEAD
    seq = qkv.shape[0]
    tile = 2 * block

    @pl.loop(0, seq // block)
    def _(p):
        at = pl.ds(pl.multiple_of(p * block, block), block)
        key_t[:, at] = transposed(qkv[at, cols : 2 * cols])
        grad_rows[at] = grad_mixed[pl.ds(pl.multiple_of(order[p] * block, block), block)]
        grad_key[at] = jnp.zeros((block, cols), jnp.float32)
        grad_value[at] = jnp.zeros((block, cols), jnp.float32)

    sums[...] = jnp.zeros_like(sums)

    def finish(p, columns, rows):
        low = rows.astype(jnp.bfloat16)
        out[pl.ds(pl.multiple_of(order[p] * block, block), block), columns] = low
        sums[:, columns] += jnp.sum(low.astype(jnp.float32), 0, keepdims=True)

    def turned_back(p, rows):
        at = pl.ds(pl.multiple_of(order[p] * block, block), block)
        return turn(rows, cosine[at], -sine_low[at], -sine_high[at], cols)

    @pl.loop(0, seq // tile)
    def _(i):
        at = pl.ds(pl.multiple_of(i * tile, tile), tile)
        query = qkv[at, :cols]
        grad = grad_rows[at]
        query_t = head_stack(transposed(query), heads)
        query_rows = row_stack(query, heads)
        grad_t = head_stack(transposed(grad), heads)
        grads = row_stack(grad, heads)
        products = jnp.transpose(grad.astype(jnp.float32) * attended[at])
        delta = jnp.concatenate(
            [
                jnp.sum(products[h * HEAD : (h + 1) * HEAD], 0, keepdims=True)
                for h in range(heads)
            ],
            1,
        )
        logs = log_total[i]
        first_keys = starts[:, at]
        grad_query[...] = jnp.zeros_like(grad_query)

        @pl.loop(lowest[i], i + 1)
        def _(j):
            keys_at = pl.ds(pl.multiple_of(j * tile, tile), tile)
            scores = jnp.dot(
                qkv[keys_at, cols : 2 * cols], query_t, preferred_element_type=jnp.float32
            )
            weights = jnp.where(
                allowed_pairs(i, j, tile, heads, first_keys), jnp.exp(scores - logs), 0.0
            )
            grad_soft = jnp.dot(
                qkv[keys_at, 2 * cols :], grad_t, preferred_element_type=jnp.float32
            )
            grad_value[keys_at] += jnp.dot(
                weights.astype(jnp.bfloat16), grads, preferred_element_type=jnp.float32
            )
            grad_scores = (weights * (grad_soft - delta)).astype(jnp.bfloat16)
            grad_key[keys_at] += jnp.dot(
                grad_scores, query_rows, preferred_element_type=jnp.float32
            )
            for h in range(heads):
                features = slice(h * HEAD, (h + 1) * HEAD)
                grad_query[features] += jnp.dot(
                    key_t[features, keys_at],
                    grad_scores[:, h * tile : (h + 1) * tile],
                    preferred_element_type=jnp.float32,
                )

        rows = jnp.transpose(grad_query[...]) * HEAD ** (-0.5)
        for part in range(2):
            p = 2 * i + part
            finish(p, slice(0, cols), turned_back(p, rows[part * block : (part + 1) * block]))

    @pl.loop(0, seq // block)
    def _(p):
        at = pl.ds(pl.multiple_of(p * block, block), block)
        finish(p, slice(cols, 2 * cols), turned_back(p, grad_key[at]))
        finish(p, slice(2 * cols, 3 * cols), grad_value[at])


def attend_back(qkv, grad_mixed, attended, log_total, order, lowest, starts, tables, heads):
    seq, wide = qkv.shape
    cols = wide // 3
    block = seq // order.shape[0]
    tile = 2 * block
    vmem = pl.BlockSpec(memory_space=pltpu.VMEM)
    smem = pl.BlockSpec(memory_space=pltpu.SMEM)
    return pl.pallas_call(
        functools.partial(attend_back_kernel, block, heads),
        in_specs=[smem, smem] + [vmem] * 8,
        out_specs=[vmem] * 2,
        out_shape=[
            jax.ShapeDtypeStruct((seq, wide), jnp.bfloat16),
            jax.ShapeDtypeStruct((1, wide), jnp.float32),
        ],
        scratch_shapes=[
            pltpu.VMEM((cols, seq), jnp.bfloat16),
            pltpu.VMEM((seq, cols), jnp.bfloat16),
            pltpu.VMEM((seq, cols), jnp.float32),
            pltpu.VMEM((seq, cols), jnp.float32),
            pltpu.VMEM((cols, tile), jnp.float32),
        ],
        compiler_params=pltpu.CompilerParams(vmem_limit_bytes=48 << 20),
        cost_estimate=pl.CostEstimate(
            flops=10 * seq * seq * cols, bytes_accessed=20 * seq * cols, transcendentals=0
        ),
    )(order, lowest, qkv, grad_mixed, attended, log_total, starts, *tables)


def rotary_tables(places):
    lane = jnp.arange(128, dtype=jnp.int32)[None, :] % HEAD
    half_rot = ROT // 2
    freq = ROTARY_BASE ** (-(lane % half_rot).astype(jnp.float32) * 2.0 / ROT)
    angles = places.astype(jnp.float32)[:, None] * freq
    sine = jnp.sin(angles)
    return (
        jnp.where(lane < ROT, jnp.cos(angles), 1.0),
        jnp.where(lane < half_rot, -sine, 0.0),
        jnp.where((lane >= half_rot) & (lane < ROT), sine, 0.0),
    )


def place_order(block_pairs, axis_size):
    device_blocks = jnp.stack([block_pairs, 2 * axis_size - 1 - block_pairs], 1).reshape(-1)
    places = jnp.arange(2 * axis_size, dtype=jnp.int32)
    return jnp.sum(
        jnp.where(device_blocks[None, :] == places[:, None], places[None, :], 0), 1
    ).astype(jnp.int32)


def document_starts(docs):
    first = jnp.sum((docs < 1).astype(jnp.int32))
    second = jnp.sum((docs < 2).astype(jnp.int32))
    return jnp.where(docs == 0, 0, jnp.where(docs == 1, first, second))


def inner(left_side, right_side):
    return lax.dot_general(
        left_side, right_side, (((0,), (0,)), ((), ())), preferred_element_type=jnp.float32
    )


def times_transposed(left_side, right_side):
    return lax.dot_general(
        left_side, right_side, (((1,), (1,)), ((), ())), preferred_element_type=jnp.float32
    )


def times(left_side, right_side):
    return jnp.dot(left_side, right_side, preferred_element_type=jnp.float32)


def after(value, *earlier):
    return lax.optimization_barrier((value,) + earlier)[0]


def body(
    tokens,
    doc_ids,
    block_pairs,
    ln1_gain,
    ln1_bias,
    w_qkv,
    b_qkv,
    w_out,
    ln2_gain,
    ln2_bias,
    w_gate,
    w_up,
    w_down,
    cotangent,
):
    rows_here = tokens.shape[1]
    width = tokens.shape[2]
    head_count = width // HEAD
    ctx_size = lax.axis_size("ctx")
    fsdp_size = lax.axis_size("fsdp")
    seq_rows = rows_here * ctx_size
    position = lax.axis_index("ctx")
    heads_here = head_count // ctx_size
    cols = width // ctx_size
    shard_rows = w_qkv.shape[0]
    hidden_shard = w_down.shape[0]
    strip = hidden_shard // ctx_size

    tile = 2 * (rows_here // 2)
    order = place_order(block_pairs, ctx_size)
    starts = document_starts(doc_ids[0])
    lowest = starts[::tile] // tile
    starts = starts[None]
    device_blocks = jnp.stack([block_pairs, 2 * ctx_size - 1 - block_pairs], 1).reshape(-1, 1)
    half_rows = rows_here // 2
    places = device_blocks * half_rows + jnp.arange(half_rows, dtype=jnp.int32)[None, :]
    tables = rotary_tables(places.reshape(-1))

    def strips(w, count, size):
        stride = w.shape[1] // count
        return [
            lax.dynamic_slice_in_dim(w, i * stride + position * size, size, 1)
            for i in range(count)
        ]

    qkv_strip = jnp.concatenate(strips(w_qkv, 3, cols), 1)
    hidden_here = fsdp_size * strip
    main = hidden_here // 128 * 128
    fused = ctx_size == 8 and hidden_here - main == 64 and rows_here == 256
    gate_strip = jnp.concatenate(strips(w_gate, fsdp_size, strip), 1)
    up_strip = jnp.concatenate(strips(w_up, fsdp_size, strip), 1)
    both_strip = jnp.concatenate(
        [gate_strip[:, :main], up_strip[:, :main], gate_strip[:, main:], up_strip[:, main:]], 1
    )
    down_strip = lax.dynamic_slice_in_dim(w_down, position * strip, strip, 0)
    out_piece = shard_rows // ctx_size
    out_strip = lax.dynamic_slice_in_dim(w_out, position * out_piece, out_piece, 0)
    qkv_here = lax.all_gather(qkv_strip, "fsdp", axis=0, tiled=True)
    both_here = lax.all_gather(both_strip, "fsdp", axis=0, tiled=True)
    down_here = lax.all_gather(down_strip, "fsdp", axis=0, tiled=True)

    small = jnp.concatenate([ln1_gain, ln1_bias, ln2_gain, ln2_bias, b_qkv])
    small_rows = -(-small.size // 2048) * 16
    small = jnp.pad(small, (0, small_rows * 128 - small.size)).reshape(small_rows, 128)
    grad_out = cotangent[0]
    gather_grads = gather_op(grad_out, ctx_size)
    if fused:
        gather_grads = gather_op(grad_out, ctx_size, row_half, tile_put, relative=True)
    small, out_here, tokens_all, grad_out_all = plane(
        ctx_size,
        1,
        z_gather_op(small, fsdp_size),
        z_gather_op(out_strip, fsdp_size),
        gather_op(tokens[0], ctx_size),
        gather_grads,
    )
    small = small.reshape(fsdp_size, small_rows * 128).astype(jnp.float32)
    gain_one, shift_one, gain_two, shift_two = (
        small[:, i * shard_rows : (i + 1) * shard_rows].reshape(1, width) for i in range(4)
    )
    bias_full = small[:, 4 * shard_rows : 4 * shard_rows + b_qkv.size]
    bias_full = bias_full.reshape(3, ctx_size, cols)
    bias_here = lax.dynamic_index_in_dim(bias_full, position, 1, keepdims=False)
    bias_here = bias_here.reshape(1, 3 * cols)
    out_full, projected, normed_all = plane(
        ctx_size,
        2,
        gather_op(
            out_here,
            ctx_size,
            column_half,
            middle_columns,
            (fsdp_size, ctx_size, out_piece, width),
        ),
        project_op(tokens_all, qkv_here, gain_one, shift_one, bias_here, tables),
    )
    out_full = out_full.reshape(width, width)
    normed_all = normed_all.reshape(seq_rows, width)
    tokens_in = tokens[0].astype(jnp.float32)
    unit_one, inverse_one = norm_rows(tokens_in, gain_one, shift_one)[1:]
    qkv_rows, attended, mixed_here, log_total = attend(
        projected.reshape(seq_rows, 3 * cols), order, lowest, starts, heads_here
    )
    mixed_here = mixed_here.reshape(ctx_size, rows_here, cols)
    to_columns = functools.partial(column_view, width=cols)
    mixed_rows = plane(
        ctx_size,
        12,
        exchange_op(mixed_here, ctx_size, (rows_here, width), block_view, to_columns),
    )
    residual = tokens_in + times(mixed_rows, out_full)
    normed_two, unit_two, inverse_two = norm_rows(residual, gain_two, shift_two)
    def blocks(rows):
        return rows.astype(jnp.bfloat16).reshape(ctx_size, rows_here, width)

    normed_two_low = normed_two.astype(jnp.bfloat16)
    if fused:
        normed_two_t, both_value, hidden, grad_down_w = forward_mlp(
            normed_two_low, both_here, grad_out_all, hidden_here, 3
        )
        grad_normed_two, grad_both_w = backward_mlp(
            grad_out_all, both_value, both_here, down_here, normed_two_t, 4
        )
    else:
        grad_out_all = grad_out_all.reshape(seq_rows, width)
        normed_two_all = plane(ctx_size, 3, gather_op(normed_two_low, ctx_size))
        normed_two_all = normed_two_all.reshape(seq_rows, width)
        both_value = times(normed_two_all, both_here)
        gate_value = jnp.concatenate(
            [both_value[:, :main], both_value[:, 2 * main : main + hidden_here]], 1
        )
        up_value = jnp.concatenate(
            [both_value[:, main : 2 * main], both_value[:, main + hidden_here :]], 1
        )
        sigmoid_gate = jax.nn.sigmoid(gate_value)
        silu_gate = gate_value * sigmoid_gate
        hidden = (silu_gate * up_value).astype(jnp.bfloat16)

        grad_down_w = inner(hidden, grad_out_all).astype(jnp.bfloat16)
        grad_hidden = times_transposed(after(grad_out_all, grad_down_w), down_here)
        grad_gate = grad_hidden * up_value * sigmoid_gate * (1.0 + gate_value * (1.0 - sigmoid_gate))
        grad_up = grad_hidden * silu_gate
        grad_both = jnp.concatenate(
            [grad_gate[:, :main], grad_up[:, :main], grad_gate[:, main:], grad_up[:, main:]], 1
        ).astype(jnp.bfloat16)
        grad_both_w = inner(normed_two_all, grad_both).astype(jnp.bfloat16)
        grad_normed_two = plane(
            ctx_size,
            4,
            scatter_op(blocks(times_transposed(after(grad_both, grad_both_w), both_here)), ctx_size),
        )
    grad_residual = grad_out.astype(jnp.float32) + norm_back(
        grad_normed_two, unit_two, inverse_two, gain_two
    )
    grad_branch = grad_residual.astype(jnp.bfloat16)
    grad_mixed_rows = times_transposed(grad_branch, out_full).astype(jnp.bfloat16)
    grad_mixed = plane(
        ctx_size,
        5,
        exchange_op(
            grad_mixed_rows, ctx_size, (ctx_size, rows_here, cols), to_columns, block_view
        ),
    )
    grad_projected, grad_bias = attend_back(
        qkv_rows,
        grad_mixed.reshape(seq_rows, cols),
        attended,
        log_total,
        order,
        lowest,
        starts,
        tables,
        heads_here,
    )
    grad_qkv_w = inner(normed_all, grad_projected).astype(jnp.bfloat16)

    def reduced(grad):
        return lax.psum_scatter(
            grad.astype(jnp.bfloat16), "fsdp", scatter_dimension=0, tiled=True
        )

    hidden = after(hidden, grad_qkv_w)
    grad_down_w, grad_both_w = reduced(grad_down_w), reduced(grad_both_w)
    if fused:
        mixed_t = jnp.transpose(
            mixed_rows.reshape(rows_here, fsdp_size, ctx_size, out_piece), (2, 1, 3, 0)
        ).reshape(ctx_size, fsdp_size * out_piece, rows_here)
        layer_op = produce_op(product_of_tiles, rows_here, width, hidden, down_here)
        out_op = produce_op(product_of_columns, rows_here, width, mixed_t, grad_branch)
    else:
        mixed_blocks = jnp.transpose(
            mixed_rows.reshape(rows_here, fsdp_size, ctx_size, out_piece), (0, 2, 1, 3)
        ).reshape(rows_here, width)
        layer_op = scatter_op(blocks(times(hidden, down_here)), ctx_size)
        out_op = scatter_op(
            inner(mixed_blocks, after(grad_branch, grad_qkv_w))
            .astype(jnp.bfloat16)
            .reshape(ctx_size, fsdp_size * out_piece, width),
            ctx_size,
        )
    grad_down_w, layer_part, grad_out_w = plane_groups(
        ctx_size,
        6,
        gather_op(grad_down_w, ctx_size, column_half, stacked_columns),
        layer_op,
        out_op,
    )
    layer_out = residual + layer_part
    grad_qkv_w = reduced(after(grad_qkv_w, layer_part, grad_both_w))
    grad_projected = after(grad_projected, layer_part)
    if fused:
        normed_op = produce_op(
            product_of_rows,
            rows_here,
            width,
            grad_projected.reshape(ctx_size, rows_here, 3 * cols),
            qkv_here,
        )
    else:
        normed_op = scatter_op(blocks(times_transposed(grad_projected, qkv_here)), ctx_size)
    grad_both_w, grad_normed = plane_groups(
        ctx_size, 9, gather_op(grad_both_w, ctx_size), normed_op
    )
    grad_tokens = grad_residual + norm_back(grad_normed, unit_one, inverse_one, gain_one)

    norm_sums = jnp.stack(
        [
            jnp.sum(grad_normed * unit_one, 0),
            jnp.sum(grad_normed, 0),
            jnp.sum(grad_normed_two * unit_two, 0),
            jnp.sum(grad_normed_two, 0),
        ]
    )
    norm_sums = jnp.transpose(norm_sums.reshape(4, fsdp_size, shard_rows), (1, 0, 2)).reshape(
        fsdp_size, 1, 4 * shard_rows
    )
    bias_sums = lax.dynamic_update_slice(
        jnp.zeros((3, ctx_size, cols), jnp.float32),
        grad_bias.reshape(3, 1, cols),
        (0, position, 0),
    ).reshape(fsdp_size, 1, 3 * width // fsdp_size)
    padded = [
        jnp.pad(rows, ((0, 0), (0, extra), (0, width - rows.shape[2])))
        for rows, extra in ((norm_sums, 0), (bias_sums, 14))
    ]
    grad_out_w = jnp.concatenate(
        [grad_out_w.reshape(fsdp_size, out_piece, width)] + padded, 1
    )
    grad_out_w = grad_out_w.astype(jnp.bfloat16)
    grad_out_w, grad_qkv_w = plane(
        ctx_size,
        13,
        z_sum_gather_op(grad_out_w, fsdp_size, ctx_size),
        gather_op(grad_qkv_w, ctx_size),
    )
    sums = jnp.sum(grad_out_w[:, out_piece : out_piece + 2].astype(jnp.float32), 0)
    norm_sums = sums[0, : 4 * shard_rows].reshape(4, shard_rows)
    bias_sums = sums[1, : b_qkv.shape[0]]
    grad_out_w = grad_out_w[:, :out_piece]
    grad_gate_w, grad_up_w = unpack_both(grad_both_w, fsdp_size)
    float32 = jnp.float32
    return (
        layer_out.astype(jnp.bfloat16)[None],
        grad_tokens[None],
        norm_sums[0],
        norm_sums[1],
        unpack_columns(grad_qkv_w, 3),
        bias_sums,
        grad_out_w.reshape(w_out.shape).astype(float32),
        norm_sums[2],
        norm_sums[3],
        grad_gate_w,
        grad_up_w,
        grad_down_w.reshape(w_down.shape).astype(float32),
    )


def solution(mesh):
    placed = (
        P("fsdp", "ctx", None),
        P("fsdp", None),
        P(),
        P("fsdp"),
        P("fsdp"),
        P("fsdp", None),
        P("fsdp"),
        P("fsdp", None),
        P("fsdp"),
        P("fsdp"),
        P("fsdp", None),
        P("fsdp", None),
        P("fsdp", None),
        P("fsdp", "ctx", None),
    )
    return jax.shard_map(
        body,
        mesh=mesh,
        in_specs=placed,
        out_specs=(
            P("fsdp", "ctx", None),
            P("fsdp", "ctx", None),
            P("fsdp"),
            P("fsdp"),
            P("fsdp", None),
            P("fsdp"),
            P("fsdp", None),
            P("fsdp"),
            P("fsdp"),
            P("fsdp", None),
            P("fsdp", None),
            P("fsdp", None),
        ),
        check_vma=False,
    )
```

```python
import functools

import jax
import jax.numpy as jnp
from jax import lax
from jax.experimental import pallas as pl
from jax.experimental.pallas import tpu as pltpu
from jax.sharding import PartitionSpec as P

HEAD = 64
ROT = 16


NORM_EPSILON = 1e-05
ROTARY_BASE = 10000.0
MASKED_SCORE = -1e30


MESH_IDS = pl.DeviceIdType.MESH


def bit_of(index, bit):
    return index // (1 << bit) % 2


def flipped(index, mask, bits):
    result = index
    for bit in range(bits):
        if mask >> bit & 1:
            result = result + (1 - 2 * bit_of(index, bit)) * (1 << bit)
    return result


def greet(partners, along_z=()):
    barrier = pltpu.get_barrier_semaphore()
    for axis, others in (("ctx", partners), ("fsdp", along_z)):
        for other in others:
            pl.semaphore_signal(barrier, inc=1, device_id={axis: other}, device_id_type=MESH_IDS)
    pl.semaphore_wait(barrier, len(partners) + len(along_z))


def half_orders(bits):
    chip_bits = list(range(1, bits))
    return [chip_bits, chip_bits[1:] + chip_bits[:1]]


def gather_plan(bits):
    steps = []
    for order in half_orders(bits):
        held = [0]
        plan = []
        for bit in order:
            plan.append((bit, list(held)))
            held = held + [mask | 1 << bit for mask in held]
        steps.append((plan, held))
    return steps


def column_half(ref, half):
    width = ref.shape[-1] // 2
    return ref.at[..., pl.ds(half * width, width)]


def row_half(ref, half):
    rows = ref.shape[-2] // 2
    if len(ref.shape) == 2:
        return ref.at[pl.ds(half * rows, rows)]
    return ref.at[..., pl.ds(half * rows, rows), :]


def stacked_rows(ref, block, half):
    return row_half(ref.at[block], half)


def stacked_columns(ref, block, half):
    return column_half(ref.at[block], half)


def middle_columns(ref, block, half):
    return column_half(ref.at[:, block], half)


def block_view(ref, block):
    return ref.at[block]


def column_view(ref, block, width):
    return ref.at[:, pl.ds(pl.multiple_of(block * width, width), width)]


def gather_run(
    bits, take, put, relative, source, out, send_sem, recv_sem, core_send, core_recv, local_sem
):
    me = lax.axis_index("ctx")
    steps = gather_plan(bits)
    finals = []
    for half in range(2):
        own = put(out, 0 if relative else me, half)
        copy = pltpu.make_async_copy(take(source, half), own, local_sem.at[half])
        copy.start()
        finals.append(copy.wait)

    def push(half, mask, bit, send, recv, index):
        block = mask if relative else flipped(me, mask, bits)
        there = mask | 1 << bit if relative else block
        copy = pltpu.make_async_remote_copy(
            src_ref=take(source, half) if mask == 0 else put(out, block, half),
            dst_ref=put(out, there, half),
            send_sem=send.at[half, index],
            recv_sem=recv.at[half, index],
            device_id={"ctx": flipped(me, 1 << bit, bits)},
            device_id_type=MESH_IDS,
        )
        copy.start()
        return copy

    def hop(half, phase, mask):
        bit, masks = steps[half][0][phase]
        index = (1 << phase) - 1 + masks.index(mask)
        copy = push(half, mask, bit, send_sem, recv_sem, index)
        finals.append(copy.wait_send)
        arriving[half, mask | 1 << bit] = copy

    def to_core(half, mask):
        copy = push(half, mask, 0, core_send, core_recv, steps[half][1].index(mask))
        finals.append(copy.wait)

    arriving = {}
    phases = bits - 1
    for phase in range(phases):
        for half in range(2):
            hop(half, phase, 0)
    for half in range(2):
        to_core(half, 0)
    yield
    for phase in range(phases):
        for half in range(2):
            bit, masks = steps[half][0][phase]
            for mask in masks:
                arrived = mask | 1 << bit
                arriving[half, arrived].wait_recv()
                for later in range(phase + 1, phases):
                    hop(half, later, arrived)
                to_core(half, arrived)
        yield
    for wait in finals:
        wait()


def gather_op(x, size, take=row_half, put=stacked_rows, out_shape=None, relative=False):
    bits = size.bit_length() - 1
    steps = size // 2 - 1
    dma = pltpu.SemaphoreType.DMA
    return dict(
        run=functools.partial(gather_run, bits, take, put, relative),
        inputs=[x],
        in_space=pl.ANY,
        outs=[jax.ShapeDtypeStruct(out_shape or (size,) + x.shape, x.dtype)],
        out_space=pl.ANY,
        scratch=[dma((2, steps)), dma((2, steps)), dma((2, steps + 1)), dma((2, steps + 1)), dma((2,))],
        moved=2 * size * x.size * 2,
    )


def add_into(target, first, second, rows, step):
    @pl.loop(0, rows // step)
    def _(i):
        at = pl.ds(pl.multiple_of(i * step, step), step)
        target[at] = first[at].astype(target.dtype) + second[at].astype(target.dtype)


def scatter_plan(bits):
    plans = []
    for order in half_orders(bits):
        kept = [mask << 1 for mask in range(1 << (bits - 1))]
        plan = []
        for bit in order:
            plan.append((bit, [mask for mask in kept if mask >> bit & 1]))
            kept = [mask for mask in kept if not mask >> bit & 1]
        plans.append(plan)
    return plans


def farthest_first(masks):
    return sorted(masks, key=lambda mask: -bin(mask).count("1"))


def scatter_run(bits, step, part_ref, out_ref, core_buf, chip_buf, core_send, core_recv, send_sem, recv_sem):
    me = lax.axis_index("ctx")
    rows = part_ref.shape[1]
    width = part_ref.shape[2] // 2
    plans = scatter_plan(bits)
    chip_masks = farthest_first([mask << 1 for mask in range(1 << (bits - 1))])
    finals = []
    core_copies = {}
    for mask in chip_masks:
        copy = pltpu.make_async_remote_copy(
            src_ref=part_ref.at[flipped(me, mask | 1, bits)],
            dst_ref=core_buf.at[mask >> 1],
            send_sem=core_send.at[mask >> 1],
            recv_sem=core_recv.at[mask >> 1],
            device_id={"ctx": flipped(me, 1, bits)},
            device_id_type=MESH_IDS,
        )
        copy.start()
        core_copies[mask] = copy
        finals.append(copy.wait_send)
    arriving = {}

    def columns(half):
        return pl.ds(half * width, width)

    def send(half, phase, bit, mask):
        slot = plans[half][phase][1].index(mask)
        copy = pltpu.make_async_remote_copy(
            src_ref=part_ref.at[flipped(me, mask, bits), :, columns(half)],
            dst_ref=chip_buf.at[half, phase, slot],
            send_sem=send_sem.at[half, phase, slot],
            recv_sem=recv_sem.at[half, phase, slot],
            device_id={"ctx": flipped(me, 1 << bit, bits)},
            device_id_type=MESH_IDS,
        )
        copy.start()
        finals.append(copy.wait_send)
        arriving[half, phase, mask & ~(1 << bit)] = (copy, slot)

    yield
    for mask in chip_masks:
        core_copies[mask].wait_recv()
        here = part_ref.at[flipped(me, mask, bits)]
        add_into(here, here, core_buf.at[mask >> 1], rows, step)
        for half in range(2):
            bit, masks = plans[half][0]
            if mask in masks:
                send(half, 0, bit, mask)
    yield
    phases = bits - 1
    for phase in range(1, phases + 1):
        for half in range(2):
            last_bit, last_masks = plans[half][phase - 1]
            kept = farthest_first([mask & ~(1 << last_bit) for mask in last_masks])
            for mask in kept:
                copy, slot = arriving[half, phase - 1, mask]
                copy.wait_recv()
                here = part_ref.at[flipped(me, mask, bits), :, columns(half)]
                buf = chip_buf.at[half, phase - 1, slot]
                if phase < phases:
                    add_into(here, here, buf, rows, step)
                    bit, masks = plans[half][phase]
                    if mask in masks:
                        send(half, phase, bit, mask)
                else:
                    add_into(out_ref.at[:, columns(half)], here, buf, rows, step)
        yield
    for wait in finals:
        wait()


def scatter_op(part, size):
    bits = size.bit_length() - 1
    chips = size // 2
    rows, width = part.shape[1:]
    dma = pltpu.SemaphoreType.DMA
    return dict(
        run=functools.partial(scatter_run, bits, 32),
        inputs=[part],
        in_space=pltpu.VMEM,
        outs=[jax.ShapeDtypeStruct((rows, width), jnp.float32)],
        out_space=pltpu.VMEM,
        scratch=[
            pltpu.VMEM((chips, rows, width), part.dtype),
            pltpu.VMEM((2, bits - 1, chips // 2, rows, width // 2), part.dtype),
            dma((chips,)),
            dma((chips,)),
            dma((2, bits - 1, chips // 2)),
            dma((2, bits - 1, chips // 2)),
        ],
        moved=4 * part.size,
    )


def exchange_run(size, take, put, source, out, send_sem, recv_sem, local_sem):
    me = lax.axis_index("ctx")
    local = pltpu.make_async_copy(take(source, me), put(out, me), local_sem)
    local.start()
    copies = []
    for step in range(1, size):
        other = lax.rem(me + step, size)
        copy = pltpu.make_async_remote_copy(
            src_ref=take(source, other),
            dst_ref=put(out, me),
            send_sem=send_sem.at[step - 1],
            recv_sem=recv_sem.at[step - 1],
            device_id={"ctx": other},
            device_id_type=MESH_IDS,
        )
        copy.start()
        copies.append(copy)
    yield
    local.wait()
    for copy in copies:
        copy.wait()


def exchange_op(x, size, out_shape, take, put):
    dma = pltpu.SemaphoreType.DMA
    return dict(
        run=functools.partial(exchange_run, size, take, put),
        inputs=[x],
        in_space=pl.ANY,
        outs=[jax.ShapeDtypeStruct(out_shape, x.dtype)],
        out_space=pl.ANY,
        scratch=[dma((size - 1,)), dma((size - 1,)), dma],
        far=True,
        moved=4 * x.size,
    )


def z_gather_run(size, source, out, send_sem, recv_sem, local_sem):
    me = lax.axis_index("fsdp")
    local = pltpu.make_async_copy(source, out.at[me], local_sem)
    local.start()
    copies = []
    for step in range(1, size):
        copy = pltpu.make_async_remote_copy(
            src_ref=source,
            dst_ref=out.at[me],
            send_sem=send_sem.at[step - 1],
            recv_sem=recv_sem.at[step - 1],
            device_id={"fsdp": lax.rem(me + step, size)},
            device_id_type=MESH_IDS,
        )
        copy.start()
        copies.append(copy)
    for _ in range(4):
        yield
    local.wait()
    for copy in copies:
        copy.wait()


def z_gather_op(x, size):
    dma = pltpu.SemaphoreType.DMA
    return dict(
        run=functools.partial(z_gather_run, size),
        inputs=[x],
        in_space=pl.ANY,
        outs=[jax.ShapeDtypeStruct((size,) + x.shape, x.dtype)],
        out_space=pl.ANY,
        scratch=[dma((size - 1,)), dma((size - 1,)), dma],
        z=size,
        moved=2 * size * x.size,
    )


def z_scatter_run(size, source, out, buf, send_sem, recv_sem):
    me = lax.axis_index("fsdp")
    copies = []
    for step in range(1, size):
        other = lax.rem(me + step, size)
        copy = pltpu.make_async_remote_copy(
            src_ref=source.at[other],
            dst_ref=buf.at[step - 1],
            send_sem=send_sem.at[step - 1],
            recv_sem=recv_sem.at[step - 1],
            device_id={"fsdp": other},
            device_id_type=MESH_IDS,
        )
        copy.start()
        copies.append(copy)
    for _ in range(4):
        yield
    total = source[me].astype(jnp.float32)
    for step, copy in enumerate(copies):
        copy.wait()
        total += buf[step].astype(jnp.float32)
    out[...] = total.astype(out.dtype)


def z_scatter_op(x, size):
    dma = pltpu.SemaphoreType.DMA
    return dict(
        run=functools.partial(z_scatter_run, size),
        inputs=[x],
        in_space=pltpu.VMEM,
        outs=[jax.ShapeDtypeStruct(x.shape[1:], x.dtype)],
        out_space=pltpu.VMEM,
        scratch=[
            pltpu.VMEM((size - 1,) + x.shape[1:], x.dtype),
            dma((size - 1,)),
            dma((size - 1,)),
        ],
        z=size,
        moved=4 * x.size,
    )


def z_sum_gather_run(bits, size, source, out, low, buf, send_sem, recv_sem, *sems):
    yield from z_scatter_run(size, source, low, buf, send_sem, recv_sem)
    yield from gather_run(bits, column_half, stacked_columns, False, low, out, *sems)


def z_sum_gather_op(x, z_size, size):
    summed = z_scatter_op(x, z_size)
    (shape,) = summed["outs"]
    gather = gather_op(shape, size)
    return dict(
        run=functools.partial(z_sum_gather_run, size.bit_length() - 1, z_size),
        inputs=[x],
        in_space=pltpu.VMEM,
        outs=gather["outs"],
        out_space=pl.ANY,
        scratch=[pltpu.VMEM(shape.shape, shape.dtype)] + summed["scratch"] + gather["scratch"],
        z=z_size,
        moved=summed["moved"] + gather["moved"],
    )


def project_run(
    cols,
    tokens,
    weights,
    gain,
    shift,
    bias,
    cosine,
    sine_low,
    sine_high,
    qkv,
    normed,
    tokens_buf,
    normed_buf,
    weights_buf,
    load_sem,
    store_sem,
    weights_sem,
):
    size, rows = tokens.shape[:2]

    def load(block):
        slot = block % 2
        return pltpu.make_async_copy(tokens.at[block], tokens_buf.at[slot], load_sem.at[slot])

    def store(block):
        slot = block % 2
        return pltpu.make_async_copy(normed_buf.at[slot], normed.at[block], store_sem.at[slot])

    load_weights = pltpu.make_async_copy(weights, weights_buf, weights_sem)
    load(0).start()
    load_weights.start()
    yield
    for block in range(size):
        if block + 1 < size:
            load(block + 1).start()
        load(block).wait()
        at = pl.ds(block * rows, rows)
        values = tokens_buf[block % 2].astype(jnp.float32)
        centered = values - jnp.mean(values, -1, keepdims=True)
        inverse = lax.rsqrt(jnp.mean(centered * centered, -1, keepdims=True) + NORM_EPSILON)
        low = (centered * inverse * gain[...] + shift[...]).astype(jnp.bfloat16)
        if block >= 2:
            store(block - 2).wait()
        normed_buf[block % 2] = low
        store(block).start()
        if block == 0:
            load_weights.wait()
        projected = jnp.dot(low, weights_buf[...], preferred_element_type=jnp.float32)
        projected += bias[...]
        tables = (cosine[at], sine_low[at], sine_high[at])
        query = turn(projected[:, :cols], *tables, cols) * HEAD ** (-0.5)
        qkv[block, :, :cols] = query.astype(jnp.bfloat16)
        key = turn(projected[:, cols : 2 * cols], *tables, cols)
        qkv[block, :, cols : 2 * cols] = key.astype(jnp.bfloat16)
        qkv[block, :, 2 * cols :] = projected[:, 2 * cols :].astype(jnp.bfloat16)
        yield
    store(size - 2).wait()
    store(size - 1).wait()


def project_op(tokens, weights, gain, shift, bias, tables):
    size, rows, width = tokens.shape
    wide = weights.shape[1]
    low = jnp.bfloat16
    dma = pltpu.SemaphoreType.DMA
    return dict(
        run=functools.partial(project_run, wide // 3),
        inputs=[tokens, weights, gain, shift, bias, *tables],
        in_spaces=[pl.ANY] * 2 + [pltpu.VMEM] * 6,
        outs=[
            jax.ShapeDtypeStruct((size, rows, wide), low),
            jax.ShapeDtypeStruct((size, rows, width), low),
        ],
        out_spaces=[pltpu.VMEM, pl.ANY],
        scratch=[
            pltpu.VMEM((2, rows, width), low),
            pltpu.VMEM((2, rows, width), low),
            pltpu.VMEM(weights.shape, low),
            dma((2,)),
            dma((2,)),
            dma,
        ],
        moved=4 * tokens.size,
    )


def plane_kernel(size, parts, far, z_size, *refs):
    bits = size.bit_length() - 1
    me = lax.axis_index("ctx")
    my_z = lax.axis_index("fsdp")
    partners = [flipped(me, 1 << bit, bits) for bit in range(bits)]
    if far:
        partners = [lax.rem(me + step, size) for step in range(1, size)]
    greet(partners, [lax.rem(my_z + step, z_size) for step in range(1, z_size)])
    ins = sum(part[1] for part in parts)
    outs = sum(part[2] for part in parts)
    groups = [list(refs[:ins]), list(refs[ins : ins + outs]), list(refs[ins + outs :])]
    running = []
    for run, *counts in parts:
        own = []
        for group, count in zip(groups, counts):
            own += group[:count]
            del group[:count]
        running.append(run(*own))
    while running:
        running = [turn_of for turn_of in running if next(turn_of, 1) is None]


def spaces(op, side):
    arrays = op["inputs"] if side == "in" else op["outs"]
    return op.get(side + "_spaces") or [op[side + "_space"]] * len(arrays)


def plane(size, collective_id, *ops):
    parts = [(op["run"], len(op["inputs"]), len(op["outs"]), len(op["scratch"])) for op in ops]
    far = any(op.get("far") for op in ops)
    z_size = max(op.get("z", 1) for op in ops)
    results = pl.pallas_call(
        functools.partial(plane_kernel, size, parts, far, z_size),
        out_shape=[out for op in ops for out in op["outs"]],
        in_specs=[pl.BlockSpec(memory_space=space) for op in ops for space in spaces(op, "in")],
        out_specs=[pl.BlockSpec(memory_space=space) for op in ops for space in spaces(op, "out")],
        scratch_shapes=[scratch for op in ops for scratch in op["scratch"]],
        compiler_params=pltpu.CompilerParams(
            collective_id=collective_id, has_side_effects=True, vmem_limit_bytes=60 << 20
        ),
        cost_estimate=pl.CostEstimate(
            flops=0, bytes_accessed=sum(op["moved"] for op in ops), transcendentals=0
        ),
    )(*[x for op in ops for x in op["inputs"]])
    return results if len(results) > 1 else results[0]


def plane_groups(size, collective_id, *ops):
    groups = []
    room = 0
    for op in ops:
        need = 0 if op.get("in_space") == pl.ANY else op["moved"] * 5 // 4
        if not groups or need > room:
            groups.append([])
            room = 52 << 20
        groups[-1].append(op)
        room -= need
    results = []
    for i, group in enumerate(groups):
        got = plane(size, collective_id + i, *group)
        results += got if isinstance(got, (list, tuple)) else [got]
    return results


def swapped(tile):
    return tile % 2 + 2 * (tile // 4 % 2) + 4 * (tile // 2 % 2)


def tile_put(ref, mask, half):
    return row_half(ref.at[mask if half == 0 else swapped(mask)], half)


def tile_partner(me, bit):
    return {"ctx": flipped(me, 1 << bit, 3)}


def tile_copy(source, target, half, bit, me, send_sem, recv_sem):
    rows = source.shape[0] // 2
    at = pl.ds(half * rows, rows)
    return pltpu.make_async_remote_copy(
        src_ref=source.at[at],
        dst_ref=target.at[at],
        send_sem=send_sem.at[half],
        recv_sem=recv_sem.at[half],
        device_id=tile_partner(me, bit),
        device_id_type=MESH_IDS,
    )


def core_copy(source, target, me, send_sem, recv_sem):
    return pltpu.make_async_remote_copy(
        src_ref=source,
        dst_ref=target,
        send_sem=send_sem,
        recv_sem=recv_sem,
        device_id=tile_partner(me, 0),
        device_id_type=MESH_IDS,
    )


class TileGather:
    def __init__(self, tiles, send_sem, recv_sem, core_send, core_recv):
        me = lax.axis_index("ctx")
        self.hops = {
            target: [
                tile_copy(
                    tiles.at[source],
                    tiles.at[target],
                    half,
                    (first, 3 - first)[half],
                    me,
                    send_sem.at[target // 2 - 1],
                    recv_sem.at[target // 2 - 1],
                )
                for half in range(2)
            ]
            for source, target, first in ((0, 2, 1), (0, 4, 2), (2, 6, 2))
        }
        self.cores = [
            core_copy(tiles.at[2 * i], tiles.at[2 * i + 1], me, core_send.at[i], core_recv.at[i])
            for i in range(4)
        ]

    def before(self, tile):
        if tile == 0:
            for copy in self.hops[2]:
                copy.start()
            self.cores[0].start()
        elif tile % 2 == 1:
            self.cores[tile // 2].wait_recv()
            if tile == 1:
                for copy in self.hops[4]:
                    copy.start()
        else:
            for copy in self.hops[tile]:
                copy.wait_recv()
            if tile == 2:
                for copy in self.hops[6]:
                    copy.start()
            self.cores[tile // 2].start()

    def finish(self):
        for copies in self.hops.values():
            for copy in copies:
                copy.wait_send()
        for copy in self.cores:
            copy.wait_send()


def gather_sems():
    dma = pltpu.SemaphoreType.DMA
    return [dma((3, 2)), dma((3, 2)), dma((4,)), dma((4,))]


def part_slot(tile):
    odd = tile % 2
    return (1 - odd) * (tile // 2) + odd * (5 - tile // 4)


SCATTER_ORDER = (7, 6, 3, 2, 5, 4, 1, 0)


class TileScatter:
    def __init__(self, parts, core_buf, chip_buf, send_sem, recv_sem, core_send, core_recv):
        me = lax.axis_index("ctx")
        self.parts, self.core_buf, self.chip_buf = parts, core_buf, chip_buf
        self.hops = {
            source: [
                tile_copy(
                    parts.at[part_slot(source)],
                    chip_buf.at[source // 2 - 1],
                    half,
                    (first, 3 - first)[half],
                    me,
                    send_sem.at[source // 2 - 1],
                    recv_sem.at[source // 2 - 1],
                )
                for half in range(2)
            ]
            for source, first in ((6, 1), (4, 2), (2, 1))
        }
        self.cores = [
            core_copy(
                parts.at[part_slot(2 * i + 1)],
                core_buf.at[i],
                me,
                core_send.at[i],
                core_recv.at[i],
            )
            for i in range(4)
        ]

    def add(self, tile, buf):
        here = self.parts.at[part_slot(tile)]
        add_into(here, here, buf, here.shape[0], 32)

    def before(self, tile):
        if tile in (5, 1):
            self.cores[tile // 2 + 1].wait_send()

    def after(self, tile):
        if tile % 2 == 1:
            self.cores[tile // 2].start()
        else:
            self.settle(tile)

    def settle(self, tile):
        self.cores[tile // 2].wait_recv()
        self.add(tile, self.core_buf.at[tile // 2])
        if tile == 6 or tile == 2:
            for copy in self.hops[tile]:
                copy.start()
        if tile == 4:
            for copy in self.hops[6]:
                copy.wait_recv()
            self.add(4, self.chip_buf.at[2])
            for copy in self.hops[4]:
                copy.start()

    def finish(self, out):
        for tile in (2, 4):
            for copy in self.hops[tile]:
                copy.wait_recv()
        rows = out.shape[0]

        @pl.loop(0, rows // 32)
        def _(i):
            at = pl.ds(pl.multiple_of(i * 32, 32), 32)
            out[at] = (
                self.parts[0, at].astype(jnp.float32)
                + self.chip_buf[0, at].astype(jnp.float32)
                + self.chip_buf[1, at].astype(jnp.float32)
            ).astype(out.dtype)

        for copies in self.hops.values():
            for copy in copies:
                copy.wait_send()
        for tile in (4, 0):
            self.cores[tile // 2].wait_send()


def scatter_scratch(rows, width):
    return [
        pltpu.VMEM((6, rows, width), jnp.bfloat16),
        pltpu.VMEM((4, rows, width), jnp.bfloat16),
        pltpu.VMEM((3, rows, width), jnp.bfloat16),
    ] + gather_sems()


def produce_run(produce, batch, late, count, *refs):
    inputs, (out, *scratch) = refs[:count], refs[count:]
    me = lax.axis_index("ctx")
    scatter = TileScatter(*scratch)
    last = None
    for tile in SCATTER_ORDER:
        scatter.before(tile)
        scatter.parts[part_slot(tile)] = produce(inputs, tile, me).astype(jnp.bfloat16)
        if tile % 2 == 1:
            scatter.after(tile)
            if batch == 1 and last is not None:
                scatter.settle(last)
        last = tile
        if tile % batch == 0:
            yield
            if batch > 1:
                scatter.settle(tile)
    if batch == 1:
        scatter.settle(0)
    for _ in range(late):
        yield
    scatter.finish(out)


def produce_op(produce, rows, width, *inputs, batch=1, late=0, kind=jnp.float32):
    return dict(
        run=functools.partial(produce_run, produce, batch, late, len(inputs)),
        inputs=list(inputs),
        in_space=pltpu.VMEM,
        outs=[jax.ShapeDtypeStruct((rows, width), kind)],
        out_space=pltpu.VMEM,
        scratch=scatter_scratch(rows, width),
        moved=32 * rows * width,
    )


def tile_rows(ref, tile, me):
    half = ref.shape[1] // 2
    return jnp.concatenate(
        [ref[flipped(me, tile, 3), :half], ref[flipped(me, swapped(tile), 3), half:]], 0
    )


def product_of_rows(refs, tile, me):
    return times_transposed(tile_rows(refs[0], tile, me), refs[1][...])


def product_of_columns(refs, tile, me):
    return jnp.dot(
        tile_rows(refs[0], tile, me), refs[1][...], preferred_element_type=jnp.float32
    )


def unpack_both_kernel(segments, count, source, gate, up):
    hidden_size = source.shape[2] // 2
    main = hidden_size // 128 * 128
    strip = hidden_size // segments
    for out, first, last in ((gate, 0, 2 * main), (up, main, main + hidden_size)):
        owners = [
            jnp.concatenate(
                [
                    source[owner, :, first : first + main],
                    source[owner, :, last : last + hidden_size - main],
                ],
                1,
            )
            for owner in range(count)
        ]
        out[...] = jnp.concatenate(
            [
                rows[:, segment * strip : (segment + 1) * strip]
                for segment in range(segments)
                for rows in owners
            ],
            1,
        ).astype(jnp.float32)


def unpack_both(gathered, segments):
    count, rows, width = gathered.shape
    step = 64
    block = pl.BlockSpec((step, count * width // 2), lambda i: (i, 0))
    return pl.pallas_call(
        functools.partial(unpack_both_kernel, segments, count),
        grid=(rows // step,),
        in_specs=[pl.BlockSpec((count, step, width), lambda i: (0, i, 0))],
        out_specs=[block, block],
        out_shape=[jax.ShapeDtypeStruct((rows, count * width // 2), jnp.float32)] * 2,
        compiler_params=pltpu.CompilerParams(vmem_limit_bytes=60 << 20),
        cost_estimate=pl.CostEstimate(
            flops=0, bytes_accessed=6 * gathered.size, transcendentals=0
        ),
    )(gathered)


def greet_near(size):
    me = lax.axis_index("ctx")
    bits = size.bit_length() - 1
    greet([flipped(me, 1 << bit, bits) for bit in range(bits)])


def centre(values):
    centered = values - jnp.mean(values, -1, keepdims=True)
    inverse = lax.rsqrt(jnp.mean(centered * centered, -1, keepdims=True) + NORM_EPSILON)
    return centered * inverse, inverse


def join_kernel(
    size,
    mixed,
    weights,
    tokens,
    gain,
    shift,
    mixed_rows,
    residual,
    normed,
    weights_buf,
    load_sem,
    send_sem,
    recv_sem,
    local_sem,
):
    me = lax.axis_index("ctx")
    cols = mixed.shape[2]

    def load(owner):
        at = pl.ds(pl.multiple_of(owner * cols, cols), cols)
        return pltpu.make_async_copy(weights.at[at], weights_buf.at[at], load_sem.at[owner])

    others = [lax.rem(me + step, size) for step in range(size)]
    for step in range(size):
        load(lax.rem(me + size - step, size)).start()
    greet(others[1:])
    here = column_view(mixed_rows, me, cols)
    local = pltpu.make_async_copy(mixed.at[me], here, local_sem)
    local.start()
    copies = []
    for step in range(1, size):
        copy = pltpu.make_async_remote_copy(
            src_ref=mixed.at[others[step]],
            dst_ref=here,
            send_sem=send_sem.at[step - 1],
            recv_sem=recv_sem.at[step - 1],
            device_id={"ctx": others[step]},
            device_id_type=MESH_IDS,
        )
        copy.start()
        copies.append(copy)
    local.wait()
    residual[...] = tokens[...].astype(jnp.float32)
    for step in range(size):
        owner = lax.rem(me + size - step, size)
        if step > 0:
            copies[step - 1].wait_recv()
        load(owner).wait()
        at = pl.ds(pl.multiple_of(owner * cols, cols), cols)
        residual[...] += jnp.dot(
            mixed_rows[:, at], weights_buf[at], preferred_element_type=jnp.float32
        )
    unit = centre(residual[...])[0]
    normed[...] = (unit * gain[...] + shift[...]).astype(jnp.bfloat16)
    for copy in copies:
        copy.wait_send()


def join_rows(mixed, weights, tokens, gain, shift, collective_id):
    size, rows, cols = mixed.shape
    width = size * cols
    vmem = pl.BlockSpec(memory_space=pltpu.VMEM)
    any_space = pl.BlockSpec(memory_space=pl.ANY)
    low = jnp.bfloat16
    dma = pltpu.SemaphoreType.DMA
    return pl.pallas_call(
        functools.partial(join_kernel, size),
        in_specs=[any_space] * 2 + [vmem] * 3,
        out_specs=[vmem] * 3,
        out_shape=[
            jax.ShapeDtypeStruct((rows, width), low),
            jax.ShapeDtypeStruct((rows, width), jnp.float32),
            jax.ShapeDtypeStruct((rows, width), low),
        ],
        scratch_shapes=[
            pltpu.VMEM((width, width), low),
            dma((size,)),
            dma((size - 1,)),
            dma((size - 1,)),
            dma,
        ],
        compiler_params=pltpu.CompilerParams(
            collective_id=collective_id, has_side_effects=True, vmem_limit_bytes=60 << 20
        ),
        cost_estimate=pl.CostEstimate(
            flops=2 * rows * width * width, bytes_accessed=2 * width * width, transcendentals=0
        ),
    )(mixed, weights, tokens, gain, shift)


def part_kernel(
    size,
    grad_normed,
    residual,
    cotangent,
    gain,
    weights,
    grad_residual,
    grad_branch,
    sums,
    grad_mixed,
    weights_buf,
    staged,
    load_sem,
    send_sem,
    recv_sem,
    local_sem,
):
    me = lax.axis_index("ctx")
    cols = staged.shape[2]
    others = [lax.rem(me + step, size) for step in range(size)]

    def load(owner):
        at = pl.ds(pl.multiple_of(owner * cols, cols), cols)
        return pltpu.make_async_copy(weights.at[at], weights_buf.at[at], load_sem.at[owner])

    order = list(range(1, size)) + [0]
    for step in order:
        load(others[step]).start()
    greet(others[1:])
    unit, inverse = centre(residual[...])
    grads = grad_normed[...]
    scaled = grads * gain[...]
    total = cotangent[...].astype(jnp.float32) + inverse * (
        scaled
        - jnp.mean(scaled, -1, keepdims=True)
        - unit * jnp.mean(scaled * unit, -1, keepdims=True)
    )
    grad_residual[...] = total
    grad_branch[...] = total.astype(jnp.bfloat16)
    copies = []
    for step in order:
        other = others[step]
        load(other).wait()
        at = pl.ds(pl.multiple_of(other * cols, cols), cols)
        staged[step] = times_transposed(grad_branch[...], weights_buf[at]).astype(jnp.bfloat16)
        if step == 0:
            copy = pltpu.make_async_copy(staged.at[0], grad_mixed.at[me], local_sem)
        else:
            copy = pltpu.make_async_remote_copy(
                src_ref=staged.at[step],
                dst_ref=grad_mixed.at[me],
                send_sem=send_sem.at[step - 1],
                recv_sem=recv_sem.at[step - 1],
                device_id={"ctx": other},
                device_id_type=MESH_IDS,
            )
        copy.start()
        copies.append(copy)
    sums[:1] = jnp.sum(grads * unit, 0, keepdims=True)
    sums[1:] = jnp.sum(grads, 0, keepdims=True)
    for copy in copies:
        copy.wait()


def part_rows(grad_normed, residual, cotangent, gain, weights, size, collective_id):
    rows, width = grad_normed.shape
    cols = width // size
    vmem = pl.BlockSpec(memory_space=pltpu.VMEM)
    any_space = pl.BlockSpec(memory_space=pl.ANY)
    low = jnp.bfloat16
    dma = pltpu.SemaphoreType.DMA
    return pl.pallas_call(
        functools.partial(part_kernel, size),
        in_specs=[vmem] * 4 + [any_space],
        out_specs=[vmem] * 3 + [any_space],
        out_shape=[
            jax.ShapeDtypeStruct((rows, width), jnp.float32),
            jax.ShapeDtypeStruct((rows, width), low),
            jax.ShapeDtypeStruct((2, width), jnp.float32),
            jax.ShapeDtypeStruct((size, rows, cols), low),
        ],
        scratch_shapes=[
            pltpu.VMEM((width, width), low),
            pltpu.VMEM((size, rows, cols), low),
            dma((size,)),
            dma((size - 1,)),
            dma((size - 1,)),
            dma,
        ],
        compiler_params=pltpu.CompilerParams(
            collective_id=collective_id, has_side_effects=True, vmem_limit_bytes=60 << 20
        ),
        cost_estimate=pl.CostEstimate(
            flops=2 * rows * width * width, bytes_accessed=2 * width * width, transcendentals=0
        ),
    )(grad_normed, residual, cotangent, gain, weights)


def forward_kernel(
    hidden_size,
    normed,
    weights,
    grads,
    normed_t,
    values,
    hidden,
    grad_down,
    tiles,
    weights_buf,
    grads_buf,
    turned,
    values_buf,
    hidden_t,
    load_sem,
    out_sem,
    *sems,
):
    greet_near(8)
    own = pltpu.make_async_copy(normed, tiles.at[0], load_sem.at[0])
    load = pltpu.make_async_copy(weights, weights_buf, load_sem.at[1])
    own.start()
    load.start()
    pltpu.make_async_copy(grads, grads_buf, load_sem.at[2]).start()
    own.wait()
    gather = TileGather(tiles, *sems)
    rows = tiles.shape[1]
    main = hidden_size // 128 * 128

    def write_out(tile, slot):
        at = pl.ds(pl.multiple_of(tile * rows, rows), rows)
        return [
            pltpu.make_async_copy(values_buf.at[slot], values.at[tile], out_sem.at[0, slot]),
            pltpu.make_async_copy(turned.at[slot], normed_t.at[:, at], out_sem.at[1, slot]),
        ]

    @pl.loop(0, 8)
    def _(t):
        for tile in range(8):

            @pl.when(t == tile)
            def _():
                gather.before(tile)
                if tile == 0:
                    load.wait()

        slot = t % 2

        @pl.when(t >= 2)
        def _():
            for copy in write_out(t - 2, slot):
                copy.wait()

        here = tiles[t]
        value = jnp.dot(here, weights_buf[...], preferred_element_type=jnp.float32)
        values_buf[slot] = value
        gate, up = value[:, :main], value[:, main : 2 * main]
        front = gate * jax.nn.sigmoid(gate) * up
        last = value[:, 2 * main :]
        behind = last * jax.nn.sigmoid(last) * pltpu.roll(last, 64, 1)
        both = jnp.concatenate([front, behind], 1)
        hidden[t] = both[:, :hidden_size].astype(jnp.bfloat16)
        at = pl.ds(pl.multiple_of(t * rows, rows), rows)
        hidden_t[:, at] = jnp.transpose(both)[:hidden_size].astype(jnp.bfloat16)
        turned[slot] = jnp.transpose(here)
        for copy in write_out(t, slot):
            copy.start()

    pltpu.make_async_copy(grads, grads_buf, load_sem.at[2]).wait()
    width = grads_buf.shape[2]
    step = 256

    @pl.loop(0, width // step)
    def _(i):
        at = pl.ds(pl.multiple_of(i * step, step), step)
        grad_down[:, at] = jnp.dot(
            hidden_t[...],
            grads_buf[:, :, at].reshape(8 * rows, step),
            preferred_element_type=jnp.float32,
        ).astype(jnp.bfloat16)

    for tile in (6, 7):
        for copy in write_out(tile, tile % 2):
            copy.wait()
    gather.finish()


def forward_mlp(normed, weights, grads, hidden_size, collective_id):
    rows, width = normed.shape
    wide = weights.shape[1]
    any_space = pl.BlockSpec(memory_space=pl.ANY)
    vmem = pl.BlockSpec(memory_space=pltpu.VMEM)
    low = jnp.bfloat16
    dma = pltpu.SemaphoreType.DMA
    return pl.pallas_call(
        functools.partial(forward_kernel, hidden_size),
        in_specs=[any_space] * 3,
        out_specs=[any_space, any_space, vmem, vmem],
        out_shape=[
            jax.ShapeDtypeStruct((width, 8 * rows), low),
            jax.ShapeDtypeStruct((8, rows, wide), jnp.float32),
            jax.ShapeDtypeStruct((8, rows, hidden_size), low),
            jax.ShapeDtypeStruct((hidden_size, width), low),
        ],
        scratch_shapes=[
            pltpu.VMEM((8, rows, width), low),
            pltpu.VMEM(weights.shape, low),
            pltpu.VMEM((8, rows, width), low),
            pltpu.VMEM((2, width, rows), low),
            pltpu.VMEM((2, rows, wide), jnp.float32),
            pltpu.VMEM((hidden_size, 8 * rows), low),
            dma((3,)),
            dma((2, 2)),
        ]
        + gather_sems(),
        compiler_params=pltpu.CompilerParams(
            collective_id=collective_id, has_side_effects=True, vmem_limit_bytes=60 << 20
        ),
        cost_estimate=pl.CostEstimate(
            flops=16 * rows * width * (wide + hidden_size),
            bytes_accessed=64 * rows * width,
            transcendentals=0,
        ),
    )(normed, weights, grads)


def backward_kernel(
    hidden_size,
    grads,
    values,
    weights,
    down,
    normed_t,
    hidden,
    grad_normed,
    grad_both_w,
    layer_part,
    grads_buf,
    values_buf,
    weights_buf,
    down_buf,
    normed_buf,
    grad_both,
    out_buf,
    hidden_buf,
    load_sem,
    tile_sem,
    out_sem,
    *scatter_refs,
):
    greet_near(8)
    scatter = TileScatter(*scatter_refs[: len(scatter_refs) // 2])
    layer = TileScatter(*scatter_refs[len(scatter_refs) // 2 :])
    rows = grads_buf.shape[1]
    main = hidden_size // 128 * 128
    load_weights = pltpu.make_async_copy(weights, weights_buf, load_sem.at[0])
    load_down = pltpu.make_async_copy(down, down_buf, load_sem.at[1])

    def load_tile(tile, slot):
        return [
            pltpu.make_async_copy(grads.at[tile], grads_buf.at[slot], tile_sem.at[0, slot]),
            pltpu.make_async_copy(values.at[tile], values_buf.at[slot], tile_sem.at[1, slot]),
            pltpu.make_async_copy(hidden.at[tile], hidden_buf.at[slot], tile_sem.at[3, slot]),
        ]

    def load_chunk(i):
        at = pl.ds(pl.multiple_of(i * rows, rows), rows)
        return pltpu.make_async_copy(normed_t.at[at], normed_buf.at[i % 2], tile_sem.at[2, i % 2])

    load_down.start()
    for copy in load_tile(7, 1):
        copy.start()
    load_weights.start()
    load_chunk(0).start()

    @pl.loop(0, 8)
    def _(u):
        t = 7 - swapped(u)
        slot = t % 2

        @pl.when(u < 7)
        def _():
            for copy in load_tile(7 - swapped(u + 1), 1 - slot):
                copy.start()

        @pl.when(u == 0)
        def _():
            load_down.wait()

        for copy in load_tile(t, slot):
            copy.wait()
        grad_hidden = lax.dot_general(
            grads_buf[slot],
            down_buf[...],
            (((1,), (1,)), ((), ())),
            preferred_element_type=jnp.float32,
        )
        value = values_buf[slot]
        gate, up, above = value[:, :main], value[:, main : 2 * main], grad_hidden[:, :main]
        sigmoid = jax.nn.sigmoid(gate)
        grad_both[t, :, :main] = (
            above * up * sigmoid * (1.0 + gate * (1.0 - sigmoid))
        ).astype(jnp.bfloat16)
        grad_both[t, :, main : 2 * main] = (above * (gate * sigmoid)).astype(jnp.bfloat16)
        last = value[:, 2 * main :]
        above = grad_hidden[:, main:]
        above = jnp.concatenate([above, jnp.zeros_like(above)], 1)
        sigmoid = jax.nn.sigmoid(last)
        to_gate = above * pltpu.roll(last, 64, 1) * sigmoid * (1.0 + last * (1.0 - sigmoid))
        to_up = pltpu.roll(above * (last * sigmoid), 64, 1)
        lane = lax.broadcasted_iota(jnp.int32, last.shape, 1)
        grad_both[t, :, 2 * main :] = jnp.where(lane < 64, to_gate, to_up).astype(jnp.bfloat16)

        @pl.when(u == 0)
        def _():
            load_weights.wait()

        for tile in (5, 1):

            @pl.when(t == tile)
            def _():
                scatter.before(tile)
                layer.before(tile)

        scatter.parts[part_slot(t)] = lax.dot_general(
            grad_both[t],
            weights_buf[...],
            (((1,), (1,)), ((), ())),
            preferred_element_type=jnp.float32,
        ).astype(jnp.bfloat16)
        for tile in range(8):

            @pl.when(t == tile)
            def _():
                scatter.after(tile)

        layer.parts[part_slot(t)] = jnp.dot(
            hidden_buf[slot], down_buf[...], preferred_element_type=jnp.float32
        ).astype(jnp.bfloat16)
        for tile in range(8):

            @pl.when(t == tile)
            def _():
                layer.after(tile)

    chunks = normed_t.shape[0] // rows

    def store_chunk(i):
        at = pl.ds(pl.multiple_of(i * rows, rows), rows)
        return pltpu.make_async_copy(out_buf.at[i % 2], grad_both_w.at[at], out_sem.at[i % 2])

    @pl.loop(0, chunks)
    def _(i):
        @pl.when(i < chunks - 1)
        def _():
            load_chunk(i + 1).start()

        load_chunk(i).wait()

        @pl.when(i >= 2)
        def _():
            store_chunk(i - 2).wait()

        out_buf[i % 2] = jnp.dot(
            normed_buf[i % 2],
            grad_both[...].reshape(8 * rows, grad_both.shape[2]),
            preferred_element_type=jnp.float32,
        ).astype(jnp.bfloat16)
        store_chunk(i).start()

    store_chunk(chunks - 2).wait()
    store_chunk(chunks - 1).wait()
    scatter.finish(grad_normed)
    layer.finish(layer_part)


def backward_mlp(grads, values, weights, down, normed_t, hidden, collective_id):
    size, rows, width = grads.shape
    hidden_size = down.shape[0]
    wide = weights.shape[1]
    any_space = pl.BlockSpec(memory_space=pl.ANY)
    vmem = pl.BlockSpec(memory_space=pltpu.VMEM)
    low = jnp.bfloat16
    dma = pltpu.SemaphoreType.DMA
    return pl.pallas_call(
        functools.partial(backward_kernel, hidden_size),
        in_specs=[any_space] * 6,
        out_specs=[vmem, any_space, vmem],
        out_shape=[
            jax.ShapeDtypeStruct((rows, width), jnp.float32),
            jax.ShapeDtypeStruct((width, wide), low),
            jax.ShapeDtypeStruct((rows, width), jnp.float32),
        ],
        scratch_shapes=[
            pltpu.VMEM((2, rows, width), low),
            pltpu.VMEM((2, rows, wide), jnp.float32),
            pltpu.VMEM(weights.shape, low),
            pltpu.VMEM(down.shape, low),
            pltpu.VMEM((2, rows, 8 * rows), low),
            pltpu.VMEM((8, rows, wide), low),
            pltpu.VMEM((2, rows, wide), low),
            pltpu.VMEM((2, rows, hidden_size), low),
            dma((2,)),
            dma((4, 2)),
            dma((2,)),
        ]
        + scatter_scratch(rows, width) * 2,
        compiler_params=pltpu.CompilerParams(
            collective_id=collective_id, has_side_effects=True, vmem_limit_bytes=60 << 20
        ),
        cost_estimate=pl.CostEstimate(
            flops=16 * rows * width * (2 * wide + hidden_size),
            bytes_accessed=64 * rows * width,
            transcendentals=0,
        ),
    )(grads, values, weights, down, normed_t, hidden)


def unpack_rows_kernel(source, out):
    out[...] = source[...].astype(jnp.float32)


def unpack_rows(gathered, rows):
    count, _, width = gathered.shape
    out = pl.pallas_call(
        unpack_rows_kernel,
        grid=(count,),
        in_specs=[pl.BlockSpec((None, rows, width), lambda i: (i, 0, 0))],
        out_specs=pl.BlockSpec((None, rows, width), lambda i: (i, 0, 0)),
        out_shape=jax.ShapeDtypeStruct((count, rows, width), jnp.float32),
        compiler_params=pltpu.CompilerParams(vmem_limit_bytes=60 << 20),
        cost_estimate=pl.CostEstimate(
            flops=0, bytes_accessed=6 * gathered.size, transcendentals=0
        ),
    )(gathered)
    return out.reshape(count * rows, width)


def unpack_kernel(segments, count, source, out):
    strip = source.shape[2] // segments
    pieces = []
    for segment in range(segments):
        for owner in range(count):
            pieces.append(source[owner, :, segment * strip : (segment + 1) * strip])
    out[...] = jnp.concatenate(pieces, 1).astype(jnp.float32)


def unpack_columns(gathered, segments):
    count, rows, width = gathered.shape
    step = 64
    return pl.pallas_call(
        functools.partial(unpack_kernel, segments, count),
        grid=(rows // step,),
        in_specs=[pl.BlockSpec((count, step, width), lambda i: (0, i, 0))],
        out_specs=pl.BlockSpec((step, count * width), lambda i: (i, 0)),
        out_shape=jax.ShapeDtypeStruct((rows, count * width), jnp.float32),
        compiler_params=pltpu.CompilerParams(vmem_limit_bytes=60 << 20),
        cost_estimate=pl.CostEstimate(
            flops=0, bytes_accessed=6 * gathered.size, transcendentals=0
        ),
    )(gathered)


def norm_rows(values, gain_row, shift_row):
    centered = values - jnp.mean(values, -1, keepdims=True)
    inverse = lax.rsqrt(jnp.mean(centered * centered, -1, keepdims=True) + NORM_EPSILON)
    unit_rows = centered * inverse
    return (unit_rows * gain_row + shift_row, unit_rows, inverse)


def norm_back(grad_rows, unit_rows, inverse, gain_row):
    scaled = grad_rows * gain_row
    return inverse * (
        scaled
        - jnp.mean(scaled, -1, keepdims=True)
        - unit_rows * jnp.mean(scaled * unit_rows, -1, keepdims=True)
    )


def turn(rows, cosine, sine_low, sine_high, width):
    repeat = width // 128
    wide = [jnp.concatenate([table] * repeat, 1) for table in (cosine, sine_low, sine_high)]
    return (
        rows * wide[0]
        + pltpu.roll(rows, width - ROT // 2, 1) * wide[1]
        + pltpu.roll(rows, ROT // 2, 1) * wide[2]
    )


def head_stack(features_first, heads):
    owner = lax.broadcasted_iota(jnp.int32, features_first.shape, 0) // HEAD
    zero = jnp.zeros_like(features_first)
    return jnp.concatenate([jnp.where(owner == h, features_first, zero) for h in range(heads)], 1)


def row_stack(rows, heads):
    owner = lax.broadcasted_iota(jnp.int32, rows.shape, 1) // HEAD
    zero = jnp.zeros_like(rows)
    return jnp.concatenate([jnp.where(owner == h, rows, zero) for h in range(heads)], 0)


def pair_bias(key_tile, tile, heads, first_keys, diagonal):
    key_place = lax.broadcasted_iota(jnp.int32, (tile, tile), 0)
    allowed = key_place + key_tile * tile >= first_keys
    if diagonal:
        allowed &= key_place <= lax.broadcasted_iota(jnp.int32, (tile, tile), 1)
    return jnp.concatenate([jnp.where(allowed, 0.0, MASKED_SCORE)] * heads, 1)


def transposed(rows):
    return jnp.transpose(rows.astype(jnp.float32)).astype(rows.dtype)


def attend_kernel(
    block,
    heads,
    order,
    lowest,
    projected,
    starts,
    qkv,
    attended,
    mixed,
    log_total,
    value_t,
    summed,
    top,
    total,
):
    cols = heads * HEAD
    seq = projected.shape[0]
    tile = 2 * block

    @pl.loop(0, seq // block)
    def _(p):
        at = pl.ds(pl.multiple_of(p * block, block), block)
        rows = projected[pl.ds(pl.multiple_of(order[p] * block, block), block)]
        qkv[at] = rows
        value_t[:, at] = transposed(rows[:, 2 * cols :])

    @pl.loop(0, seq // tile)
    def _(i):
        at = pl.ds(pl.multiple_of(i * tile, tile), tile)
        query_t = head_stack(transposed(qkv[at, :cols]), heads)
        first_keys = starts[:, at]
        top[...] = jnp.full(top.shape, MASKED_SCORE, jnp.float32)
        total[...] = jnp.zeros_like(total)
        summed[...] = jnp.zeros_like(summed)

        def step(j, diagonal):
            keys_at = pl.ds(pl.multiple_of(j * tile, tile), tile)
            scores = jnp.dot(
                qkv[keys_at, cols : 2 * cols], query_t, preferred_element_type=jnp.float32
            )
            scores += pair_bias(j, tile, heads, first_keys, diagonal)
            old_top = top[...]
            new_top = jnp.maximum(old_top, jnp.max(scores, 0, keepdims=True))
            exps = jnp.exp(scores - new_top)
            fade = jnp.exp(old_top - new_top)
            total[...] = total[...] * fade + jnp.sum(exps, 0, keepdims=True)
            top[...] = new_top
            low = exps.astype(jnp.bfloat16)
            for h in range(heads):
                own = slice(h * tile, (h + 1) * tile)
                features = slice(h * HEAD, (h + 1) * HEAD)
                summed[features] = summed[features] * fade[:, own] + jnp.dot(
                    value_t[features, keys_at], low[:, own], preferred_element_type=jnp.float32
                )

        @pl.loop(lowest[i], i)
        def _(j):
            step(j, False)

        step(i, True)

        log_total[i] = top[...] + jnp.log(total[...])
        scale = 1.0 / total[...]
        for h in range(heads):
            features = slice(h * HEAD, (h + 1) * HEAD)
            summed[features] = summed[features] * scale[:, h * tile : (h + 1) * tile]
        rows = jnp.transpose(summed[...])
        attended[at] = rows
        for part in range(2):
            place = pl.ds(pl.multiple_of(order[2 * i + part] * block, block), block)
            mixed[place] = rows[part * block : (part + 1) * block].astype(jnp.bfloat16)


def attend(projected, order, lowest, starts, heads):
    seq, wide = projected.shape
    cols = wide // 3
    block = seq // order.shape[0]
    tile = 2 * block
    vmem = pl.BlockSpec(memory_space=pltpu.VMEM)
    smem = pl.BlockSpec(memory_space=pltpu.SMEM)
    return pl.pallas_call(
        functools.partial(attend_kernel, block, heads),
        in_specs=[smem, smem] + [vmem] * 2,
        out_specs=[vmem] * 4,
        out_shape=[
            jax.ShapeDtypeStruct((seq, wide), jnp.bfloat16),
            jax.ShapeDtypeStruct((seq, cols), jnp.float32),
            jax.ShapeDtypeStruct((seq, cols), jnp.bfloat16),
            jax.ShapeDtypeStruct((seq // tile, 1, heads * tile), jnp.float32),
        ],
        scratch_shapes=[
            pltpu.VMEM((cols, seq), jnp.bfloat16),
            pltpu.VMEM((cols, tile), jnp.float32),
            pltpu.VMEM((1, heads * tile), jnp.float32),
            pltpu.VMEM((1, heads * tile), jnp.float32),
        ],
        compiler_params=pltpu.CompilerParams(vmem_limit_bytes=48 << 20),
        cost_estimate=pl.CostEstimate(
            flops=4 * seq * seq * cols, bytes_accessed=12 * seq * cols, transcendentals=0
        ),
    )(order, lowest, projected, starts)


def attend_back_run(
    block,
    heads,
    order,
    places,
    qkv,
    grad_mixed,
    attended,
    log_total,
    starts,
    cosine,
    sine_low,
    sine_high,
    out,
    sums,
    key_t,
    grad_key,
    grad_value,
    grad_query,
    query_sum,
):
    cols = heads * HEAD
    seq = qkv.shape[0]
    tile = 2 * block

    @pl.loop(0, seq // block)
    def _(p):
        at = pl.ds(pl.multiple_of(p * block, block), block)
        key_t[:, at] = transposed(qkv[at, cols : 2 * cols])
        grad_key[p] = jnp.zeros((block, cols), jnp.float32)
        grad_value[p] = jnp.zeros((block, cols), jnp.float32)

    yield
    for i in reversed(range(seq // tile)):
        at = pl.ds(i * tile, tile)
        query = qkv[at, :cols]
        grad = jnp.concatenate(
            [
                grad_mixed[order[2 * i + part]]
                for part in range(2)
            ],
            0,
        )
        query_t = head_stack(transposed(query), heads)
        query_rows = row_stack(query, heads)
        grad_t = head_stack(transposed(grad), heads)
        grads = row_stack(grad, heads)
        products = jnp.transpose(grad.astype(jnp.float32) * attended[at])
        delta = jnp.concatenate(
            [
                jnp.sum(products[h * HEAD : (h + 1) * HEAD], 0, keepdims=True)
                for h in range(heads)
            ],
            1,
        )
        logs = log_total[i]
        first_keys = starts[:, at]
        query_sum[...] = jnp.zeros_like(query_sum)

        def step(j, diagonal):
            keys_at = pl.ds(pl.multiple_of(j * tile, tile), tile)
            scores = jnp.dot(
                qkv[keys_at, cols : 2 * cols], query_t, preferred_element_type=jnp.float32
            )
            scores += pair_bias(j, tile, heads, first_keys, diagonal)
            weights = jnp.exp(scores - logs)
            grad_soft = jnp.dot(
                qkv[keys_at, 2 * cols :], grad_t, preferred_element_type=jnp.float32
            )
            pair = pl.ds(2 * j, 2)
            grad_value[pair] += jnp.dot(
                weights.astype(jnp.bfloat16), grads, preferred_element_type=jnp.float32
            ).reshape(2, block, cols)
            grad_scores = (weights * (grad_soft - delta)).astype(jnp.bfloat16)
            grad_key[pair] += jnp.dot(
                grad_scores, query_rows, preferred_element_type=jnp.float32
            ).reshape(2, block, cols)
            for h in range(heads):
                features = slice(h * HEAD, (h + 1) * HEAD)
                query_sum[features] += jnp.dot(
                    key_t[features, keys_at],
                    grad_scores[:, h * tile : (h + 1) * tile],
                    preferred_element_type=jnp.float32,
                )

        if i > 0:

            @pl.loop(0, i)
            def _(j):
                step(j, False)

        step(i, True)
        grad_query[2 * i : 2 * i + 2] = (
            jnp.transpose(query_sum[...]) * HEAD ** (-0.5)
        ).reshape(2, block, cols)
        yield
    sums[...] = jnp.zeros_like(sums)

    @pl.loop(0, seq // block)
    def _(d):
        at = pl.ds(pl.multiple_of(d * block, block), block)
        place = places[d]
        tables = (cosine[at], -sine_low[at], -sine_high[at])
        for k, rows in enumerate(
            (
                turn(grad_query[place], *tables, cols),
                turn(grad_key[place], *tables, cols),
                grad_value[place],
            )
        ):
            columns = slice(k * cols, (k + 1) * cols)
            low = rows.astype(jnp.bfloat16)
            out[at, columns] = low
            sums[:, columns] += jnp.sum(low.astype(jnp.float32), 0, keepdims=True)


def attend_back_op(qkv, grad_mixed, attended, log_total, order, places, starts, tables, heads):
    seq, wide = qkv.shape
    cols = wide // 3
    block = seq // order.shape[0]
    tile = 2 * block
    low = jnp.bfloat16
    return dict(
        run=functools.partial(attend_back_run, block, heads),
        inputs=[order, places, qkv, grad_mixed, attended, log_total, starts, *tables],
        in_spaces=[pltpu.SMEM] * 2 + [pltpu.VMEM] * 8,
        outs=[
            jax.ShapeDtypeStruct((seq, wide), low),
            jax.ShapeDtypeStruct((1, wide), jnp.float32),
        ],
        out_spaces=[pltpu.VMEM] * 2,
        scratch=[
            pltpu.VMEM((cols, seq), low),
            pltpu.VMEM((seq // block, block, cols), jnp.float32),
            pltpu.VMEM((seq // block, block, cols), jnp.float32),
            pltpu.VMEM((seq // block, block, cols), jnp.float32),
            pltpu.VMEM((cols, tile), jnp.float32),
        ],
        moved=20 * seq * cols,
    )


def rotary_tables(places):
    half_rot = ROT // 2
    turns = jnp.arange(half_rot, dtype=jnp.int32)[:, None]
    freq = ROTARY_BASE ** (-turns.astype(jnp.float32) * 2.0 / ROT)
    angles = places.astype(jnp.float32)[None, :] * freq
    cosine, sine = lax.optimization_barrier((jnp.cos(angles), jnp.sin(angles)))
    lane = jnp.arange(128, dtype=jnp.int32)[None, :] % HEAD
    chosen = (lane % half_rot == turns) & (lane < ROT)

    def spread_out(values, picks):
        return lax.dot_general(
            values,
            picks.astype(jnp.float32),
            (((0,), (0,)), ((), ())),
            precision=lax.Precision.HIGHEST,
            preferred_element_type=jnp.float32,
        )

    return (
        spread_out(cosine, chosen) + (lane >= ROT).astype(jnp.float32),
        -spread_out(sine, chosen & (lane < half_rot)),
        spread_out(sine, chosen & (lane >= half_rot)),
    )


def place_order(block_pairs, axis_size):
    device_blocks = jnp.stack([block_pairs, 2 * axis_size - 1 - block_pairs], 1).reshape(-1)
    places = jnp.arange(2 * axis_size, dtype=jnp.int32)
    return jnp.sum(
        jnp.where(device_blocks[None, :] == places[:, None], places[None, :], 0), 1
    ).astype(jnp.int32)


def document_starts(docs):
    first = jnp.sum((docs < 1).astype(jnp.int32))
    second = jnp.sum((docs < 2).astype(jnp.int32))
    return jnp.where(docs == 0, 0, jnp.where(docs == 1, first, second))


def inner(left_side, right_side):
    return lax.dot_general(
        left_side, right_side, (((0,), (0,)), ((), ())), preferred_element_type=jnp.float32
    )


def times_transposed(left_side, right_side):
    return lax.dot_general(
        left_side, right_side, (((1,), (1,)), ((), ())), preferred_element_type=jnp.float32
    )


def times(left_side, right_side):
    return jnp.dot(left_side, right_side, preferred_element_type=jnp.float32)


def after(value, *earlier):
    return lax.optimization_barrier((value,) + earlier)[0]


def body(
    tokens,
    doc_ids,
    block_pairs,
    ln1_gain,
    ln1_bias,
    w_qkv,
    b_qkv,
    w_out,
    ln2_gain,
    ln2_bias,
    w_gate,
    w_up,
    w_down,
    cotangent,
):
    rows_here = tokens.shape[1]
    width = tokens.shape[2]
    head_count = width // HEAD
    ctx_size = lax.axis_size("ctx")
    fsdp_size = lax.axis_size("fsdp")
    seq_rows = rows_here * ctx_size
    position = lax.axis_index("ctx")
    heads_here = head_count // ctx_size
    cols = width // ctx_size
    shard_rows = w_qkv.shape[0]
    hidden_shard = w_down.shape[0]
    strip = hidden_shard // ctx_size

    tile = 2 * (rows_here // 2)
    order = place_order(block_pairs, ctx_size)
    starts = document_starts(doc_ids[0])
    lowest = starts[::tile] // tile
    starts = starts[None]
    device_blocks = jnp.stack([block_pairs, 2 * ctx_size - 1 - block_pairs], 1).reshape(-1, 1)
    half_rows = rows_here // 2
    places = device_blocks * half_rows + jnp.arange(half_rows, dtype=jnp.int32)[None, :]

    def strips(w, count, size):
        stride = w.shape[1] // count
        return [
            lax.dynamic_slice_in_dim(w, i * stride + position * size, size, 1)
            for i in range(count)
        ]

    qkv_strip = jnp.concatenate(strips(w_qkv, 3, cols), 1)
    hidden_here = fsdp_size * strip
    main = hidden_here // 128 * 128
    fused = ctx_size == 8 and hidden_here - main == 64 and rows_here == 256
    gate_strip = jnp.concatenate(strips(w_gate, fsdp_size, strip), 1)
    up_strip = jnp.concatenate(strips(w_up, fsdp_size, strip), 1)
    both_strip = jnp.concatenate(
        [gate_strip[:, :main], up_strip[:, :main], gate_strip[:, main:], up_strip[:, main:]], 1
    )
    down_strip = lax.dynamic_slice_in_dim(w_down, position * strip, strip, 0)
    out_piece = shard_rows // ctx_size
    out_strip = lax.dynamic_slice_in_dim(w_out, position * out_piece, out_piece, 0)
    qkv_here = lax.all_gather(qkv_strip, "fsdp", axis=0, tiled=True)
    both_here = lax.all_gather(both_strip, "fsdp", axis=0, tiled=True)
    down_here = lax.all_gather(down_strip, "fsdp", axis=0, tiled=True)

    small = jnp.concatenate([ln1_gain, ln1_bias, ln2_gain, ln2_bias, b_qkv])
    small_rows = -(-small.size // 2048) * 16
    small = jnp.pad(small, (0, small_rows * 128 - small.size)).reshape(small_rows, 128)
    grad_out = cotangent[0]
    gather_grads = gather_op(grad_out, ctx_size)
    if fused:
        gather_grads = gather_op(grad_out, ctx_size, row_half, tile_put, relative=True)
    tables = rotary_tables(places.reshape(-1))
    small, *tables = lax.optimization_barrier((small, *tables))
    small, out_here, tokens_all, grad_out_all = plane(
        ctx_size,
        1,
        z_gather_op(small, fsdp_size),
        z_gather_op(out_strip, fsdp_size),
        gather_op(tokens[0], ctx_size),
        gather_grads,
    )
    small = small.reshape(fsdp_size, small_rows * 128).astype(jnp.float32)
    gain_one, shift_one, gain_two, shift_two = (
        small[:, i * shard_rows : (i + 1) * shard_rows].reshape(1, width) for i in range(4)
    )
    bias_full = small[:, 4 * shard_rows : 4 * shard_rows + b_qkv.size]
    bias_full = bias_full.reshape(3, ctx_size, cols)
    bias_here = lax.dynamic_index_in_dim(bias_full, position, 1, keepdims=False)
    bias_here = bias_here.reshape(1, 3 * cols)
    out_full, projected, normed_all = plane(
        ctx_size,
        2,
        gather_op(
            out_here,
            ctx_size,
            column_half,
            middle_columns,
            (fsdp_size, ctx_size, out_piece, width),
        ),
        project_op(tokens_all, qkv_here, gain_one, shift_one, bias_here, tables),
    )
    out_full = out_full.reshape(width, width)
    normed_all = normed_all.reshape(seq_rows, width)
    tokens_in = tokens[0].astype(jnp.float32)
    unit_one, inverse_one = norm_rows(tokens_in, gain_one, shift_one)[1:]
    qkv_rows, attended, mixed_here, log_total = attend(
        projected.reshape(seq_rows, 3 * cols), order, lowest, starts, heads_here
    )
    mixed_here = mixed_here.reshape(ctx_size, rows_here, cols)
    mixed_rows, residual, normed_two_low = join_rows(
        mixed_here, out_full, tokens[0], gain_two, shift_two, 12
    )

    def blocks(rows):
        return rows.astype(jnp.bfloat16).reshape(ctx_size, rows_here, width)

    if fused:
        normed_two_t, both_value, hidden, grad_down_w = forward_mlp(
            normed_two_low, both_here, grad_out_all, hidden_here, 3
        )
        grad_normed_two, grad_both_w, layer_part = backward_mlp(
            grad_out_all, both_value, both_here, down_here, normed_two_t, hidden, 4
        )
    else:
        grad_out_all = grad_out_all.reshape(seq_rows, width)
        normed_two_all = plane(ctx_size, 3, gather_op(normed_two_low, ctx_size))
        normed_two_all = normed_two_all.reshape(seq_rows, width)
        both_value = times(normed_two_all, both_here)
        gate_value = jnp.concatenate(
            [both_value[:, :main], both_value[:, 2 * main : main + hidden_here]], 1
        )
        up_value = jnp.concatenate(
            [both_value[:, main : 2 * main], both_value[:, main + hidden_here :]], 1
        )
        sigmoid_gate = jax.nn.sigmoid(gate_value)
        silu_gate = gate_value * sigmoid_gate
        hidden = (silu_gate * up_value).astype(jnp.bfloat16)

        grad_down_w = inner(hidden, grad_out_all).astype(jnp.bfloat16)
        grad_hidden = times_transposed(after(grad_out_all, grad_down_w), down_here)
        grad_gate = grad_hidden * up_value * sigmoid_gate * (1.0 + gate_value * (1.0 - sigmoid_gate))
        grad_up = grad_hidden * silu_gate
        grad_both = jnp.concatenate(
            [grad_gate[:, :main], grad_up[:, :main], grad_gate[:, main:], grad_up[:, main:]], 1
        ).astype(jnp.bfloat16)
        grad_both_w = inner(normed_two_all, grad_both).astype(jnp.bfloat16)
        grad_normed_two = plane(
            ctx_size,
            4,
            scatter_op(blocks(times_transposed(after(grad_both, grad_both_w), both_here)), ctx_size),
        )
    grad_residual, grad_branch, norm_two_sums, grad_mixed = part_rows(
        grad_normed_two, residual, grad_out, gain_two, out_full, ctx_size, 5
    )

    def reduced(grad):
        return lax.psum_scatter(
            grad.astype(jnp.bfloat16), "fsdp", scatter_dimension=0, tiled=True
        )

    grad_down_w, grad_both_w = reduced(grad_down_w), reduced(grad_both_w)
    attend_op = attend_back_op(
        qkv_rows,
        grad_mixed.reshape(2 * ctx_size, half_rows, cols),
        attended,
        log_total,
        order,
        places[:, 0] // half_rows,
        starts,
        tables,
        heads_here,
    )
    down_op = gather_op(grad_down_w, ctx_size, column_half, stacked_columns)
    if fused:
        mixed_t = jnp.transpose(
            mixed_rows.reshape(rows_here, fsdp_size, ctx_size, out_piece), (2, 1, 3, 0)
        ).reshape(ctx_size, fsdp_size * out_piece, rows_here)
        out_op = produce_op(
            product_of_columns,
            rows_here,
            width,
            mixed_t,
            grad_branch,
            batch=2,
            late=4,
            kind=jnp.bfloat16,
        )
    else:
        mixed_blocks = jnp.transpose(
            mixed_rows.reshape(rows_here, fsdp_size, ctx_size, out_piece), (0, 2, 1, 3)
        ).reshape(rows_here, width)
        out_op = scatter_op(
            inner(mixed_blocks, grad_branch)
            .astype(jnp.bfloat16)
            .reshape(ctx_size, fsdp_size * out_piece, width),
            ctx_size,
        )
    if fused:
        grad_down_w, grad_out_w, grad_projected, grad_bias = plane(
            ctx_size, 6, down_op, out_op, attend_op
        )
    else:
        grad_projected, grad_bias = plane(ctx_size, 6, attend_op)
        grad_down_w, grad_out_w = plane(ctx_size, 7, down_op, out_op)
        layer_part = plane(ctx_size, 10, scatter_op(blocks(times(hidden, down_here)), ctx_size))
    grad_qkv_w = inner(normed_all, grad_projected).astype(jnp.bfloat16)
    grad_projected = after(grad_projected, grad_qkv_w)
    if fused:
        normed_op = produce_op(
            product_of_rows,
            rows_here,
            width,
            grad_projected.reshape(ctx_size, rows_here, 3 * cols),
            qkv_here,
        )
    else:
        normed_op = scatter_op(blocks(times_transposed(grad_projected, qkv_here)), ctx_size)
    grad_normed = plane(ctx_size, 8, normed_op)
    grad_down_w = unpack_rows(after(grad_down_w, grad_normed), strip)
    layer_out = residual + layer_part
    grad_qkv_w = reduced(grad_qkv_w)
    grad_tokens = grad_residual + norm_back(grad_normed, unit_one, inverse_one, gain_one)

    norm_sums = jnp.stack(
        [
            jnp.sum(grad_normed * unit_one, 0),
            jnp.sum(grad_normed, 0),
            norm_two_sums[0],
            norm_two_sums[1],
        ]
    )
    norm_sums = jnp.transpose(norm_sums.reshape(4, fsdp_size, shard_rows), (1, 0, 2)).reshape(
        fsdp_size, 1, 4 * shard_rows
    )
    bias_sums = lax.dynamic_update_slice(
        jnp.zeros((3, ctx_size, cols), jnp.float32),
        grad_bias.reshape(3, 1, cols),
        (0, position, 0),
    ).reshape(fsdp_size, 1, 3 * width // fsdp_size)
    padded = [
        jnp.pad(rows, ((0, 0), (0, extra), (0, width - rows.shape[2])))
        for rows, extra in ((norm_sums, 0), (bias_sums, 14))
    ]
    grad_out_w = jnp.concatenate(
        [grad_out_w.reshape(fsdp_size, out_piece, width)] + padded, 1
    )
    grad_out_w = grad_out_w.astype(jnp.bfloat16)
    grad_both_w, grad_qkv_w, grad_out_w = plane(
        ctx_size,
        13,
        gather_op(after(grad_both_w, grad_down_w), ctx_size),
        gather_op(grad_qkv_w, ctx_size),
        z_sum_gather_op(grad_out_w, fsdp_size, ctx_size),
    )
    sums = jnp.sum(grad_out_w[:, out_piece : out_piece + 2].astype(jnp.float32), 0)
    norm_sums = sums[0, : 4 * shard_rows].reshape(4, shard_rows)
    bias_sums = sums[1, : b_qkv.shape[0]]
    grad_out_w = unpack_rows(grad_out_w, out_piece)
    grad_gate_w, grad_up_w = unpack_both(grad_both_w, fsdp_size)
    float32 = jnp.float32
    return (
        layer_out.astype(jnp.bfloat16)[None],
        grad_tokens[None],
        norm_sums[0],
        norm_sums[1],
        unpack_columns(grad_qkv_w, 3),
        bias_sums,
        grad_out_w,
        norm_sums[2],
        norm_sums[3],
        grad_gate_w,
        grad_up_w,
        grad_down_w,
    )


def solution(mesh):
    placed = (
        P("fsdp", "ctx", None),
        P("fsdp", None),
        P(),
        P("fsdp"),
        P("fsdp"),
        P("fsdp", None),
        P("fsdp"),
        P("fsdp", None),
        P("fsdp"),
        P("fsdp"),
        P("fsdp", None),
        P("fsdp", None),
        P("fsdp", None),
        P("fsdp", "ctx", None),
    )
    return jax.shard_map(
        body,
        mesh=mesh,
        in_specs=placed,
        out_specs=(
            P("fsdp", "ctx", None),
            P("fsdp", "ctx", None),
            P("fsdp"),
            P("fsdp"),
            P("fsdp", None),
            P("fsdp"),
            P("fsdp", None),
            P("fsdp"),
            P("fsdp"),
            P("fsdp", None),
            P("fsdp", None),
            P("fsdp", None),
        ),
        check_vma=False,
    )
```

```python
import functools

import jax
import jax.numpy as jnp
from jax import lax
from jax.experimental import pallas as pl
from jax.experimental.pallas import tpu as pltpu
from jax.sharding import PartitionSpec as P

HEAD = 64
ROT = 16


NORM_EPSILON = 1e-05
ROTARY_BASE = 10000.0
MASKED_SCORE = -1e30


MESH_IDS = pl.DeviceIdType.MESH


def bit_of(index, bit):
    return index // (1 << bit) % 2


def flipped(index, mask, bits):
    result = index
    for bit in range(bits):
        if mask >> bit & 1:
            result = result + (1 - 2 * bit_of(index, bit)) * (1 << bit)
    return result


def greet(partners, along_z=()):
    barrier = pltpu.get_barrier_semaphore()
    for axis, others in (("ctx", partners), ("fsdp", along_z)):
        for other in others:
            pl.semaphore_signal(barrier, inc=1, device_id={axis: other}, device_id_type=MESH_IDS)
    pl.semaphore_wait(barrier, len(partners) + len(along_z))


def half_orders(bits):
    chip_bits = list(range(1, bits))
    return [chip_bits, chip_bits[1:] + chip_bits[:1]]


def gather_plan(bits):
    steps = []
    for order in half_orders(bits):
        held = [0]
        plan = []
        for bit in order:
            plan.append((bit, list(held)))
            held = held + [mask | 1 << bit for mask in held]
        steps.append((plan, held))
    return steps


def column_half(ref, half):
    width = ref.shape[-1] // 2
    return ref.at[..., pl.ds(half * width, width)]


def row_half(ref, half):
    rows = ref.shape[-2] // 2
    if len(ref.shape) == 2:
        return ref.at[pl.ds(half * rows, rows)]
    return ref.at[..., pl.ds(half * rows, rows), :]


def stacked_rows(ref, block, half):
    return row_half(ref.at[block], half)


def stacked_columns(ref, block, half):
    return column_half(ref.at[block], half)


def column_strip(ref, block, half, cols):
    rows = ref.shape[0] // 2
    at = block * cols if isinstance(block, int) else pl.multiple_of(block * cols, cols)
    return ref.at[pl.ds(half * rows, rows), pl.ds(at, cols)]


def last_strip(cols, ref, half):
    return column_strip(ref, ref.shape[1] // cols - 1, half, cols)


def block_view(ref, block):
    return ref.at[block]


def column_view(ref, block, width):
    return ref.at[:, pl.ds(pl.multiple_of(block * width, width), width)]


def gather_run(
    bits, take, put, relative, pace, source, out, send_sem, recv_sem, core_send, core_recv, local_sem
):
    me = lax.axis_index("ctx")
    steps = gather_plan(bits)
    finals = []
    for half in range(2):
        own = put(out, 0 if relative else me, half)
        copy = pltpu.make_async_copy(take(source, half), own, local_sem.at[half])
        copy.start()
        finals.append(copy.wait)

    def push(half, mask, bit, send, recv, index):
        block = mask if relative else flipped(me, mask, bits)
        there = mask | 1 << bit if relative else block
        copy = pltpu.make_async_remote_copy(
            src_ref=take(source, half) if mask == 0 else put(out, block, half),
            dst_ref=put(out, there, half),
            send_sem=send.at[half, index],
            recv_sem=recv.at[half, index],
            device_id={"ctx": flipped(me, 1 << bit, bits)},
            device_id_type=MESH_IDS,
        )
        copy.start()
        return copy

    def hop(half, phase, mask):
        bit, masks = steps[half][0][phase]
        index = (1 << phase) - 1 + masks.index(mask)
        copy = push(half, mask, bit, send_sem, recv_sem, index)
        finals.append(copy.wait_send)
        arriving[half, mask | 1 << bit] = copy

    def to_core(half, mask):
        copy = push(half, mask, 0, core_send, core_recv, steps[half][1].index(mask))
        finals.append(copy.wait)

    arriving = {}
    phases = bits - 1
    for phase in range(phases):
        for half in range(2):
            hop(half, phase, 0)
    for half in range(2):
        to_core(half, 0)
    for _ in range(pace):
        yield
    for phase in range(phases):
        for half in range(2):
            bit, masks = steps[half][0][phase]
            for mask in masks:
                arrived = mask | 1 << bit
                arriving[half, arrived].wait_recv()
                for later in range(phase + 1, phases):
                    hop(half, later, arrived)
                to_core(half, arrived)
        for _ in range(pace):
            yield
    for wait in finals:
        wait()


def gather_op(
    x, size, take=row_half, put=stacked_rows, out_shape=None, relative=False, pace=1
):
    bits = size.bit_length() - 1
    steps = size // 2 - 1
    dma = pltpu.SemaphoreType.DMA
    return dict(
        run=functools.partial(gather_run, bits, take, put, relative, pace),
        inputs=[x],
        in_space=pl.ANY,
        outs=[jax.ShapeDtypeStruct(out_shape or (size,) + x.shape, x.dtype)],
        out_space=pl.ANY,
        scratch=[dma((2, steps)), dma((2, steps)), dma((2, steps + 1)), dma((2, steps + 1)), dma((2,))],
        moved=2 * size * x.size * 2,
    )


def add_into(target, first, second, rows, step):
    @pl.loop(0, rows // step)
    def _(i):
        at = pl.ds(pl.multiple_of(i * step, step), step)
        target[at] = first[at].astype(target.dtype) + second[at].astype(target.dtype)


def scatter_plan(bits):
    plans = []
    for order in half_orders(bits):
        kept = [mask << 1 for mask in range(1 << (bits - 1))]
        plan = []
        for bit in order:
            plan.append((bit, [mask for mask in kept if mask >> bit & 1]))
            kept = [mask for mask in kept if not mask >> bit & 1]
        plans.append(plan)
    return plans


def farthest_first(masks):
    return sorted(masks, key=lambda mask: -bin(mask).count("1"))


def scatter_run(bits, step, part_ref, out_ref, core_buf, chip_buf, core_send, core_recv, send_sem, recv_sem):
    me = lax.axis_index("ctx")
    rows = part_ref.shape[1]
    width = part_ref.shape[2] // 2
    plans = scatter_plan(bits)
    chip_masks = farthest_first([mask << 1 for mask in range(1 << (bits - 1))])
    finals = []
    core_copies = {}
    for mask in chip_masks:
        copy = pltpu.make_async_remote_copy(
            src_ref=part_ref.at[flipped(me, mask | 1, bits)],
            dst_ref=core_buf.at[mask >> 1],
            send_sem=core_send.at[mask >> 1],
            recv_sem=core_recv.at[mask >> 1],
            device_id={"ctx": flipped(me, 1, bits)},
            device_id_type=MESH_IDS,
        )
        copy.start()
        core_copies[mask] = copy
        finals.append(copy.wait_send)
    arriving = {}

    def columns(half):
        return pl.ds(half * width, width)

    def send(half, phase, bit, mask):
        slot = plans[half][phase][1].index(mask)
        copy = pltpu.make_async_remote_copy(
            src_ref=part_ref.at[flipped(me, mask, bits), :, columns(half)],
            dst_ref=chip_buf.at[half, phase, slot],
            send_sem=send_sem.at[half, phase, slot],
            recv_sem=recv_sem.at[half, phase, slot],
            device_id={"ctx": flipped(me, 1 << bit, bits)},
            device_id_type=MESH_IDS,
        )
        copy.start()
        finals.append(copy.wait_send)
        arriving[half, phase, mask & ~(1 << bit)] = (copy, slot)

    yield
    for mask in chip_masks:
        core_copies[mask].wait_recv()
        here = part_ref.at[flipped(me, mask, bits)]
        add_into(here, here, core_buf.at[mask >> 1], rows, step)
        for half in range(2):
            bit, masks = plans[half][0]
            if mask in masks:
                send(half, 0, bit, mask)
    yield
    phases = bits - 1
    for phase in range(1, phases + 1):
        for half in range(2):
            last_bit, last_masks = plans[half][phase - 1]
            kept = farthest_first([mask & ~(1 << last_bit) for mask in last_masks])
            for mask in kept:
                copy, slot = arriving[half, phase - 1, mask]
                copy.wait_recv()
                here = part_ref.at[flipped(me, mask, bits), :, columns(half)]
                buf = chip_buf.at[half, phase - 1, slot]
                if phase < phases:
                    add_into(here, here, buf, rows, step)
                    bit, masks = plans[half][phase]
                    if mask in masks:
                        send(half, phase, bit, mask)
                else:
                    add_into(out_ref.at[:, columns(half)], here, buf, rows, step)
        yield
    for wait in finals:
        wait()


def scatter_op(part, size):
    bits = size.bit_length() - 1
    chips = size // 2
    rows, width = part.shape[1:]
    dma = pltpu.SemaphoreType.DMA
    return dict(
        run=functools.partial(scatter_run, bits, 32),
        inputs=[part],
        in_space=pltpu.VMEM,
        outs=[jax.ShapeDtypeStruct((rows, width), jnp.float32)],
        out_space=pltpu.VMEM,
        scratch=[
            pltpu.VMEM((chips, rows, width), part.dtype),
            pltpu.VMEM((2, bits - 1, chips // 2, rows, width // 2), part.dtype),
            dma((chips,)),
            dma((chips,)),
            dma((2, bits - 1, chips // 2)),
            dma((2, bits - 1, chips // 2)),
        ],
        moved=4 * part.size,
    )


def exchange_run(size, take, put, source, out, send_sem, recv_sem, local_sem):
    me = lax.axis_index("ctx")
    local = pltpu.make_async_copy(take(source, me), put(out, me), local_sem)
    local.start()
    copies = []
    for step in range(1, size):
        other = lax.rem(me + step, size)
        copy = pltpu.make_async_remote_copy(
            src_ref=take(source, other),
            dst_ref=put(out, me),
            send_sem=send_sem.at[step - 1],
            recv_sem=recv_sem.at[step - 1],
            device_id={"ctx": other},
            device_id_type=MESH_IDS,
        )
        copy.start()
        copies.append(copy)
    yield
    local.wait()
    for copy in copies:
        copy.wait()


def exchange_op(x, size, out_shape, take, put):
    dma = pltpu.SemaphoreType.DMA
    return dict(
        run=functools.partial(exchange_run, size, take, put),
        inputs=[x],
        in_space=pl.ANY,
        outs=[jax.ShapeDtypeStruct(out_shape, x.dtype)],
        out_space=pl.ANY,
        scratch=[dma((size - 1,)), dma((size - 1,)), dma],
        far=True,
        moved=4 * x.size,
    )


def z_gather_run(size, source, out, send_sem, recv_sem, local_sem):
    me = lax.axis_index("fsdp")
    local = pltpu.make_async_copy(source, out.at[me], local_sem)
    local.start()
    copies = []
    for step in range(1, size):
        copy = pltpu.make_async_remote_copy(
            src_ref=source,
            dst_ref=out.at[me],
            send_sem=send_sem.at[step - 1],
            recv_sem=recv_sem.at[step - 1],
            device_id={"fsdp": lax.rem(me + step, size)},
            device_id_type=MESH_IDS,
        )
        copy.start()
        copies.append(copy)
    for _ in range(4):
        yield
    local.wait()
    for copy in copies:
        copy.wait()


def z_gather_op(x, size):
    dma = pltpu.SemaphoreType.DMA
    return dict(
        run=functools.partial(z_gather_run, size),
        inputs=[x],
        in_space=pl.ANY,
        outs=[jax.ShapeDtypeStruct((size,) + x.shape, x.dtype)],
        out_space=pl.ANY,
        scratch=[dma((size - 1,)), dma((size - 1,)), dma],
        z=size,
        moved=2 * size * x.size,
    )


def z_scatter_run(size, source, out, buf, send_sem, recv_sem):
    me = lax.axis_index("fsdp")
    copies = []
    for step in range(1, size):
        other = lax.rem(me + step, size)
        copy = pltpu.make_async_remote_copy(
            src_ref=source.at[other],
            dst_ref=buf.at[step - 1],
            send_sem=send_sem.at[step - 1],
            recv_sem=recv_sem.at[step - 1],
            device_id={"fsdp": other},
            device_id_type=MESH_IDS,
        )
        copy.start()
        copies.append(copy)
    for _ in range(4):
        yield
    total = source[me].astype(jnp.float32)
    for step, copy in enumerate(copies):
        copy.wait()
        total += buf[step].astype(jnp.float32)
    out[...] = total.astype(out.dtype)


def z_scatter_op(x, size):
    dma = pltpu.SemaphoreType.DMA
    return dict(
        run=functools.partial(z_scatter_run, size),
        inputs=[x],
        in_space=pltpu.VMEM,
        outs=[jax.ShapeDtypeStruct(x.shape[1:], x.dtype)],
        out_space=pltpu.VMEM,
        scratch=[
            pltpu.VMEM((size - 1,) + x.shape[1:], x.dtype),
            dma((size - 1,)),
            dma((size - 1,)),
        ],
        z=size,
        moved=4 * x.size,
    )


def z_sum_gather_run(bits, size, source, out, low, buf, send_sem, recv_sem, *sems):
    yield from z_scatter_run(size, source, low, buf, send_sem, recv_sem)
    yield from gather_run(bits, column_half, stacked_columns, False, 1, low, out, *sems)


def z_sum_gather_op(x, z_size, size):
    summed = z_scatter_op(x, z_size)
    (shape,) = summed["outs"]
    gather = gather_op(shape, size)
    return dict(
        run=functools.partial(z_sum_gather_run, size.bit_length() - 1, z_size),
        inputs=[x],
        in_space=pltpu.VMEM,
        outs=gather["outs"],
        out_space=pl.ANY,
        scratch=[pltpu.VMEM(shape.shape, shape.dtype)] + summed["scratch"] + gather["scratch"],
        z=z_size,
        moved=summed["moved"] + gather["moved"],
    )


def project_run(
    cols,
    tokens,
    weights,
    gain,
    shift,
    bias,
    cosine,
    sine_low,
    sine_high,
    qkv,
    normed,
    tokens_buf,
    normed_buf,
    weights_buf,
    load_sem,
    store_sem,
    weights_sem,
):
    size, rows = tokens.shape[:2]

    def load(block):
        slot = block % 2
        return pltpu.make_async_copy(tokens.at[block], tokens_buf.at[slot], load_sem.at[slot])

    def store(block):
        slot = block % 2
        return pltpu.make_async_copy(normed_buf.at[slot], normed.at[block], store_sem.at[slot])

    load_weights = pltpu.make_async_copy(
        weights.at[:, pl.ds(0, 3 * cols)], weights_buf, weights_sem
    )
    load(0).start()
    load_weights.start()
    yield
    for block in range(size):
        if block + 1 < size:
            load(block + 1).start()
        load(block).wait()
        at = pl.ds(block * rows, rows)
        values = tokens_buf[block % 2].astype(jnp.float32)
        centered = values - jnp.mean(values, -1, keepdims=True)
        inverse = lax.rsqrt(jnp.mean(centered * centered, -1, keepdims=True) + NORM_EPSILON)
        low = (centered * inverse * gain[...] + shift[...]).astype(jnp.bfloat16)
        if block >= 2:
            store(block - 2).wait()
        normed_buf[block % 2] = low
        store(block).start()
        if block == 0:
            load_weights.wait()
        projected = jnp.dot(low, weights_buf[...], preferred_element_type=jnp.float32)
        projected += bias[...]
        tables = (cosine[at], sine_low[at], sine_high[at])
        query = turn(projected[:, :cols], *tables, cols) * HEAD ** (-0.5)
        qkv[block, :, :cols] = query.astype(jnp.bfloat16)
        key = turn(projected[:, cols : 2 * cols], *tables, cols)
        qkv[block, :, cols : 2 * cols] = key.astype(jnp.bfloat16)
        qkv[block, :, 2 * cols :] = projected[:, 2 * cols :].astype(jnp.bfloat16)
        yield
    store(size - 2).wait()
    store(size - 1).wait()


def project_op(tokens, weights, gain, shift, bias, tables):
    size, rows, width = tokens.shape
    wide = bias.shape[1]
    low = jnp.bfloat16
    dma = pltpu.SemaphoreType.DMA
    return dict(
        run=functools.partial(project_run, wide // 3),
        inputs=[tokens, weights, gain, shift, bias, *tables],
        in_spaces=[pl.ANY] * 2 + [pltpu.VMEM] * 6,
        outs=[
            jax.ShapeDtypeStruct((size, rows, wide), low),
            jax.ShapeDtypeStruct((size, rows, width), low),
        ],
        out_spaces=[pltpu.VMEM, pl.ANY],
        scratch=[
            pltpu.VMEM((2, rows, width), low),
            pltpu.VMEM((2, rows, width), low),
            pltpu.VMEM((width, wide), low),
            dma((2,)),
            dma((2,)),
            dma,
        ],
        moved=4 * tokens.size,
    )


def plane_kernel(size, parts, far, z_size, *refs):
    bits = size.bit_length() - 1
    me = lax.axis_index("ctx")
    my_z = lax.axis_index("fsdp")
    partners = [flipped(me, 1 << bit, bits) for bit in range(bits)]
    if far:
        partners = [lax.rem(me + step, size) for step in range(1, size)]
    greet(partners, [lax.rem(my_z + step, z_size) for step in range(1, z_size)])
    ins = sum(part[1] for part in parts)
    outs = sum(part[2] for part in parts)
    groups = [list(refs[:ins]), list(refs[ins : ins + outs]), list(refs[ins + outs :])]
    running = []
    for run, *counts in parts:
        own = []
        for group, count in zip(groups, counts):
            own += group[:count]
            del group[:count]
        running.append(run(*own))
    while running:
        running = [turn_of for turn_of in running if next(turn_of, 1) is None]


def spaces(op, side):
    arrays = op["inputs"] if side == "in" else op["outs"]
    return op.get(side + "_spaces") or [op[side + "_space"]] * len(arrays)


def plane(size, collective_id, *ops):
    parts = [(op["run"], len(op["inputs"]), len(op["outs"]), len(op["scratch"])) for op in ops]
    far = any(op.get("far") for op in ops)
    z_size = max(op.get("z", 1) for op in ops)
    results = pl.pallas_call(
        functools.partial(plane_kernel, size, parts, far, z_size),
        out_shape=[out for op in ops for out in op["outs"]],
        in_specs=[pl.BlockSpec(memory_space=space) for op in ops for space in spaces(op, "in")],
        out_specs=[pl.BlockSpec(memory_space=space) for op in ops for space in spaces(op, "out")],
        scratch_shapes=[scratch for op in ops for scratch in op["scratch"]],
        compiler_params=pltpu.CompilerParams(
            collective_id=collective_id, has_side_effects=True, vmem_limit_bytes=60 << 20
        ),
        cost_estimate=pl.CostEstimate(
            flops=0, bytes_accessed=sum(op["moved"] for op in ops), transcendentals=0
        ),
    )(*[x for op in ops for x in op["inputs"]])
    return results if len(results) > 1 else results[0]


def plane_groups(size, collective_id, *ops):
    groups = []
    room = 0
    for op in ops:
        need = 0 if op.get("in_space") == pl.ANY else op["moved"] * 5 // 4
        if not groups or need > room:
            groups.append([])
            room = 52 << 20
        groups[-1].append(op)
        room -= need
    results = []
    for i, group in enumerate(groups):
        got = plane(size, collective_id + i, *group)
        results += got if isinstance(got, (list, tuple)) else [got]
    return results


def swapped(tile):
    return tile % 2 + 2 * (tile // 4 % 2) + 4 * (tile // 2 % 2)


def tile_put(ref, mask, half):
    return row_half(ref.at[mask if half == 0 else swapped(mask)], half)


def tile_partner(me, bit):
    return {"ctx": flipped(me, 1 << bit, 3)}


def tile_copy(source, target, half, bit, me, send_sem, recv_sem):
    rows = source.shape[0] // 2
    at = pl.ds(half * rows, rows)
    return pltpu.make_async_remote_copy(
        src_ref=source.at[at],
        dst_ref=target.at[at],
        send_sem=send_sem.at[half],
        recv_sem=recv_sem.at[half],
        device_id=tile_partner(me, bit),
        device_id_type=MESH_IDS,
    )


def core_copy(source, target, me, send_sem, recv_sem):
    return pltpu.make_async_remote_copy(
        src_ref=source,
        dst_ref=target,
        send_sem=send_sem,
        recv_sem=recv_sem,
        device_id=tile_partner(me, 0),
        device_id_type=MESH_IDS,
    )


class TileGather:
    def __init__(self, tiles, send_sem, recv_sem, core_send, core_recv):
        me = lax.axis_index("ctx")
        self.hops = {
            target: [
                tile_copy(
                    tiles.at[source],
                    tiles.at[target],
                    half,
                    (first, 3 - first)[half],
                    me,
                    send_sem.at[target // 2 - 1],
                    recv_sem.at[target // 2 - 1],
                )
                for half in range(2)
            ]
            for source, target, first in ((0, 2, 1), (0, 4, 2), (2, 6, 2))
        }
        self.cores = [
            core_copy(tiles.at[2 * i], tiles.at[2 * i + 1], me, core_send.at[i], core_recv.at[i])
            for i in range(4)
        ]

    def before(self, tile):
        if tile == 0:
            for copy in self.hops[2]:
                copy.start()
            self.cores[0].start()
        elif tile % 2 == 1:
            self.cores[tile // 2].wait_recv()
            if tile == 1:
                for copy in self.hops[4]:
                    copy.start()
        else:
            for copy in self.hops[tile]:
                copy.wait_recv()
            if tile == 2:
                for copy in self.hops[6]:
                    copy.start()
            self.cores[tile // 2].start()

    def finish(self):
        for copies in self.hops.values():
            for copy in copies:
                copy.wait_send()
        for copy in self.cores:
            copy.wait_send()


def gather_sems():
    dma = pltpu.SemaphoreType.DMA
    return [dma((3, 2)), dma((3, 2)), dma((4,)), dma((4,))]


def part_slot(tile):
    odd = tile % 2
    return (1 - odd) * (tile // 2) + odd * (5 - tile // 4)


SCATTER_ORDER = (7, 6, 3, 2, 5, 4, 1, 0)


class TileScatter:
    def __init__(self, parts, core_buf, chip_buf, send_sem, recv_sem, core_send, core_recv):
        me = lax.axis_index("ctx")
        self.parts, self.core_buf, self.chip_buf = parts, core_buf, chip_buf
        self.hops = {
            source: [
                tile_copy(
                    parts.at[part_slot(source)],
                    chip_buf.at[source // 2 - 1],
                    half,
                    (first, 3 - first)[half],
                    me,
                    send_sem.at[source // 2 - 1],
                    recv_sem.at[source // 2 - 1],
                )
                for half in range(2)
            ]
            for source, first in ((6, 1), (4, 2), (2, 1))
        }
        self.cores = [
            core_copy(
                parts.at[part_slot(2 * i + 1)],
                core_buf.at[i],
                me,
                core_send.at[i],
                core_recv.at[i],
            )
            for i in range(4)
        ]

    def add(self, tile, buf):
        here = self.parts.at[part_slot(tile)]
        add_into(here, here, buf, here.shape[0], 32)

    def before(self, tile):
        if tile in (5, 1):
            self.cores[tile // 2 + 1].wait_send()

    def after(self, tile):
        if tile % 2 == 1:
            self.cores[tile // 2].start()
        else:
            self.settle(tile)

    def settle(self, tile):
        self.cores[tile // 2].wait_recv()
        self.add(tile, self.core_buf.at[tile // 2])
        if tile == 6 or tile == 2:
            for copy in self.hops[tile]:
                copy.start()
        if tile == 4:
            for copy in self.hops[6]:
                copy.wait_recv()
            self.add(4, self.chip_buf.at[2])
            for copy in self.hops[4]:
                copy.start()

    def finish(self, out):
        for tile in (2, 4):
            for copy in self.hops[tile]:
                copy.wait_recv()
        rows = out.shape[0]

        @pl.loop(0, rows // 32)
        def _(i):
            at = pl.ds(pl.multiple_of(i * 32, 32), 32)
            out[at] = (
                self.parts[0, at].astype(jnp.float32)
                + self.chip_buf[0, at].astype(jnp.float32)
                + self.chip_buf[1, at].astype(jnp.float32)
            ).astype(out.dtype)

        for copies in self.hops.values():
            for copy in copies:
                copy.wait_send()
        for tile in (4, 0):
            self.cores[tile // 2].wait_send()


def scatter_scratch(rows, width):
    return [
        pltpu.VMEM((6, rows, width), jnp.bfloat16),
        pltpu.VMEM((4, rows, width), jnp.bfloat16),
        pltpu.VMEM((3, rows, width), jnp.bfloat16),
    ] + gather_sems()


def produce_run(produce, batch, late, count, *refs):
    inputs, (out, *scratch) = refs[:count], refs[count:]
    me = lax.axis_index("ctx")
    scatter = TileScatter(*scratch)
    last = None
    for tile in SCATTER_ORDER:
        scatter.before(tile)
        scatter.parts[part_slot(tile)] = produce(inputs, tile, me).astype(jnp.bfloat16)
        if tile % 2 == 1:
            scatter.after(tile)
            if batch == 1 and last is not None:
                scatter.settle(last)
        last = tile
        if tile % batch == 0:
            yield
            if batch > 1:
                scatter.settle(tile)
    if batch == 1:
        scatter.settle(0)
    for _ in range(late):
        yield
    scatter.finish(out)


def produce_op(produce, rows, width, *inputs, batch=1, late=0, kind=jnp.float32):
    return dict(
        run=functools.partial(produce_run, produce, batch, late, len(inputs)),
        inputs=list(inputs),
        in_space=pltpu.VMEM,
        outs=[jax.ShapeDtypeStruct((rows, width), kind)],
        out_space=pltpu.VMEM,
        scratch=scatter_scratch(rows, width),
        moved=32 * rows * width,
    )


def tile_rows(ref, tile, me):
    half = ref.shape[1] // 2
    return jnp.concatenate(
        [ref[flipped(me, tile, 3), :half], ref[flipped(me, swapped(tile), 3), half:]], 0
    )


def product_of_rows(refs, tile, me):
    rows = tile_rows(refs[0], tile, me)
    return times_transposed(rows, refs[1][:, : rows.shape[1]])


def product_of_columns(refs, tile, me):
    return jnp.dot(
        tile_rows(refs[0], tile, me), refs[1][...], preferred_element_type=jnp.float32
    )


def unpack_both_kernel(segments, count, source, gate, up):
    hidden_size = source.shape[2] // 2
    main = hidden_size // 128 * 128
    strip = hidden_size // segments
    for out, first, last in ((gate, 0, 2 * main), (up, main, main + hidden_size)):
        owners = [
            jnp.concatenate(
                [
                    source[owner, :, first : first + main],
                    source[owner, :, last : last + hidden_size - main],
                ],
                1,
            )
            for owner in range(count)
        ]
        out[...] = jnp.concatenate(
            [
                rows[:, segment * strip : (segment + 1) * strip]
                for segment in range(segments)
                for rows in owners
            ],
            1,
        ).astype(jnp.float32)


def unpack_both(gathered, segments):
    count, rows, width = gathered.shape
    step = 64
    block = pl.BlockSpec((step, count * width // 2), lambda i: (i, 0))
    return pl.pallas_call(
        functools.partial(unpack_both_kernel, segments, count),
        grid=(rows // step,),
        in_specs=[pl.BlockSpec((count, step, width), lambda i: (0, i, 0))],
        out_specs=[block, block],
        out_shape=[jax.ShapeDtypeStruct((rows, count * width // 2), jnp.float32)] * 2,
        compiler_params=pltpu.CompilerParams(vmem_limit_bytes=60 << 20),
        cost_estimate=pl.CostEstimate(
            flops=0, bytes_accessed=6 * gathered.size, transcendentals=0
        ),
    )(gathered)


def greet_near(size):
    me = lax.axis_index("ctx")
    bits = size.bit_length() - 1
    greet([flipped(me, 1 << bit, bits) for bit in range(bits)])


def centre(values):
    centered = values - jnp.mean(values, -1, keepdims=True)
    inverse = lax.rsqrt(jnp.mean(centered * centered, -1, keepdims=True) + NORM_EPSILON)
    return centered * inverse, inverse


def join_kernel(
    size,
    mixed,
    weights,
    tokens,
    gain,
    shift,
    mixed_rows,
    residual,
    normed,
    weights_buf,
    load_sem,
    send_sem,
    recv_sem,
    local_sem,
):
    me = lax.axis_index("ctx")
    cols = mixed.shape[2]

    def load(owner):
        at = pl.ds(pl.multiple_of(owner * cols, cols), cols)
        return pltpu.make_async_copy(weights.at[at], weights_buf.at[at], load_sem.at[owner])

    others = [lax.rem(me + step, size) for step in range(size)]
    for step in range(size):
        load(lax.rem(me + size - step, size)).start()
    greet(others[1:])
    here = column_view(mixed_rows, me, cols)
    local = pltpu.make_async_copy(mixed.at[me], here, local_sem)
    local.start()
    copies = []
    for step in range(1, size):
        copy = pltpu.make_async_remote_copy(
            src_ref=mixed.at[others[step]],
            dst_ref=here,
            send_sem=send_sem.at[step - 1],
            recv_sem=recv_sem.at[step - 1],
            device_id={"ctx": others[step]},
            device_id_type=MESH_IDS,
        )
        copy.start()
        copies.append(copy)
    local.wait()
    residual[...] = tokens[...].astype(jnp.float32)
    for step in range(size):
        owner = lax.rem(me + size - step, size)
        if step > 0:
            copies[step - 1].wait_recv()
        load(owner).wait()
        at = pl.ds(pl.multiple_of(owner * cols, cols), cols)
        residual[...] += jnp.dot(
            mixed_rows[:, at], weights_buf[at], preferred_element_type=jnp.float32
        )
    unit = centre(residual[...])[0]
    normed[...] = (unit * gain[...] + shift[...]).astype(jnp.bfloat16)
    for copy in copies:
        copy.wait_send()


def join_rows(mixed, weights, tokens, gain, shift, collective_id):
    size, rows, cols = mixed.shape
    width = size * cols
    vmem = pl.BlockSpec(memory_space=pltpu.VMEM)
    any_space = pl.BlockSpec(memory_space=pl.ANY)
    low = jnp.bfloat16
    dma = pltpu.SemaphoreType.DMA
    return pl.pallas_call(
        functools.partial(join_kernel, size),
        in_specs=[any_space] * 2 + [vmem] * 3,
        out_specs=[vmem] * 3,
        out_shape=[
            jax.ShapeDtypeStruct((rows, width), low),
            jax.ShapeDtypeStruct((rows, width), jnp.float32),
            jax.ShapeDtypeStruct((rows, width), low),
        ],
        scratch_shapes=[
            pltpu.VMEM((width, width), low),
            dma((size,)),
            dma((size - 1,)),
            dma((size - 1,)),
            dma,
        ],
        compiler_params=pltpu.CompilerParams(
            collective_id=collective_id, has_side_effects=True, vmem_limit_bytes=60 << 20
        ),
        cost_estimate=pl.CostEstimate(
            flops=2 * rows * width * width, bytes_accessed=2 * width * width, transcendentals=0
        ),
    )(mixed, weights, tokens, gain, shift)


def part_kernel(
    size,
    grad_normed,
    residual,
    cotangent,
    gain,
    weights,
    grad_residual,
    grad_branch,
    sums,
    grad_mixed,
    weights_buf,
    staged,
    load_sem,
    send_sem,
    recv_sem,
    local_sem,
):
    me = lax.axis_index("ctx")
    cols = staged.shape[2]
    others = [lax.rem(me + step, size) for step in range(size)]

    def load(owner):
        at = pl.ds(pl.multiple_of(owner * cols, cols), cols)
        return pltpu.make_async_copy(weights.at[at], weights_buf.at[at], load_sem.at[owner])

    order = list(range(1, size)) + [0]
    for step in order:
        load(others[step]).start()
    greet(others[1:])
    unit, inverse = centre(residual[...])
    grads = grad_normed[...]
    scaled = grads * gain[...]
    total = cotangent[...].astype(jnp.float32) + inverse * (
        scaled
        - jnp.mean(scaled, -1, keepdims=True)
        - unit * jnp.mean(scaled * unit, -1, keepdims=True)
    )
    grad_residual[...] = total
    grad_branch[...] = total.astype(jnp.bfloat16)
    copies = []
    for step in order:
        other = others[step]
        load(other).wait()
        at = pl.ds(pl.multiple_of(other * cols, cols), cols)
        staged[step] = times_transposed(grad_branch[...], weights_buf[at]).astype(jnp.bfloat16)
        if step == 0:
            copy = pltpu.make_async_copy(staged.at[0], grad_mixed.at[me], local_sem)
        else:
            copy = pltpu.make_async_remote_copy(
                src_ref=staged.at[step],
                dst_ref=grad_mixed.at[me],
                send_sem=send_sem.at[step - 1],
                recv_sem=recv_sem.at[step - 1],
                device_id={"ctx": other},
                device_id_type=MESH_IDS,
            )
        copy.start()
        copies.append(copy)
    sums[:1] = jnp.sum(grads * unit, 0, keepdims=True)
    sums[1:] = jnp.sum(grads, 0, keepdims=True)
    for copy in copies:
        copy.wait()


def part_rows(grad_normed, residual, cotangent, gain, weights, size, collective_id):
    rows, width = grad_normed.shape
    cols = width // size
    vmem = pl.BlockSpec(memory_space=pltpu.VMEM)
    any_space = pl.BlockSpec(memory_space=pl.ANY)
    low = jnp.bfloat16
    dma = pltpu.SemaphoreType.DMA
    return pl.pallas_call(
        functools.partial(part_kernel, size),
        in_specs=[vmem] * 4 + [any_space],
        out_specs=[vmem] * 3 + [any_space],
        out_shape=[
            jax.ShapeDtypeStruct((rows, width), jnp.float32),
            jax.ShapeDtypeStruct((rows, width), low),
            jax.ShapeDtypeStruct((2, width), jnp.float32),
            jax.ShapeDtypeStruct((size, rows, cols), low),
        ],
        scratch_shapes=[
            pltpu.VMEM((width, width), low),
            pltpu.VMEM((size, rows, cols), low),
            dma((size,)),
            dma((size - 1,)),
            dma((size - 1,)),
            dma,
        ],
        compiler_params=pltpu.CompilerParams(
            collective_id=collective_id, has_side_effects=True, vmem_limit_bytes=60 << 20
        ),
        cost_estimate=pl.CostEstimate(
            flops=2 * rows * width * width, bytes_accessed=2 * width * width, transcendentals=0
        ),
    )(grad_normed, residual, cotangent, gain, weights)


def forward_kernel(
    hidden_size,
    normed,
    weights,
    grads,
    normed_t,
    values,
    hidden,
    grad_down,
    tiles,
    weights_buf,
    grads_buf,
    turned,
    values_buf,
    hidden_t,
    load_sem,
    out_sem,
    *sems,
):
    greet_near(8)
    own = pltpu.make_async_copy(normed, tiles.at[0], load_sem.at[0])
    load = pltpu.make_async_copy(weights, weights_buf, load_sem.at[1])
    own.start()
    load.start()
    pltpu.make_async_copy(grads, grads_buf, load_sem.at[2]).start()
    own.wait()
    gather = TileGather(tiles, *sems)
    rows = tiles.shape[1]
    main = hidden_size // 128 * 128

    def write_out(tile, slot):
        at = pl.ds(pl.multiple_of(tile * rows, rows), rows)
        return [
            pltpu.make_async_copy(values_buf.at[slot], values.at[tile], out_sem.at[0, slot]),
            pltpu.make_async_copy(turned.at[slot], normed_t.at[:, at], out_sem.at[1, slot]),
        ]

    @pl.loop(0, 8)
    def _(t):
        for tile in range(8):

            @pl.when(t == tile)
            def _():
                gather.before(tile)
                if tile == 0:
                    load.wait()

        slot = t % 2

        @pl.when(t >= 2)
        def _():
            for copy in write_out(t - 2, slot):
                copy.wait()

        here = tiles[t]
        value = jnp.dot(here, weights_buf[...], preferred_element_type=jnp.float32)
        values_buf[slot] = value
        gate, up = value[:, :main], value[:, main : 2 * main]
        front = gate * jax.nn.sigmoid(gate) * up
        last = value[:, 2 * main :]
        behind = last * jax.nn.sigmoid(last) * pltpu.roll(last, 64, 1)
        both = jnp.concatenate([front, behind], 1)
        hidden[t] = both[:, :hidden_size].astype(jnp.bfloat16)
        at = pl.ds(pl.multiple_of(t * rows, rows), rows)
        hidden_t[:, at] = jnp.transpose(both)[:hidden_size].astype(jnp.bfloat16)
        turned[slot] = jnp.transpose(here)
        for copy in write_out(t, slot):
            copy.start()

    pltpu.make_async_copy(grads, grads_buf, load_sem.at[2]).wait()
    width = grads_buf.shape[2]
    step = 256

    @pl.loop(0, width // step)
    def _(i):
        at = pl.ds(pl.multiple_of(i * step, step), step)
        grad_down[:, at] = jnp.dot(
            hidden_t[...],
            grads_buf[:, :, at].reshape(8 * rows, step),
            preferred_element_type=jnp.float32,
        ).astype(jnp.bfloat16)

    for tile in (6, 7):
        for copy in write_out(tile, tile % 2):
            copy.wait()
    gather.finish()


def forward_mlp(normed, weights, grads, hidden_size, collective_id):
    rows, width = normed.shape
    wide = weights.shape[1]
    any_space = pl.BlockSpec(memory_space=pl.ANY)
    vmem = pl.BlockSpec(memory_space=pltpu.VMEM)
    low = jnp.bfloat16
    dma = pltpu.SemaphoreType.DMA
    return pl.pallas_call(
        functools.partial(forward_kernel, hidden_size),
        in_specs=[any_space] * 3,
        out_specs=[any_space, any_space, vmem, vmem],
        out_shape=[
            jax.ShapeDtypeStruct((width, 8 * rows), low),
            jax.ShapeDtypeStruct((8, rows, wide), jnp.float32),
            jax.ShapeDtypeStruct((8, rows, hidden_size), low),
            jax.ShapeDtypeStruct((hidden_size, width), low),
        ],
        scratch_shapes=[
            pltpu.VMEM((8, rows, width), low),
            pltpu.VMEM(weights.shape, low),
            pltpu.VMEM((8, rows, width), low),
            pltpu.VMEM((2, width, rows), low),
            pltpu.VMEM((2, rows, wide), jnp.float32),
            pltpu.VMEM((hidden_size, 8 * rows), low),
            dma((3,)),
            dma((2, 2)),
        ]
        + gather_sems(),
        compiler_params=pltpu.CompilerParams(
            collective_id=collective_id, has_side_effects=True, vmem_limit_bytes=60 << 20
        ),
        cost_estimate=pl.CostEstimate(
            flops=16 * rows * width * (wide + hidden_size),
            bytes_accessed=64 * rows * width,
            transcendentals=0,
        ),
    )(normed, weights, grads)


def backward_kernel(
    hidden_size,
    grads,
    values,
    weights,
    down,
    normed_t,
    hidden,
    grad_normed,
    grad_both_w,
    layer_part,
    grads_buf,
    values_buf,
    weights_buf,
    down_buf,
    normed_buf,
    grad_both,
    out_buf,
    hidden_buf,
    load_sem,
    tile_sem,
    out_sem,
    *scatter_refs,
):
    greet_near(8)
    scatter = TileScatter(*scatter_refs[: len(scatter_refs) // 2])
    layer = TileScatter(*scatter_refs[len(scatter_refs) // 2 :])
    rows = grads_buf.shape[1]
    main = hidden_size // 128 * 128
    load_weights = pltpu.make_async_copy(weights, weights_buf, load_sem.at[0])
    load_down = pltpu.make_async_copy(down, down_buf, load_sem.at[1])

    def load_tile(tile, slot):
        return [
            pltpu.make_async_copy(grads.at[tile], grads_buf.at[slot], tile_sem.at[0, slot]),
            pltpu.make_async_copy(values.at[tile], values_buf.at[slot], tile_sem.at[1, slot]),
            pltpu.make_async_copy(hidden.at[tile], hidden_buf.at[slot], tile_sem.at[3, slot]),
        ]

    def load_chunk(i):
        at = pl.ds(pl.multiple_of(i * rows, rows), rows)
        return pltpu.make_async_copy(normed_t.at[at], normed_buf.at[i % 2], tile_sem.at[2, i % 2])

    load_down.start()
    for copy in load_tile(7, 1):
        copy.start()
    load_weights.start()
    load_chunk(0).start()

    @pl.loop(0, 8)
    def _(u):
        t = 7 - swapped(u)
        slot = t % 2

        @pl.when(u < 7)
        def _():
            for copy in load_tile(7 - swapped(u + 1), 1 - slot):
                copy.start()

        @pl.when(u == 0)
        def _():
            load_down.wait()

        for copy in load_tile(t, slot):
            copy.wait()
        for tile in (5, 1):

            @pl.when(t == tile)
            def _():
                scatter.before(tile)
                layer.before(tile)

        layer.parts[part_slot(t)] = jnp.dot(
            hidden_buf[slot], down_buf[...], preferred_element_type=jnp.float32
        ).astype(jnp.bfloat16)
        for tile in range(8):

            @pl.when(t == tile)
            def _():
                layer.after(tile)

        grad_hidden = lax.dot_general(
            grads_buf[slot],
            down_buf[...],
            (((1,), (1,)), ((), ())),
            preferred_element_type=jnp.float32,
        )
        value = values_buf[slot]
        gate, up, above = value[:, :main], value[:, main : 2 * main], grad_hidden[:, :main]
        sigmoid = jax.nn.sigmoid(gate)
        grad_both[t, :, :main] = (
            above * up * sigmoid * (1.0 + gate * (1.0 - sigmoid))
        ).astype(jnp.bfloat16)
        grad_both[t, :, main : 2 * main] = (above * (gate * sigmoid)).astype(jnp.bfloat16)
        last = value[:, 2 * main :]
        above = grad_hidden[:, main:]
        above = jnp.concatenate([above, jnp.zeros_like(above)], 1)
        sigmoid = jax.nn.sigmoid(last)
        to_gate = above * pltpu.roll(last, 64, 1) * sigmoid * (1.0 + last * (1.0 - sigmoid))
        to_up = pltpu.roll(above * (last * sigmoid), 64, 1)
        lane = lax.broadcasted_iota(jnp.int32, last.shape, 1)
        grad_both[t, :, 2 * main :] = jnp.where(lane < 64, to_gate, to_up).astype(jnp.bfloat16)

        @pl.when(u == 0)
        def _():
            load_weights.wait()

        scatter.parts[part_slot(t)] = lax.dot_general(
            grad_both[t],
            weights_buf[...],
            (((1,), (1,)), ((), ())),
            preferred_element_type=jnp.float32,
        ).astype(jnp.bfloat16)
        for tile in range(8):

            @pl.when(t == tile)
            def _():
                scatter.after(tile)


    chunks = normed_t.shape[0] // rows

    def store_chunk(i):
        at = pl.ds(pl.multiple_of(i * rows, rows), rows)
        return pltpu.make_async_copy(out_buf.at[i % 2], grad_both_w.at[at], out_sem.at[i % 2])

    @pl.loop(0, chunks)
    def _(i):
        @pl.when(i < chunks - 1)
        def _():
            load_chunk(i + 1).start()

        load_chunk(i).wait()

        @pl.when(i >= 2)
        def _():
            store_chunk(i - 2).wait()

        out_buf[i % 2] = jnp.dot(
            normed_buf[i % 2],
            grad_both[...].reshape(8 * rows, grad_both.shape[2]),
            preferred_element_type=jnp.float32,
        ).astype(jnp.bfloat16)
        store_chunk(i).start()

    store_chunk(chunks - 2).wait()
    store_chunk(chunks - 1).wait()
    scatter.finish(grad_normed)
    layer.finish(layer_part)


def backward_mlp(grads, values, weights, down, normed_t, hidden, collective_id):
    size, rows, width = grads.shape
    hidden_size = down.shape[0]
    wide = weights.shape[1]
    any_space = pl.BlockSpec(memory_space=pl.ANY)
    vmem = pl.BlockSpec(memory_space=pltpu.VMEM)
    low = jnp.bfloat16
    dma = pltpu.SemaphoreType.DMA
    return pl.pallas_call(
        functools.partial(backward_kernel, hidden_size),
        in_specs=[any_space] * 6,
        out_specs=[vmem, any_space, vmem],
        out_shape=[
            jax.ShapeDtypeStruct((rows, width), jnp.float32),
            jax.ShapeDtypeStruct((width, wide), low),
            jax.ShapeDtypeStruct((rows, width), jnp.float32),
        ],
        scratch_shapes=[
            pltpu.VMEM((2, rows, width), low),
            pltpu.VMEM((2, rows, wide), jnp.float32),
            pltpu.VMEM(weights.shape, low),
            pltpu.VMEM(down.shape, low),
            pltpu.VMEM((2, rows, 8 * rows), low),
            pltpu.VMEM((8, rows, wide), low),
            pltpu.VMEM((2, rows, wide), low),
            pltpu.VMEM((2, rows, hidden_size), low),
            dma((2,)),
            dma((4, 2)),
            dma((2,)),
        ]
        + scatter_scratch(rows, width) * 2,
        compiler_params=pltpu.CompilerParams(
            collective_id=collective_id, has_side_effects=True, vmem_limit_bytes=60 << 20
        ),
        cost_estimate=pl.CostEstimate(
            flops=16 * rows * width * (2 * wide + hidden_size),
            bytes_accessed=64 * rows * width,
            transcendentals=0,
        ),
    )(grads, values, weights, down, normed_t, hidden)


def unpack_rows_kernel(source, out):
    out[...] = source[...].astype(jnp.float32)


def unpack_rows(gathered, rows):
    count, _, width = gathered.shape
    out = pl.pallas_call(
        unpack_rows_kernel,
        grid=(count,),
        in_specs=[pl.BlockSpec((None, rows, width), lambda i: (i, 0, 0))],
        out_specs=pl.BlockSpec((None, rows, width), lambda i: (i, 0, 0)),
        out_shape=jax.ShapeDtypeStruct((count, rows, width), jnp.float32),
        compiler_params=pltpu.CompilerParams(vmem_limit_bytes=60 << 20),
        cost_estimate=pl.CostEstimate(
            flops=0, bytes_accessed=6 * gathered.size, transcendentals=0
        ),
    )(gathered)
    return out.reshape(count * rows, width)


def unpack_kernel(segments, count, source, out):
    strip = source.shape[2] // segments
    pieces = []
    for segment in range(segments):
        for owner in range(count):
            pieces.append(source[owner, :, segment * strip : (segment + 1) * strip])
    out[...] = jnp.concatenate(pieces, 1).astype(jnp.float32)


def unpack_columns(gathered, segments):
    count, rows, width = gathered.shape
    step = 64
    return pl.pallas_call(
        functools.partial(unpack_kernel, segments, count),
        grid=(rows // step,),
        in_specs=[pl.BlockSpec((count, step, width), lambda i: (0, i, 0))],
        out_specs=pl.BlockSpec((step, count * width), lambda i: (i, 0)),
        out_shape=jax.ShapeDtypeStruct((rows, count * width), jnp.float32),
        compiler_params=pltpu.CompilerParams(vmem_limit_bytes=60 << 20),
        cost_estimate=pl.CostEstimate(
            flops=0, bytes_accessed=6 * gathered.size, transcendentals=0
        ),
    )(gathered)


def norm_rows(values, gain_row, shift_row):
    centered = values - jnp.mean(values, -1, keepdims=True)
    inverse = lax.rsqrt(jnp.mean(centered * centered, -1, keepdims=True) + NORM_EPSILON)
    unit_rows = centered * inverse
    return (unit_rows * gain_row + shift_row, unit_rows, inverse)


def norm_back(grad_rows, unit_rows, inverse, gain_row):
    scaled = grad_rows * gain_row
    return inverse * (
        scaled
        - jnp.mean(scaled, -1, keepdims=True)
        - unit_rows * jnp.mean(scaled * unit_rows, -1, keepdims=True)
    )


def turn(rows, cosine, sine_low, sine_high, width):
    repeat = width // 128
    wide = [jnp.concatenate([table] * repeat, 1) for table in (cosine, sine_low, sine_high)]
    return (
        rows * wide[0]
        + pltpu.roll(rows, width - ROT // 2, 1) * wide[1]
        + pltpu.roll(rows, ROT // 2, 1) * wide[2]
    )


def head_stack(features_first, heads):
    owner = lax.broadcasted_iota(jnp.int32, features_first.shape, 0) // HEAD
    zero = jnp.zeros_like(features_first)
    return jnp.concatenate([jnp.where(owner == h, features_first, zero) for h in range(heads)], 1)


def row_stack(rows, heads):
    owner = lax.broadcasted_iota(jnp.int32, rows.shape, 1) // HEAD
    zero = jnp.zeros_like(rows)
    return jnp.concatenate([jnp.where(owner == h, rows, zero) for h in range(heads)], 0)


def pair_bias(key_tile, tile, heads, first_keys, diagonal):
    key_place = lax.broadcasted_iota(jnp.int32, (tile, tile), 0)
    allowed = key_place + key_tile * tile >= first_keys
    if diagonal:
        allowed &= key_place <= lax.broadcasted_iota(jnp.int32, (tile, tile), 1)
    return jnp.concatenate([jnp.where(allowed, 0.0, MASKED_SCORE)] * heads, 1)


def transposed(rows):
    return jnp.transpose(rows.astype(jnp.float32)).astype(rows.dtype)


def attend_kernel(
    block,
    heads,
    order,
    lowest,
    projected,
    starts,
    qkv,
    attended,
    mixed,
    log_total,
    value_t,
    summed,
    top,
    total,
):
    cols = heads * HEAD
    seq = projected.shape[0]
    tile = 2 * block

    @pl.loop(0, seq // block)
    def _(p):
        at = pl.ds(pl.multiple_of(p * block, block), block)
        rows = projected[pl.ds(pl.multiple_of(order[p] * block, block), block)]
        qkv[at] = rows
        value_t[:, at] = transposed(rows[:, 2 * cols :])

    @pl.loop(0, seq // tile)
    def _(i):
        at = pl.ds(pl.multiple_of(i * tile, tile), tile)
        query_t = head_stack(transposed(qkv[at, :cols]), heads)
        first_keys = starts[:, at]
        top[...] = jnp.full(top.shape, MASKED_SCORE, jnp.float32)
        total[...] = jnp.zeros_like(total)
        summed[...] = jnp.zeros_like(summed)

        def step(j, diagonal):
            keys_at = pl.ds(pl.multiple_of(j * tile, tile), tile)
            scores = jnp.dot(
                qkv[keys_at, cols : 2 * cols], query_t, preferred_element_type=jnp.float32
            )
            scores += pair_bias(j, tile, heads, first_keys, diagonal)
            old_top = top[...]
            new_top = jnp.maximum(old_top, jnp.max(scores, 0, keepdims=True))
            exps = jnp.exp(scores - new_top)
            fade = jnp.exp(old_top - new_top)
            total[...] = total[...] * fade + jnp.sum(exps, 0, keepdims=True)
            top[...] = new_top
            low = exps.astype(jnp.bfloat16)
            for h in range(heads):
                own = slice(h * tile, (h + 1) * tile)
                features = slice(h * HEAD, (h + 1) * HEAD)
                summed[features] = summed[features] * fade[:, own] + jnp.dot(
                    value_t[features, keys_at], low[:, own], preferred_element_type=jnp.float32
                )

        @pl.loop(lowest[i], i)
        def _(j):
            step(j, False)

        step(i, True)

        log_total[i] = top[...] + jnp.log(total[...])
        scale = 1.0 / total[...]
        for h in range(heads):
            features = slice(h * HEAD, (h + 1) * HEAD)
            summed[features] = summed[features] * scale[:, h * tile : (h + 1) * tile]
        rows = jnp.transpose(summed[...])
        attended[at] = rows
        for part in range(2):
            place = pl.ds(pl.multiple_of(order[2 * i + part] * block, block), block)
            mixed[place] = rows[part * block : (part + 1) * block].astype(jnp.bfloat16)


def attend(projected, order, lowest, starts, heads):
    seq, wide = projected.shape
    cols = wide // 3
    block = seq // order.shape[0]
    tile = 2 * block
    vmem = pl.BlockSpec(memory_space=pltpu.VMEM)
    smem = pl.BlockSpec(memory_space=pltpu.SMEM)
    return pl.pallas_call(
        functools.partial(attend_kernel, block, heads),
        in_specs=[smem, smem] + [vmem] * 2,
        out_specs=[vmem] * 4,
        out_shape=[
            jax.ShapeDtypeStruct((seq, wide), jnp.bfloat16),
            jax.ShapeDtypeStruct((seq, cols), jnp.float32),
            jax.ShapeDtypeStruct((seq, cols), jnp.bfloat16),
            jax.ShapeDtypeStruct((seq // tile, 1, heads * tile), jnp.float32),
        ],
        scratch_shapes=[
            pltpu.VMEM((cols, seq), jnp.bfloat16),
            pltpu.VMEM((cols, tile), jnp.float32),
            pltpu.VMEM((1, heads * tile), jnp.float32),
            pltpu.VMEM((1, heads * tile), jnp.float32),
        ],
        compiler_params=pltpu.CompilerParams(vmem_limit_bytes=48 << 20),
        cost_estimate=pl.CostEstimate(
            flops=4 * seq * seq * cols, bytes_accessed=12 * seq * cols, transcendentals=0
        ),
    )(order, lowest, projected, starts)


def attend_back_run(
    block,
    heads,
    order,
    places,
    qkv,
    grad_mixed,
    attended,
    log_total,
    starts,
    cosine,
    sine_low,
    sine_high,
    out,
    sums,
    key_t,
    grad_key,
    grad_value,
    grad_query,
    query_sum,
):
    cols = heads * HEAD
    seq = qkv.shape[0]
    tile = 2 * block

    @pl.loop(0, seq // block)
    def _(p):
        at = pl.ds(pl.multiple_of(p * block, block), block)
        key_t[:, at] = transposed(qkv[at, cols : 2 * cols])
        grad_key[p] = jnp.zeros((block, cols), jnp.float32)
        grad_value[p] = jnp.zeros((block, cols), jnp.float32)

    yield
    for i in reversed(range(seq // tile)):
        at = pl.ds(i * tile, tile)
        query = qkv[at, :cols]
        grad = jnp.concatenate(
            [
                grad_mixed[order[2 * i + part]]
                for part in range(2)
            ],
            0,
        )
        query_t = head_stack(transposed(query), heads)
        query_rows = row_stack(query, heads)
        grad_t = head_stack(transposed(grad), heads)
        grads = row_stack(grad, heads)
        products = jnp.transpose(grad.astype(jnp.float32) * attended[at])
        delta = jnp.concatenate(
            [
                jnp.sum(products[h * HEAD : (h + 1) * HEAD], 0, keepdims=True)
                for h in range(heads)
            ],
            1,
        )
        logs = log_total[i]
        first_keys = starts[:, at]
        query_sum[...] = jnp.zeros_like(query_sum)

        def step(j, diagonal):
            keys_at = pl.ds(pl.multiple_of(j * tile, tile), tile)
            scores = jnp.dot(
                qkv[keys_at, cols : 2 * cols], query_t, preferred_element_type=jnp.float32
            )
            scores += pair_bias(j, tile, heads, first_keys, diagonal)
            weights = jnp.exp(scores - logs)
            grad_soft = jnp.dot(
                qkv[keys_at, 2 * cols :], grad_t, preferred_element_type=jnp.float32
            )
            pair = pl.ds(2 * j, 2)
            grad_value[pair] += jnp.dot(
                weights.astype(jnp.bfloat16), grads, preferred_element_type=jnp.float32
            ).reshape(2, block, cols)
            grad_scores = (weights * (grad_soft - delta)).astype(jnp.bfloat16)
            grad_key[pair] += jnp.dot(
                grad_scores, query_rows, preferred_element_type=jnp.float32
            ).reshape(2, block, cols)
            for h in range(heads):
                features = slice(h * HEAD, (h + 1) * HEAD)
                query_sum[features] += jnp.dot(
                    key_t[features, keys_at],
                    grad_scores[:, h * tile : (h + 1) * tile],
                    preferred_element_type=jnp.float32,
                )

        if i > 0:

            @pl.loop(0, i)
            def _(j):
                step(j, False)

        step(i, True)
        grad_query[2 * i : 2 * i + 2] = (
            jnp.transpose(query_sum[...]) * HEAD ** (-0.5)
        ).reshape(2, block, cols)
        yield
    sums[...] = jnp.zeros_like(sums)

    @pl.loop(0, seq // block)
    def _(d):
        at = pl.ds(pl.multiple_of(d * block, block), block)
        place = places[d]
        tables = (cosine[at], -sine_low[at], -sine_high[at])
        for k, rows in enumerate(
            (
                turn(grad_query[place], *tables, cols),
                turn(grad_key[place], *tables, cols),
                grad_value[place],
            )
        ):
            columns = slice(k * cols, (k + 1) * cols)
            low = rows.astype(jnp.bfloat16)
            out[at, columns] = low
            sums[:, columns] += jnp.sum(low.astype(jnp.float32), 0, keepdims=True)


def attend_back_op(qkv, grad_mixed, attended, log_total, order, places, starts, tables, heads):
    seq, wide = qkv.shape
    cols = wide // 3
    block = seq // order.shape[0]
    tile = 2 * block
    low = jnp.bfloat16
    return dict(
        run=functools.partial(attend_back_run, block, heads),
        inputs=[order, places, qkv, grad_mixed, attended, log_total, starts, *tables],
        in_spaces=[pltpu.SMEM] * 2 + [pltpu.VMEM] * 8,
        outs=[
            jax.ShapeDtypeStruct((seq, wide), low),
            jax.ShapeDtypeStruct((1, wide), jnp.float32),
        ],
        out_spaces=[pltpu.VMEM] * 2,
        scratch=[
            pltpu.VMEM((cols, seq), low),
            pltpu.VMEM((seq // block, block, cols), jnp.float32),
            pltpu.VMEM((seq // block, block, cols), jnp.float32),
            pltpu.VMEM((seq // block, block, cols), jnp.float32),
            pltpu.VMEM((cols, tile), jnp.float32),
        ],
        moved=20 * seq * cols,
    )


def tables_run(cosines, sines, cosine, sine_low, sine_high):
    half_rot = ROT // 2
    step = 256
    yield

    @pl.loop(0, cosine.shape[0] // step)
    def _(i):
        at = pl.ds(pl.multiple_of(i * step, step), step)
        cos_rows, sin_rows = jnp.transpose(cosines[:, at]), jnp.transpose(sines[:, at])
        lane = lax.broadcasted_iota(jnp.int32, (step, 128), 1) % HEAD
        cos_wide = jnp.ones((step, 128), jnp.float32)
        sin_wide = jnp.zeros((step, 128), jnp.float32)
        for k in range(half_rot):
            own = (lane == k) | (lane == k + half_rot)
            cos_wide = jnp.where(own, cos_rows[:, k : k + 1], cos_wide)
            sin_wide = jnp.where(own, sin_rows[:, k : k + 1], sin_wide)
        cosine[at] = cos_wide
        sine_low[at] = jnp.where(lane < half_rot, -sin_wide, 0.0)
        sine_high[at] = jnp.where(lane >= half_rot, sin_wide, 0.0)


def tables_op(places):
    turns = jnp.arange(ROT // 2, dtype=jnp.int32)[:, None]
    freq = ROTARY_BASE ** (-turns.astype(jnp.float32) * 2.0 / ROT)
    angles = places.astype(jnp.float32)[None, :] * freq
    return dict(
        run=tables_run,
        inputs=[jnp.cos(angles), jnp.sin(angles)],
        in_space=pltpu.VMEM,
        outs=[jax.ShapeDtypeStruct((places.size, 128), jnp.float32)] * 3,
        out_space=pltpu.VMEM,
        scratch=[],
        moved=1024 * places.size,
    )


def place_order(block_pairs, axis_size):
    device_blocks = jnp.stack([block_pairs, 2 * axis_size - 1 - block_pairs], 1).reshape(-1)
    places = jnp.arange(2 * axis_size, dtype=jnp.int32)
    return jnp.sum(
        jnp.where(device_blocks[None, :] == places[:, None], places[None, :], 0), 1
    ).astype(jnp.int32)


def document_starts(docs):
    first = jnp.sum((docs < 1).astype(jnp.int32))
    second = jnp.sum((docs < 2).astype(jnp.int32))
    return jnp.where(docs == 0, 0, jnp.where(docs == 1, first, second))


def inner(left_side, right_side):
    return lax.dot_general(
        left_side, right_side, (((0,), (0,)), ((), ())), preferred_element_type=jnp.float32
    )


def times_transposed(left_side, right_side):
    return lax.dot_general(
        left_side, right_side, (((1,), (1,)), ((), ())), preferred_element_type=jnp.float32
    )


def times(left_side, right_side):
    return jnp.dot(left_side, right_side, preferred_element_type=jnp.float32)


def after(value, *earlier):
    return lax.optimization_barrier((value,) + earlier)[0]


def body(
    tokens,
    doc_ids,
    block_pairs,
    ln1_gain,
    ln1_bias,
    w_qkv,
    b_qkv,
    w_out,
    ln2_gain,
    ln2_bias,
    w_gate,
    w_up,
    w_down,
    cotangent,
):
    rows_here = tokens.shape[1]
    width = tokens.shape[2]
    head_count = width // HEAD
    ctx_size = lax.axis_size("ctx")
    fsdp_size = lax.axis_size("fsdp")
    seq_rows = rows_here * ctx_size
    position = lax.axis_index("ctx")
    heads_here = head_count // ctx_size
    cols = width // ctx_size
    shard_rows = w_qkv.shape[0]
    hidden_shard = w_down.shape[0]
    strip = hidden_shard // ctx_size

    tile = 2 * (rows_here // 2)
    order = place_order(block_pairs, ctx_size)
    starts = document_starts(doc_ids[0])
    lowest = starts[::tile] // tile
    starts = starts[None]
    device_blocks = jnp.stack([block_pairs, 2 * ctx_size - 1 - block_pairs], 1).reshape(-1, 1)
    half_rows = rows_here // 2
    places = device_blocks * half_rows + jnp.arange(half_rows, dtype=jnp.int32)[None, :]

    def strips(w, count, size):
        stride = w.shape[1] // count
        return [
            lax.dynamic_slice_in_dim(w, i * stride + position * size, size, 1)
            for i in range(count)
        ]

    qkv_strip = jnp.concatenate(strips(w_qkv, 3, cols) + strips(w_out, 1, cols), 1)
    hidden_here = fsdp_size * strip
    main = hidden_here // 128 * 128
    fused = ctx_size == 8 and hidden_here - main == 64 and rows_here == 256
    gate_strip = jnp.concatenate(strips(w_gate, fsdp_size, strip), 1)
    up_strip = jnp.concatenate(strips(w_up, fsdp_size, strip), 1)
    both_strip = jnp.concatenate(
        [gate_strip[:, :main], up_strip[:, :main], gate_strip[:, main:], up_strip[:, main:]], 1
    )
    down_strip = lax.dynamic_slice_in_dim(w_down, position * strip, strip, 0)
    out_piece = shard_rows // ctx_size
    qkv_here = lax.all_gather(qkv_strip, "fsdp", axis=0, tiled=True)
    both_here = lax.all_gather(both_strip, "fsdp", axis=0, tiled=True)
    down_here = lax.all_gather(down_strip, "fsdp", axis=0, tiled=True)

    small = jnp.concatenate([ln1_gain, ln1_bias, ln2_gain, ln2_bias, b_qkv])
    small_rows = -(-small.size // 2048) * 16
    small = jnp.pad(small, (0, small_rows * 128 - small.size)).reshape(small_rows, 128)
    grad_out = cotangent[0]
    gather_grads = gather_op(grad_out, ctx_size)
    if fused:
        gather_grads = gather_op(grad_out, ctx_size, row_half, tile_put, relative=True)
    *tables, small, tokens_all, grad_out_all = plane(
        ctx_size,
        1,
        tables_op(places.reshape(-1)),
        z_gather_op(small, fsdp_size),
        gather_op(tokens[0], ctx_size),
        gather_grads,
    )
    small = small.reshape(fsdp_size, small_rows * 128).astype(jnp.float32)
    gain_one, shift_one, gain_two, shift_two = (
        small[:, i * shard_rows : (i + 1) * shard_rows].reshape(1, width) for i in range(4)
    )
    bias_full = small[:, 4 * shard_rows : 4 * shard_rows + b_qkv.size]
    bias_full = bias_full.reshape(3, ctx_size, cols)
    bias_here = lax.dynamic_index_in_dim(bias_full, position, 1, keepdims=False)
    bias_here = bias_here.reshape(1, 3 * cols)
    out_full, projected, normed_all = plane(
        ctx_size,
        2,
        gather_op(
            qkv_here,
            ctx_size,
            functools.partial(last_strip, cols),
            functools.partial(column_strip, cols=cols),
            (width, width),
            pace=4,
        ),
        project_op(tokens_all, qkv_here, gain_one, shift_one, bias_here, tables),
    )
    normed_all = normed_all.reshape(seq_rows, width)
    tokens_in = tokens[0].astype(jnp.float32)
    unit_one, inverse_one = norm_rows(tokens_in, gain_one, shift_one)[1:]
    qkv_rows, attended, mixed_here, log_total = attend(
        projected.reshape(seq_rows, 3 * cols), order, lowest, starts, heads_here
    )
    mixed_here = mixed_here.reshape(ctx_size, rows_here, cols)
    mixed_rows, residual, normed_two_low = join_rows(
        mixed_here, out_full, tokens[0], gain_two, shift_two, 12
    )

    def blocks(rows):
        return rows.astype(jnp.bfloat16).reshape(ctx_size, rows_here, width)

    if fused:
        normed_two_t, both_value, hidden, grad_down_w = forward_mlp(
            normed_two_low, both_here, grad_out_all, hidden_here, 3
        )
        grad_normed_two, grad_both_w, layer_part = backward_mlp(
            grad_out_all, both_value, both_here, down_here, normed_two_t, hidden, 4
        )
    else:
        grad_out_all = grad_out_all.reshape(seq_rows, width)
        normed_two_all = plane(ctx_size, 3, gather_op(normed_two_low, ctx_size))
        normed_two_all = normed_two_all.reshape(seq_rows, width)
        both_value = times(normed_two_all, both_here)
        gate_value = jnp.concatenate(
            [both_value[:, :main], both_value[:, 2 * main : main + hidden_here]], 1
        )
        up_value = jnp.concatenate(
            [both_value[:, main : 2 * main], both_value[:, main + hidden_here :]], 1
        )
        sigmoid_gate = jax.nn.sigmoid(gate_value)
        silu_gate = gate_value * sigmoid_gate
        hidden = (silu_gate * up_value).astype(jnp.bfloat16)

        grad_down_w = inner(hidden, grad_out_all).astype(jnp.bfloat16)
        grad_hidden = times_transposed(after(grad_out_all, grad_down_w), down_here)
        grad_gate = grad_hidden * up_value * sigmoid_gate * (1.0 + gate_value * (1.0 - sigmoid_gate))
        grad_up = grad_hidden * silu_gate
        grad_both = jnp.concatenate(
            [grad_gate[:, :main], grad_up[:, :main], grad_gate[:, main:], grad_up[:, main:]], 1
        ).astype(jnp.bfloat16)
        grad_both_w = inner(normed_two_all, grad_both).astype(jnp.bfloat16)
        grad_normed_two = plane(
            ctx_size,
            4,
            scatter_op(blocks(times_transposed(after(grad_both, grad_both_w), both_here)), ctx_size),
        )
    grad_residual, grad_branch, norm_two_sums, grad_mixed = part_rows(
        grad_normed_two, residual, grad_out, gain_two, out_full, ctx_size, 5
    )

    def reduced(grad):
        return lax.psum_scatter(
            grad.astype(jnp.bfloat16), "fsdp", scatter_dimension=0, tiled=True
        )

    grad_down_w, grad_both_w = reduced(grad_down_w), reduced(grad_both_w)
    attend_op = attend_back_op(
        qkv_rows,
        grad_mixed.reshape(2 * ctx_size, half_rows, cols),
        attended,
        log_total,
        order,
        places[:, 0] // half_rows,
        starts,
        tables,
        heads_here,
    )
    down_op = gather_op(grad_down_w, ctx_size, column_half, stacked_columns)
    if fused:
        mixed_t = jnp.transpose(
            mixed_rows.reshape(rows_here, fsdp_size, ctx_size, out_piece), (2, 1, 3, 0)
        ).reshape(ctx_size, fsdp_size * out_piece, rows_here)
        out_op = produce_op(
            product_of_columns,
            rows_here,
            width,
            mixed_t,
            grad_branch,
            batch=2,
            late=4,
            kind=jnp.bfloat16,
        )
    else:
        mixed_blocks = jnp.transpose(
            mixed_rows.reshape(rows_here, fsdp_size, ctx_size, out_piece), (0, 2, 1, 3)
        ).reshape(rows_here, width)
        out_op = scatter_op(
            inner(mixed_blocks, grad_branch)
            .astype(jnp.bfloat16)
            .reshape(ctx_size, fsdp_size * out_piece, width),
            ctx_size,
        )
    if fused:
        grad_down_w, grad_out_w, grad_projected, grad_bias = plane(
            ctx_size, 6, down_op, out_op, attend_op
        )
    else:
        grad_projected, grad_bias = plane(ctx_size, 6, attend_op)
        grad_down_w, grad_out_w = plane(ctx_size, 7, down_op, out_op)
        layer_part = plane(ctx_size, 10, scatter_op(blocks(times(hidden, down_here)), ctx_size))
    grad_qkv_w = inner(normed_all, grad_projected).astype(jnp.bfloat16)
    grad_projected = after(grad_projected, grad_qkv_w)
    if fused:
        normed_op = produce_op(
            product_of_rows,
            rows_here,
            width,
            grad_projected.reshape(ctx_size, rows_here, 3 * cols),
            qkv_here,
        )
    else:
        normed_op = scatter_op(
            blocks(times_transposed(grad_projected, qkv_here[:, : 3 * cols])), ctx_size
        )
    grad_both_w, grad_normed = plane_groups(
        ctx_size, 8, gather_op(grad_both_w, ctx_size), normed_op
    )
    grad_out_w = reduced(grad_out_w)
    layer_out = residual + layer_part
    grad_qkv_w = reduced(grad_qkv_w)
    grad_tokens = grad_residual + norm_back(grad_normed, unit_one, inverse_one, gain_one)

    norm_sums = jnp.concatenate(
        [
            jnp.sum(grad_normed * unit_one, 0, keepdims=True),
            jnp.sum(grad_normed, 0, keepdims=True),
            norm_two_sums,
        ]
    )
    norm_sums = jnp.transpose(norm_sums.reshape(4, fsdp_size, shard_rows), (1, 0, 2)).reshape(
        fsdp_size, 1, 4 * shard_rows
    )
    bias_sums = lax.dynamic_update_slice(
        jnp.zeros((3, ctx_size, cols), jnp.float32),
        grad_bias.reshape(3, 1, cols),
        (0, position, 0),
    ).reshape(fsdp_size, 1, 3 * width // fsdp_size)
    sums = jnp.concatenate(
        [
            jnp.pad(rows, ((0, 0), (0, extra), (0, width - rows.shape[2])))
            for rows, extra in ((norm_sums, 0), (bias_sums, 6))
        ],
        1,
    )
    grad_qkv_w, grad_out_w, sums = plane(
        ctx_size,
        13,
        gather_op(grad_qkv_w, ctx_size, pace=2),
        gather_op(grad_out_w, ctx_size, column_half, stacked_columns, pace=2),
        z_sum_gather_op(sums, fsdp_size, ctx_size),
    )
    sums = jnp.sum(sums, 0)
    norm_sums = sums[0, : 4 * shard_rows].reshape(4, shard_rows)
    bias_sums = sums[1, : b_qkv.shape[0]]
    grad_out_w = unpack_rows(grad_out_w, out_piece)
    grad_gate_w, grad_up_w = unpack_both(grad_both_w, fsdp_size)
    float32 = jnp.float32
    return (
        layer_out.astype(jnp.bfloat16)[None],
        grad_tokens[None],
        norm_sums[0],
        norm_sums[1],
        unpack_columns(grad_qkv_w, 3),
        bias_sums,
        grad_out_w,
        norm_sums[2],
        norm_sums[3],
        grad_gate_w,
        grad_up_w,
        unpack_rows(grad_down_w, strip),
    )


def solution(mesh):
    placed = (
        P("fsdp", "ctx", None),
        P("fsdp", None),
        P(),
        P("fsdp"),
        P("fsdp"),
        P("fsdp", None),
        P("fsdp"),
        P("fsdp", None),
        P("fsdp"),
        P("fsdp"),
        P("fsdp", None),
        P("fsdp", None),
        P("fsdp", None),
        P("fsdp", "ctx", None),
    )
    return jax.shard_map(
        body,
        mesh=mesh,
        in_specs=placed,
        out_specs=(
            P("fsdp", "ctx", None),
            P("fsdp", "ctx", None),
            P("fsdp"),
            P("fsdp"),
            P("fsdp", None),
            P("fsdp"),
            P("fsdp", None),
            P("fsdp"),
            P("fsdp"),
            P("fsdp", None),
            P("fsdp", None),
            P("fsdp", None),
        ),
        check_vma=False,
    )
```

```python
import functools

import jax
import jax.numpy as jnp
from jax import lax
from jax.experimental import pallas as pl
from jax.experimental.pallas import tpu as pltpu
from jax.sharding import PartitionSpec as P

HEAD = 64
ROT = 16


NORM_EPSILON = 1e-05
ROTARY_BASE = 10000.0
MASKED_SCORE = -1e30


MESH_IDS = pl.DeviceIdType.MESH


def bit_of(index, bit):
    return index // (1 << bit) % 2


def flipped(index, mask, bits):
    result = index
    for bit in range(bits):
        if mask >> bit & 1:
            result = result + (1 - 2 * bit_of(index, bit)) * (1 << bit)
    return result


def greet(partners, along_z=()):
    barrier = pltpu.get_barrier_semaphore()
    for axis, others in (("ctx", partners), ("fsdp", along_z)):
        for other in others:
            pl.semaphore_signal(barrier, inc=1, device_id={axis: other}, device_id_type=MESH_IDS)
    pl.semaphore_wait(barrier, len(partners) + len(along_z))


def half_orders(bits):
    chip_bits = list(range(1, bits))
    return [chip_bits, chip_bits[1:] + chip_bits[:1]]


def gather_plan(bits):
    steps = []
    for order in half_orders(bits):
        held = [0]
        plan = []
        for bit in order:
            plan.append((bit, list(held)))
            held = held + [mask | 1 << bit for mask in held]
        steps.append((plan, held))
    return steps


def column_half(ref, half):
    width = ref.shape[-1] // 2
    return ref.at[..., pl.ds(half * width, width)]


def row_half(ref, half):
    rows = ref.shape[-2] // 2
    if len(ref.shape) == 2:
        return ref.at[pl.ds(half * rows, rows)]
    return ref.at[..., pl.ds(half * rows, rows), :]


def stacked_rows(ref, block, half):
    return row_half(ref.at[block], half)


def stacked_columns(ref, block, half):
    return column_half(ref.at[block], half)


def column_strip(ref, block, half, cols):
    rows = ref.shape[0] // 2
    at = block * cols if isinstance(block, int) else pl.multiple_of(block * cols, cols)
    return ref.at[pl.ds(half * rows, rows), pl.ds(at, cols)]


def last_strip(cols, ref, half):
    return column_strip(ref, ref.shape[1] // cols - 1, half, cols)


def block_view(ref, block):
    return ref.at[block]


def column_view(ref, block, width):
    return ref.at[:, pl.ds(pl.multiple_of(block * width, width), width)]


def gather_run(
    bits, take, put, relative, pace, source, out, send_sem, recv_sem, core_send, core_recv, local_sem
):
    me = lax.axis_index("ctx")
    steps = gather_plan(bits)
    finals = []
    for half in range(2):
        own = put(out, 0 if relative else me, half)
        copy = pltpu.make_async_copy(take(source, half), own, local_sem.at[half])
        copy.start()
        finals.append(copy.wait)

    def push(half, mask, bit, send, recv, index):
        block = mask if relative else flipped(me, mask, bits)
        there = mask | 1 << bit if relative else block
        copy = pltpu.make_async_remote_copy(
            src_ref=take(source, half) if mask == 0 else put(out, block, half),
            dst_ref=put(out, there, half),
            send_sem=send.at[half, index],
            recv_sem=recv.at[half, index],
            device_id={"ctx": flipped(me, 1 << bit, bits)},
            device_id_type=MESH_IDS,
        )
        copy.start()
        return copy

    def hop(half, phase, mask):
        bit, masks = steps[half][0][phase]
        index = (1 << phase) - 1 + masks.index(mask)
        copy = push(half, mask, bit, send_sem, recv_sem, index)
        finals.append(copy.wait_send)
        arriving[half, mask | 1 << bit] = copy

    def to_core(half, mask):
        copy = push(half, mask, 0, core_send, core_recv, steps[half][1].index(mask))
        finals.append(copy.wait)

    arriving = {}
    phases = bits - 1
    for phase in range(phases):
        for half in range(2):
            hop(half, phase, 0)
    for half in range(2):
        to_core(half, 0)
    for _ in range(pace):
        yield
    for phase in range(phases):
        for half in range(2):
            bit, masks = steps[half][0][phase]
            for mask in masks:
                arrived = mask | 1 << bit
                arriving[half, arrived].wait_recv()
                for later in range(phase + 1, phases):
                    hop(half, later, arrived)
                to_core(half, arrived)
        for _ in range(pace):
            yield
    for wait in finals:
        wait()


def gather_op(
    x, size, take=row_half, put=stacked_rows, out_shape=None, relative=False, pace=1
):
    bits = size.bit_length() - 1
    steps = size // 2 - 1
    dma = pltpu.SemaphoreType.DMA
    return dict(
        run=functools.partial(gather_run, bits, take, put, relative, pace),
        inputs=[x],
        in_space=pl.ANY,
        outs=[jax.ShapeDtypeStruct(out_shape or (size,) + x.shape, x.dtype)],
        out_space=pl.ANY,
        scratch=[dma((2, steps)), dma((2, steps)), dma((2, steps + 1)), dma((2, steps + 1)), dma((2,))],
        moved=2 * size * x.size * 2,
    )


def add_into(target, first, second, rows, step):
    @pl.loop(0, rows // step)
    def _(i):
        at = pl.ds(pl.multiple_of(i * step, step), step)
        target[at] = first[at].astype(target.dtype) + second[at].astype(target.dtype)


def scatter_plan(bits):
    plans = []
    for order in half_orders(bits):
        kept = [mask << 1 for mask in range(1 << (bits - 1))]
        plan = []
        for bit in order:
            plan.append((bit, [mask for mask in kept if mask >> bit & 1]))
            kept = [mask for mask in kept if not mask >> bit & 1]
        plans.append(plan)
    return plans


def farthest_first(masks):
    return sorted(masks, key=lambda mask: -bin(mask).count("1"))


def scatter_run(bits, step, part_ref, out_ref, core_buf, chip_buf, core_send, core_recv, send_sem, recv_sem):
    me = lax.axis_index("ctx")
    rows = part_ref.shape[1]
    width = part_ref.shape[2] // 2
    plans = scatter_plan(bits)
    chip_masks = farthest_first([mask << 1 for mask in range(1 << (bits - 1))])
    finals = []
    core_copies = {}
    for mask in chip_masks:
        copy = pltpu.make_async_remote_copy(
            src_ref=part_ref.at[flipped(me, mask | 1, bits)],
            dst_ref=core_buf.at[mask >> 1],
            send_sem=core_send.at[mask >> 1],
            recv_sem=core_recv.at[mask >> 1],
            device_id={"ctx": flipped(me, 1, bits)},
            device_id_type=MESH_IDS,
        )
        copy.start()
        core_copies[mask] = copy
        finals.append(copy.wait_send)
    arriving = {}

    def columns(half):
        return pl.ds(half * width, width)

    def send(half, phase, bit, mask):
        slot = plans[half][phase][1].index(mask)
        copy = pltpu.make_async_remote_copy(
            src_ref=part_ref.at[flipped(me, mask, bits), :, columns(half)],
            dst_ref=chip_buf.at[half, phase, slot],
            send_sem=send_sem.at[half, phase, slot],
            recv_sem=recv_sem.at[half, phase, slot],
            device_id={"ctx": flipped(me, 1 << bit, bits)},
            device_id_type=MESH_IDS,
        )
        copy.start()
        finals.append(copy.wait_send)
        arriving[half, phase, mask & ~(1 << bit)] = (copy, slot)

    yield
    for mask in chip_masks:
        core_copies[mask].wait_recv()
        here = part_ref.at[flipped(me, mask, bits)]
        add_into(here, here, core_buf.at[mask >> 1], rows, step)
        for half in range(2):
            bit, masks = plans[half][0]
            if mask in masks:
                send(half, 0, bit, mask)
    yield
    phases = bits - 1
    for phase in range(1, phases + 1):
        for half in range(2):
            last_bit, last_masks = plans[half][phase - 1]
            kept = farthest_first([mask & ~(1 << last_bit) for mask in last_masks])
            for mask in kept:
                copy, slot = arriving[half, phase - 1, mask]
                copy.wait_recv()
                here = part_ref.at[flipped(me, mask, bits), :, columns(half)]
                buf = chip_buf.at[half, phase - 1, slot]
                if phase < phases:
                    add_into(here, here, buf, rows, step)
                    bit, masks = plans[half][phase]
                    if mask in masks:
                        send(half, phase, bit, mask)
                else:
                    add_into(out_ref.at[:, columns(half)], here, buf, rows, step)
        yield
    for wait in finals:
        wait()


def scatter_op(part, size):
    bits = size.bit_length() - 1
    chips = size // 2
    rows, width = part.shape[1:]
    dma = pltpu.SemaphoreType.DMA
    return dict(
        run=functools.partial(scatter_run, bits, 32),
        inputs=[part],
        in_space=pltpu.VMEM,
        outs=[jax.ShapeDtypeStruct((rows, width), jnp.float32)],
        out_space=pltpu.VMEM,
        scratch=[
            pltpu.VMEM((chips, rows, width), part.dtype),
            pltpu.VMEM((2, bits - 1, chips // 2, rows, width // 2), part.dtype),
            dma((chips,)),
            dma((chips,)),
            dma((2, bits - 1, chips // 2)),
            dma((2, bits - 1, chips // 2)),
        ],
        moved=4 * part.size,
    )


def exchange_run(size, take, put, source, out, send_sem, recv_sem, local_sem):
    me = lax.axis_index("ctx")
    local = pltpu.make_async_copy(take(source, me), put(out, me), local_sem)
    local.start()
    copies = []
    for step in range(1, size):
        other = lax.rem(me + step, size)
        copy = pltpu.make_async_remote_copy(
            src_ref=take(source, other),
            dst_ref=put(out, me),
            send_sem=send_sem.at[step - 1],
            recv_sem=recv_sem.at[step - 1],
            device_id={"ctx": other},
            device_id_type=MESH_IDS,
        )
        copy.start()
        copies.append(copy)
    yield
    local.wait()
    for copy in copies:
        copy.wait()


def exchange_op(x, size, out_shape, take, put):
    dma = pltpu.SemaphoreType.DMA
    return dict(
        run=functools.partial(exchange_run, size, take, put),
        inputs=[x],
        in_space=pl.ANY,
        outs=[jax.ShapeDtypeStruct(out_shape, x.dtype)],
        out_space=pl.ANY,
        scratch=[dma((size - 1,)), dma((size - 1,)), dma],
        far=True,
        moved=4 * x.size,
    )


def z_gather_run(size, source, out, send_sem, recv_sem, local_sem):
    me = lax.axis_index("fsdp")
    local = pltpu.make_async_copy(source, out.at[me], local_sem)
    local.start()
    copies = []
    for step in range(1, size):
        copy = pltpu.make_async_remote_copy(
            src_ref=source,
            dst_ref=out.at[me],
            send_sem=send_sem.at[step - 1],
            recv_sem=recv_sem.at[step - 1],
            device_id={"fsdp": lax.rem(me + step, size)},
            device_id_type=MESH_IDS,
        )
        copy.start()
        copies.append(copy)
    for _ in range(4):
        yield
    local.wait()
    for copy in copies:
        copy.wait()


def z_gather_op(x, size):
    dma = pltpu.SemaphoreType.DMA
    return dict(
        run=functools.partial(z_gather_run, size),
        inputs=[x],
        in_space=pl.ANY,
        outs=[jax.ShapeDtypeStruct((size,) + x.shape, x.dtype)],
        out_space=pl.ANY,
        scratch=[dma((size - 1,)), dma((size - 1,)), dma],
        z=size,
        moved=2 * size * x.size,
    )


def z_scatter_run(size, source, out, buf, send_sem, recv_sem):
    me = lax.axis_index("fsdp")
    copies = []
    for step in range(1, size):
        other = lax.rem(me + step, size)
        copy = pltpu.make_async_remote_copy(
            src_ref=source.at[other],
            dst_ref=buf.at[step - 1],
            send_sem=send_sem.at[step - 1],
            recv_sem=recv_sem.at[step - 1],
            device_id={"fsdp": other},
            device_id_type=MESH_IDS,
        )
        copy.start()
        copies.append(copy)
    for _ in range(4):
        yield
    total = source[me].astype(jnp.float32)
    for step, copy in enumerate(copies):
        copy.wait()
        total += buf[step].astype(jnp.float32)
    out[...] = total.astype(out.dtype)


def z_scatter_op(x, size):
    dma = pltpu.SemaphoreType.DMA
    return dict(
        run=functools.partial(z_scatter_run, size),
        inputs=[x],
        in_space=pltpu.VMEM,
        outs=[jax.ShapeDtypeStruct(x.shape[1:], x.dtype)],
        out_space=pltpu.VMEM,
        scratch=[
            pltpu.VMEM((size - 1,) + x.shape[1:], x.dtype),
            dma((size - 1,)),
            dma((size - 1,)),
        ],
        z=size,
        moved=4 * x.size,
    )


def z_sum_gather_run(bits, size, source, out, low, buf, send_sem, recv_sem, *sems):
    yield from z_scatter_run(size, source, low, buf, send_sem, recv_sem)
    yield from gather_run(bits, column_half, stacked_columns, False, 1, low, out, *sems)


def z_sum_gather_op(x, z_size, size):
    summed = z_scatter_op(x, z_size)
    (shape,) = summed["outs"]
    gather = gather_op(shape, size)
    return dict(
        run=functools.partial(z_sum_gather_run, size.bit_length() - 1, z_size),
        inputs=[x],
        in_space=pltpu.VMEM,
        outs=gather["outs"],
        out_space=pl.ANY,
        scratch=[pltpu.VMEM(shape.shape, shape.dtype)] + summed["scratch"] + gather["scratch"],
        z=z_size,
        moved=summed["moved"] + gather["moved"],
    )


def project_run(
    cols,
    tokens,
    weights,
    gain,
    shift,
    bias,
    cosine,
    sine_low,
    sine_high,
    qkv,
    normed,
    tokens_buf,
    normed_buf,
    weights_buf,
    load_sem,
    store_sem,
    weights_sem,
):
    size, rows = tokens.shape[:2]

    def load(block):
        slot = block % 2
        return pltpu.make_async_copy(tokens.at[block], tokens_buf.at[slot], load_sem.at[slot])

    def store(block):
        slot = block % 2
        at = pl.ds(block * rows, rows)
        return pltpu.make_async_copy(normed_buf.at[slot], normed.at[:, at], store_sem.at[slot])

    load_weights = pltpu.make_async_copy(
        weights.at[:, pl.ds(0, 3 * cols)], weights_buf, weights_sem
    )
    load(0).start()
    load_weights.start()
    yield
    for block in range(size):
        if block + 1 < size:
            load(block + 1).start()
        load(block).wait()
        at = pl.ds(block * rows, rows)
        values = tokens_buf[block % 2].astype(jnp.float32)
        centered = values - jnp.mean(values, -1, keepdims=True)
        inverse = lax.rsqrt(jnp.mean(centered * centered, -1, keepdims=True) + NORM_EPSILON)
        low = (centered * inverse * gain[...] + shift[...]).astype(jnp.bfloat16)
        if block >= 2:
            store(block - 2).wait()
        normed_buf[block % 2] = jnp.transpose(low)
        store(block).start()
        if block == 0:
            load_weights.wait()
        projected = jnp.dot(low, weights_buf[...], preferred_element_type=jnp.float32)
        projected += bias[...]
        tables = (cosine[at], sine_low[at], sine_high[at])
        query = turn(projected[:, :cols], *tables, cols) * HEAD ** (-0.5)
        qkv[block, :, :cols] = query.astype(jnp.bfloat16)
        key = turn(projected[:, cols : 2 * cols], *tables, cols)
        qkv[block, :, cols : 2 * cols] = key.astype(jnp.bfloat16)
        qkv[block, :, 2 * cols :] = projected[:, 2 * cols :].astype(jnp.bfloat16)
        yield
    store(size - 2).wait()
    store(size - 1).wait()


def project_op(tokens, weights, gain, shift, bias, tables):
    size, rows, width = tokens.shape
    wide = bias.shape[1]
    low = jnp.bfloat16
    dma = pltpu.SemaphoreType.DMA
    return dict(
        run=functools.partial(project_run, wide // 3),
        inputs=[tokens, weights, gain, shift, bias, *tables],
        in_spaces=[pl.ANY] * 2 + [pltpu.VMEM] * 6,
        outs=[
            jax.ShapeDtypeStruct((size, rows, wide), low),
            jax.ShapeDtypeStruct((width, size * rows), low),
        ],
        out_spaces=[pltpu.VMEM, pl.ANY],
        scratch=[
            pltpu.VMEM((2, rows, width), low),
            pltpu.VMEM((2, width, rows), low),
            pltpu.VMEM((width, wide), low),
            dma((2,)),
            dma((2,)),
            dma,
        ],
        moved=4 * tokens.size,
    )


def plane_kernel(size, parts, far, z_size, *refs):
    bits = size.bit_length() - 1
    me = lax.axis_index("ctx")
    my_z = lax.axis_index("fsdp")
    partners = [flipped(me, 1 << bit, bits) for bit in range(bits)]
    if far:
        partners = [lax.rem(me + step, size) for step in range(1, size)]
    greet(partners, [lax.rem(my_z + step, z_size) for step in range(1, z_size)])
    ins = sum(part[1] for part in parts)
    outs = sum(part[2] for part in parts)
    groups = [list(refs[:ins]), list(refs[ins : ins + outs]), list(refs[ins + outs :])]
    running = []
    for run, *counts in parts:
        own = []
        for group, count in zip(groups, counts):
            own += group[:count]
            del group[:count]
        running.append(run(*own))
    while running:
        running = [turn_of for turn_of in running if next(turn_of, 1) is None]


def spaces(op, side):
    arrays = op["inputs"] if side == "in" else op["outs"]
    return op.get(side + "_spaces") or [op[side + "_space"]] * len(arrays)


def plane(size, collective_id, *ops):
    parts = [(op["run"], len(op["inputs"]), len(op["outs"]), len(op["scratch"])) for op in ops]
    far = any(op.get("far") for op in ops)
    z_size = max(op.get("z", 1) for op in ops)
    results = pl.pallas_call(
        functools.partial(plane_kernel, size, parts, far, z_size),
        out_shape=[out for op in ops for out in op["outs"]],
        in_specs=[pl.BlockSpec(memory_space=space) for op in ops for space in spaces(op, "in")],
        out_specs=[pl.BlockSpec(memory_space=space) for op in ops for space in spaces(op, "out")],
        scratch_shapes=[scratch for op in ops for scratch in op["scratch"]],
        compiler_params=pltpu.CompilerParams(
            collective_id=collective_id, has_side_effects=True, vmem_limit_bytes=60 << 20
        ),
        cost_estimate=pl.CostEstimate(
            flops=0, bytes_accessed=sum(op["moved"] for op in ops), transcendentals=0
        ),
    )(*[x for op in ops for x in op["inputs"]])
    return results if len(results) > 1 else results[0]


def plane_groups(size, collective_id, *ops):
    groups = []
    room = 0
    for op in ops:
        need = 0 if op.get("in_space") == pl.ANY else op["moved"] * 5 // 4
        if not groups or need > room:
            groups.append([])
            room = 52 << 20
        groups[-1].append(op)
        room -= need
    results = []
    for i, group in enumerate(groups):
        got = plane(size, collective_id + i, *group)
        results += got if isinstance(got, (list, tuple)) else [got]
    return results


def swapped(tile):
    return tile % 2 + 2 * (tile // 4 % 2) + 4 * (tile // 2 % 2)


def tile_put(ref, mask, half):
    return row_half(ref.at[mask if half == 0 else swapped(mask)], half)


def tile_partner(me, bit):
    return {"ctx": flipped(me, 1 << bit, 3)}


def tile_copy(source, target, half, bit, me, send_sem, recv_sem):
    rows = source.shape[0] // 2
    at = pl.ds(half * rows, rows)
    return pltpu.make_async_remote_copy(
        src_ref=source.at[at],
        dst_ref=target.at[at],
        send_sem=send_sem.at[half],
        recv_sem=recv_sem.at[half],
        device_id=tile_partner(me, bit),
        device_id_type=MESH_IDS,
    )


def core_copy(source, target, me, send_sem, recv_sem):
    return pltpu.make_async_remote_copy(
        src_ref=source,
        dst_ref=target,
        send_sem=send_sem,
        recv_sem=recv_sem,
        device_id=tile_partner(me, 0),
        device_id_type=MESH_IDS,
    )


class TileGather:
    def __init__(self, tiles, send_sem, recv_sem, core_send, core_recv):
        me = lax.axis_index("ctx")
        self.hops = {
            target: [
                tile_copy(
                    tiles.at[source],
                    tiles.at[target],
                    half,
                    (first, 3 - first)[half],
                    me,
                    send_sem.at[target // 2 - 1],
                    recv_sem.at[target // 2 - 1],
                )
                for half in range(2)
            ]
            for source, target, first in ((0, 2, 1), (0, 4, 2), (2, 6, 2))
        }
        self.cores = [
            core_copy(tiles.at[2 * i], tiles.at[2 * i + 1], me, core_send.at[i], core_recv.at[i])
            for i in range(4)
        ]

    def before(self, tile):
        if tile == 0:
            for copy in self.hops[2]:
                copy.start()
            self.cores[0].start()
        elif tile % 2 == 1:
            self.cores[tile // 2].wait_recv()
            if tile == 1:
                for copy in self.hops[4]:
                    copy.start()
        else:
            for copy in self.hops[tile]:
                copy.wait_recv()
            if tile == 2:
                for copy in self.hops[6]:
                    copy.start()
            self.cores[tile // 2].start()

    def finish(self):
        for copies in self.hops.values():
            for copy in copies:
                copy.wait_send()
        for copy in self.cores:
            copy.wait_send()


def gather_sems():
    dma = pltpu.SemaphoreType.DMA
    return [dma((3, 2)), dma((3, 2)), dma((4,)), dma((4,))]


def part_slot(tile):
    odd = tile % 2
    return (1 - odd) * (tile // 2) + odd * (5 - tile // 4)


SCATTER_ORDER = (7, 6, 3, 2, 5, 4, 1, 0)


class TileScatter:
    def __init__(self, parts, core_buf, chip_buf, send_sem, recv_sem, core_send, core_recv):
        me = lax.axis_index("ctx")
        self.parts, self.core_buf, self.chip_buf = parts, core_buf, chip_buf
        self.hops = {
            source: [
                tile_copy(
                    parts.at[part_slot(source)],
                    chip_buf.at[source // 2 - 1],
                    half,
                    (first, 3 - first)[half],
                    me,
                    send_sem.at[source // 2 - 1],
                    recv_sem.at[source // 2 - 1],
                )
                for half in range(2)
            ]
            for source, first in ((6, 1), (4, 2), (2, 1))
        }
        self.cores = [
            core_copy(
                parts.at[part_slot(2 * i + 1)],
                core_buf.at[i],
                me,
                core_send.at[i],
                core_recv.at[i],
            )
            for i in range(4)
        ]

    def add(self, tile, buf):
        here = self.parts.at[part_slot(tile)]
        add_into(here, here, buf, here.shape[0], 32)

    def before(self, tile):
        if tile in (5, 1):
            self.cores[tile // 2 + 1].wait_send()

    def after(self, tile):
        if tile % 2 == 1:
            self.cores[tile // 2].start()
        else:
            self.settle(tile)

    def settle(self, tile):
        self.cores[tile // 2].wait_recv()
        self.add(tile, self.core_buf.at[tile // 2])
        if tile == 6 or tile == 2:
            for copy in self.hops[tile]:
                copy.start()
        if tile == 4:
            for copy in self.hops[6]:
                copy.wait_recv()
            self.add(4, self.chip_buf.at[2])
            for copy in self.hops[4]:
                copy.start()

    def finish(self, out):
        for tile in (2, 4):
            for copy in self.hops[tile]:
                copy.wait_recv()
        rows = out.shape[0]

        @pl.loop(0, rows // 32)
        def _(i):
            at = pl.ds(pl.multiple_of(i * 32, 32), 32)
            out[at] = (
                self.parts[0, at].astype(jnp.float32)
                + self.chip_buf[0, at].astype(jnp.float32)
                + self.chip_buf[1, at].astype(jnp.float32)
            ).astype(out.dtype)

        for copies in self.hops.values():
            for copy in copies:
                copy.wait_send()
        for tile in (4, 0):
            self.cores[tile // 2].wait_send()


def scatter_scratch(rows, width):
    return [
        pltpu.VMEM((6, rows, width), jnp.bfloat16),
        pltpu.VMEM((4, rows, width), jnp.bfloat16),
        pltpu.VMEM((3, rows, width), jnp.bfloat16),
    ] + gather_sems()


def produce_run(produce, batch, late, count, *refs):
    inputs, (out, *scratch) = refs[:count], refs[count:]
    me = lax.axis_index("ctx")
    scatter = TileScatter(*scratch)
    last = None
    for tile in SCATTER_ORDER:
        scatter.before(tile)
        scatter.parts[part_slot(tile)] = produce(inputs, tile, me).astype(jnp.bfloat16)
        if tile % 2 == 1:
            scatter.after(tile)
            if batch == 1 and last is not None:
                scatter.settle(last)
        last = tile
        if tile % batch == 0:
            yield
            if batch > 1:
                scatter.settle(tile)
    if batch == 1:
        scatter.settle(0)
    for _ in range(late):
        yield
    scatter.finish(out)


def produce_op(produce, rows, width, *inputs, batch=1, late=0, kind=jnp.float32):
    return dict(
        run=functools.partial(produce_run, produce, batch, late, len(inputs)),
        inputs=list(inputs),
        in_space=pltpu.VMEM,
        outs=[jax.ShapeDtypeStruct((rows, width), kind)],
        out_space=pltpu.VMEM,
        scratch=scatter_scratch(rows, width),
        moved=32 * rows * width,
    )


def tile_rows(ref, tile, me):
    half = ref.shape[1] // 2
    return jnp.concatenate(
        [ref[flipped(me, tile, 3), :half], ref[flipped(me, swapped(tile), 3), half:]], 0
    )


def product_of_rows(refs, tile, me):
    rows = tile_rows(refs[0], tile, me)
    return times_transposed(rows, refs[1][:, : rows.shape[1]])


def product_of_columns(refs, tile, me):
    return jnp.dot(
        tile_rows(refs[0], tile, me), refs[1][...], preferred_element_type=jnp.float32
    )


def unpack_both_kernel(segments, count, source, gate, up):
    hidden_size = source.shape[2] // 2
    main = hidden_size // 128 * 128
    strip = hidden_size // segments
    for out, first, last in ((gate, 0, 2 * main), (up, main, main + hidden_size)):
        owners = [
            jnp.concatenate(
                [
                    source[owner, :, first : first + main],
                    source[owner, :, last : last + hidden_size - main],
                ],
                1,
            )
            for owner in range(count)
        ]
        out[...] = jnp.concatenate(
            [
                rows[:, segment * strip : (segment + 1) * strip]
                for segment in range(segments)
                for rows in owners
            ],
            1,
        ).astype(jnp.float32)


def unpack_both(gathered, segments):
    count, rows, width = gathered.shape
    step = min(128, rows)
    block = pl.BlockSpec((step, count * width // 2), lambda i: (i, 0))
    return pl.pallas_call(
        functools.partial(unpack_both_kernel, segments, count),
        grid=(rows // step,),
        in_specs=[pl.BlockSpec((count, step, width), lambda i: (0, i, 0))],
        out_specs=[block, block],
        out_shape=[jax.ShapeDtypeStruct((rows, count * width // 2), jnp.float32)] * 2,
        compiler_params=pltpu.CompilerParams(vmem_limit_bytes=60 << 20),
        cost_estimate=pl.CostEstimate(
            flops=0, bytes_accessed=6 * gathered.size, transcendentals=0
        ),
    )(gathered)


def greet_near(size):
    me = lax.axis_index("ctx")
    bits = size.bit_length() - 1
    greet([flipped(me, 1 << bit, bits) for bit in range(bits)])


def centre(values):
    centered = values - jnp.mean(values, -1, keepdims=True)
    inverse = lax.rsqrt(jnp.mean(centered * centered, -1, keepdims=True) + NORM_EPSILON)
    return centered * inverse, inverse


def join_kernel(
    size,
    mixed,
    weights,
    tokens,
    gain,
    shift,
    mixed_rows,
    residual,
    normed,
    weights_buf,
    load_sem,
    send_sem,
    recv_sem,
    local_sem,
):
    me = lax.axis_index("ctx")
    cols = mixed.shape[2]

    def load(owner):
        at = pl.ds(pl.multiple_of(owner * cols, cols), cols)
        return pltpu.make_async_copy(weights.at[at], weights_buf.at[at], load_sem.at[owner])

    others = [lax.rem(me + step, size) for step in range(size)]
    for step in range(size):
        load(lax.rem(me + size - step, size)).start()
    greet(others[1:])
    here = column_view(mixed_rows, me, cols)
    local = pltpu.make_async_copy(mixed.at[me], here, local_sem)
    local.start()
    copies = []
    for step in range(1, size):
        copy = pltpu.make_async_remote_copy(
            src_ref=mixed.at[others[step]],
            dst_ref=here,
            send_sem=send_sem.at[step - 1],
            recv_sem=recv_sem.at[step - 1],
            device_id={"ctx": others[step]},
            device_id_type=MESH_IDS,
        )
        copy.start()
        copies.append(copy)
    local.wait()
    residual[...] = tokens[...].astype(jnp.float32)
    for step in range(size):
        owner = lax.rem(me + size - step, size)
        if step > 0:
            copies[step - 1].wait_recv()
        load(owner).wait()
        at = pl.ds(pl.multiple_of(owner * cols, cols), cols)
        residual[...] += jnp.dot(
            mixed_rows[:, at], weights_buf[at], preferred_element_type=jnp.float32
        )
    unit = centre(residual[...])[0]
    normed[...] = (unit * gain[...] + shift[...]).astype(jnp.bfloat16)
    for copy in copies:
        copy.wait_send()


def join_rows(mixed, weights, tokens, gain, shift, collective_id):
    size, rows, cols = mixed.shape
    width = size * cols
    vmem = pl.BlockSpec(memory_space=pltpu.VMEM)
    any_space = pl.BlockSpec(memory_space=pl.ANY)
    low = jnp.bfloat16
    dma = pltpu.SemaphoreType.DMA
    return pl.pallas_call(
        functools.partial(join_kernel, size),
        in_specs=[any_space] * 2 + [vmem] * 3,
        out_specs=[vmem] * 3,
        out_shape=[
            jax.ShapeDtypeStruct((rows, width), low),
            jax.ShapeDtypeStruct((rows, width), jnp.float32),
            jax.ShapeDtypeStruct((rows, width), low),
        ],
        scratch_shapes=[
            pltpu.VMEM((width, width), low),
            dma((size,)),
            dma((size - 1,)),
            dma((size - 1,)),
            dma,
        ],
        compiler_params=pltpu.CompilerParams(
            collective_id=collective_id, has_side_effects=True, vmem_limit_bytes=60 << 20
        ),
        cost_estimate=pl.CostEstimate(
            flops=2 * rows * width * width, bytes_accessed=2 * width * width, transcendentals=0
        ),
    )(mixed, weights, tokens, gain, shift)


def part_kernel(
    size,
    grad_normed,
    residual,
    cotangent,
    gain,
    weights,
    grad_residual,
    grad_branch,
    sums,
    grad_mixed,
    weights_buf,
    staged,
    load_sem,
    send_sem,
    recv_sem,
    local_sem,
):
    me = lax.axis_index("ctx")
    cols = staged.shape[2]
    others = [lax.rem(me + step, size) for step in range(size)]

    def load(owner):
        at = pl.ds(pl.multiple_of(owner * cols, cols), cols)
        return pltpu.make_async_copy(weights.at[at], weights_buf.at[at], load_sem.at[owner])

    order = list(range(1, size)) + [0]
    for step in order:
        load(others[step]).start()
    greet(others[1:])
    sums[...] = jnp.zeros_like(sums)
    chunk = 32

    @pl.loop(0, residual.shape[0] // chunk)
    def _(i):
        at = pl.ds(pl.multiple_of(i * chunk, chunk), chunk)
        unit, inverse = centre(residual[at])
        grads = grad_normed[at]
        sums[:1] += jnp.sum(grads * unit, 0, keepdims=True)
        sums[1:] += jnp.sum(grads, 0, keepdims=True)
        scaled = grads * gain[...]
        total = cotangent[at].astype(jnp.float32) + inverse * (
            scaled
            - jnp.mean(scaled, -1, keepdims=True)
            - unit * jnp.mean(scaled * unit, -1, keepdims=True)
        )
        grad_residual[at] = total
        grad_branch[at] = total.astype(jnp.bfloat16)

    copies = []
    for step in order:
        other = others[step]
        load(other).wait()
        at = pl.ds(pl.multiple_of(other * cols, cols), cols)
        staged[step] = times_transposed(grad_branch[...], weights_buf[at]).astype(jnp.bfloat16)
        if step == 0:
            copy = pltpu.make_async_copy(staged.at[0], grad_mixed.at[me], local_sem)
        else:
            copy = pltpu.make_async_remote_copy(
                src_ref=staged.at[step],
                dst_ref=grad_mixed.at[me],
                send_sem=send_sem.at[step - 1],
                recv_sem=recv_sem.at[step - 1],
                device_id={"ctx": other},
                device_id_type=MESH_IDS,
            )
        copy.start()
        copies.append(copy)
    for copy in copies:
        copy.wait()


def part_rows(grad_normed, residual, cotangent, gain, weights, size, collective_id):
    rows, width = grad_normed.shape
    cols = width // size
    vmem = pl.BlockSpec(memory_space=pltpu.VMEM)
    any_space = pl.BlockSpec(memory_space=pl.ANY)
    low = jnp.bfloat16
    dma = pltpu.SemaphoreType.DMA
    return pl.pallas_call(
        functools.partial(part_kernel, size),
        in_specs=[vmem] * 4 + [any_space],
        out_specs=[vmem] * 3 + [any_space],
        out_shape=[
            jax.ShapeDtypeStruct((rows, width), jnp.float32),
            jax.ShapeDtypeStruct((rows, width), low),
            jax.ShapeDtypeStruct((2, width), jnp.float32),
            jax.ShapeDtypeStruct((size, rows, cols), low),
        ],
        scratch_shapes=[
            pltpu.VMEM((width, width), low),
            pltpu.VMEM((size, rows, cols), low),
            dma((size,)),
            dma((size - 1,)),
            dma((size - 1,)),
            dma,
        ],
        compiler_params=pltpu.CompilerParams(
            collective_id=collective_id, has_side_effects=True, vmem_limit_bytes=60 << 20
        ),
        cost_estimate=pl.CostEstimate(
            flops=2 * rows * width * width, bytes_accessed=2 * width * width, transcendentals=0
        ),
    )(grad_normed, residual, cotangent, gain, weights)


def forward_kernel(
    hidden_size,
    normed,
    weights,
    grads,
    normed_t,
    values,
    hidden,
    grad_down,
    tiles,
    weights_buf,
    grads_buf,
    turned,
    values_buf,
    hidden_t,
    load_sem,
    out_sem,
    *sems,
):
    greet_near(8)
    own = pltpu.make_async_copy(normed, tiles.at[0], load_sem.at[0])
    load = pltpu.make_async_copy(weights, weights_buf, load_sem.at[1])
    own.start()
    load.start()
    pltpu.make_async_copy(grads, grads_buf, load_sem.at[2]).start()
    own.wait()
    gather = TileGather(tiles, *sems)
    rows = tiles.shape[1]
    main = hidden_size // 128 * 128

    def write_out(tile, slot):
        at = pl.ds(pl.multiple_of(tile * rows, rows), rows)
        return [
            pltpu.make_async_copy(values_buf.at[slot], values.at[tile], out_sem.at[0, slot]),
            pltpu.make_async_copy(turned.at[slot], normed_t.at[:, at], out_sem.at[1, slot]),
        ]

    @pl.loop(0, 8)
    def _(t):
        for tile in range(8):

            @pl.when(t == tile)
            def _():
                gather.before(tile)
                if tile == 0:
                    load.wait()

        slot = t % 2

        @pl.when(t >= 2)
        def _():
            for copy in write_out(t - 2, slot):
                copy.wait()

        here = tiles[t]
        value = jnp.dot(here, weights_buf[...], preferred_element_type=jnp.float32)
        values_buf[slot] = value
        gate, up = value[:, :main], value[:, main : 2 * main]
        front = gate * jax.nn.sigmoid(gate) * up
        last = value[:, 2 * main :]
        behind = last * jax.nn.sigmoid(last) * pltpu.roll(last, 64, 1)
        both = jnp.concatenate([front, behind], 1)
        hidden[t] = both[:, :hidden_size].astype(jnp.bfloat16)
        at = pl.ds(pl.multiple_of(t * rows, rows), rows)
        hidden_t[:, at] = jnp.transpose(both)[:hidden_size].astype(jnp.bfloat16)
        turned[slot] = jnp.transpose(here)
        for copy in write_out(t, slot):
            copy.start()

    pltpu.make_async_copy(grads, grads_buf, load_sem.at[2]).wait()
    width = grads_buf.shape[2]
    step = 256

    @pl.loop(0, width // step)
    def _(i):
        at = pl.ds(pl.multiple_of(i * step, step), step)
        grad_down[:, at] = jnp.dot(
            hidden_t[...],
            grads_buf[:, :, at].reshape(8 * rows, step),
            preferred_element_type=jnp.float32,
        ).astype(jnp.bfloat16)

    for tile in (6, 7):
        for copy in write_out(tile, tile % 2):
            copy.wait()
    gather.finish()


def forward_mlp(normed, weights, grads, hidden_size, collective_id):
    rows, width = normed.shape
    wide = weights.shape[1]
    any_space = pl.BlockSpec(memory_space=pl.ANY)
    vmem = pl.BlockSpec(memory_space=pltpu.VMEM)
    low = jnp.bfloat16
    dma = pltpu.SemaphoreType.DMA
    return pl.pallas_call(
        functools.partial(forward_kernel, hidden_size),
        in_specs=[any_space] * 3,
        out_specs=[any_space, any_space, vmem, vmem],
        out_shape=[
            jax.ShapeDtypeStruct((width, 8 * rows), low),
            jax.ShapeDtypeStruct((8, rows, wide), jnp.float32),
            jax.ShapeDtypeStruct((8, rows, hidden_size), low),
            jax.ShapeDtypeStruct((hidden_size, width), low),
        ],
        scratch_shapes=[
            pltpu.VMEM((8, rows, width), low),
            pltpu.VMEM(weights.shape, low),
            pltpu.VMEM((8, rows, width), low),
            pltpu.VMEM((2, width, rows), low),
            pltpu.VMEM((2, rows, wide), jnp.float32),
            pltpu.VMEM((hidden_size, 8 * rows), low),
            dma((3,)),
            dma((2, 2)),
        ]
        + gather_sems(),
        compiler_params=pltpu.CompilerParams(
            collective_id=collective_id, has_side_effects=True, vmem_limit_bytes=60 << 20
        ),
        cost_estimate=pl.CostEstimate(
            flops=16 * rows * width * (wide + hidden_size),
            bytes_accessed=64 * rows * width,
            transcendentals=0,
        ),
    )(normed, weights, grads)


def backward_kernel(
    hidden_size,
    grads,
    values,
    weights,
    down,
    normed_t,
    hidden,
    grad_normed,
    grad_both_w,
    layer_part,
    grads_buf,
    values_buf,
    weights_buf,
    down_buf,
    normed_buf,
    grad_both,
    out_buf,
    hidden_buf,
    load_sem,
    tile_sem,
    out_sem,
    *scatter_refs,
):
    greet_near(8)
    scatter = TileScatter(*scatter_refs[: len(scatter_refs) // 2])
    layer = TileScatter(*scatter_refs[len(scatter_refs) // 2 :])
    rows = grads_buf.shape[1]
    main = hidden_size // 128 * 128
    load_weights = pltpu.make_async_copy(weights, weights_buf, load_sem.at[0])
    load_down = pltpu.make_async_copy(down, down_buf, load_sem.at[1])

    def load_tile(tile, slot):
        return [
            pltpu.make_async_copy(grads.at[tile], grads_buf.at[slot], tile_sem.at[0, slot]),
            pltpu.make_async_copy(values.at[tile], values_buf.at[slot], tile_sem.at[1, slot]),
            pltpu.make_async_copy(hidden.at[tile], hidden_buf.at[slot], tile_sem.at[3, slot]),
        ]

    def load_chunk(i):
        at = pl.ds(pl.multiple_of(i * rows, rows), rows)
        return pltpu.make_async_copy(normed_t.at[at], normed_buf.at[i % 2], tile_sem.at[2, i % 2])

    load_down.start()
    for copy in load_tile(7, 1):
        copy.start()
    load_weights.start()
    load_chunk(0).start()

    @pl.loop(0, 8)
    def _(u):
        t = 7 - swapped(u)
        slot = t % 2

        @pl.when(u < 7)
        def _():
            for copy in load_tile(7 - swapped(u + 1), 1 - slot):
                copy.start()

        @pl.when(u == 0)
        def _():
            load_down.wait()

        for copy in load_tile(t, slot):
            copy.wait()
        for tile in (5, 1):

            @pl.when(t == tile)
            def _():
                scatter.before(tile)
                layer.before(tile)

        layer.parts[part_slot(t)] = jnp.dot(
            hidden_buf[slot], down_buf[...], preferred_element_type=jnp.float32
        ).astype(jnp.bfloat16)
        for tile in range(8):

            @pl.when(t == tile)
            def _():
                layer.after(tile)

        grad_hidden = lax.dot_general(
            grads_buf[slot],
            down_buf[...],
            (((1,), (1,)), ((), ())),
            preferred_element_type=jnp.float32,
        )
        value = values_buf[slot]
        gate, up, above = value[:, :main], value[:, main : 2 * main], grad_hidden[:, :main]
        sigmoid = jax.nn.sigmoid(gate)
        grad_both[t, :, :main] = (
            above * up * sigmoid * (1.0 + gate * (1.0 - sigmoid))
        ).astype(jnp.bfloat16)
        grad_both[t, :, main : 2 * main] = (above * (gate * sigmoid)).astype(jnp.bfloat16)
        last = value[:, 2 * main :]
        above = grad_hidden[:, main:]
        above = jnp.concatenate([above, jnp.zeros_like(above)], 1)
        sigmoid = jax.nn.sigmoid(last)
        to_gate = above * pltpu.roll(last, 64, 1) * sigmoid * (1.0 + last * (1.0 - sigmoid))
        to_up = pltpu.roll(above * (last * sigmoid), 64, 1)
        lane = lax.broadcasted_iota(jnp.int32, last.shape, 1)
        grad_both[t, :, 2 * main :] = jnp.where(lane < 64, to_gate, to_up).astype(jnp.bfloat16)

        @pl.when(u == 0)
        def _():
            load_weights.wait()

        scatter.parts[part_slot(t)] = lax.dot_general(
            grad_both[t],
            weights_buf[...],
            (((1,), (1,)), ((), ())),
            preferred_element_type=jnp.float32,
        ).astype(jnp.bfloat16)
        for tile in range(8):

            @pl.when(t == tile)
            def _():
                scatter.after(tile)


    chunks = normed_t.shape[0] // rows

    def store_chunk(i):
        at = pl.ds(pl.multiple_of(i * rows, rows), rows)
        return pltpu.make_async_copy(out_buf.at[i % 2], grad_both_w.at[at], out_sem.at[i % 2])

    @pl.loop(0, chunks)
    def _(i):
        @pl.when(i < chunks - 1)
        def _():
            load_chunk(i + 1).start()

        load_chunk(i).wait()

        @pl.when(i >= 2)
        def _():
            store_chunk(i - 2).wait()

        out_buf[i % 2] = jnp.dot(
            normed_buf[i % 2],
            grad_both[...].reshape(8 * rows, grad_both.shape[2]),
            preferred_element_type=jnp.float32,
        ).astype(jnp.bfloat16)
        store_chunk(i).start()

    store_chunk(chunks - 2).wait()
    store_chunk(chunks - 1).wait()
    scatter.finish(grad_normed)
    layer.finish(layer_part)


def backward_mlp(grads, values, weights, down, normed_t, hidden, collective_id):
    size, rows, width = grads.shape
    hidden_size = down.shape[0]
    wide = weights.shape[1]
    any_space = pl.BlockSpec(memory_space=pl.ANY)
    vmem = pl.BlockSpec(memory_space=pltpu.VMEM)
    low = jnp.bfloat16
    dma = pltpu.SemaphoreType.DMA
    return pl.pallas_call(
        functools.partial(backward_kernel, hidden_size),
        in_specs=[any_space] * 6,
        out_specs=[vmem, any_space, vmem],
        out_shape=[
            jax.ShapeDtypeStruct((rows, width), jnp.float32),
            jax.ShapeDtypeStruct((width, wide), low),
            jax.ShapeDtypeStruct((rows, width), jnp.float32),
        ],
        scratch_shapes=[
            pltpu.VMEM((2, rows, width), low),
            pltpu.VMEM((2, rows, wide), jnp.float32),
            pltpu.VMEM(weights.shape, low),
            pltpu.VMEM(down.shape, low),
            pltpu.VMEM((2, rows, 8 * rows), low),
            pltpu.VMEM((8, rows, wide), low),
            pltpu.VMEM((2, rows, wide), low),
            pltpu.VMEM((2, rows, hidden_size), low),
            dma((2,)),
            dma((4, 2)),
            dma((2,)),
        ]
        + scatter_scratch(rows, width) * 2,
        compiler_params=pltpu.CompilerParams(
            collective_id=collective_id, has_side_effects=True, vmem_limit_bytes=60 << 20
        ),
        cost_estimate=pl.CostEstimate(
            flops=16 * rows * width * (2 * wide + hidden_size),
            bytes_accessed=64 * rows * width,
            transcendentals=0,
        ),
    )(grads, values, weights, down, normed_t, hidden)


def unpack_rows_kernel(source, out):
    out[...] = source[...].astype(jnp.float32)


def unpack_rows(gathered, rows):
    count, _, width = gathered.shape
    group = min(count, 1 << max(1, 352 // rows).bit_length() - 1)
    out = pl.pallas_call(
        unpack_rows_kernel,
        grid=(count // group,),
        in_specs=[pl.BlockSpec((group, rows, width), lambda i: (i, 0, 0))],
        out_specs=pl.BlockSpec((group, rows, width), lambda i: (i, 0, 0)),
        out_shape=jax.ShapeDtypeStruct((count, rows, width), jnp.float32),
        compiler_params=pltpu.CompilerParams(vmem_limit_bytes=60 << 20),
        cost_estimate=pl.CostEstimate(
            flops=0, bytes_accessed=6 * gathered.size, transcendentals=0
        ),
    )(gathered)
    return out.reshape(count * rows, width)


def unpack_kernel(segments, count, source, out):
    strip = source.shape[2] // segments
    pieces = []
    for segment in range(segments):
        for owner in range(count):
            pieces.append(source[owner, :, segment * strip : (segment + 1) * strip])
    out[...] = jnp.concatenate(pieces, 1).astype(jnp.float32)


def unpack_columns(gathered, segments):
    count, rows, width = gathered.shape
    step = min(128, rows)
    return pl.pallas_call(
        functools.partial(unpack_kernel, segments, count),
        grid=(rows // step,),
        in_specs=[pl.BlockSpec((count, step, width), lambda i: (0, i, 0))],
        out_specs=pl.BlockSpec((step, count * width), lambda i: (i, 0)),
        out_shape=jax.ShapeDtypeStruct((rows, count * width), jnp.float32),
        compiler_params=pltpu.CompilerParams(vmem_limit_bytes=60 << 20),
        cost_estimate=pl.CostEstimate(
            flops=0, bytes_accessed=6 * gathered.size, transcendentals=0
        ),
    )(gathered)


def norm_rows(values, gain_row, shift_row):
    centered = values - jnp.mean(values, -1, keepdims=True)
    inverse = lax.rsqrt(jnp.mean(centered * centered, -1, keepdims=True) + NORM_EPSILON)
    unit_rows = centered * inverse
    return (unit_rows * gain_row + shift_row, unit_rows, inverse)


def norm_back(grad_rows, unit_rows, inverse, gain_row):
    scaled = grad_rows * gain_row
    return inverse * (
        scaled
        - jnp.mean(scaled, -1, keepdims=True)
        - unit_rows * jnp.mean(scaled * unit_rows, -1, keepdims=True)
    )


def turn(rows, cosine, sine_low, sine_high, width):
    repeat = width // 128
    wide = [jnp.concatenate([table] * repeat, 1) for table in (cosine, sine_low, sine_high)]
    return (
        rows * wide[0]
        + pltpu.roll(rows, width - ROT // 2, 1) * wide[1]
        + pltpu.roll(rows, ROT // 2, 1) * wide[2]
    )


def head_stack(features_first, heads):
    owner = lax.broadcasted_iota(jnp.int32, features_first.shape, 0) // HEAD
    zero = jnp.zeros_like(features_first)
    return jnp.concatenate([jnp.where(owner == h, features_first, zero) for h in range(heads)], 1)


def row_stack(rows, heads):
    owner = lax.broadcasted_iota(jnp.int32, rows.shape, 1) // HEAD
    zero = jnp.zeros_like(rows)
    return jnp.concatenate([jnp.where(owner == h, rows, zero) for h in range(heads)], 0)


def pair_bias(key_tile, tile, heads, first_keys, diagonal):
    key_place = lax.broadcasted_iota(jnp.int32, (tile, tile), 0)
    allowed = key_place + key_tile * tile >= first_keys
    if diagonal:
        allowed &= key_place <= lax.broadcasted_iota(jnp.int32, (tile, tile), 1)
    return jnp.concatenate([jnp.where(allowed, 0.0, MASKED_SCORE)] * heads, 1)


def transposed(rows):
    return jnp.transpose(rows.astype(jnp.float32)).astype(rows.dtype)


def attend_kernel(
    block,
    heads,
    order,
    lowest,
    projected,
    starts,
    qkv,
    attended,
    mixed,
    log_total,
    value_t,
    summed,
    top,
    total,
):
    cols = heads * HEAD
    seq = projected.shape[0]
    tile = 2 * block

    @pl.loop(0, seq // block)
    def _(p):
        at = pl.ds(pl.multiple_of(p * block, block), block)
        rows = projected[pl.ds(pl.multiple_of(order[p] * block, block), block)]
        qkv[at] = rows
        value_t[:, at] = transposed(rows[:, 2 * cols :])

    @pl.loop(0, seq // tile)
    def _(i):
        at = pl.ds(pl.multiple_of(i * tile, tile), tile)
        query_t = head_stack(transposed(qkv[at, :cols]), heads)
        first_keys = starts[:, at]
        top[...] = jnp.full(top.shape, MASKED_SCORE, jnp.float32)
        total[...] = jnp.zeros_like(total)
        summed[...] = jnp.zeros_like(summed)

        def step(j, diagonal):
            keys_at = pl.ds(pl.multiple_of(j * tile, tile), tile)
            scores = jnp.dot(
                qkv[keys_at, cols : 2 * cols], query_t, preferred_element_type=jnp.float32
            )
            scores += pair_bias(j, tile, heads, first_keys, diagonal)
            old_top = top[...]
            new_top = jnp.maximum(old_top, jnp.max(scores, 0, keepdims=True))
            exps = jnp.exp(scores - new_top)
            fade = jnp.exp(old_top - new_top)
            total[...] = total[...] * fade + jnp.sum(exps, 0, keepdims=True)
            top[...] = new_top
            low = exps.astype(jnp.bfloat16)
            for h in range(heads):
                own = slice(h * tile, (h + 1) * tile)
                features = slice(h * HEAD, (h + 1) * HEAD)
                summed[features] = summed[features] * fade[:, own] + jnp.dot(
                    value_t[features, keys_at], low[:, own], preferred_element_type=jnp.float32
                )

        @pl.loop(lowest[i], i)
        def _(j):
            step(j, False)

        step(i, True)

        log_total[i] = top[...] + jnp.log(total[...])
        scale = 1.0 / total[...]
        for h in range(heads):
            features = slice(h * HEAD, (h + 1) * HEAD)
            summed[features] = summed[features] * scale[:, h * tile : (h + 1) * tile]
        rows = jnp.transpose(summed[...])
        attended[at] = rows
        for part in range(2):
            place = pl.ds(pl.multiple_of(order[2 * i + part] * block, block), block)
            mixed[place] = rows[part * block : (part + 1) * block].astype(jnp.bfloat16)


def attend(projected, order, lowest, starts, heads):
    seq, wide = projected.shape
    cols = wide // 3
    block = seq // order.shape[0]
    tile = 2 * block
    vmem = pl.BlockSpec(memory_space=pltpu.VMEM)
    smem = pl.BlockSpec(memory_space=pltpu.SMEM)
    return pl.pallas_call(
        functools.partial(attend_kernel, block, heads),
        in_specs=[smem, smem] + [vmem] * 2,
        out_specs=[vmem] * 4,
        out_shape=[
            jax.ShapeDtypeStruct((seq, wide), jnp.bfloat16),
            jax.ShapeDtypeStruct((seq, cols), jnp.float32),
            jax.ShapeDtypeStruct((seq, cols), jnp.bfloat16),
            jax.ShapeDtypeStruct((seq // tile, 1, heads * tile), jnp.float32),
        ],
        scratch_shapes=[
            pltpu.VMEM((cols, seq), jnp.bfloat16),
            pltpu.VMEM((cols, tile), jnp.float32),
            pltpu.VMEM((1, heads * tile), jnp.float32),
            pltpu.VMEM((1, heads * tile), jnp.float32),
        ],
        compiler_params=pltpu.CompilerParams(vmem_limit_bytes=48 << 20),
        cost_estimate=pl.CostEstimate(
            flops=4 * seq * seq * cols, bytes_accessed=12 * seq * cols, transcendentals=0
        ),
    )(order, lowest, projected, starts)


def attend_back_run(
    block,
    heads,
    order,
    places,
    qkv,
    grad_mixed,
    attended,
    log_total,
    starts,
    cosine,
    sine_low,
    sine_high,
    normed_t,
    out,
    sums,
    grad_weights,
    normed_buf,
    load_sem,
    key_t,
    grad_key,
    grad_value,
    grad_query,
    query_sum,
):
    cols = heads * HEAD
    seq = qkv.shape[0]
    tile = 2 * block
    chunk = normed_buf.shape[1]
    chunks = normed_t.shape[0] // chunk

    def load(i):
        at = pl.ds(pl.multiple_of(i * chunk, chunk), chunk)
        return pltpu.make_async_copy(normed_t.at[at], normed_buf.at[i % 2], load_sem.at[i % 2])

    load(0).start()

    @pl.loop(0, seq // block)
    def _(p):
        at = pl.ds(pl.multiple_of(p * block, block), block)
        key_t[:, at] = transposed(qkv[at, cols : 2 * cols])
        grad_key[p] = jnp.zeros((block, cols), jnp.float32)
        grad_value[p] = jnp.zeros((block, cols), jnp.float32)

    yield
    for i in reversed(range(seq // tile)):
        at = pl.ds(i * tile, tile)
        query = qkv[at, :cols]
        grad = jnp.concatenate(
            [
                grad_mixed[order[2 * i + part]]
                for part in range(2)
            ],
            0,
        )
        query_t = head_stack(transposed(query), heads)
        query_rows = row_stack(query, heads)
        grad_t = head_stack(transposed(grad), heads)
        grads = row_stack(grad, heads)
        products = jnp.transpose(grad.astype(jnp.float32) * attended[at])
        delta = jnp.concatenate(
            [
                jnp.sum(products[h * HEAD : (h + 1) * HEAD], 0, keepdims=True)
                for h in range(heads)
            ],
            1,
        )
        logs = log_total[i]
        first_keys = starts[:, at]
        query_sum[...] = jnp.zeros_like(query_sum)

        def step(j, diagonal):
            keys_at = pl.ds(pl.multiple_of(j * tile, tile), tile)
            scores = jnp.dot(
                qkv[keys_at, cols : 2 * cols], query_t, preferred_element_type=jnp.float32
            )
            scores += pair_bias(j, tile, heads, first_keys, diagonal)
            weights = jnp.exp(scores - logs)
            grad_soft = jnp.dot(
                qkv[keys_at, 2 * cols :], grad_t, preferred_element_type=jnp.float32
            )
            pair = pl.ds(2 * j, 2)
            grad_value[pair] += jnp.dot(
                weights.astype(jnp.bfloat16), grads, preferred_element_type=jnp.float32
            ).reshape(2, block, cols)
            grad_scores = (weights * (grad_soft - delta)).astype(jnp.bfloat16)
            grad_key[pair] += jnp.dot(
                grad_scores, query_rows, preferred_element_type=jnp.float32
            ).reshape(2, block, cols)
            for h in range(heads):
                features = slice(h * HEAD, (h + 1) * HEAD)
                query_sum[features] += jnp.dot(
                    key_t[features, keys_at],
                    grad_scores[:, h * tile : (h + 1) * tile],
                    preferred_element_type=jnp.float32,
                )

        if i > 0:

            @pl.loop(0, i)
            def _(j):
                step(j, False)

        step(i, True)
        grad_query[2 * i : 2 * i + 2] = (
            jnp.transpose(query_sum[...]) * HEAD ** (-0.5)
        ).reshape(2, block, cols)
        yield
    sums[...] = jnp.zeros_like(sums)

    @pl.loop(0, seq // block)
    def _(d):
        at = pl.ds(pl.multiple_of(d * block, block), block)
        place = places[d]
        tables = (cosine[at], -sine_low[at], -sine_high[at])
        for k, rows in enumerate(
            (
                turn(grad_query[place], *tables, cols),
                turn(grad_key[place], *tables, cols),
                grad_value[place],
            )
        ):
            columns = slice(k * cols, (k + 1) * cols)
            low = rows.astype(jnp.bfloat16)
            out[at, columns] = low
            sums[:, columns] += jnp.sum(low.astype(jnp.float32), 0, keepdims=True)

    @pl.loop(0, chunks)
    def _(i):
        @pl.when(i < chunks - 1)
        def _():
            load(i + 1).start()

        load(i).wait()
        at = pl.ds(pl.multiple_of(i * chunk, chunk), chunk)
        grad_weights[at] = jnp.dot(
            normed_buf[i % 2], out[...], preferred_element_type=jnp.float32
        ).astype(jnp.bfloat16)


def attend_back_op(
    qkv, grad_mixed, attended, log_total, order, places, starts, tables, normed_t, heads
):
    seq, wide = qkv.shape
    cols = wide // 3
    block = seq // order.shape[0]
    tile = 2 * block
    low = jnp.bfloat16
    return dict(
        run=functools.partial(attend_back_run, block, heads),
        inputs=[order, places, qkv, grad_mixed, attended, log_total, starts, *tables, normed_t],
        in_spaces=[pltpu.SMEM] * 2 + [pltpu.VMEM] * 8 + [pl.ANY],
        outs=[
            jax.ShapeDtypeStruct((seq, wide), low),
            jax.ShapeDtypeStruct((1, wide), jnp.float32),
            jax.ShapeDtypeStruct((normed_t.shape[0], wide), low),
        ],
        out_spaces=[pltpu.VMEM] * 3,
        scratch=[
            pltpu.VMEM((2, 256, seq), low),
            pltpu.SemaphoreType.DMA((2,)),
            pltpu.VMEM((cols, seq), low),
            pltpu.VMEM((seq // block, block, cols), jnp.float32),
            pltpu.VMEM((seq // block, block, cols), jnp.float32),
            pltpu.VMEM((seq // block, block, cols), jnp.float32),
            pltpu.VMEM((cols, tile), jnp.float32),
        ],
        moved=20 * seq * cols,
    )


def tables_run(cosines, sines, cosine, sine_low, sine_high):
    half_rot = ROT // 2
    step = 256
    yield

    @pl.loop(0, cosine.shape[0] // step)
    def _(i):
        at = pl.ds(pl.multiple_of(i * step, step), step)
        cos_rows, sin_rows = jnp.transpose(cosines[:, at]), jnp.transpose(sines[:, at])
        lane = lax.broadcasted_iota(jnp.int32, (step, 128), 1) % HEAD
        cos_wide = jnp.ones((step, 128), jnp.float32)
        sin_wide = jnp.zeros((step, 128), jnp.float32)
        for k in range(half_rot):
            own = (lane == k) | (lane == k + half_rot)
            cos_wide = jnp.where(own, cos_rows[:, k : k + 1], cos_wide)
            sin_wide = jnp.where(own, sin_rows[:, k : k + 1], sin_wide)
        cosine[at] = cos_wide
        sine_low[at] = jnp.where(lane < half_rot, -sin_wide, 0.0)
        sine_high[at] = jnp.where(lane >= half_rot, sin_wide, 0.0)


def tables_op(places):
    turns = jnp.arange(ROT // 2, dtype=jnp.int32)[:, None]
    freq = ROTARY_BASE ** (-turns.astype(jnp.float32) * 2.0 / ROT)
    angles = places.astype(jnp.float32)[None, :] * freq
    return dict(
        run=tables_run,
        inputs=[jnp.cos(angles), jnp.sin(angles)],
        in_space=pltpu.VMEM,
        outs=[jax.ShapeDtypeStruct((places.size, 128), jnp.float32)] * 3,
        out_space=pltpu.VMEM,
        scratch=[],
        moved=1024 * places.size,
    )


def place_order(block_pairs, axis_size):
    device_blocks = jnp.stack([block_pairs, 2 * axis_size - 1 - block_pairs], 1).reshape(-1)
    places = jnp.arange(2 * axis_size, dtype=jnp.int32)
    return jnp.sum(
        jnp.where(device_blocks[None, :] == places[:, None], places[None, :], 0), 1
    ).astype(jnp.int32)


def document_starts(docs):
    first = jnp.sum((docs < 1).astype(jnp.int32))
    second = jnp.sum((docs < 2).astype(jnp.int32))
    return jnp.where(docs == 0, 0, jnp.where(docs == 1, first, second))


def inner(left_side, right_side):
    return lax.dot_general(
        left_side, right_side, (((0,), (0,)), ((), ())), preferred_element_type=jnp.float32
    )


def times_transposed(left_side, right_side):
    return lax.dot_general(
        left_side, right_side, (((1,), (1,)), ((), ())), preferred_element_type=jnp.float32
    )


def times(left_side, right_side):
    return jnp.dot(left_side, right_side, preferred_element_type=jnp.float32)


def after(value, *earlier):
    return lax.optimization_barrier((value,) + earlier)[0]


def body(
    tokens,
    doc_ids,
    block_pairs,
    ln1_gain,
    ln1_bias,
    w_qkv,
    b_qkv,
    w_out,
    ln2_gain,
    ln2_bias,
    w_gate,
    w_up,
    w_down,
    cotangent,
):
    rows_here = tokens.shape[1]
    width = tokens.shape[2]
    head_count = width // HEAD
    ctx_size = lax.axis_size("ctx")
    fsdp_size = lax.axis_size("fsdp")
    seq_rows = rows_here * ctx_size
    position = lax.axis_index("ctx")
    heads_here = head_count // ctx_size
    cols = width // ctx_size
    shard_rows = w_qkv.shape[0]
    hidden_shard = w_down.shape[0]
    strip = hidden_shard // ctx_size

    tile = 2 * (rows_here // 2)
    order = place_order(block_pairs, ctx_size)
    starts = document_starts(doc_ids[0])
    lowest = starts[::tile] // tile
    starts = starts[None]
    device_blocks = jnp.stack([block_pairs, 2 * ctx_size - 1 - block_pairs], 1).reshape(-1, 1)
    half_rows = rows_here // 2
    places = device_blocks * half_rows + jnp.arange(half_rows, dtype=jnp.int32)[None, :]

    def strips(w, count, size):
        stride = w.shape[1] // count
        return [
            lax.dynamic_slice_in_dim(w, i * stride + position * size, size, 1)
            for i in range(count)
        ]

    qkv_strip = jnp.concatenate(strips(w_qkv, 3, cols) + strips(w_out, 1, cols), 1)
    hidden_here = fsdp_size * strip
    main = hidden_here // 128 * 128
    fused = ctx_size == 8 and hidden_here - main == 64 and rows_here == 256
    gate_strip = jnp.concatenate(strips(w_gate, fsdp_size, strip), 1)
    up_strip = jnp.concatenate(strips(w_up, fsdp_size, strip), 1)
    both_strip = jnp.concatenate(
        [gate_strip[:, :main], up_strip[:, :main], gate_strip[:, main:], up_strip[:, main:]], 1
    )
    down_strip = lax.dynamic_slice_in_dim(w_down, position * strip, strip, 0)
    out_piece = shard_rows // ctx_size
    qkv_here = lax.all_gather(qkv_strip, "fsdp", axis=0, tiled=True)
    both_here = lax.all_gather(both_strip, "fsdp", axis=0, tiled=True)
    down_here = lax.all_gather(down_strip, "fsdp", axis=0, tiled=True)

    small = jnp.concatenate([ln1_gain, ln1_bias, ln2_gain, ln2_bias, b_qkv])
    small_rows = -(-small.size // 2048) * 16
    small = jnp.pad(small, (0, small_rows * 128 - small.size)).reshape(small_rows, 128)
    grad_out = cotangent[0]
    gather_grads = gather_op(grad_out, ctx_size)
    if fused:
        gather_grads = gather_op(grad_out, ctx_size, row_half, tile_put, relative=True)
    *tables, small, tokens_all, grad_out_all = plane(
        ctx_size,
        1,
        tables_op(places.reshape(-1)),
        z_gather_op(small, fsdp_size),
        gather_op(tokens[0], ctx_size),
        gather_grads,
    )
    small = small.reshape(fsdp_size, small_rows * 128).astype(jnp.float32)
    gain_one, shift_one, gain_two, shift_two = (
        small[:, i * shard_rows : (i + 1) * shard_rows].reshape(1, width) for i in range(4)
    )
    bias_full = small[:, 4 * shard_rows : 4 * shard_rows + b_qkv.size]
    bias_full = bias_full.reshape(3, ctx_size, cols)
    bias_here = lax.dynamic_index_in_dim(bias_full, position, 1, keepdims=False)
    bias_here = bias_here.reshape(1, 3 * cols)
    out_full, projected, normed_t = plane(
        ctx_size,
        2,
        gather_op(
            qkv_here,
            ctx_size,
            functools.partial(last_strip, cols),
            functools.partial(column_strip, cols=cols),
            (width, width),
            pace=4,
        ),
        project_op(tokens_all, qkv_here, gain_one, shift_one, bias_here, tables),
    )
    tokens_in = tokens[0].astype(jnp.float32)
    unit_one, inverse_one = norm_rows(tokens_in, gain_one, shift_one)[1:]
    qkv_rows, attended, mixed_here, log_total = attend(
        projected.reshape(seq_rows, 3 * cols), order, lowest, starts, heads_here
    )
    mixed_here = mixed_here.reshape(ctx_size, rows_here, cols)
    mixed_rows, residual, normed_two_low = join_rows(
        mixed_here, out_full, tokens[0], gain_two, shift_two, 12
    )

    def blocks(rows):
        return rows.astype(jnp.bfloat16).reshape(ctx_size, rows_here, width)

    if fused:
        normed_two_t, both_value, hidden, grad_down_w = forward_mlp(
            normed_two_low, both_here, grad_out_all, hidden_here, 3
        )
        grad_normed_two, grad_both_w, layer_part = backward_mlp(
            grad_out_all, both_value, both_here, down_here, normed_two_t, hidden, 4
        )
    else:
        grad_out_all = grad_out_all.reshape(seq_rows, width)
        normed_two_all = plane(ctx_size, 3, gather_op(normed_two_low, ctx_size))
        normed_two_all = normed_two_all.reshape(seq_rows, width)
        both_value = times(normed_two_all, both_here)
        gate_value = jnp.concatenate(
            [both_value[:, :main], both_value[:, 2 * main : main + hidden_here]], 1
        )
        up_value = jnp.concatenate(
            [both_value[:, main : 2 * main], both_value[:, main + hidden_here :]], 1
        )
        sigmoid_gate = jax.nn.sigmoid(gate_value)
        silu_gate = gate_value * sigmoid_gate
        hidden = (silu_gate * up_value).astype(jnp.bfloat16)

        grad_down_w = inner(hidden, grad_out_all).astype(jnp.bfloat16)
        grad_hidden = times_transposed(after(grad_out_all, grad_down_w), down_here)
        grad_gate = grad_hidden * up_value * sigmoid_gate * (1.0 + gate_value * (1.0 - sigmoid_gate))
        grad_up = grad_hidden * silu_gate
        grad_both = jnp.concatenate(
            [grad_gate[:, :main], grad_up[:, :main], grad_gate[:, main:], grad_up[:, main:]], 1
        ).astype(jnp.bfloat16)
        grad_both_w = inner(normed_two_all, grad_both).astype(jnp.bfloat16)
        grad_normed_two = plane(
            ctx_size,
            4,
            scatter_op(blocks(times_transposed(after(grad_both, grad_both_w), both_here)), ctx_size),
        )
    grad_residual, grad_branch, norm_two_sums, grad_mixed = part_rows(
        grad_normed_two, residual, grad_out, gain_two, out_full, ctx_size, 5
    )

    def reduced(grad):
        return lax.psum_scatter(
            grad.astype(jnp.bfloat16), "fsdp", scatter_dimension=0, tiled=True
        )

    grad_down_w, grad_both_w = reduced(grad_down_w), reduced(grad_both_w)
    attend_op = attend_back_op(
        qkv_rows,
        grad_mixed.reshape(2 * ctx_size, half_rows, cols),
        attended,
        log_total,
        order,
        places[:, 0] // half_rows,
        starts,
        tables,
        normed_t,
        heads_here,
    )
    down_op = gather_op(grad_down_w, ctx_size, column_half, stacked_columns, pace=2)
    if fused:
        mixed_t = jnp.transpose(
            mixed_rows.reshape(rows_here, fsdp_size, ctx_size, out_piece), (2, 1, 3, 0)
        ).reshape(ctx_size, fsdp_size * out_piece, rows_here)
        out_op = produce_op(
            product_of_columns,
            rows_here,
            width,
            mixed_t,
            grad_branch,
            batch=2,
            late=5,
            kind=jnp.bfloat16,
        )
    else:
        mixed_blocks = jnp.transpose(
            mixed_rows.reshape(rows_here, fsdp_size, ctx_size, out_piece), (0, 2, 1, 3)
        ).reshape(rows_here, width)
        out_op = scatter_op(
            inner(mixed_blocks, grad_branch)
            .astype(jnp.bfloat16)
            .reshape(ctx_size, fsdp_size * out_piece, width),
            ctx_size,
        )
    if fused:
        grad_down_w, grad_out_w, grad_projected, grad_bias, grad_qkv_w = plane(
            ctx_size, 6, down_op, out_op, attend_op
        )
    else:
        grad_projected, grad_bias, grad_qkv_w = plane(ctx_size, 6, attend_op)
        grad_down_w, grad_out_w = plane(ctx_size, 7, down_op, out_op)
        layer_part = plane(ctx_size, 10, scatter_op(blocks(times(hidden, down_here)), ctx_size))
    if fused:
        normed_op = produce_op(
            product_of_rows,
            rows_here,
            width,
            grad_projected.reshape(ctx_size, rows_here, 3 * cols),
            qkv_here,
        )
    else:
        normed_op = scatter_op(
            blocks(times_transposed(grad_projected, qkv_here[:, : 3 * cols])), ctx_size
        )
    grad_both_w, grad_normed = plane_groups(
        ctx_size, 8, gather_op(grad_both_w, ctx_size), normed_op
    )
    grad_out_w = reduced(grad_out_w)
    layer_out = residual + layer_part
    grad_qkv_w = reduced(grad_qkv_w)
    grad_tokens = grad_residual + norm_back(grad_normed, unit_one, inverse_one, gain_one)

    norm_sums = jnp.concatenate(
        [
            jnp.sum(grad_normed * unit_one, 0, keepdims=True),
            jnp.sum(grad_normed, 0, keepdims=True),
            norm_two_sums,
        ]
    )
    norm_sums = jnp.transpose(norm_sums.reshape(4, fsdp_size, shard_rows), (1, 0, 2)).reshape(
        fsdp_size, 1, 4 * shard_rows
    )
    bias_sums = lax.dynamic_update_slice(
        jnp.zeros((3, ctx_size, cols), jnp.float32),
        grad_bias.reshape(3, 1, cols),
        (0, position, 0),
    ).reshape(fsdp_size, 1, 3 * width // fsdp_size)
    sums = jnp.concatenate(
        [
            jnp.pad(rows, ((0, 0), (0, extra), (0, width - rows.shape[2])))
            for rows, extra in ((norm_sums, 0), (bias_sums, 6))
        ],
        1,
    )
    grad_qkv_w, grad_out_w, sums = plane(
        ctx_size,
        13,
        gather_op(grad_qkv_w, ctx_size, pace=2),
        gather_op(grad_out_w, ctx_size, column_half, stacked_columns, pace=2),
        z_sum_gather_op(sums, fsdp_size, ctx_size),
    )
    sums = jnp.sum(sums, 0)
    norm_sums = sums[0, : 4 * shard_rows].reshape(4, shard_rows)
    bias_sums = sums[1, : b_qkv.shape[0]]
    grad_out_w = unpack_rows(grad_out_w, out_piece)
    grad_gate_w, grad_up_w = unpack_both(grad_both_w, fsdp_size)
    float32 = jnp.float32
    return (
        layer_out.astype(jnp.bfloat16)[None],
        grad_tokens[None],
        norm_sums[0],
        norm_sums[1],
        unpack_columns(grad_qkv_w, 3),
        bias_sums,
        grad_out_w,
        norm_sums[2],
        norm_sums[3],
        grad_gate_w,
        grad_up_w,
        unpack_rows(grad_down_w, strip),
    )


def solution(mesh):
    placed = (
        P("fsdp", "ctx", None),
        P("fsdp", None),
        P(),
        P("fsdp"),
        P("fsdp"),
        P("fsdp", None),
        P("fsdp"),
        P("fsdp", None),
        P("fsdp"),
        P("fsdp"),
        P("fsdp", None),
        P("fsdp", None),
        P("fsdp", None),
        P("fsdp", "ctx", None),
    )
    return jax.shard_map(
        body,
        mesh=mesh,
        in_specs=placed,
        out_specs=(
            P("fsdp", "ctx", None),
            P("fsdp", "ctx", None),
            P("fsdp"),
            P("fsdp"),
            P("fsdp", None),
            P("fsdp"),
            P("fsdp", None),
            P("fsdp"),
            P("fsdp"),
            P("fsdp", None),
            P("fsdp", None),
            P("fsdp", None),
        ),
        check_vma=False,
    )
```

```python
import functools

import jax
import jax.numpy as jnp
from jax import lax
from jax.experimental import pallas as pl
from jax.experimental.pallas import tpu as pltpu
from jax.sharding import PartitionSpec as P

HEAD = 64
ROT = 16


NORM_EPSILON = 1e-05
ROTARY_BASE = 10000.0
MASKED_SCORE = -1e30


MESH_IDS = pl.DeviceIdType.MESH


def bit_of(index, bit):
    return index // (1 << bit) % 2


def flipped(index, mask, bits):
    result = index
    for bit in range(bits):
        if mask >> bit & 1:
            result = result + (1 - 2 * bit_of(index, bit)) * (1 << bit)
    return result


def greet(partners, along_z=()):
    barrier = pltpu.get_barrier_semaphore()
    for axis, others in (("ctx", partners), ("fsdp", along_z)):
        for other in others:
            pl.semaphore_signal(barrier, inc=1, device_id={axis: other}, device_id_type=MESH_IDS)
    pl.semaphore_wait(barrier, len(partners) + len(along_z))


def half_orders(bits):
    chip_bits = list(range(1, bits))
    return [chip_bits, chip_bits[1:] + chip_bits[:1]]


def gather_plan(bits):
    steps = []
    for order in half_orders(bits):
        held = [0]
        plan = []
        for bit in order:
            plan.append((bit, list(held)))
            held = held + [mask | 1 << bit for mask in held]
        steps.append((plan, held))
    return steps


def column_half(ref, half):
    width = ref.shape[-1] // 2
    return ref.at[..., pl.ds(half * width, width)]


def row_half(ref, half):
    rows = ref.shape[-2] // 2
    if len(ref.shape) == 2:
        return ref.at[pl.ds(half * rows, rows)]
    return ref.at[..., pl.ds(half * rows, rows), :]


def stacked_rows(ref, block, half):
    return row_half(ref.at[block], half)


def stacked_columns(ref, block, half):
    return column_half(ref.at[block], half)


def column_strip(ref, block, half, cols):
    rows = ref.shape[0] // 2
    at = block * cols if isinstance(block, int) else pl.multiple_of(block * cols, cols)
    return ref.at[pl.ds(half * rows, rows), pl.ds(at, cols)]


def last_strip(cols, ref, half):
    return column_strip(ref, ref.shape[1] // cols - 1, half, cols)


def block_view(ref, block):
    return ref.at[block]


def column_view(ref, block, width):
    return ref.at[:, pl.ds(pl.multiple_of(block * width, width), width)]


def gather_run(
    bits, take, put, relative, pace, source, out, send_sem, recv_sem, core_send, core_recv, local_sem
):
    me = lax.axis_index("ctx")
    steps = gather_plan(bits)
    finals = []
    for half in range(2):
        own = put(out, 0 if relative else me, half)
        copy = pltpu.make_async_copy(take(source, half), own, local_sem.at[half])
        copy.start()
        finals.append(copy.wait)

    def push(half, mask, bit, send, recv, index):
        block = mask if relative else flipped(me, mask, bits)
        there = mask | 1 << bit if relative else block
        copy = pltpu.make_async_remote_copy(
            src_ref=take(source, half) if mask == 0 else put(out, block, half),
            dst_ref=put(out, there, half),
            send_sem=send.at[half, index],
            recv_sem=recv.at[half, index],
            device_id={"ctx": flipped(me, 1 << bit, bits)},
            device_id_type=MESH_IDS,
        )
        copy.start()
        return copy

    def hop(half, phase, mask):
        bit, masks = steps[half][0][phase]
        index = (1 << phase) - 1 + masks.index(mask)
        copy = push(half, mask, bit, send_sem, recv_sem, index)
        finals.append(copy.wait_send)
        arriving[half, mask | 1 << bit] = copy

    def to_core(half, mask):
        copy = push(half, mask, 0, core_send, core_recv, steps[half][1].index(mask))
        finals.append(copy.wait)

    arriving = {}
    phases = bits - 1
    for phase in range(phases):
        for half in range(2):
            hop(half, phase, 0)
    for half in range(2):
        to_core(half, 0)
    for _ in range(pace):
        yield
    for phase in range(phases):
        for half in range(2):
            bit, masks = steps[half][0][phase]
            for mask in masks:
                arrived = mask | 1 << bit
                arriving[half, arrived].wait_recv()
                for later in range(phase + 1, phases):
                    hop(half, later, arrived)
                to_core(half, arrived)
        for _ in range(pace):
            yield
    for wait in finals:
        wait()


def gather_op(
    x, size, take=row_half, put=stacked_rows, out_shape=None, relative=False, pace=1
):
    bits = size.bit_length() - 1
    steps = size // 2 - 1
    dma = pltpu.SemaphoreType.DMA
    return dict(
        run=functools.partial(gather_run, bits, take, put, relative, pace),
        inputs=[x],
        in_space=pl.ANY,
        outs=[jax.ShapeDtypeStruct(out_shape or (size,) + x.shape, x.dtype)],
        out_space=pl.ANY,
        scratch=[dma((2, steps)), dma((2, steps)), dma((2, steps + 1)), dma((2, steps + 1)), dma((2,))],
        moved=2 * size * x.size * 2,
    )


def add_into(target, first, second, rows, step):
    @pl.loop(0, rows // step)
    def _(i):
        at = pl.ds(pl.multiple_of(i * step, step), step)
        target[at] = first[at].astype(target.dtype) + second[at].astype(target.dtype)


def scatter_plan(bits):
    plans = []
    for order in half_orders(bits):
        kept = [mask << 1 for mask in range(1 << (bits - 1))]
        plan = []
        for bit in order:
            plan.append((bit, [mask for mask in kept if mask >> bit & 1]))
            kept = [mask for mask in kept if not mask >> bit & 1]
        plans.append(plan)
    return plans


def farthest_first(masks):
    return sorted(masks, key=lambda mask: -bin(mask).count("1"))


def scatter_run(bits, step, part_ref, out_ref, core_buf, chip_buf, core_send, core_recv, send_sem, recv_sem):
    me = lax.axis_index("ctx")
    rows = part_ref.shape[1]
    width = part_ref.shape[2] // 2
    plans = scatter_plan(bits)
    chip_masks = farthest_first([mask << 1 for mask in range(1 << (bits - 1))])
    finals = []
    core_copies = {}
    for mask in chip_masks:
        copy = pltpu.make_async_remote_copy(
            src_ref=part_ref.at[flipped(me, mask | 1, bits)],
            dst_ref=core_buf.at[mask >> 1],
            send_sem=core_send.at[mask >> 1],
            recv_sem=core_recv.at[mask >> 1],
            device_id={"ctx": flipped(me, 1, bits)},
            device_id_type=MESH_IDS,
        )
        copy.start()
        core_copies[mask] = copy
        finals.append(copy.wait_send)
    arriving = {}

    def columns(half):
        return pl.ds(half * width, width)

    def send(half, phase, bit, mask):
        slot = plans[half][phase][1].index(mask)
        copy = pltpu.make_async_remote_copy(
            src_ref=part_ref.at[flipped(me, mask, bits), :, columns(half)],
            dst_ref=chip_buf.at[half, phase, slot],
            send_sem=send_sem.at[half, phase, slot],
            recv_sem=recv_sem.at[half, phase, slot],
            device_id={"ctx": flipped(me, 1 << bit, bits)},
            device_id_type=MESH_IDS,
        )
        copy.start()
        finals.append(copy.wait_send)
        arriving[half, phase, mask & ~(1 << bit)] = (copy, slot)

    yield
    for mask in chip_masks:
        core_copies[mask].wait_recv()
        here = part_ref.at[flipped(me, mask, bits)]
        add_into(here, here, core_buf.at[mask >> 1], rows, step)
        for half in range(2):
            bit, masks = plans[half][0]
            if mask in masks:
                send(half, 0, bit, mask)
    yield
    phases = bits - 1
    for phase in range(1, phases + 1):
        for half in range(2):
            last_bit, last_masks = plans[half][phase - 1]
            kept = farthest_first([mask & ~(1 << last_bit) for mask in last_masks])
            for mask in kept:
                copy, slot = arriving[half, phase - 1, mask]
                copy.wait_recv()
                here = part_ref.at[flipped(me, mask, bits), :, columns(half)]
                buf = chip_buf.at[half, phase - 1, slot]
                if phase < phases:
                    add_into(here, here, buf, rows, step)
                    bit, masks = plans[half][phase]
                    if mask in masks:
                        send(half, phase, bit, mask)
                else:
                    add_into(out_ref.at[:, columns(half)], here, buf, rows, step)
        yield
    for wait in finals:
        wait()


def scatter_op(part, size):
    bits = size.bit_length() - 1
    chips = size // 2
    rows, width = part.shape[1:]
    dma = pltpu.SemaphoreType.DMA
    return dict(
        run=functools.partial(scatter_run, bits, 32),
        inputs=[part],
        in_space=pltpu.VMEM,
        outs=[jax.ShapeDtypeStruct((rows, width), jnp.float32)],
        out_space=pltpu.VMEM,
        scratch=[
            pltpu.VMEM((chips, rows, width), part.dtype),
            pltpu.VMEM((2, bits - 1, chips // 2, rows, width // 2), part.dtype),
            dma((chips,)),
            dma((chips,)),
            dma((2, bits - 1, chips // 2)),
            dma((2, bits - 1, chips // 2)),
        ],
        moved=4 * part.size,
    )


def exchange_run(size, take, put, source, out, send_sem, recv_sem, local_sem):
    me = lax.axis_index("ctx")
    local = pltpu.make_async_copy(take(source, me), put(out, me), local_sem)
    local.start()
    copies = []
    for step in range(1, size):
        other = lax.rem(me + step, size)
        copy = pltpu.make_async_remote_copy(
            src_ref=take(source, other),
            dst_ref=put(out, me),
            send_sem=send_sem.at[step - 1],
            recv_sem=recv_sem.at[step - 1],
            device_id={"ctx": other},
            device_id_type=MESH_IDS,
        )
        copy.start()
        copies.append(copy)
    yield
    local.wait()
    for copy in copies:
        copy.wait()


def exchange_op(x, size, out_shape, take, put):
    dma = pltpu.SemaphoreType.DMA
    return dict(
        run=functools.partial(exchange_run, size, take, put),
        inputs=[x],
        in_space=pl.ANY,
        outs=[jax.ShapeDtypeStruct(out_shape, x.dtype)],
        out_space=pl.ANY,
        scratch=[dma((size - 1,)), dma((size - 1,)), dma],
        far=True,
        moved=4 * x.size,
    )


def z_gather_run(size, source, out, send_sem, recv_sem, local_sem):
    me = lax.axis_index("fsdp")
    local = pltpu.make_async_copy(source, out.at[me], local_sem)
    local.start()
    copies = []
    for step in range(1, size):
        copy = pltpu.make_async_remote_copy(
            src_ref=source,
            dst_ref=out.at[me],
            send_sem=send_sem.at[step - 1],
            recv_sem=recv_sem.at[step - 1],
            device_id={"fsdp": lax.rem(me + step, size)},
            device_id_type=MESH_IDS,
        )
        copy.start()
        copies.append(copy)
    for _ in range(4):
        yield
    local.wait()
    for copy in copies:
        copy.wait()


def z_gather_op(x, size):
    dma = pltpu.SemaphoreType.DMA
    return dict(
        run=functools.partial(z_gather_run, size),
        inputs=[x],
        in_space=pl.ANY,
        outs=[jax.ShapeDtypeStruct((size,) + x.shape, x.dtype)],
        out_space=pl.ANY,
        scratch=[dma((size - 1,)), dma((size - 1,)), dma],
        z=size,
        moved=2 * size * x.size,
    )


def z_scatter_run(size, source, out, buf, send_sem, recv_sem):
    me = lax.axis_index("fsdp")
    copies = []
    for step in range(1, size):
        other = lax.rem(me + step, size)
        copy = pltpu.make_async_remote_copy(
            src_ref=source.at[other],
            dst_ref=buf.at[step - 1],
            send_sem=send_sem.at[step - 1],
            recv_sem=recv_sem.at[step - 1],
            device_id={"fsdp": other},
            device_id_type=MESH_IDS,
        )
        copy.start()
        copies.append(copy)
    for _ in range(4):
        yield
    total = source[me].astype(jnp.float32)
    for step, copy in enumerate(copies):
        copy.wait()
        total += buf[step].astype(jnp.float32)
    out[...] = total.astype(out.dtype)


def z_scatter_op(x, size):
    dma = pltpu.SemaphoreType.DMA
    return dict(
        run=functools.partial(z_scatter_run, size),
        inputs=[x],
        in_space=pltpu.VMEM,
        outs=[jax.ShapeDtypeStruct(x.shape[1:], x.dtype)],
        out_space=pltpu.VMEM,
        scratch=[
            pltpu.VMEM((size - 1,) + x.shape[1:], x.dtype),
            dma((size - 1,)),
            dma((size - 1,)),
        ],
        z=size,
        moved=4 * x.size,
    )


def z_sum_gather_run(bits, size, source, out, low, buf, send_sem, recv_sem, *sems):
    yield from z_scatter_run(size, source, low, buf, send_sem, recv_sem)
    yield from gather_run(bits, column_half, stacked_columns, False, 1, low, out, *sems)


def z_sum_gather_op(x, z_size, size):
    summed = z_scatter_op(x, z_size)
    (shape,) = summed["outs"]
    gather = gather_op(shape, size)
    return dict(
        run=functools.partial(z_sum_gather_run, size.bit_length() - 1, z_size),
        inputs=[x],
        in_space=pltpu.VMEM,
        outs=gather["outs"],
        out_space=pl.ANY,
        scratch=[pltpu.VMEM(shape.shape, shape.dtype)] + summed["scratch"] + gather["scratch"],
        z=z_size,
        moved=summed["moved"] + gather["moved"],
    )


def project_run(
    cols,
    tokens,
    weights,
    gain,
    shift,
    bias,
    cosine,
    sine_low,
    sine_high,
    qkv,
    normed,
    tokens_buf,
    normed_buf,
    weights_buf,
    load_sem,
    store_sem,
    weights_sem,
):
    size, rows = tokens.shape[:2]

    def load(block):
        slot = block % 2
        return pltpu.make_async_copy(tokens.at[block], tokens_buf.at[slot], load_sem.at[slot])

    def store(block):
        slot = block % 2
        at = pl.ds(block * rows, rows)
        return pltpu.make_async_copy(normed_buf.at[slot], normed.at[:, at], store_sem.at[slot])

    load_weights = pltpu.make_async_copy(
        weights.at[:, pl.ds(0, 3 * cols)], weights_buf, weights_sem
    )
    load(0).start()
    load_weights.start()
    yield
    for block in range(size):
        if block + 1 < size:
            load(block + 1).start()
        load(block).wait()
        at = pl.ds(block * rows, rows)
        values = tokens_buf[block % 2].astype(jnp.float32)
        centered = values - jnp.mean(values, -1, keepdims=True)
        inverse = lax.rsqrt(jnp.mean(centered * centered, -1, keepdims=True) + NORM_EPSILON)
        low = (centered * inverse * gain[...] + shift[...]).astype(jnp.bfloat16)
        if block >= 2:
            store(block - 2).wait()
        normed_buf[block % 2] = jnp.transpose(low)
        store(block).start()
        if block == 0:
            load_weights.wait()
        projected = jnp.dot(low, weights_buf[...], preferred_element_type=jnp.float32)
        projected += bias[...]
        tables = (cosine[at], sine_low[at], sine_high[at])
        query = turn(projected[:, :cols], *tables, cols) * HEAD ** (-0.5)
        qkv[block, :, :cols] = query.astype(jnp.bfloat16)
        key = turn(projected[:, cols : 2 * cols], *tables, cols)
        qkv[block, :, cols : 2 * cols] = key.astype(jnp.bfloat16)
        qkv[block, :, 2 * cols :] = projected[:, 2 * cols :].astype(jnp.bfloat16)
        yield
    store(size - 2).wait()
    store(size - 1).wait()


def project_op(tokens, weights, gain, shift, bias, tables):
    size, rows, width = tokens.shape
    wide = bias.shape[1]
    low = jnp.bfloat16
    dma = pltpu.SemaphoreType.DMA
    return dict(
        run=functools.partial(project_run, wide // 3),
        inputs=[tokens, weights, gain, shift, bias, *tables],
        in_spaces=[pl.ANY] * 2 + [pltpu.VMEM] * 6,
        outs=[
            jax.ShapeDtypeStruct((size, rows, wide), low),
            jax.ShapeDtypeStruct((width, size * rows), low),
        ],
        out_spaces=[pltpu.VMEM, pl.ANY],
        scratch=[
            pltpu.VMEM((2, rows, width), low),
            pltpu.VMEM((2, width, rows), low),
            pltpu.VMEM((width, wide), low),
            dma((2,)),
            dma((2,)),
            dma,
        ],
        moved=4 * tokens.size,
    )


def plane_kernel(size, parts, far, z_size, *refs):
    bits = size.bit_length() - 1
    me = lax.axis_index("ctx")
    my_z = lax.axis_index("fsdp")
    partners = [flipped(me, 1 << bit, bits) for bit in range(bits)]
    if far:
        partners = [lax.rem(me + step, size) for step in range(1, size)]
    greet(partners, [lax.rem(my_z + step, z_size) for step in range(1, z_size)])
    ins = sum(part[1] for part in parts)
    outs = sum(part[2] for part in parts)
    groups = [list(refs[:ins]), list(refs[ins : ins + outs]), list(refs[ins + outs :])]
    running = []
    for run, *counts in parts:
        own = []
        for group, count in zip(groups, counts):
            own += group[:count]
            del group[:count]
        running.append(run(*own))
    while running:
        running = [turn_of for turn_of in running if next(turn_of, 1) is None]


def spaces(op, side):
    arrays = op["inputs"] if side == "in" else op["outs"]
    return op.get(side + "_spaces") or [op[side + "_space"]] * len(arrays)


def plane(size, collective_id, *ops):
    parts = [(op["run"], len(op["inputs"]), len(op["outs"]), len(op["scratch"])) for op in ops]
    far = any(op.get("far") for op in ops)
    z_size = max(op.get("z", 1) for op in ops)
    results = pl.pallas_call(
        functools.partial(plane_kernel, size, parts, far, z_size),
        out_shape=[out for op in ops for out in op["outs"]],
        in_specs=[pl.BlockSpec(memory_space=space) for op in ops for space in spaces(op, "in")],
        out_specs=[pl.BlockSpec(memory_space=space) for op in ops for space in spaces(op, "out")],
        scratch_shapes=[scratch for op in ops for scratch in op["scratch"]],
        compiler_params=pltpu.CompilerParams(
            collective_id=collective_id, has_side_effects=True, vmem_limit_bytes=60 << 20
        ),
        cost_estimate=pl.CostEstimate(
            flops=0, bytes_accessed=sum(op["moved"] for op in ops), transcendentals=0
        ),
    )(*[x for op in ops for x in op["inputs"]])
    return results if len(results) > 1 else results[0]


def plane_groups(size, collective_id, *ops):
    groups = []
    room = 0
    for op in ops:
        need = 0 if op.get("in_space") == pl.ANY else op["moved"] * 5 // 4
        if not groups or need > room:
            groups.append([])
            room = 52 << 20
        groups[-1].append(op)
        room -= need
    results = []
    for i, group in enumerate(groups):
        got = plane(size, collective_id + i, *group)
        results += got if isinstance(got, (list, tuple)) else [got]
    return results


def swapped(tile):
    return tile % 2 + 2 * (tile // 4 % 2) + 4 * (tile // 2 % 2)


def tile_put(ref, mask, half):
    return row_half(ref.at[mask if half == 0 else swapped(mask)], half)


def tile_partner(me, bit):
    return {"ctx": flipped(me, 1 << bit, 3)}


def tile_copy(source, target, half, bit, me, send_sem, recv_sem):
    rows = source.shape[0] // 2
    at = pl.ds(half * rows, rows)
    return pltpu.make_async_remote_copy(
        src_ref=source.at[at],
        dst_ref=target.at[at],
        send_sem=send_sem.at[half],
        recv_sem=recv_sem.at[half],
        device_id=tile_partner(me, bit),
        device_id_type=MESH_IDS,
    )


def core_copy(source, target, me, send_sem, recv_sem):
    return pltpu.make_async_remote_copy(
        src_ref=source,
        dst_ref=target,
        send_sem=send_sem,
        recv_sem=recv_sem,
        device_id=tile_partner(me, 0),
        device_id_type=MESH_IDS,
    )


class TileGather:
    def __init__(self, tiles, send_sem, recv_sem, core_send, core_recv):
        me = lax.axis_index("ctx")
        self.hops = {
            target: [
                tile_copy(
                    tiles.at[source],
                    tiles.at[target],
                    half,
                    (first, 3 - first)[half],
                    me,
                    send_sem.at[target // 2 - 1],
                    recv_sem.at[target // 2 - 1],
                )
                for half in range(2)
            ]
            for source, target, first in ((0, 2, 1), (0, 4, 2), (2, 6, 2))
        }
        self.cores = [
            core_copy(tiles.at[2 * i], tiles.at[2 * i + 1], me, core_send.at[i], core_recv.at[i])
            for i in range(4)
        ]

    def before(self, tile):
        if tile == 0:
            for copy in self.hops[2]:
                copy.start()
            self.cores[0].start()
        elif tile % 2 == 1:
            self.cores[tile // 2].wait_recv()
            if tile == 1:
                for copy in self.hops[4]:
                    copy.start()
        else:
            for copy in self.hops[tile]:
                copy.wait_recv()
            if tile == 2:
                for copy in self.hops[6]:
                    copy.start()
            self.cores[tile // 2].start()

    def finish(self):
        for copies in self.hops.values():
            for copy in copies:
                copy.wait_send()
        for copy in self.cores:
            copy.wait_send()


def gather_sems():
    dma = pltpu.SemaphoreType.DMA
    return [dma((3, 2)), dma((3, 2)), dma((4,)), dma((4,))]


def part_slot(tile):
    odd = tile % 2
    return (1 - odd) * (tile // 2) + odd * (5 - tile // 4)


SCATTER_ORDER = (7, 6, 3, 2, 5, 4, 1, 0)


class TileScatter:
    def __init__(self, parts, core_buf, chip_buf, send_sem, recv_sem, core_send, core_recv):
        me = lax.axis_index("ctx")
        self.parts, self.core_buf, self.chip_buf = parts, core_buf, chip_buf
        self.hops = {
            source: [
                tile_copy(
                    parts.at[part_slot(source)],
                    chip_buf.at[source // 2 - 1],
                    half,
                    (first, 3 - first)[half],
                    me,
                    send_sem.at[source // 2 - 1],
                    recv_sem.at[source // 2 - 1],
                )
                for half in range(2)
            ]
            for source, first in ((6, 1), (4, 2), (2, 1))
        }
        self.cores = [
            core_copy(
                parts.at[part_slot(2 * i + 1)],
                core_buf.at[i],
                me,
                core_send.at[i],
                core_recv.at[i],
            )
            for i in range(4)
        ]

    def add(self, tile, buf):
        here = self.parts.at[part_slot(tile)]
        add_into(here, here, buf, here.shape[0], 32)

    def before(self, tile):
        if tile in (5, 1):
            self.cores[tile // 2 + 1].wait_send()

    def after(self, tile):
        if tile % 2 == 1:
            self.cores[tile // 2].start()
        else:
            self.settle(tile)

    def settle(self, tile):
        self.cores[tile // 2].wait_recv()
        self.add(tile, self.core_buf.at[tile // 2])
        if tile == 6 or tile == 2:
            for copy in self.hops[tile]:
                copy.start()
        if tile == 4:
            for copy in self.hops[6]:
                copy.wait_recv()
            self.add(4, self.chip_buf.at[2])
            for copy in self.hops[4]:
                copy.start()

    def finish(self, out):
        for tile in (2, 4):
            for copy in self.hops[tile]:
                copy.wait_recv()
        rows = out.shape[0]

        @pl.loop(0, rows // 32)
        def _(i):
            at = pl.ds(pl.multiple_of(i * 32, 32), 32)
            out[at] = (
                self.parts[0, at].astype(jnp.float32)
                + self.chip_buf[0, at].astype(jnp.float32)
                + self.chip_buf[1, at].astype(jnp.float32)
            ).astype(out.dtype)

        for copies in self.hops.values():
            for copy in copies:
                copy.wait_send()
        for tile in (4, 0):
            self.cores[tile // 2].wait_send()


def scatter_scratch(rows, width):
    return [
        pltpu.VMEM((6, rows, width), jnp.bfloat16),
        pltpu.VMEM((4, rows, width), jnp.bfloat16),
        pltpu.VMEM((3, rows, width), jnp.bfloat16),
    ] + gather_sems()


def produce_run(produce, batch, late, count, *refs):
    inputs, (out, *scratch) = refs[:count], refs[count:]
    me = lax.axis_index("ctx")
    scatter = TileScatter(*scratch)
    last = None
    for tile in SCATTER_ORDER:
        scatter.before(tile)
        scatter.parts[part_slot(tile)] = produce(inputs, tile, me).astype(jnp.bfloat16)
        if tile % 2 == 1:
            scatter.after(tile)
            if batch == 1 and last is not None:
                scatter.settle(last)
        last = tile
        if tile % batch == 0:
            yield
            if batch > 1:
                scatter.settle(tile)
    if batch == 1:
        scatter.settle(0)
    for _ in range(late):
        yield
    scatter.finish(out)


def produce_op(produce, rows, width, *inputs, batch=1, late=0, kind=jnp.float32):
    return dict(
        run=functools.partial(produce_run, produce, batch, late, len(inputs)),
        inputs=list(inputs),
        in_space=pltpu.VMEM,
        outs=[jax.ShapeDtypeStruct((rows, width), kind)],
        out_space=pltpu.VMEM,
        scratch=scatter_scratch(rows, width),
        moved=32 * rows * width,
    )


def norm_produce_run(produce, *refs):
    grads, weights, tokens, grad_residual, gain, grad_tokens, sums, grad_normed, *scratch = refs
    yield from produce_run(produce, 1, 0, 2, grads, weights, grad_normed, *scratch)
    sums[...] = jnp.zeros_like(sums)
    chunk = 32

    @pl.loop(0, tokens.shape[0] // chunk)
    def _(i):
        at = pl.ds(pl.multiple_of(i * chunk, chunk), chunk)
        unit, inverse = centre(tokens[at].astype(jnp.float32))
        rows = grad_normed[at]
        sums[:1] += jnp.sum(rows * unit, 0, keepdims=True)
        sums[1:] += jnp.sum(rows, 0, keepdims=True)
        scaled = rows * gain[...]
        grad_tokens[at] = grad_residual[at] + inverse * (
            scaled
            - jnp.mean(scaled, -1, keepdims=True)
            - unit * jnp.mean(scaled * unit, -1, keepdims=True)
        )


def norm_produce_op(produce, grads, weights, tokens, grad_residual, gain):
    rows, width = tokens.shape
    return dict(
        run=functools.partial(norm_produce_run, produce),
        inputs=[grads, weights, tokens, grad_residual, gain],
        in_space=pltpu.VMEM,
        outs=[
            jax.ShapeDtypeStruct((rows, width), jnp.float32),
            jax.ShapeDtypeStruct((2, width), jnp.float32),
        ],
        out_space=pltpu.VMEM,
        scratch=[pltpu.VMEM((rows, width), jnp.float32)] + scatter_scratch(rows, width),
        moved=32 * rows * width,
    )


def tile_rows(ref, tile, me):
    half = ref.shape[1] // 2
    return jnp.concatenate(
        [ref[flipped(me, tile, 3), :half], ref[flipped(me, swapped(tile), 3), half:]], 0
    )


def product_of_rows(refs, tile, me):
    rows = tile_rows(refs[0], tile, me)
    return times_transposed(rows, refs[1][:, : rows.shape[1]])


def product_of_columns(refs, tile, me):
    return jnp.dot(
        tile_rows(refs[0], tile, me), refs[1][...], preferred_element_type=jnp.float32
    )


def unpack_both_kernel(segments, count, source, gate, up):
    hidden_size = source.shape[2] // 2
    main = hidden_size // 128 * 128
    strip = hidden_size // segments
    for out, first, last in ((gate, 0, 2 * main), (up, main, main + hidden_size)):
        owners = [
            jnp.concatenate(
                [
                    source[owner, :, first : first + main],
                    source[owner, :, last : last + hidden_size - main],
                ],
                1,
            )
            for owner in range(count)
        ]
        out[...] = jnp.concatenate(
            [
                rows[:, segment * strip : (segment + 1) * strip]
                for segment in range(segments)
                for rows in owners
            ],
            1,
        ).astype(jnp.float32)


def unpack_both(gathered, segments):
    count, rows, width = gathered.shape
    step = min(128, rows)
    block = pl.BlockSpec((step, count * width // 2), lambda i: (i, 0))
    return pl.pallas_call(
        functools.partial(unpack_both_kernel, segments, count),
        grid=(rows // step,),
        in_specs=[pl.BlockSpec((count, step, width), lambda i: (0, i, 0))],
        out_specs=[block, block],
        out_shape=[jax.ShapeDtypeStruct((rows, count * width // 2), jnp.float32)] * 2,
        compiler_params=pltpu.CompilerParams(vmem_limit_bytes=60 << 20),
        cost_estimate=pl.CostEstimate(
            flops=0, bytes_accessed=6 * gathered.size, transcendentals=0
        ),
    )(gathered)


def greet_near(size):
    me = lax.axis_index("ctx")
    bits = size.bit_length() - 1
    greet([flipped(me, 1 << bit, bits) for bit in range(bits)])


def centre(values):
    centered = values - jnp.mean(values, -1, keepdims=True)
    inverse = lax.rsqrt(jnp.mean(centered * centered, -1, keepdims=True) + NORM_EPSILON)
    return centered * inverse, inverse


def join_kernel(
    size,
    mixed,
    weights,
    tokens,
    gain,
    shift,
    mixed_rows,
    residual,
    normed,
    weights_buf,
    load_sem,
    send_sem,
    recv_sem,
    local_sem,
):
    me = lax.axis_index("ctx")
    cols = mixed.shape[2]

    def load(owner):
        at = pl.ds(pl.multiple_of(owner * cols, cols), cols)
        return pltpu.make_async_copy(weights.at[at], weights_buf.at[at], load_sem.at[owner])

    others = [lax.rem(me + step, size) for step in range(size)]
    for step in range(size):
        load(lax.rem(me + size - step, size)).start()
    greet(others[1:])
    here = column_view(mixed_rows, me, cols)
    local = pltpu.make_async_copy(mixed.at[me], here, local_sem)
    local.start()
    copies = []
    for step in range(1, size):
        copy = pltpu.make_async_remote_copy(
            src_ref=mixed.at[others[step]],
            dst_ref=here,
            send_sem=send_sem.at[step - 1],
            recv_sem=recv_sem.at[step - 1],
            device_id={"ctx": others[step]},
            device_id_type=MESH_IDS,
        )
        copy.start()
        copies.append(copy)
    local.wait()
    residual[...] = tokens[...].astype(jnp.float32)
    for step in range(size):
        owner = lax.rem(me + size - step, size)
        if step > 0:
            copies[step - 1].wait_recv()
        load(owner).wait()
        at = pl.ds(pl.multiple_of(owner * cols, cols), cols)
        residual[...] += jnp.dot(
            mixed_rows[:, at], weights_buf[at], preferred_element_type=jnp.float32
        )
    unit = centre(residual[...])[0]
    normed[...] = (unit * gain[...] + shift[...]).astype(jnp.bfloat16)
    for copy in copies:
        copy.wait_send()


def join_rows(mixed, weights, tokens, gain, shift, collective_id):
    size, rows, cols = mixed.shape
    width = size * cols
    vmem = pl.BlockSpec(memory_space=pltpu.VMEM)
    any_space = pl.BlockSpec(memory_space=pl.ANY)
    low = jnp.bfloat16
    dma = pltpu.SemaphoreType.DMA
    return pl.pallas_call(
        functools.partial(join_kernel, size),
        in_specs=[any_space] * 2 + [vmem] * 3,
        out_specs=[vmem] * 3,
        out_shape=[
            jax.ShapeDtypeStruct((rows, width), low),
            jax.ShapeDtypeStruct((rows, width), jnp.float32),
            jax.ShapeDtypeStruct((rows, width), low),
        ],
        scratch_shapes=[
            pltpu.VMEM((width, width), low),
            dma((size,)),
            dma((size - 1,)),
            dma((size - 1,)),
            dma,
        ],
        compiler_params=pltpu.CompilerParams(
            collective_id=collective_id, has_side_effects=True, vmem_limit_bytes=60 << 20
        ),
        cost_estimate=pl.CostEstimate(
            flops=2 * rows * width * width, bytes_accessed=2 * width * width, transcendentals=0
        ),
    )(mixed, weights, tokens, gain, shift)


def part_kernel(
    size,
    grad_normed,
    residual,
    cotangent,
    gain,
    weights,
    grad_residual,
    grad_branch,
    sums,
    grad_mixed,
    weights_buf,
    staged,
    load_sem,
    send_sem,
    recv_sem,
    local_sem,
):
    me = lax.axis_index("ctx")
    cols = staged.shape[2]
    others = [lax.rem(me + step, size) for step in range(size)]

    def load(owner):
        at = pl.ds(pl.multiple_of(owner * cols, cols), cols)
        return pltpu.make_async_copy(weights.at[at], weights_buf.at[at], load_sem.at[owner])

    order = list(range(1, size)) + [0]
    for step in order:
        load(others[step]).start()
    greet(others[1:])
    unit, inverse = centre(residual[...])
    grads = grad_normed[...]
    scaled = grads * gain[...]
    total = cotangent[...].astype(jnp.float32) + inverse * (
        scaled
        - jnp.mean(scaled, -1, keepdims=True)
        - unit * jnp.mean(scaled * unit, -1, keepdims=True)
    )
    grad_residual[...] = total
    grad_branch[...] = total.astype(jnp.bfloat16)
    copies = []
    for step in order:
        other = others[step]
        load(other).wait()
        at = pl.ds(pl.multiple_of(other * cols, cols), cols)
        staged[step] = times_transposed(grad_branch[...], weights_buf[at]).astype(jnp.bfloat16)
        if step == 0:
            copy = pltpu.make_async_copy(staged.at[0], grad_mixed.at[me], local_sem)
        else:
            copy = pltpu.make_async_remote_copy(
                src_ref=staged.at[step],
                dst_ref=grad_mixed.at[me],
                send_sem=send_sem.at[step - 1],
                recv_sem=recv_sem.at[step - 1],
                device_id={"ctx": other},
                device_id_type=MESH_IDS,
            )
        copy.start()
        copies.append(copy)
    sums[:1] = jnp.sum(grads * unit, 0, keepdims=True)
    sums[1:] = jnp.sum(grads, 0, keepdims=True)
    for copy in copies:
        copy.wait()


def part_rows(grad_normed, residual, cotangent, gain, weights, size, collective_id):
    rows, width = grad_normed.shape
    cols = width // size
    vmem = pl.BlockSpec(memory_space=pltpu.VMEM)
    any_space = pl.BlockSpec(memory_space=pl.ANY)
    low = jnp.bfloat16
    dma = pltpu.SemaphoreType.DMA
    return pl.pallas_call(
        functools.partial(part_kernel, size),
        in_specs=[vmem] * 4 + [any_space],
        out_specs=[vmem] * 3 + [any_space],
        out_shape=[
            jax.ShapeDtypeStruct((rows, width), jnp.float32),
            jax.ShapeDtypeStruct((rows, width), low),
            jax.ShapeDtypeStruct((2, width), jnp.float32),
            jax.ShapeDtypeStruct((size, rows, cols), low),
        ],
        scratch_shapes=[
            pltpu.VMEM((width, width), low),
            pltpu.VMEM((size, rows, cols), low),
            dma((size,)),
            dma((size - 1,)),
            dma((size - 1,)),
            dma,
        ],
        compiler_params=pltpu.CompilerParams(
            collective_id=collective_id, has_side_effects=True, vmem_limit_bytes=60 << 20
        ),
        cost_estimate=pl.CostEstimate(
            flops=2 * rows * width * width, bytes_accessed=2 * width * width, transcendentals=0
        ),
    )(grad_normed, residual, cotangent, gain, weights)


def forward_kernel(
    hidden_size,
    normed,
    weights,
    grads,
    normed_t,
    values,
    hidden,
    grad_down,
    tiles,
    weights_buf,
    grads_buf,
    turned,
    values_buf,
    hidden_t,
    load_sem,
    out_sem,
    *sems,
):
    greet_near(8)
    own = pltpu.make_async_copy(normed, tiles.at[0], load_sem.at[0])
    load = pltpu.make_async_copy(weights, weights_buf, load_sem.at[1])
    own.start()
    load.start()
    pltpu.make_async_copy(grads, grads_buf, load_sem.at[2]).start()
    own.wait()
    gather = TileGather(tiles, *sems)
    rows = tiles.shape[1]
    main = hidden_size // 128 * 128

    def write_out(tile, slot):
        at = pl.ds(pl.multiple_of(tile * rows, rows), rows)
        return [
            pltpu.make_async_copy(values_buf.at[slot], values.at[tile], out_sem.at[0, slot]),
            pltpu.make_async_copy(turned.at[slot], normed_t.at[:, at], out_sem.at[1, slot]),
        ]

    @pl.loop(0, 8)
    def _(t):
        for tile in range(8):

            @pl.when(t == tile)
            def _():
                gather.before(tile)
                if tile == 0:
                    load.wait()

        slot = t % 2

        @pl.when(t >= 2)
        def _():
            for copy in write_out(t - 2, slot):
                copy.wait()

        here = tiles[t]
        value = jnp.dot(here, weights_buf[...], preferred_element_type=jnp.float32)
        values_buf[slot] = value
        gate, up = value[:, :main], value[:, main : 2 * main]
        front = gate * jax.nn.sigmoid(gate) * up
        last = value[:, 2 * main :]
        behind = last * jax.nn.sigmoid(last) * pltpu.roll(last, 64, 1)
        both = jnp.concatenate([front, behind], 1)
        hidden[t] = both[:, :hidden_size].astype(jnp.bfloat16)
        at = pl.ds(pl.multiple_of(t * rows, rows), rows)
        hidden_t[:, at] = jnp.transpose(both)[:hidden_size].astype(jnp.bfloat16)
        turned[slot] = jnp.transpose(here)
        for copy in write_out(t, slot):
            copy.start()

    pltpu.make_async_copy(grads, grads_buf, load_sem.at[2]).wait()
    width = grads_buf.shape[2]
    step = 256

    @pl.loop(0, width // step)
    def _(i):
        at = pl.ds(pl.multiple_of(i * step, step), step)
        grad_down[:, at] = jnp.dot(
            hidden_t[...],
            grads_buf[:, :, at].reshape(8 * rows, step),
            preferred_element_type=jnp.float32,
        ).astype(jnp.bfloat16)

    for tile in (6, 7):
        for copy in write_out(tile, tile % 2):
            copy.wait()
    gather.finish()


def forward_mlp(normed, weights, grads, hidden_size, collective_id):
    rows, width = normed.shape
    wide = weights.shape[1]
    any_space = pl.BlockSpec(memory_space=pl.ANY)
    vmem = pl.BlockSpec(memory_space=pltpu.VMEM)
    low = jnp.bfloat16
    dma = pltpu.SemaphoreType.DMA
    return pl.pallas_call(
        functools.partial(forward_kernel, hidden_size),
        in_specs=[any_space] * 3,
        out_specs=[any_space, any_space, vmem, vmem],
        out_shape=[
            jax.ShapeDtypeStruct((width, 8 * rows), low),
            jax.ShapeDtypeStruct((8, rows, wide), jnp.float32),
            jax.ShapeDtypeStruct((8, rows, hidden_size), low),
            jax.ShapeDtypeStruct((hidden_size, width), low),
        ],
        scratch_shapes=[
            pltpu.VMEM((8, rows, width), low),
            pltpu.VMEM(weights.shape, low),
            pltpu.VMEM((8, rows, width), low),
            pltpu.VMEM((2, width, rows), low),
            pltpu.VMEM((2, rows, wide), jnp.float32),
            pltpu.VMEM((hidden_size, 8 * rows), low),
            dma((3,)),
            dma((2, 2)),
        ]
        + gather_sems(),
        compiler_params=pltpu.CompilerParams(
            collective_id=collective_id, has_side_effects=True, vmem_limit_bytes=60 << 20
        ),
        cost_estimate=pl.CostEstimate(
            flops=16 * rows * width * (wide + hidden_size),
            bytes_accessed=64 * rows * width,
            transcendentals=0,
        ),
    )(normed, weights, grads)


def backward_kernel(
    hidden_size,
    grads,
    values,
    weights,
    down,
    normed_t,
    hidden,
    grad_normed,
    grad_both_w,
    layer_part,
    grads_buf,
    values_buf,
    weights_buf,
    down_buf,
    normed_buf,
    grad_both,
    out_buf,
    hidden_buf,
    load_sem,
    tile_sem,
    out_sem,
    *scatter_refs,
):
    greet_near(8)
    scatter = TileScatter(*scatter_refs[: len(scatter_refs) // 2])
    layer = TileScatter(*scatter_refs[len(scatter_refs) // 2 :])
    rows = grads_buf.shape[1]
    main = hidden_size // 128 * 128
    load_weights = pltpu.make_async_copy(weights, weights_buf, load_sem.at[0])
    load_down = pltpu.make_async_copy(down, down_buf, load_sem.at[1])

    def load_tile(tile, slot):
        return [
            pltpu.make_async_copy(grads.at[tile], grads_buf.at[slot], tile_sem.at[0, slot]),
            pltpu.make_async_copy(values.at[tile], values_buf.at[slot], tile_sem.at[1, slot]),
            pltpu.make_async_copy(hidden.at[tile], hidden_buf.at[slot], tile_sem.at[3, slot]),
        ]

    def load_chunk(i):
        at = pl.ds(pl.multiple_of(i * rows, rows), rows)
        return pltpu.make_async_copy(normed_t.at[at], normed_buf.at[i % 2], tile_sem.at[2, i % 2])

    load_down.start()
    for copy in load_tile(7, 1):
        copy.start()
    load_weights.start()
    load_chunk(0).start()

    @pl.loop(0, 8)
    def _(u):
        t = 7 - swapped(u)
        slot = t % 2

        @pl.when(u < 7)
        def _():
            for copy in load_tile(7 - swapped(u + 1), 1 - slot):
                copy.start()

        @pl.when(u == 0)
        def _():
            load_down.wait()

        for copy in load_tile(t, slot):
            copy.wait()
        for tile in (5, 1):

            @pl.when(t == tile)
            def _():
                scatter.before(tile)
                layer.before(tile)

        layer.parts[part_slot(t)] = jnp.dot(
            hidden_buf[slot], down_buf[...], preferred_element_type=jnp.float32
        ).astype(jnp.bfloat16)
        for tile in range(8):

            @pl.when(t == tile)
            def _():
                layer.after(tile)

        grad_hidden = lax.dot_general(
            grads_buf[slot],
            down_buf[...],
            (((1,), (1,)), ((), ())),
            preferred_element_type=jnp.float32,
        )
        value = values_buf[slot]
        gate, up, above = value[:, :main], value[:, main : 2 * main], grad_hidden[:, :main]
        sigmoid = jax.nn.sigmoid(gate)
        grad_both[t, :, :main] = (
            above * up * sigmoid * (1.0 + gate * (1.0 - sigmoid))
        ).astype(jnp.bfloat16)
        grad_both[t, :, main : 2 * main] = (above * (gate * sigmoid)).astype(jnp.bfloat16)
        last = value[:, 2 * main :]
        above = grad_hidden[:, main:]
        above = jnp.concatenate([above, jnp.zeros_like(above)], 1)
        sigmoid = jax.nn.sigmoid(last)
        to_gate = above * pltpu.roll(last, 64, 1) * sigmoid * (1.0 + last * (1.0 - sigmoid))
        to_up = pltpu.roll(above * (last * sigmoid), 64, 1)
        lane = lax.broadcasted_iota(jnp.int32, last.shape, 1)
        grad_both[t, :, 2 * main :] = jnp.where(lane < 64, to_gate, to_up).astype(jnp.bfloat16)

        @pl.when(u == 0)
        def _():
            load_weights.wait()

        scatter.parts[part_slot(t)] = lax.dot_general(
            grad_both[t],
            weights_buf[...],
            (((1,), (1,)), ((), ())),
            preferred_element_type=jnp.float32,
        ).astype(jnp.bfloat16)
        for tile in range(8):

            @pl.when(t == tile)
            def _():
                scatter.after(tile)


    chunks = normed_t.shape[0] // rows

    def store_chunk(i):
        at = pl.ds(pl.multiple_of(i * rows, rows), rows)
        return pltpu.make_async_copy(out_buf.at[i % 2], grad_both_w.at[at], out_sem.at[i % 2])

    @pl.loop(0, chunks)
    def _(i):
        @pl.when(i < chunks - 1)
        def _():
            load_chunk(i + 1).start()

        load_chunk(i).wait()

        @pl.when(i >= 2)
        def _():
            store_chunk(i - 2).wait()

        out_buf[i % 2] = jnp.dot(
            normed_buf[i % 2],
            grad_both[...].reshape(8 * rows, grad_both.shape[2]),
            preferred_element_type=jnp.float32,
        ).astype(jnp.bfloat16)
        store_chunk(i).start()

    store_chunk(chunks - 2).wait()
    store_chunk(chunks - 1).wait()
    scatter.finish(grad_normed)
    layer.finish(layer_part)


def backward_mlp(grads, values, weights, down, normed_t, hidden, collective_id):
    size, rows, width = grads.shape
    hidden_size = down.shape[0]
    wide = weights.shape[1]
    any_space = pl.BlockSpec(memory_space=pl.ANY)
    vmem = pl.BlockSpec(memory_space=pltpu.VMEM)
    low = jnp.bfloat16
    dma = pltpu.SemaphoreType.DMA
    return pl.pallas_call(
        functools.partial(backward_kernel, hidden_size),
        in_specs=[any_space] * 6,
        out_specs=[vmem, any_space, vmem],
        out_shape=[
            jax.ShapeDtypeStruct((rows, width), jnp.float32),
            jax.ShapeDtypeStruct((width, wide), low),
            jax.ShapeDtypeStruct((rows, width), jnp.float32),
        ],
        scratch_shapes=[
            pltpu.VMEM((2, rows, width), low),
            pltpu.VMEM((2, rows, wide), jnp.float32),
            pltpu.VMEM(weights.shape, low),
            pltpu.VMEM(down.shape, low),
            pltpu.VMEM((2, rows, 8 * rows), low),
            pltpu.VMEM((8, rows, wide), low),
            pltpu.VMEM((2, rows, wide), low),
            pltpu.VMEM((2, rows, hidden_size), low),
            dma((2,)),
            dma((4, 2)),
            dma((2,)),
        ]
        + scatter_scratch(rows, width) * 2,
        compiler_params=pltpu.CompilerParams(
            collective_id=collective_id, has_side_effects=True, vmem_limit_bytes=60 << 20
        ),
        cost_estimate=pl.CostEstimate(
            flops=16 * rows * width * (2 * wide + hidden_size),
            bytes_accessed=64 * rows * width,
            transcendentals=0,
        ),
    )(grads, values, weights, down, normed_t, hidden)


def unpack_rows_kernel(source, out):
    out[...] = source[...].astype(jnp.float32)


def unpack_rows(gathered, rows):
    count, _, width = gathered.shape
    group = min(count, 1 << max(1, 352 // rows).bit_length() - 1)
    out = pl.pallas_call(
        unpack_rows_kernel,
        grid=(count // group,),
        in_specs=[pl.BlockSpec((group, rows, width), lambda i: (i, 0, 0))],
        out_specs=pl.BlockSpec((group, rows, width), lambda i: (i, 0, 0)),
        out_shape=jax.ShapeDtypeStruct((count, rows, width), jnp.float32),
        compiler_params=pltpu.CompilerParams(vmem_limit_bytes=60 << 20),
        cost_estimate=pl.CostEstimate(
            flops=0, bytes_accessed=6 * gathered.size, transcendentals=0
        ),
    )(gathered)
    return out.reshape(count * rows, width)


def unpack_kernel(segments, count, source, out):
    strip = source.shape[2] // segments
    pieces = []
    for segment in range(segments):
        for owner in range(count):
            pieces.append(source[owner, :, segment * strip : (segment + 1) * strip])
    out[...] = jnp.concatenate(pieces, 1).astype(jnp.float32)


def unpack_columns(gathered, segments):
    count, rows, width = gathered.shape
    step = min(128, rows)
    return pl.pallas_call(
        functools.partial(unpack_kernel, segments, count),
        grid=(rows // step,),
        in_specs=[pl.BlockSpec((count, step, width), lambda i: (0, i, 0))],
        out_specs=pl.BlockSpec((step, count * width), lambda i: (i, 0)),
        out_shape=jax.ShapeDtypeStruct((rows, count * width), jnp.float32),
        compiler_params=pltpu.CompilerParams(vmem_limit_bytes=60 << 20),
        cost_estimate=pl.CostEstimate(
            flops=0, bytes_accessed=6 * gathered.size, transcendentals=0
        ),
    )(gathered)


def norm_rows(values, gain_row, shift_row):
    centered = values - jnp.mean(values, -1, keepdims=True)
    inverse = lax.rsqrt(jnp.mean(centered * centered, -1, keepdims=True) + NORM_EPSILON)
    unit_rows = centered * inverse
    return (unit_rows * gain_row + shift_row, unit_rows, inverse)


def norm_back(grad_rows, unit_rows, inverse, gain_row):
    scaled = grad_rows * gain_row
    return inverse * (
        scaled
        - jnp.mean(scaled, -1, keepdims=True)
        - unit_rows * jnp.mean(scaled * unit_rows, -1, keepdims=True)
    )


def turn(rows, cosine, sine_low, sine_high, width):
    repeat = width // 128
    wide = [jnp.concatenate([table] * repeat, 1) for table in (cosine, sine_low, sine_high)]
    return (
        rows * wide[0]
        + pltpu.roll(rows, width - ROT // 2, 1) * wide[1]
        + pltpu.roll(rows, ROT // 2, 1) * wide[2]
    )


def head_stack(features_first, heads):
    owner = lax.broadcasted_iota(jnp.int32, features_first.shape, 0) // HEAD
    zero = jnp.zeros_like(features_first)
    return jnp.concatenate([jnp.where(owner == h, features_first, zero) for h in range(heads)], 1)


def row_stack(rows, heads):
    owner = lax.broadcasted_iota(jnp.int32, rows.shape, 1) // HEAD
    zero = jnp.zeros_like(rows)
    return jnp.concatenate([jnp.where(owner == h, rows, zero) for h in range(heads)], 0)


def pair_bias(key_tile, tile, heads, first_keys, diagonal):
    key_place = lax.broadcasted_iota(jnp.int32, (tile, tile), 0)
    allowed = key_place + key_tile * tile >= first_keys
    if diagonal:
        allowed &= key_place <= lax.broadcasted_iota(jnp.int32, (tile, tile), 1)
    return jnp.concatenate([jnp.where(allowed, 0.0, MASKED_SCORE)] * heads, 1)


def transposed(rows):
    return jnp.transpose(rows.astype(jnp.float32)).astype(rows.dtype)


def attend_kernel(
    block,
    heads,
    order,
    lowest,
    projected,
    starts,
    qkv,
    attended,
    mixed,
    log_total,
    value_t,
    summed,
    top,
    total,
):
    cols = heads * HEAD
    seq = projected.shape[0]
    tile = 2 * block

    @pl.loop(0, seq // block)
    def _(p):
        at = pl.ds(pl.multiple_of(p * block, block), block)
        rows = projected[pl.ds(pl.multiple_of(order[p] * block, block), block)]
        qkv[at] = rows
        value_t[:, at] = transposed(rows[:, 2 * cols :])

    @pl.loop(0, seq // tile)
    def _(i):
        at = pl.ds(pl.multiple_of(i * tile, tile), tile)
        query_t = head_stack(transposed(qkv[at, :cols]), heads)
        first_keys = starts[:, at]
        top[...] = jnp.full(top.shape, MASKED_SCORE, jnp.float32)
        total[...] = jnp.zeros_like(total)
        summed[...] = jnp.zeros_like(summed)

        def step(j, diagonal):
            keys_at = pl.ds(pl.multiple_of(j * tile, tile), tile)
            scores = jnp.dot(
                qkv[keys_at, cols : 2 * cols], query_t, preferred_element_type=jnp.float32
            )
            scores += pair_bias(j, tile, heads, first_keys, diagonal)
            old_top = top[...]
            new_top = jnp.maximum(old_top, jnp.max(scores, 0, keepdims=True))
            exps = jnp.exp(scores - new_top)
            fade = jnp.exp(old_top - new_top)
            total[...] = total[...] * fade + jnp.sum(exps, 0, keepdims=True)
            top[...] = new_top
            low = exps.astype(jnp.bfloat16)
            for h in range(heads):
                own = slice(h * tile, (h + 1) * tile)
                features = slice(h * HEAD, (h + 1) * HEAD)
                summed[features] = summed[features] * fade[:, own] + jnp.dot(
                    value_t[features, keys_at], low[:, own], preferred_element_type=jnp.float32
                )

        @pl.loop(lowest[i], i)
        def _(j):
            step(j, False)

        step(i, True)

        log_total[i] = top[...] + jnp.log(total[...])
        scale = 1.0 / total[...]
        for h in range(heads):
            features = slice(h * HEAD, (h + 1) * HEAD)
            summed[features] = summed[features] * scale[:, h * tile : (h + 1) * tile]
        rows = jnp.transpose(summed[...])
        attended[at] = rows
        for part in range(2):
            place = pl.ds(pl.multiple_of(order[2 * i + part] * block, block), block)
            mixed[place] = rows[part * block : (part + 1) * block].astype(jnp.bfloat16)


def attend(projected, order, lowest, starts, heads):
    seq, wide = projected.shape
    cols = wide // 3
    block = seq // order.shape[0]
    tile = 2 * block
    vmem = pl.BlockSpec(memory_space=pltpu.VMEM)
    smem = pl.BlockSpec(memory_space=pltpu.SMEM)
    return pl.pallas_call(
        functools.partial(attend_kernel, block, heads),
        in_specs=[smem, smem] + [vmem] * 2,
        out_specs=[vmem] * 4,
        out_shape=[
            jax.ShapeDtypeStruct((seq, wide), jnp.bfloat16),
            jax.ShapeDtypeStruct((seq, cols), jnp.float32),
            jax.ShapeDtypeStruct((seq, cols), jnp.bfloat16),
            jax.ShapeDtypeStruct((seq // tile, 1, heads * tile), jnp.float32),
        ],
        scratch_shapes=[
            pltpu.VMEM((cols, seq), jnp.bfloat16),
            pltpu.VMEM((cols, tile), jnp.float32),
            pltpu.VMEM((1, heads * tile), jnp.float32),
            pltpu.VMEM((1, heads * tile), jnp.float32),
        ],
        compiler_params=pltpu.CompilerParams(vmem_limit_bytes=48 << 20),
        cost_estimate=pl.CostEstimate(
            flops=4 * seq * seq * cols, bytes_accessed=12 * seq * cols, transcendentals=0
        ),
    )(order, lowest, projected, starts)


def attend_back_run(
    block,
    heads,
    order,
    places,
    qkv,
    grad_mixed,
    attended,
    log_total,
    starts,
    cosine,
    sine_low,
    sine_high,
    normed_t,
    out,
    sums,
    grad_weights,
    normed_buf,
    load_sem,
    key_t,
    grad_key,
    grad_value,
    grad_query,
    query_sum,
):
    cols = heads * HEAD
    seq = qkv.shape[0]
    tile = 2 * block
    chunk = normed_buf.shape[1]
    chunks = normed_t.shape[0] // chunk

    def load(i):
        at = pl.ds(pl.multiple_of(i * chunk, chunk), chunk)
        return pltpu.make_async_copy(normed_t.at[at], normed_buf.at[i % 2], load_sem.at[i % 2])

    load(0).start()

    @pl.loop(0, seq // block)
    def _(p):
        at = pl.ds(pl.multiple_of(p * block, block), block)
        key_t[:, at] = transposed(qkv[at, cols : 2 * cols])
        grad_key[p] = jnp.zeros((block, cols), jnp.float32)
        grad_value[p] = jnp.zeros((block, cols), jnp.float32)

    yield
    for i in reversed(range(seq // tile)):
        at = pl.ds(i * tile, tile)
        query = qkv[at, :cols]
        grad = jnp.concatenate(
            [
                grad_mixed[order[2 * i + part]]
                for part in range(2)
            ],
            0,
        )
        query_t = head_stack(transposed(query), heads)
        query_rows = row_stack(query, heads)
        grad_t = head_stack(transposed(grad), heads)
        grads = row_stack(grad, heads)
        products = jnp.transpose(grad.astype(jnp.float32) * attended[at])
        delta = jnp.concatenate(
            [
                jnp.sum(products[h * HEAD : (h + 1) * HEAD], 0, keepdims=True)
                for h in range(heads)
            ],
            1,
        )
        logs = log_total[i]
        first_keys = starts[:, at]
        query_sum[...] = jnp.zeros_like(query_sum)

        def step(j, diagonal):
            keys_at = pl.ds(pl.multiple_of(j * tile, tile), tile)
            scores = jnp.dot(
                qkv[keys_at, cols : 2 * cols], query_t, preferred_element_type=jnp.float32
            )
            scores += pair_bias(j, tile, heads, first_keys, diagonal)
            weights = jnp.exp(scores - logs)
            grad_soft = jnp.dot(
                qkv[keys_at, 2 * cols :], grad_t, preferred_element_type=jnp.float32
            )
            pair = pl.ds(2 * j, 2)
            grad_value[pair] += jnp.dot(
                weights.astype(jnp.bfloat16), grads, preferred_element_type=jnp.float32
            ).reshape(2, block, cols)
            grad_scores = (weights * (grad_soft - delta)).astype(jnp.bfloat16)
            grad_key[pair] += jnp.dot(
                grad_scores, query_rows, preferred_element_type=jnp.float32
            ).reshape(2, block, cols)
            for h in range(heads):
                features = slice(h * HEAD, (h + 1) * HEAD)
                query_sum[features] += jnp.dot(
                    key_t[features, keys_at],
                    grad_scores[:, h * tile : (h + 1) * tile],
                    preferred_element_type=jnp.float32,
                )

        if i > 0:

            @pl.loop(0, i)
            def _(j):
                step(j, False)

        step(i, True)
        grad_query[2 * i : 2 * i + 2] = (
            jnp.transpose(query_sum[...]) * HEAD ** (-0.5)
        ).reshape(2, block, cols)
        yield
    sums[...] = jnp.zeros_like(sums)

    @pl.loop(0, seq // block)
    def _(d):
        at = pl.ds(pl.multiple_of(d * block, block), block)
        place = places[d]
        tables = (cosine[at], -sine_low[at], -sine_high[at])
        for k, rows in enumerate(
            (
                turn(grad_query[place], *tables, cols),
                turn(grad_key[place], *tables, cols),
                grad_value[place],
            )
        ):
            columns = slice(k * cols, (k + 1) * cols)
            low = rows.astype(jnp.bfloat16)
            out[at, columns] = low
            sums[:, columns] += jnp.sum(low.astype(jnp.float32), 0, keepdims=True)

    @pl.loop(0, chunks)
    def _(i):
        @pl.when(i < chunks - 1)
        def _():
            load(i + 1).start()

        load(i).wait()
        at = pl.ds(pl.multiple_of(i * chunk, chunk), chunk)
        grad_weights[at] = jnp.dot(
            normed_buf[i % 2], out[...], preferred_element_type=jnp.float32
        ).astype(jnp.bfloat16)


def attend_back_op(
    qkv, grad_mixed, attended, log_total, order, places, starts, tables, normed_t, heads
):
    seq, wide = qkv.shape
    cols = wide // 3
    block = seq // order.shape[0]
    tile = 2 * block
    low = jnp.bfloat16
    return dict(
        run=functools.partial(attend_back_run, block, heads),
        inputs=[order, places, qkv, grad_mixed, attended, log_total, starts, *tables, normed_t],
        in_spaces=[pltpu.SMEM] * 2 + [pltpu.VMEM] * 8 + [pl.ANY],
        outs=[
            jax.ShapeDtypeStruct((seq, wide), low),
            jax.ShapeDtypeStruct((1, wide), jnp.float32),
            jax.ShapeDtypeStruct((normed_t.shape[0], wide), low),
        ],
        out_spaces=[pltpu.VMEM] * 3,
        scratch=[
            pltpu.VMEM((2, 256, seq), low),
            pltpu.SemaphoreType.DMA((2,)),
            pltpu.VMEM((cols, seq), low),
            pltpu.VMEM((seq // block, block, cols), jnp.float32),
            pltpu.VMEM((seq // block, block, cols), jnp.float32),
            pltpu.VMEM((seq // block, block, cols), jnp.float32),
            pltpu.VMEM((cols, tile), jnp.float32),
        ],
        moved=20 * seq * cols,
    )


def tables_run(cosines, sines, cosine, sine_low, sine_high):
    half_rot = ROT // 2
    step = 256
    yield

    @pl.loop(0, cosine.shape[0] // step)
    def _(i):
        at = pl.ds(pl.multiple_of(i * step, step), step)
        cos_rows, sin_rows = jnp.transpose(cosines[:, at]), jnp.transpose(sines[:, at])
        lane = lax.broadcasted_iota(jnp.int32, (step, 128), 1) % HEAD
        cos_wide = jnp.ones((step, 128), jnp.float32)
        sin_wide = jnp.zeros((step, 128), jnp.float32)
        for k in range(half_rot):
            own = (lane == k) | (lane == k + half_rot)
            cos_wide = jnp.where(own, cos_rows[:, k : k + 1], cos_wide)
            sin_wide = jnp.where(own, sin_rows[:, k : k + 1], sin_wide)
        cosine[at] = cos_wide
        sine_low[at] = jnp.where(lane < half_rot, -sin_wide, 0.0)
        sine_high[at] = jnp.where(lane >= half_rot, sin_wide, 0.0)


def tables_op(places):
    turns = jnp.arange(ROT // 2, dtype=jnp.int32)[:, None]
    freq = ROTARY_BASE ** (-turns.astype(jnp.float32) * 2.0 / ROT)
    angles = places.astype(jnp.float32)[None, :] * freq
    return dict(
        run=tables_run,
        inputs=[jnp.cos(angles), jnp.sin(angles)],
        in_space=pltpu.VMEM,
        outs=[jax.ShapeDtypeStruct((places.size, 128), jnp.float32)] * 3,
        out_space=pltpu.VMEM,
        scratch=[],
        moved=1024 * places.size,
    )


def place_order(block_pairs, axis_size):
    device_blocks = jnp.stack([block_pairs, 2 * axis_size - 1 - block_pairs], 1).reshape(-1)
    places = jnp.arange(2 * axis_size, dtype=jnp.int32)
    return jnp.sum(
        jnp.where(device_blocks[None, :] == places[:, None], places[None, :], 0), 1
    ).astype(jnp.int32)


def document_starts(docs):
    first = jnp.sum((docs < 1).astype(jnp.int32))
    second = jnp.sum((docs < 2).astype(jnp.int32))
    return jnp.where(docs == 0, 0, jnp.where(docs == 1, first, second))


def inner(left_side, right_side):
    return lax.dot_general(
        left_side, right_side, (((0,), (0,)), ((), ())), preferred_element_type=jnp.float32
    )


def times_transposed(left_side, right_side):
    return lax.dot_general(
        left_side, right_side, (((1,), (1,)), ((), ())), preferred_element_type=jnp.float32
    )


def times(left_side, right_side):
    return jnp.dot(left_side, right_side, preferred_element_type=jnp.float32)


def after(value, *earlier):
    return lax.optimization_barrier((value,) + earlier)[0]


def body(
    tokens,
    doc_ids,
    block_pairs,
    ln1_gain,
    ln1_bias,
    w_qkv,
    b_qkv,
    w_out,
    ln2_gain,
    ln2_bias,
    w_gate,
    w_up,
    w_down,
    cotangent,
):
    rows_here = tokens.shape[1]
    width = tokens.shape[2]
    head_count = width // HEAD
    ctx_size = lax.axis_size("ctx")
    fsdp_size = lax.axis_size("fsdp")
    seq_rows = rows_here * ctx_size
    position = lax.axis_index("ctx")
    heads_here = head_count // ctx_size
    cols = width // ctx_size
    shard_rows = w_qkv.shape[0]
    hidden_shard = w_down.shape[0]
    strip = hidden_shard // ctx_size

    tile = 2 * (rows_here // 2)
    order = place_order(block_pairs, ctx_size)
    starts = document_starts(doc_ids[0])
    lowest = starts[::tile] // tile
    starts = starts[None]
    device_blocks = jnp.stack([block_pairs, 2 * ctx_size - 1 - block_pairs], 1).reshape(-1, 1)
    half_rows = rows_here // 2
    places = device_blocks * half_rows + jnp.arange(half_rows, dtype=jnp.int32)[None, :]

    def strips(w, count, size):
        stride = w.shape[1] // count
        return [
            lax.dynamic_slice_in_dim(w, i * stride + position * size, size, 1)
            for i in range(count)
        ]

    qkv_strip = jnp.concatenate(strips(w_qkv, 3, cols) + strips(w_out, 1, cols), 1)
    hidden_here = fsdp_size * strip
    main = hidden_here // 128 * 128
    fused = ctx_size == 8 and hidden_here - main == 64 and rows_here == 256
    gate_strip = jnp.concatenate(strips(w_gate, fsdp_size, strip), 1)
    up_strip = jnp.concatenate(strips(w_up, fsdp_size, strip), 1)
    both_strip = jnp.concatenate(
        [gate_strip[:, :main], up_strip[:, :main], gate_strip[:, main:], up_strip[:, main:]], 1
    )
    down_strip = lax.dynamic_slice_in_dim(w_down, position * strip, strip, 0)
    out_piece = shard_rows // ctx_size
    qkv_here = lax.all_gather(qkv_strip, "fsdp", axis=0, tiled=True)
    both_here = lax.all_gather(both_strip, "fsdp", axis=0, tiled=True)
    down_here = lax.all_gather(down_strip, "fsdp", axis=0, tiled=True)

    small = jnp.concatenate([ln1_gain, ln1_bias, ln2_gain, ln2_bias, b_qkv])
    small_rows = -(-small.size // 2048) * 16
    small = jnp.pad(small, (0, small_rows * 128 - small.size)).reshape(small_rows, 128)
    grad_out = cotangent[0]
    gather_grads = gather_op(grad_out, ctx_size)
    if fused:
        gather_grads = gather_op(grad_out, ctx_size, row_half, tile_put, relative=True)
    *tables, small, tokens_all, grad_out_all = plane(
        ctx_size,
        1,
        tables_op(places.reshape(-1)),
        z_gather_op(small, fsdp_size),
        gather_op(tokens[0], ctx_size),
        gather_grads,
    )
    small = small.reshape(fsdp_size, small_rows * 128).astype(jnp.float32)
    gain_one, shift_one, gain_two, shift_two = (
        small[:, i * shard_rows : (i + 1) * shard_rows].reshape(1, width) for i in range(4)
    )
    bias_full = small[:, 4 * shard_rows : 4 * shard_rows + b_qkv.size]
    bias_full = bias_full.reshape(3, ctx_size, cols)
    bias_here = lax.dynamic_index_in_dim(bias_full, position, 1, keepdims=False)
    bias_here = bias_here.reshape(1, 3 * cols)
    out_full, projected, normed_t = plane(
        ctx_size,
        2,
        gather_op(
            qkv_here,
            ctx_size,
            functools.partial(last_strip, cols),
            functools.partial(column_strip, cols=cols),
            (width, width),
            pace=4,
        ),
        project_op(tokens_all, qkv_here, gain_one, shift_one, bias_here, tables),
    )
    tokens_in = tokens[0].astype(jnp.float32)
    unit_one, inverse_one = norm_rows(tokens_in, gain_one, shift_one)[1:]
    qkv_rows, attended, mixed_here, log_total = attend(
        projected.reshape(seq_rows, 3 * cols), order, lowest, starts, heads_here
    )
    mixed_here = mixed_here.reshape(ctx_size, rows_here, cols)
    mixed_rows, residual, normed_two_low = join_rows(
        mixed_here, out_full, tokens[0], gain_two, shift_two, 12
    )

    def blocks(rows):
        return rows.astype(jnp.bfloat16).reshape(ctx_size, rows_here, width)

    if fused:
        normed_two_t, both_value, hidden, grad_down_w = forward_mlp(
            normed_two_low, both_here, grad_out_all, hidden_here, 3
        )
        grad_normed_two, grad_both_w, layer_part = backward_mlp(
            grad_out_all, both_value, both_here, down_here, normed_two_t, hidden, 4
        )
    else:
        grad_out_all = grad_out_all.reshape(seq_rows, width)
        normed_two_all = plane(ctx_size, 3, gather_op(normed_two_low, ctx_size))
        normed_two_all = normed_two_all.reshape(seq_rows, width)
        both_value = times(normed_two_all, both_here)
        gate_value = jnp.concatenate(
            [both_value[:, :main], both_value[:, 2 * main : main + hidden_here]], 1
        )
        up_value = jnp.concatenate(
            [both_value[:, main : 2 * main], both_value[:, main + hidden_here :]], 1
        )
        sigmoid_gate = jax.nn.sigmoid(gate_value)
        silu_gate = gate_value * sigmoid_gate
        hidden = (silu_gate * up_value).astype(jnp.bfloat16)

        grad_down_w = inner(hidden, grad_out_all).astype(jnp.bfloat16)
        grad_hidden = times_transposed(after(grad_out_all, grad_down_w), down_here)
        grad_gate = grad_hidden * up_value * sigmoid_gate * (1.0 + gate_value * (1.0 - sigmoid_gate))
        grad_up = grad_hidden * silu_gate
        grad_both = jnp.concatenate(
            [grad_gate[:, :main], grad_up[:, :main], grad_gate[:, main:], grad_up[:, main:]], 1
        ).astype(jnp.bfloat16)
        grad_both_w = inner(normed_two_all, grad_both).astype(jnp.bfloat16)
        grad_normed_two = plane(
            ctx_size,
            4,
            scatter_op(blocks(times_transposed(after(grad_both, grad_both_w), both_here)), ctx_size),
        )
    grad_residual, grad_branch, norm_two_sums, grad_mixed = part_rows(
        grad_normed_two, residual, grad_out, gain_two, out_full, ctx_size, 5
    )

    def reduced(grad):
        return lax.psum_scatter(
            grad.astype(jnp.bfloat16), "fsdp", scatter_dimension=0, tiled=True
        )

    grad_down_w, grad_both_w = reduced(grad_down_w), reduced(grad_both_w)
    attend_op = attend_back_op(
        qkv_rows,
        grad_mixed.reshape(2 * ctx_size, half_rows, cols),
        attended,
        log_total,
        order,
        places[:, 0] // half_rows,
        starts,
        tables,
        normed_t,
        heads_here,
    )
    down_op = gather_op(grad_down_w, ctx_size, column_half, stacked_columns, pace=2)
    if fused:
        mixed_t = jnp.transpose(
            mixed_rows.reshape(rows_here, fsdp_size, ctx_size, out_piece), (2, 1, 3, 0)
        ).reshape(ctx_size, fsdp_size * out_piece, rows_here)
        out_op = produce_op(
            product_of_columns,
            rows_here,
            width,
            mixed_t,
            grad_branch,
            batch=2,
            late=5,
            kind=jnp.bfloat16,
        )
    else:
        mixed_blocks = jnp.transpose(
            mixed_rows.reshape(rows_here, fsdp_size, ctx_size, out_piece), (0, 2, 1, 3)
        ).reshape(rows_here, width)
        out_op = scatter_op(
            inner(mixed_blocks, grad_branch)
            .astype(jnp.bfloat16)
            .reshape(ctx_size, fsdp_size * out_piece, width),
            ctx_size,
        )
    if fused:
        grad_down_w, grad_out_w, grad_projected, grad_bias, grad_qkv_w = plane(
            ctx_size, 6, down_op, out_op, attend_op
        )
    else:
        grad_projected, grad_bias, grad_qkv_w = plane(ctx_size, 6, attend_op)
        grad_down_w, grad_out_w = plane(ctx_size, 7, down_op, out_op)
        layer_part = plane(ctx_size, 10, scatter_op(blocks(times(hidden, down_here)), ctx_size))
    if fused:
        grad_both_w, grad_tokens, norm_one_sums = plane(
            ctx_size,
            8,
            gather_op(grad_both_w, ctx_size, pace=3),
            norm_produce_op(
                product_of_rows,
                grad_projected.reshape(ctx_size, rows_here, 3 * cols),
                qkv_here,
                tokens[0],
                grad_residual,
                gain_one,
            ),
        )
    else:
        grad_both_w, grad_normed = plane_groups(
            ctx_size,
            8,
            gather_op(grad_both_w, ctx_size),
            scatter_op(
                blocks(times_transposed(grad_projected, qkv_here[:, : 3 * cols])), ctx_size
            ),
        )
        grad_tokens = grad_residual + norm_back(grad_normed, unit_one, inverse_one, gain_one)
        norm_one_sums = jnp.stack([jnp.sum(grad_normed * unit_one, 0), jnp.sum(grad_normed, 0)])
    layer_out = residual + layer_part
    grad_qkv_w = reduced(grad_qkv_w)
    grad_out_w = reduced(grad_out_w)

    norm_sums = jnp.concatenate([norm_one_sums, norm_two_sums])
    norm_sums = jnp.transpose(norm_sums.reshape(4, fsdp_size, shard_rows), (1, 0, 2)).reshape(
        fsdp_size, 1, 4 * shard_rows
    )
    bias_sums = lax.dynamic_update_slice(
        jnp.zeros((3, ctx_size, cols), jnp.float32),
        grad_bias.reshape(3, 1, cols),
        (0, position, 0),
    ).reshape(fsdp_size, 1, 3 * width // fsdp_size)
    sums = jnp.concatenate(
        [
            jnp.pad(rows, ((0, 0), (0, extra), (0, width - rows.shape[2])))
            for rows, extra in ((norm_sums, 0), (bias_sums, 6))
        ],
        1,
    )
    grad_qkv_w, grad_out_w, sums = plane(
        ctx_size,
        13,
        gather_op(grad_qkv_w, ctx_size, pace=2),
        gather_op(grad_out_w, ctx_size, column_half, stacked_columns, pace=2),
        z_sum_gather_op(sums, fsdp_size, ctx_size),
    )
    sums = jnp.sum(sums, 0)
    norm_sums = sums[0, : 4 * shard_rows].reshape(4, shard_rows)
    bias_sums = sums[1, : b_qkv.shape[0]]
    grad_out_w = unpack_rows(grad_out_w, out_piece)
    grad_gate_w, grad_up_w = unpack_both(grad_both_w, fsdp_size)
    float32 = jnp.float32
    return (
        layer_out.astype(jnp.bfloat16)[None],
        grad_tokens[None],
        norm_sums[0],
        norm_sums[1],
        unpack_columns(grad_qkv_w, 3),
        bias_sums,
        grad_out_w,
        norm_sums[2],
        norm_sums[3],
        grad_gate_w,
        grad_up_w,
        unpack_rows(grad_down_w, strip),
    )


def solution(mesh):
    placed = (
        P("fsdp", "ctx", None),
        P("fsdp", None),
        P(),
        P("fsdp"),
        P("fsdp"),
        P("fsdp", None),
        P("fsdp"),
        P("fsdp", None),
        P("fsdp"),
        P("fsdp"),
        P("fsdp", None),
        P("fsdp", None),
        P("fsdp", None),
        P("fsdp", "ctx", None),
    )
    return jax.shard_map(
        body,
        mesh=mesh,
        in_specs=placed,
        out_specs=(
            P("fsdp", "ctx", None),
            P("fsdp", "ctx", None),
            P("fsdp"),
            P("fsdp"),
            P("fsdp", None),
            P("fsdp"),
            P("fsdp", None),
            P("fsdp"),
            P("fsdp"),
            P("fsdp", None),
            P("fsdp", None),
            P("fsdp", None),
        ),
        check_vma=False,
    )
```

```python
import functools

import jax
import jax.numpy as jnp
from jax import lax
from jax.experimental import pallas as pl
from jax.experimental.pallas import tpu as pltpu
from jax.sharding import PartitionSpec as P

HEAD = 64
ROT = 16


NORM_EPSILON = 1e-05
ROTARY_BASE = 10000.0
MASKED_SCORE = -1e30


MESH_IDS = pl.DeviceIdType.MESH


def bit_of(index, bit):
    return index // (1 << bit) % 2


def flipped(index, mask, bits):
    result = index
    for bit in range(bits):
        if mask >> bit & 1:
            result = result + (1 - 2 * bit_of(index, bit)) * (1 << bit)
    return result


def greet(partners, along_z=()):
    barrier = pltpu.get_barrier_semaphore()
    for axis, others in (("ctx", partners), ("fsdp", along_z)):
        for other in others:
            pl.semaphore_signal(barrier, inc=1, device_id={axis: other}, device_id_type=MESH_IDS)
    pl.semaphore_wait(barrier, len(partners) + len(along_z))


def half_orders(bits):
    chip_bits = list(range(1, bits))
    return [chip_bits, chip_bits[1:] + chip_bits[:1]]


def gather_plan(bits):
    steps = []
    for order in half_orders(bits):
        held = [0]
        plan = []
        for bit in order:
            plan.append((bit, list(held)))
            held = held + [mask | 1 << bit for mask in held]
        steps.append((plan, held))
    return steps


def column_half(ref, half):
    width = ref.shape[-1] // 2
    return ref.at[..., pl.ds(half * width, width)]


def row_half(ref, half):
    rows = ref.shape[-2] // 2
    if len(ref.shape) == 2:
        return ref.at[pl.ds(half * rows, rows)]
    return ref.at[..., pl.ds(half * rows, rows), :]


def stacked_rows(ref, block, half):
    return row_half(ref.at[block], half)


def stacked_columns(ref, block, half):
    return column_half(ref.at[block], half)


def column_strip(ref, block, half, cols):
    rows = ref.shape[0] // 2
    at = block * cols if isinstance(block, int) else pl.multiple_of(block * cols, cols)
    return ref.at[pl.ds(half * rows, rows), pl.ds(at, cols)]


def last_strip(cols, ref, half):
    return column_strip(ref, ref.shape[1] // cols - 1, half, cols)


def block_view(ref, block):
    return ref.at[block]


def column_view(ref, block, width):
    return ref.at[:, pl.ds(pl.multiple_of(block * width, width), width)]


def gather_run(
    bits, take, put, relative, pace, source, out, send_sem, recv_sem, core_send, core_recv, local_sem
):
    me = lax.axis_index("ctx")
    steps = gather_plan(bits)
    finals = []
    for half in range(2):
        own = put(out, 0 if relative else me, half)
        copy = pltpu.make_async_copy(take(source, half), own, local_sem.at[half])
        copy.start()
        finals.append(copy.wait)

    def push(half, mask, bit, send, recv, index):
        block = mask if relative else flipped(me, mask, bits)
        there = mask | 1 << bit if relative else block
        copy = pltpu.make_async_remote_copy(
            src_ref=take(source, half) if mask == 0 else put(out, block, half),
            dst_ref=put(out, there, half),
            send_sem=send.at[half, index],
            recv_sem=recv.at[half, index],
            device_id={"ctx": flipped(me, 1 << bit, bits)},
            device_id_type=MESH_IDS,
        )
        copy.start()
        return copy

    def hop(half, phase, mask):
        bit, masks = steps[half][0][phase]
        index = (1 << phase) - 1 + masks.index(mask)
        copy = push(half, mask, bit, send_sem, recv_sem, index)
        finals.append(copy.wait_send)
        arriving[half, mask | 1 << bit] = copy

    def to_core(half, mask):
        copy = push(half, mask, 0, core_send, core_recv, steps[half][1].index(mask))
        finals.append(copy.wait)

    arriving = {}
    phases = bits - 1
    for phase in range(phases):
        for half in range(2):
            hop(half, phase, 0)
    for half in range(2):
        to_core(half, 0)
    for _ in range(pace):
        yield
    for phase in range(phases):
        for half in range(2):
            bit, masks = steps[half][0][phase]
            for mask in masks:
                arrived = mask | 1 << bit
                arriving[half, arrived].wait_recv()
                for later in range(phase + 1, phases):
                    hop(half, later, arrived)
                to_core(half, arrived)
        for _ in range(pace):
            yield
    for wait in finals:
        wait()


def gather_op(
    x, size, take=row_half, put=stacked_rows, out_shape=None, relative=False, pace=1
):
    bits = size.bit_length() - 1
    steps = size // 2 - 1
    dma = pltpu.SemaphoreType.DMA
    return dict(
        run=functools.partial(gather_run, bits, take, put, relative, pace),
        inputs=[x],
        in_space=pl.ANY,
        outs=[jax.ShapeDtypeStruct(out_shape or (size,) + x.shape, x.dtype)],
        out_space=pl.ANY,
        scratch=[dma((2, steps)), dma((2, steps)), dma((2, steps + 1)), dma((2, steps + 1)), dma((2,))],
        moved=2 * size * x.size * 2,
    )


def add_into(target, first, second, rows, step):
    @pl.loop(0, rows // step)
    def _(i):
        at = pl.ds(pl.multiple_of(i * step, step), step)
        target[at] = first[at].astype(target.dtype) + second[at].astype(target.dtype)


def scatter_plan(bits):
    plans = []
    for order in half_orders(bits):
        kept = [mask << 1 for mask in range(1 << (bits - 1))]
        plan = []
        for bit in order:
            plan.append((bit, [mask for mask in kept if mask >> bit & 1]))
            kept = [mask for mask in kept if not mask >> bit & 1]
        plans.append(plan)
    return plans


def farthest_first(masks):
    return sorted(masks, key=lambda mask: -bin(mask).count("1"))


def scatter_run(bits, step, part_ref, out_ref, core_buf, chip_buf, core_send, core_recv, send_sem, recv_sem):
    me = lax.axis_index("ctx")
    rows = part_ref.shape[1]
    width = part_ref.shape[2] // 2
    plans = scatter_plan(bits)
    chip_masks = farthest_first([mask << 1 for mask in range(1 << (bits - 1))])
    finals = []
    core_copies = {}
    for mask in chip_masks:
        copy = pltpu.make_async_remote_copy(
            src_ref=part_ref.at[flipped(me, mask | 1, bits)],
            dst_ref=core_buf.at[mask >> 1],
            send_sem=core_send.at[mask >> 1],
            recv_sem=core_recv.at[mask >> 1],
            device_id={"ctx": flipped(me, 1, bits)},
            device_id_type=MESH_IDS,
        )
        copy.start()
        core_copies[mask] = copy
        finals.append(copy.wait_send)
    arriving = {}

    def columns(half):
        return pl.ds(half * width, width)

    def send(half, phase, bit, mask):
        slot = plans[half][phase][1].index(mask)
        copy = pltpu.make_async_remote_copy(
            src_ref=part_ref.at[flipped(me, mask, bits), :, columns(half)],
            dst_ref=chip_buf.at[half, phase, slot],
            send_sem=send_sem.at[half, phase, slot],
            recv_sem=recv_sem.at[half, phase, slot],
            device_id={"ctx": flipped(me, 1 << bit, bits)},
            device_id_type=MESH_IDS,
        )
        copy.start()
        finals.append(copy.wait_send)
        arriving[half, phase, mask & ~(1 << bit)] = (copy, slot)

    yield
    for mask in chip_masks:
        core_copies[mask].wait_recv()
        here = part_ref.at[flipped(me, mask, bits)]
        add_into(here, here, core_buf.at[mask >> 1], rows, step)
        for half in range(2):
            bit, masks = plans[half][0]
            if mask in masks:
                send(half, 0, bit, mask)
    yield
    phases = bits - 1
    for phase in range(1, phases + 1):
        for half in range(2):
            last_bit, last_masks = plans[half][phase - 1]
            kept = farthest_first([mask & ~(1 << last_bit) for mask in last_masks])
            for mask in kept:
                copy, slot = arriving[half, phase - 1, mask]
                copy.wait_recv()
                here = part_ref.at[flipped(me, mask, bits), :, columns(half)]
                buf = chip_buf.at[half, phase - 1, slot]
                if phase < phases:
                    add_into(here, here, buf, rows, step)
                    bit, masks = plans[half][phase]
                    if mask in masks:
                        send(half, phase, bit, mask)
                else:
                    add_into(out_ref.at[:, columns(half)], here, buf, rows, step)
        yield
    for wait in finals:
        wait()


def scatter_op(part, size):
    bits = size.bit_length() - 1
    chips = size // 2
    rows, width = part.shape[1:]
    dma = pltpu.SemaphoreType.DMA
    return dict(
        run=functools.partial(scatter_run, bits, 32),
        inputs=[part],
        in_space=pltpu.VMEM,
        outs=[jax.ShapeDtypeStruct((rows, width), jnp.float32)],
        out_space=pltpu.VMEM,
        scratch=[
            pltpu.VMEM((chips, rows, width), part.dtype),
            pltpu.VMEM((2, bits - 1, chips // 2, rows, width // 2), part.dtype),
            dma((chips,)),
            dma((chips,)),
            dma((2, bits - 1, chips // 2)),
            dma((2, bits - 1, chips // 2)),
        ],
        moved=4 * part.size,
    )


def exchange_run(size, take, put, source, out, send_sem, recv_sem, local_sem):
    me = lax.axis_index("ctx")
    local = pltpu.make_async_copy(take(source, me), put(out, me), local_sem)
    local.start()
    copies = []
    for step in range(1, size):
        other = lax.rem(me + step, size)
        copy = pltpu.make_async_remote_copy(
            src_ref=take(source, other),
            dst_ref=put(out, me),
            send_sem=send_sem.at[step - 1],
            recv_sem=recv_sem.at[step - 1],
            device_id={"ctx": other},
            device_id_type=MESH_IDS,
        )
        copy.start()
        copies.append(copy)
    yield
    local.wait()
    for copy in copies:
        copy.wait()


def exchange_op(x, size, out_shape, take, put):
    dma = pltpu.SemaphoreType.DMA
    return dict(
        run=functools.partial(exchange_run, size, take, put),
        inputs=[x],
        in_space=pl.ANY,
        outs=[jax.ShapeDtypeStruct(out_shape, x.dtype)],
        out_space=pl.ANY,
        scratch=[dma((size - 1,)), dma((size - 1,)), dma],
        far=True,
        moved=4 * x.size,
    )


def z_gather_run(size, source, out, send_sem, recv_sem, local_sem):
    me = lax.axis_index("fsdp")
    local = pltpu.make_async_copy(source, out.at[me], local_sem)
    local.start()
    copies = []
    for step in range(1, size):
        copy = pltpu.make_async_remote_copy(
            src_ref=source,
            dst_ref=out.at[me],
            send_sem=send_sem.at[step - 1],
            recv_sem=recv_sem.at[step - 1],
            device_id={"fsdp": lax.rem(me + step, size)},
            device_id_type=MESH_IDS,
        )
        copy.start()
        copies.append(copy)
    for _ in range(4):
        yield
    local.wait()
    for copy in copies:
        copy.wait()


def z_gather_op(x, size):
    dma = pltpu.SemaphoreType.DMA
    return dict(
        run=functools.partial(z_gather_run, size),
        inputs=[x],
        in_space=pl.ANY,
        outs=[jax.ShapeDtypeStruct((size,) + x.shape, x.dtype)],
        out_space=pl.ANY,
        scratch=[dma((size - 1,)), dma((size - 1,)), dma],
        z=size,
        moved=2 * size * x.size,
    )


def z_scatter_run(size, source, out, buf, send_sem, recv_sem):
    me = lax.axis_index("fsdp")
    copies = []
    for step in range(1, size):
        other = lax.rem(me + step, size)
        copy = pltpu.make_async_remote_copy(
            src_ref=source.at[other],
            dst_ref=buf.at[step - 1],
            send_sem=send_sem.at[step - 1],
            recv_sem=recv_sem.at[step - 1],
            device_id={"fsdp": other},
            device_id_type=MESH_IDS,
        )
        copy.start()
        copies.append(copy)
    for _ in range(4):
        yield
    total = source[me].astype(jnp.float32)
    for step, copy in enumerate(copies):
        copy.wait()
        total += buf[step].astype(jnp.float32)
    out[...] = total.astype(out.dtype)


def z_scatter_op(x, size):
    dma = pltpu.SemaphoreType.DMA
    return dict(
        run=functools.partial(z_scatter_run, size),
        inputs=[x],
        in_space=pltpu.VMEM,
        outs=[jax.ShapeDtypeStruct(x.shape[1:], x.dtype)],
        out_space=pltpu.VMEM,
        scratch=[
            pltpu.VMEM((size - 1,) + x.shape[1:], x.dtype),
            dma((size - 1,)),
            dma((size - 1,)),
        ],
        z=size,
        moved=4 * x.size,
    )


def z_sum_gather_run(bits, size, source, out, low, buf, send_sem, recv_sem, *sems):
    yield from z_scatter_run(size, source, low, buf, send_sem, recv_sem)
    yield from gather_run(bits, column_half, stacked_columns, False, 1, low, out, *sems)


def z_sum_gather_op(x, z_size, size):
    summed = z_scatter_op(x, z_size)
    (shape,) = summed["outs"]
    gather = gather_op(shape, size)
    return dict(
        run=functools.partial(z_sum_gather_run, size.bit_length() - 1, z_size),
        inputs=[x],
        in_space=pltpu.VMEM,
        outs=gather["outs"],
        out_space=pl.ANY,
        scratch=[pltpu.VMEM(shape.shape, shape.dtype)] + summed["scratch"] + gather["scratch"],
        z=z_size,
        moved=summed["moved"] + gather["moved"],
    )


def project_run(
    cols,
    tokens,
    weights,
    gain,
    shift,
    bias,
    cosine,
    sine_low,
    sine_high,
    qkv,
    normed,
    tokens_buf,
    normed_buf,
    weights_buf,
    load_sem,
    store_sem,
    weights_sem,
):
    size, rows = tokens.shape[:2]

    def load(block):
        slot = block % 2
        return pltpu.make_async_copy(tokens.at[block], tokens_buf.at[slot], load_sem.at[slot])

    def store(block):
        slot = block % 2
        at = pl.ds(block * rows, rows)
        return pltpu.make_async_copy(normed_buf.at[slot], normed.at[:, at], store_sem.at[slot])

    load_weights = pltpu.make_async_copy(
        weights.at[:, pl.ds(0, 3 * cols)], weights_buf, weights_sem
    )
    load(0).start()
    load_weights.start()
    yield
    for block in range(size):
        if block + 1 < size:
            load(block + 1).start()
        load(block).wait()
        at = pl.ds(block * rows, rows)
        values = tokens_buf[block % 2].astype(jnp.float32)
        centered = values - jnp.mean(values, -1, keepdims=True)
        inverse = lax.rsqrt(jnp.mean(centered * centered, -1, keepdims=True) + NORM_EPSILON)
        low = (centered * inverse * gain[...] + shift[...]).astype(jnp.bfloat16)
        if block >= 2:
            store(block - 2).wait()
        normed_buf[block % 2] = jnp.transpose(low)
        store(block).start()
        if block == 0:
            load_weights.wait()
        projected = jnp.dot(low, weights_buf[...], preferred_element_type=jnp.float32)
        projected += bias[...]
        tables = (cosine[at], sine_low[at], sine_high[at])
        query = turn(projected[:, :cols], *tables, cols) * HEAD ** (-0.5)
        qkv[block, :, :cols] = query.astype(jnp.bfloat16)
        key = turn(projected[:, cols : 2 * cols], *tables, cols)
        qkv[block, :, cols : 2 * cols] = key.astype(jnp.bfloat16)
        qkv[block, :, 2 * cols :] = projected[:, 2 * cols :].astype(jnp.bfloat16)
        yield
    store(size - 2).wait()
    store(size - 1).wait()


def project_op(tokens, weights, gain, shift, bias, tables):
    size, rows, width = tokens.shape
    wide = bias.shape[1]
    low = jnp.bfloat16
    dma = pltpu.SemaphoreType.DMA
    return dict(
        run=functools.partial(project_run, wide // 3),
        inputs=[tokens, weights, gain, shift, bias, *tables],
        in_spaces=[pl.ANY] * 2 + [pltpu.VMEM] * 6,
        outs=[
            jax.ShapeDtypeStruct((size, rows, wide), low),
            jax.ShapeDtypeStruct((width, size * rows), low),
        ],
        out_spaces=[pltpu.VMEM, pl.ANY],
        scratch=[
            pltpu.VMEM((2, rows, width), low),
            pltpu.VMEM((2, width, rows), low),
            pltpu.VMEM((width, wide), low),
            dma((2,)),
            dma((2,)),
            dma,
        ],
        moved=4 * tokens.size,
    )


def plane_kernel(size, parts, far, z_size, *refs):
    bits = size.bit_length() - 1
    me = lax.axis_index("ctx")
    my_z = lax.axis_index("fsdp")
    partners = [flipped(me, 1 << bit, bits) for bit in range(bits)]
    if far:
        partners = [lax.rem(me + step, size) for step in range(1, size)]
    greet(partners, [lax.rem(my_z + step, z_size) for step in range(1, z_size)])
    ins = sum(part[1] for part in parts)
    outs = sum(part[2] for part in parts)
    groups = [list(refs[:ins]), list(refs[ins : ins + outs]), list(refs[ins + outs :])]
    running = []
    for run, *counts in parts:
        own = []
        for group, count in zip(groups, counts):
            own += group[:count]
            del group[:count]
        running.append(run(*own))
    while running:
        running = [turn_of for turn_of in running if next(turn_of, 1) is None]


def spaces(op, side):
    arrays = op["inputs"] if side == "in" else op["outs"]
    return op.get(side + "_spaces") or [op[side + "_space"]] * len(arrays)


def plane(size, collective_id, *ops):
    parts = [(op["run"], len(op["inputs"]), len(op["outs"]), len(op["scratch"])) for op in ops]
    far = any(op.get("far") for op in ops)
    z_size = max(op.get("z", 1) for op in ops)
    results = pl.pallas_call(
        functools.partial(plane_kernel, size, parts, far, z_size),
        out_shape=[out for op in ops for out in op["outs"]],
        in_specs=[pl.BlockSpec(memory_space=space) for op in ops for space in spaces(op, "in")],
        out_specs=[pl.BlockSpec(memory_space=space) for op in ops for space in spaces(op, "out")],
        scratch_shapes=[scratch for op in ops for scratch in op["scratch"]],
        compiler_params=pltpu.CompilerParams(
            collective_id=collective_id, has_side_effects=True, vmem_limit_bytes=60 << 20
        ),
        cost_estimate=pl.CostEstimate(
            flops=0, bytes_accessed=sum(op["moved"] for op in ops), transcendentals=0
        ),
    )(*[x for op in ops for x in op["inputs"]])
    return results if len(results) > 1 else results[0]


def plane_groups(size, collective_id, *ops):
    groups = []
    room = 0
    for op in ops:
        need = 0 if op.get("in_space") == pl.ANY else op["moved"] * 5 // 4
        if not groups or need > room:
            groups.append([])
            room = 52 << 20
        groups[-1].append(op)
        room -= need
    results = []
    for i, group in enumerate(groups):
        got = plane(size, collective_id + i, *group)
        results += got if isinstance(got, (list, tuple)) else [got]
    return results


def swapped(tile):
    return tile % 2 + 2 * (tile // 4 % 2) + 4 * (tile // 2 % 2)


def tile_put(ref, mask, half):
    return row_half(ref.at[mask if half == 0 else swapped(mask)], half)


def tile_partner(me, bit):
    return {"ctx": flipped(me, 1 << bit, 3)}


def tile_copy(source, target, half, bit, me, send_sem, recv_sem):
    rows = source.shape[0] // 2
    at = pl.ds(half * rows, rows)
    return pltpu.make_async_remote_copy(
        src_ref=source.at[at],
        dst_ref=target.at[at],
        send_sem=send_sem.at[half],
        recv_sem=recv_sem.at[half],
        device_id=tile_partner(me, bit),
        device_id_type=MESH_IDS,
    )


def core_copy(source, target, me, send_sem, recv_sem):
    return pltpu.make_async_remote_copy(
        src_ref=source,
        dst_ref=target,
        send_sem=send_sem,
        recv_sem=recv_sem,
        device_id=tile_partner(me, 0),
        device_id_type=MESH_IDS,
    )


class TileGather:
    def __init__(self, tiles, send_sem, recv_sem, core_send, core_recv):
        me = lax.axis_index("ctx")
        self.hops = {
            target: [
                tile_copy(
                    tiles.at[source],
                    tiles.at[target],
                    half,
                    (first, 3 - first)[half],
                    me,
                    send_sem.at[target // 2 - 1],
                    recv_sem.at[target // 2 - 1],
                )
                for half in range(2)
            ]
            for source, target, first in ((0, 2, 1), (0, 4, 2), (2, 6, 2))
        }
        self.cores = [
            core_copy(tiles.at[2 * i], tiles.at[2 * i + 1], me, core_send.at[i], core_recv.at[i])
            for i in range(4)
        ]

    def before(self, tile):
        if tile == 0:
            for copy in self.hops[2]:
                copy.start()
            self.cores[0].start()
        elif tile % 2 == 1:
            self.cores[tile // 2].wait_recv()
            if tile == 1:
                for copy in self.hops[4]:
                    copy.start()
        else:
            for copy in self.hops[tile]:
                copy.wait_recv()
            if tile == 2:
                for copy in self.hops[6]:
                    copy.start()
            self.cores[tile // 2].start()

    def finish(self):
        for copies in self.hops.values():
            for copy in copies:
                copy.wait_send()
        for copy in self.cores:
            copy.wait_send()


def gather_sems():
    dma = pltpu.SemaphoreType.DMA
    return [dma((3, 2)), dma((3, 2)), dma((4,)), dma((4,))]


def part_slot(tile):
    odd = tile % 2
    return (1 - odd) * (tile // 2) + odd * (5 - tile // 4)


SCATTER_ORDER = (7, 6, 3, 2, 5, 4, 1, 0)


class TileScatter:
    def __init__(self, parts, core_buf, chip_buf, send_sem, recv_sem, core_send, core_recv):
        me = lax.axis_index("ctx")
        self.parts, self.core_buf, self.chip_buf = parts, core_buf, chip_buf
        self.hops = {
            source: [
                tile_copy(
                    parts.at[part_slot(source)],
                    chip_buf.at[source // 2 - 1],
                    half,
                    (first, 3 - first)[half],
                    me,
                    send_sem.at[source // 2 - 1],
                    recv_sem.at[source // 2 - 1],
                )
                for half in range(2)
            ]
            for source, first in ((6, 1), (4, 2), (2, 1))
        }
        self.cores = [
            core_copy(
                parts.at[part_slot(2 * i + 1)],
                core_buf.at[i],
                me,
                core_send.at[i],
                core_recv.at[i],
            )
            for i in range(4)
        ]

    def add(self, tile, buf):
        here = self.parts.at[part_slot(tile)]
        add_into(here, here, buf, here.shape[0], 32)

    def before(self, tile):
        if tile in (5, 1):
            self.cores[tile // 2 + 1].wait_send()

    def after(self, tile):
        if tile % 2 == 1:
            self.cores[tile // 2].start()
        else:
            self.settle(tile)

    def settle(self, tile):
        self.cores[tile // 2].wait_recv()
        self.add(tile, self.core_buf.at[tile // 2])
        if tile == 6 or tile == 2:
            for copy in self.hops[tile]:
                copy.start()
        if tile == 4:
            for copy in self.hops[6]:
                copy.wait_recv()
            self.add(4, self.chip_buf.at[2])
            for copy in self.hops[4]:
                copy.start()

    def finish(self, out):
        for tile in (2, 4):
            for copy in self.hops[tile]:
                copy.wait_recv()
        rows = out.shape[0]

        @pl.loop(0, rows // 32)
        def _(i):
            at = pl.ds(pl.multiple_of(i * 32, 32), 32)
            out[at] = (
                self.parts[0, at].astype(jnp.float32)
                + self.chip_buf[0, at].astype(jnp.float32)
                + self.chip_buf[1, at].astype(jnp.float32)
            ).astype(out.dtype)

        for copies in self.hops.values():
            for copy in copies:
                copy.wait_send()
        for tile in (4, 0):
            self.cores[tile // 2].wait_send()


def scatter_scratch(rows, width):
    return [
        pltpu.VMEM((6, rows, width), jnp.bfloat16),
        pltpu.VMEM((4, rows, width), jnp.bfloat16),
        pltpu.VMEM((3, rows, width), jnp.bfloat16),
    ] + gather_sems()


def produce_run(produce, batch, late, count, *refs):
    inputs, (out, *scratch) = refs[:count], refs[count:]
    me = lax.axis_index("ctx")
    scatter = TileScatter(*scratch)
    last = None
    for tile in SCATTER_ORDER:
        scatter.before(tile)
        scatter.parts[part_slot(tile)] = produce(inputs, tile, me).astype(jnp.bfloat16)
        if tile % 2 == 1:
            scatter.after(tile)
            if batch == 1 and last is not None:
                scatter.settle(last)
        last = tile
        if tile % batch == 0:
            yield
            if batch > 1:
                scatter.settle(tile)
    if batch == 1:
        scatter.settle(0)
    for _ in range(late):
        yield
    scatter.finish(out)


def produce_op(produce, rows, width, *inputs, batch=1, late=0, kind=jnp.float32):
    return dict(
        run=functools.partial(produce_run, produce, batch, late, len(inputs)),
        inputs=list(inputs),
        in_space=pltpu.VMEM,
        outs=[jax.ShapeDtypeStruct((rows, width), kind)],
        out_space=pltpu.VMEM,
        scratch=scatter_scratch(rows, width),
        moved=32 * rows * width,
    )


def norm_produce_run(produce, *refs):
    grads, weights, tokens, grad_residual, gain, grad_tokens, sums, grad_normed, *scratch = refs
    yield from produce_run(produce, 1, 0, 2, grads, weights, grad_normed, *scratch)
    sums[...] = jnp.zeros_like(sums)
    chunk = 32

    @pl.loop(0, tokens.shape[0] // chunk)
    def _(i):
        at = pl.ds(pl.multiple_of(i * chunk, chunk), chunk)
        unit, inverse = centre(tokens[at].astype(jnp.float32))
        rows = grad_normed[at]
        sums[...] += two_rows(
            jnp.sum(rows * unit, 0, keepdims=True), jnp.sum(rows, 0, keepdims=True)
        )
        scaled = rows * gain[...]
        grad_tokens[at] = grad_residual[at] + inverse * (
            scaled
            - jnp.mean(scaled, -1, keepdims=True)
            - unit * jnp.mean(scaled * unit, -1, keepdims=True)
        )


def norm_produce_op(produce, grads, weights, tokens, grad_residual, gain):
    rows, width = tokens.shape
    return dict(
        run=functools.partial(norm_produce_run, produce),
        inputs=[grads, weights, tokens, grad_residual, gain],
        in_space=pltpu.VMEM,
        outs=[
            jax.ShapeDtypeStruct((rows, width), jnp.float32),
            jax.ShapeDtypeStruct((2, width), jnp.float32),
        ],
        out_space=pltpu.VMEM,
        scratch=[pltpu.VMEM((rows, width), jnp.float32)] + scatter_scratch(rows, width),
        moved=32 * rows * width,
    )


def tile_rows(ref, tile, me):
    half = ref.shape[1] // 2
    return jnp.concatenate(
        [ref[flipped(me, tile, 3), :half], ref[flipped(me, swapped(tile), 3), half:]], 0
    )


def product_of_rows(refs, tile, me):
    rows = tile_rows(refs[0], tile, me)
    return times_transposed(rows, refs[1][:, : rows.shape[1]])


def product_of_columns(refs, tile, me):
    return jnp.dot(
        tile_rows(refs[0], tile, me), refs[1][...], preferred_element_type=jnp.float32
    )


def unpack_both_kernel(segments, count, source, gate, up):
    hidden_size = source.shape[2] // 2
    main = hidden_size // 128 * 128
    strip = hidden_size // segments
    for out, first, last in ((gate, 0, 2 * main), (up, main, main + hidden_size)):
        owners = [
            jnp.concatenate(
                [
                    source[owner, :, first : first + main],
                    source[owner, :, last : last + hidden_size - main],
                ],
                1,
            )
            for owner in range(count)
        ]
        out[...] = jnp.concatenate(
            [
                rows[:, segment * strip : (segment + 1) * strip]
                for segment in range(segments)
                for rows in owners
            ],
            1,
        ).astype(jnp.float32)


def unpack_both(gathered, segments):
    count, rows, width = gathered.shape
    step = min(128, rows)
    block = pl.BlockSpec((step, count * width // 2), lambda i: (i, 0))
    return pl.pallas_call(
        functools.partial(unpack_both_kernel, segments, count),
        grid=(rows // step,),
        in_specs=[pl.BlockSpec((count, step, width), lambda i: (0, i, 0))],
        out_specs=[block, block],
        out_shape=[jax.ShapeDtypeStruct((rows, count * width // 2), jnp.float32)] * 2,
        compiler_params=pltpu.CompilerParams(vmem_limit_bytes=60 << 20),
        cost_estimate=pl.CostEstimate(
            flops=0, bytes_accessed=6 * gathered.size, transcendentals=0
        ),
    )(gathered)


def greet_near(size):
    me = lax.axis_index("ctx")
    bits = size.bit_length() - 1
    greet([flipped(me, 1 << bit, bits) for bit in range(bits)])


def two_rows(first, second):
    row = lax.broadcasted_iota(jnp.int32, (2, first.shape[1]), 0)
    return jnp.where(row == 0, first, second)


def centre(values):
    centered = values - jnp.mean(values, -1, keepdims=True)
    inverse = lax.rsqrt(jnp.mean(centered * centered, -1, keepdims=True) + NORM_EPSILON)
    return centered * inverse, inverse


def join_kernel(
    size,
    mixed,
    weights,
    tokens,
    gain,
    shift,
    mixed_rows,
    residual,
    normed,
    weights_buf,
    load_sem,
    send_sem,
    recv_sem,
    local_sem,
):
    me = lax.axis_index("ctx")
    cols = mixed.shape[2]

    def load(owner):
        at = pl.ds(pl.multiple_of(owner * cols, cols), cols)
        return pltpu.make_async_copy(weights.at[at], weights_buf.at[at], load_sem.at[owner])

    others = [lax.rem(me + step, size) for step in range(size)]
    for step in range(size):
        load(lax.rem(me + size - step, size)).start()
    greet(others[1:])
    here = column_view(mixed_rows, me, cols)
    local = pltpu.make_async_copy(mixed.at[me], here, local_sem)
    local.start()
    copies = []
    for step in range(1, size):
        copy = pltpu.make_async_remote_copy(
            src_ref=mixed.at[others[step]],
            dst_ref=here,
            send_sem=send_sem.at[step - 1],
            recv_sem=recv_sem.at[step - 1],
            device_id={"ctx": others[step]},
            device_id_type=MESH_IDS,
        )
        copy.start()
        copies.append(copy)
    local.wait()
    residual[...] = tokens[...].astype(jnp.float32)
    for step in range(size):
        owner = lax.rem(me + size - step, size)
        if step > 0:
            copies[step - 1].wait_recv()
        load(owner).wait()
        at = pl.ds(pl.multiple_of(owner * cols, cols), cols)
        residual[...] += jnp.dot(
            mixed_rows[:, at], weights_buf[at], preferred_element_type=jnp.float32
        )
    unit = centre(residual[...])[0]
    normed[...] = (unit * gain[...] + shift[...]).astype(jnp.bfloat16)
    for copy in copies:
        copy.wait_send()


def join_rows(mixed, weights, tokens, gain, shift, collective_id):
    size, rows, cols = mixed.shape
    width = size * cols
    vmem = pl.BlockSpec(memory_space=pltpu.VMEM)
    any_space = pl.BlockSpec(memory_space=pl.ANY)
    low = jnp.bfloat16
    dma = pltpu.SemaphoreType.DMA
    return pl.pallas_call(
        functools.partial(join_kernel, size),
        in_specs=[any_space] * 2 + [vmem] * 3,
        out_specs=[vmem] * 3,
        out_shape=[
            jax.ShapeDtypeStruct((rows, width), low),
            jax.ShapeDtypeStruct((rows, width), jnp.float32),
            jax.ShapeDtypeStruct((rows, width), low),
        ],
        scratch_shapes=[
            pltpu.VMEM((width, width), low),
            dma((size,)),
            dma((size - 1,)),
            dma((size - 1,)),
            dma,
        ],
        compiler_params=pltpu.CompilerParams(
            collective_id=collective_id, has_side_effects=True, vmem_limit_bytes=60 << 20
        ),
        cost_estimate=pl.CostEstimate(
            flops=2 * rows * width * width, bytes_accessed=2 * width * width, transcendentals=0
        ),
    )(mixed, weights, tokens, gain, shift)


def part_kernel(
    size,
    grad_normed,
    residual,
    cotangent,
    gain,
    weights,
    grad_residual,
    grad_branch,
    sums,
    grad_mixed,
    weights_buf,
    staged,
    load_sem,
    send_sem,
    recv_sem,
    local_sem,
):
    me = lax.axis_index("ctx")
    cols = staged.shape[2]
    others = [lax.rem(me + step, size) for step in range(size)]

    def load(owner):
        at = pl.ds(pl.multiple_of(owner * cols, cols), cols)
        return pltpu.make_async_copy(weights.at[at], weights_buf.at[at], load_sem.at[owner])

    order = list(range(1, size)) + [0]
    for step in order:
        load(others[step]).start()
    greet(others[1:])
    unit, inverse = centre(residual[...])
    grads = grad_normed[...]
    scaled = grads * gain[...]
    total = cotangent[...].astype(jnp.float32) + inverse * (
        scaled
        - jnp.mean(scaled, -1, keepdims=True)
        - unit * jnp.mean(scaled * unit, -1, keepdims=True)
    )
    grad_residual[...] = total
    grad_branch[...] = total.astype(jnp.bfloat16)
    copies = []
    for step in order:
        other = others[step]
        load(other).wait()
        at = pl.ds(pl.multiple_of(other * cols, cols), cols)
        staged[step] = times_transposed(grad_branch[...], weights_buf[at]).astype(jnp.bfloat16)
        if step == 0:
            copy = pltpu.make_async_copy(staged.at[0], grad_mixed.at[me], local_sem)
        else:
            copy = pltpu.make_async_remote_copy(
                src_ref=staged.at[step],
                dst_ref=grad_mixed.at[me],
                send_sem=send_sem.at[step - 1],
                recv_sem=recv_sem.at[step - 1],
                device_id={"ctx": other},
                device_id_type=MESH_IDS,
            )
        copy.start()
        copies.append(copy)
    sums[...] = two_rows(
        jnp.sum(grads * unit, 0, keepdims=True), jnp.sum(grads, 0, keepdims=True)
    )
    for copy in copies:
        copy.wait()


def part_rows(grad_normed, residual, cotangent, gain, weights, size, collective_id):
    rows, width = grad_normed.shape
    cols = width // size
    vmem = pl.BlockSpec(memory_space=pltpu.VMEM)
    any_space = pl.BlockSpec(memory_space=pl.ANY)
    low = jnp.bfloat16
    dma = pltpu.SemaphoreType.DMA
    return pl.pallas_call(
        functools.partial(part_kernel, size),
        in_specs=[vmem] * 4 + [any_space],
        out_specs=[vmem] * 3 + [any_space],
        out_shape=[
            jax.ShapeDtypeStruct((rows, width), jnp.float32),
            jax.ShapeDtypeStruct((rows, width), low),
            jax.ShapeDtypeStruct((2, width), jnp.float32),
            jax.ShapeDtypeStruct((size, rows, cols), low),
        ],
        scratch_shapes=[
            pltpu.VMEM((width, width), low),
            pltpu.VMEM((size, rows, cols), low),
            dma((size,)),
            dma((size - 1,)),
            dma((size - 1,)),
            dma,
        ],
        compiler_params=pltpu.CompilerParams(
            collective_id=collective_id, has_side_effects=True, vmem_limit_bytes=60 << 20
        ),
        cost_estimate=pl.CostEstimate(
            flops=2 * rows * width * width, bytes_accessed=2 * width * width, transcendentals=0
        ),
    )(grad_normed, residual, cotangent, gain, weights)


def forward_kernel(
    hidden_size,
    normed,
    weights,
    grads,
    normed_t,
    values,
    hidden,
    grad_down,
    tiles,
    weights_buf,
    grads_buf,
    turned,
    values_buf,
    hidden_t,
    load_sem,
    out_sem,
    *sems,
):
    greet_near(8)
    own = pltpu.make_async_copy(normed, tiles.at[0], load_sem.at[0])
    load = pltpu.make_async_copy(weights, weights_buf, load_sem.at[1])
    own.start()
    load.start()
    pltpu.make_async_copy(grads, grads_buf, load_sem.at[2]).start()
    own.wait()
    gather = TileGather(tiles, *sems)
    rows = tiles.shape[1]
    main = hidden_size // 128 * 128

    def write_out(tile, slot):
        at = pl.ds(pl.multiple_of(tile * rows, rows), rows)
        return [
            pltpu.make_async_copy(values_buf.at[slot], values.at[tile], out_sem.at[0, slot]),
            pltpu.make_async_copy(turned.at[slot], normed_t.at[:, at], out_sem.at[1, slot]),
        ]

    @pl.loop(0, 8)
    def _(t):
        for tile in range(8):

            @pl.when(t == tile)
            def _():
                gather.before(tile)
                if tile == 0:
                    load.wait()

        slot = t % 2

        @pl.when(t >= 2)
        def _():
            for copy in write_out(t - 2, slot):
                copy.wait()

        here = tiles[t]
        value = jnp.dot(here, weights_buf[...], preferred_element_type=jnp.float32)
        values_buf[slot] = value
        gate, up = value[:, :main], value[:, main : 2 * main]
        front = gate * jax.nn.sigmoid(gate) * up
        last = value[:, 2 * main :]
        behind = last * jax.nn.sigmoid(last) * pltpu.roll(last, 64, 1)
        both = jnp.concatenate([front, behind], 1)
        hidden[t] = both[:, :hidden_size].astype(jnp.bfloat16)
        at = pl.ds(pl.multiple_of(t * rows, rows), rows)
        hidden_t[:, at] = jnp.transpose(both)[:hidden_size].astype(jnp.bfloat16)
        turned[slot] = jnp.transpose(here)
        for copy in write_out(t, slot):
            copy.start()

    pltpu.make_async_copy(grads, grads_buf, load_sem.at[2]).wait()
    width = grads_buf.shape[2]
    step = 256

    @pl.loop(0, width // step)
    def _(i):
        at = pl.ds(pl.multiple_of(i * step, step), step)
        grad_down[:, at] = jnp.dot(
            hidden_t[...],
            grads_buf[:, :, at].reshape(8 * rows, step),
            preferred_element_type=jnp.float32,
        ).astype(jnp.bfloat16)

    for tile in (6, 7):
        for copy in write_out(tile, tile % 2):
            copy.wait()
    gather.finish()


def forward_mlp(normed, weights, grads, hidden_size, collective_id):
    rows, width = normed.shape
    wide = weights.shape[1]
    any_space = pl.BlockSpec(memory_space=pl.ANY)
    vmem = pl.BlockSpec(memory_space=pltpu.VMEM)
    low = jnp.bfloat16
    dma = pltpu.SemaphoreType.DMA
    return pl.pallas_call(
        functools.partial(forward_kernel, hidden_size),
        in_specs=[any_space] * 3,
        out_specs=[any_space, any_space, vmem, vmem],
        out_shape=[
            jax.ShapeDtypeStruct((width, 8 * rows), low),
            jax.ShapeDtypeStruct((8, rows, wide), jnp.float32),
            jax.ShapeDtypeStruct((8, rows, hidden_size), low),
            jax.ShapeDtypeStruct((hidden_size, width), low),
        ],
        scratch_shapes=[
            pltpu.VMEM((8, rows, width), low),
            pltpu.VMEM(weights.shape, low),
            pltpu.VMEM((8, rows, width), low),
            pltpu.VMEM((2, width, rows), low),
            pltpu.VMEM((2, rows, wide), jnp.float32),
            pltpu.VMEM((hidden_size, 8 * rows), low),
            dma((3,)),
            dma((2, 2)),
        ]
        + gather_sems(),
        compiler_params=pltpu.CompilerParams(
            collective_id=collective_id, has_side_effects=True, vmem_limit_bytes=60 << 20
        ),
        cost_estimate=pl.CostEstimate(
            flops=16 * rows * width * (wide + hidden_size),
            bytes_accessed=64 * rows * width,
            transcendentals=0,
        ),
    )(normed, weights, grads)


def backward_kernel(
    hidden_size,
    grads,
    values,
    weights,
    down,
    normed_t,
    hidden,
    grad_normed,
    grad_both_w,
    layer_part,
    grads_buf,
    values_buf,
    weights_buf,
    down_buf,
    normed_buf,
    grad_both,
    out_buf,
    hidden_buf,
    load_sem,
    tile_sem,
    out_sem,
    *scatter_refs,
):
    greet_near(8)
    scatter = TileScatter(*scatter_refs[: len(scatter_refs) // 2])
    layer = TileScatter(*scatter_refs[len(scatter_refs) // 2 :])
    rows = grads_buf.shape[1]
    main = hidden_size // 128 * 128
    load_weights = pltpu.make_async_copy(weights, weights_buf, load_sem.at[0])
    load_down = pltpu.make_async_copy(down, down_buf, load_sem.at[1])

    def load_tile(tile, slot):
        return [
            pltpu.make_async_copy(grads.at[tile], grads_buf.at[slot], tile_sem.at[0, slot]),
            pltpu.make_async_copy(values.at[tile], values_buf.at[slot], tile_sem.at[1, slot]),
            pltpu.make_async_copy(hidden.at[tile], hidden_buf.at[slot], tile_sem.at[3, slot]),
        ]

    def load_chunk(i):
        at = pl.ds(pl.multiple_of(i * rows, rows), rows)
        return pltpu.make_async_copy(normed_t.at[at], normed_buf.at[i % 2], tile_sem.at[2, i % 2])

    load_down.start()
    for copy in load_tile(7, 1):
        copy.start()
    load_weights.start()
    load_chunk(0).start()

    @pl.loop(0, 8)
    def _(u):
        t = 7 - swapped(u)
        slot = t % 2

        @pl.when(u < 7)
        def _():
            for copy in load_tile(7 - swapped(u + 1), 1 - slot):
                copy.start()

        @pl.when(u == 0)
        def _():
            load_down.wait()

        for copy in load_tile(t, slot):
            copy.wait()
        for tile in (5, 1):

            @pl.when(t == tile)
            def _():
                scatter.before(tile)
                layer.before(tile)

        layer.parts[part_slot(t)] = jnp.dot(
            hidden_buf[slot], down_buf[...], preferred_element_type=jnp.float32
        ).astype(jnp.bfloat16)
        for tile in range(8):

            @pl.when(t == tile)
            def _():
                layer.after(tile)

        grad_hidden = lax.dot_general(
            grads_buf[slot],
            down_buf[...],
            (((1,), (1,)), ((), ())),
            preferred_element_type=jnp.float32,
        )
        value = values_buf[slot]
        gate, up, above = value[:, :main], value[:, main : 2 * main], grad_hidden[:, :main]
        sigmoid = jax.nn.sigmoid(gate)
        grad_both[t, :, :main] = (
            above * up * sigmoid * (1.0 + gate * (1.0 - sigmoid))
        ).astype(jnp.bfloat16)
        grad_both[t, :, main : 2 * main] = (above * (gate * sigmoid)).astype(jnp.bfloat16)
        last = value[:, 2 * main :]
        above = grad_hidden[:, main:]
        above = jnp.concatenate([above, jnp.zeros_like(above)], 1)
        sigmoid = jax.nn.sigmoid(last)
        to_gate = above * pltpu.roll(last, 64, 1) * sigmoid * (1.0 + last * (1.0 - sigmoid))
        to_up = pltpu.roll(above * (last * sigmoid), 64, 1)
        lane = lax.broadcasted_iota(jnp.int32, last.shape, 1)
        grad_both[t, :, 2 * main :] = jnp.where(lane < 64, to_gate, to_up).astype(jnp.bfloat16)

        @pl.when(u == 0)
        def _():
            load_weights.wait()

        scatter.parts[part_slot(t)] = lax.dot_general(
            grad_both[t],
            weights_buf[...],
            (((1,), (1,)), ((), ())),
            preferred_element_type=jnp.float32,
        ).astype(jnp.bfloat16)
        for tile in range(8):

            @pl.when(t == tile)
            def _():
                scatter.after(tile)


    chunks = normed_t.shape[0] // rows

    def store_chunk(i):
        at = pl.ds(pl.multiple_of(i * rows, rows), rows)
        return pltpu.make_async_copy(out_buf.at[i % 2], grad_both_w.at[at], out_sem.at[i % 2])

    @pl.loop(0, chunks)
    def _(i):
        @pl.when(i < chunks - 1)
        def _():
            load_chunk(i + 1).start()

        load_chunk(i).wait()

        @pl.when(i >= 2)
        def _():
            store_chunk(i - 2).wait()

        out_buf[i % 2] = jnp.dot(
            normed_buf[i % 2],
            grad_both[...].reshape(8 * rows, grad_both.shape[2]),
            preferred_element_type=jnp.float32,
        ).astype(jnp.bfloat16)
        store_chunk(i).start()

    store_chunk(chunks - 2).wait()
    store_chunk(chunks - 1).wait()
    scatter.finish(grad_normed)
    layer.finish(layer_part)


def backward_mlp(grads, values, weights, down, normed_t, hidden, collective_id):
    size, rows, width = grads.shape
    hidden_size = down.shape[0]
    wide = weights.shape[1]
    any_space = pl.BlockSpec(memory_space=pl.ANY)
    vmem = pl.BlockSpec(memory_space=pltpu.VMEM)
    low = jnp.bfloat16
    dma = pltpu.SemaphoreType.DMA
    return pl.pallas_call(
        functools.partial(backward_kernel, hidden_size),
        in_specs=[any_space] * 6,
        out_specs=[vmem, any_space, vmem],
        out_shape=[
            jax.ShapeDtypeStruct((rows, width), jnp.float32),
            jax.ShapeDtypeStruct((width, wide), low),
            jax.ShapeDtypeStruct((rows, width), jnp.float32),
        ],
        scratch_shapes=[
            pltpu.VMEM((2, rows, width), low),
            pltpu.VMEM((2, rows, wide), jnp.float32),
            pltpu.VMEM(weights.shape, low),
            pltpu.VMEM(down.shape, low),
            pltpu.VMEM((2, rows, 8 * rows), low),
            pltpu.VMEM((8, rows, wide), low),
            pltpu.VMEM((2, rows, wide), low),
            pltpu.VMEM((2, rows, hidden_size), low),
            dma((2,)),
            dma((4, 2)),
            dma((2,)),
        ]
        + scatter_scratch(rows, width) * 2,
        compiler_params=pltpu.CompilerParams(
            collective_id=collective_id, has_side_effects=True, vmem_limit_bytes=60 << 20
        ),
        cost_estimate=pl.CostEstimate(
            flops=16 * rows * width * (2 * wide + hidden_size),
            bytes_accessed=64 * rows * width,
            transcendentals=0,
        ),
    )(grads, values, weights, down, normed_t, hidden)


def unpack_rows_kernel(source, out):
    out[...] = source[...].astype(jnp.float32)


def unpack_rows(gathered, rows):
    count, _, width = gathered.shape
    group = min(count, 1 << max(1, 352 // rows).bit_length() - 1)
    out = pl.pallas_call(
        unpack_rows_kernel,
        grid=(count // group,),
        in_specs=[pl.BlockSpec((group, rows, width), lambda i: (i, 0, 0))],
        out_specs=pl.BlockSpec((group, rows, width), lambda i: (i, 0, 0)),
        out_shape=jax.ShapeDtypeStruct((count, rows, width), jnp.float32),
        compiler_params=pltpu.CompilerParams(vmem_limit_bytes=60 << 20),
        cost_estimate=pl.CostEstimate(
            flops=0, bytes_accessed=6 * gathered.size, transcendentals=0
        ),
    )(gathered)
    return out.reshape(count * rows, width)


def unpack_kernel(segments, count, source, out):
    strip = source.shape[2] // segments
    pieces = []
    for segment in range(segments):
        for owner in range(count):
            pieces.append(source[owner, :, segment * strip : (segment + 1) * strip])
    out[...] = jnp.concatenate(pieces, 1).astype(jnp.float32)


def unpack_columns(gathered, segments):
    count, rows, width = gathered.shape
    step = min(128, rows)
    return pl.pallas_call(
        functools.partial(unpack_kernel, segments, count),
        grid=(rows // step,),
        in_specs=[pl.BlockSpec((count, step, width), lambda i: (0, i, 0))],
        out_specs=pl.BlockSpec((step, count * width), lambda i: (i, 0)),
        out_shape=jax.ShapeDtypeStruct((rows, count * width), jnp.float32),
        compiler_params=pltpu.CompilerParams(vmem_limit_bytes=60 << 20),
        cost_estimate=pl.CostEstimate(
            flops=0, bytes_accessed=6 * gathered.size, transcendentals=0
        ),
    )(gathered)


def norm_rows(values, gain_row, shift_row):
    centered = values - jnp.mean(values, -1, keepdims=True)
    inverse = lax.rsqrt(jnp.mean(centered * centered, -1, keepdims=True) + NORM_EPSILON)
    unit_rows = centered * inverse
    return (unit_rows * gain_row + shift_row, unit_rows, inverse)


def norm_back(grad_rows, unit_rows, inverse, gain_row):
    scaled = grad_rows * gain_row
    return inverse * (
        scaled
        - jnp.mean(scaled, -1, keepdims=True)
        - unit_rows * jnp.mean(scaled * unit_rows, -1, keepdims=True)
    )


def turn(rows, cosine, sine_low, sine_high, width):
    repeat = width // 128
    wide = [jnp.concatenate([table] * repeat, 1) for table in (cosine, sine_low, sine_high)]
    return (
        rows * wide[0]
        + pltpu.roll(rows, width - ROT // 2, 1) * wide[1]
        + pltpu.roll(rows, ROT // 2, 1) * wide[2]
    )


def head_stack(features_first, heads):
    owner = lax.broadcasted_iota(jnp.int32, features_first.shape, 0) // HEAD
    zero = jnp.zeros_like(features_first)
    return jnp.concatenate([jnp.where(owner == h, features_first, zero) for h in range(heads)], 1)


def row_stack(rows, heads):
    owner = lax.broadcasted_iota(jnp.int32, rows.shape, 1) // HEAD
    zero = jnp.zeros_like(rows)
    return jnp.concatenate([jnp.where(owner == h, rows, zero) for h in range(heads)], 0)


def pair_bias(key_tile, tile, heads, first_keys, diagonal):
    key_place = lax.broadcasted_iota(jnp.int32, (tile, tile), 0)
    allowed = key_place + key_tile * tile >= first_keys
    if diagonal:
        allowed &= key_place <= lax.broadcasted_iota(jnp.int32, (tile, tile), 1)
    return jnp.concatenate([jnp.where(allowed, 0.0, MASKED_SCORE)] * heads, 1)


def transposed(rows):
    return jnp.transpose(rows.astype(jnp.float32)).astype(rows.dtype)


def attend_kernel(
    block,
    heads,
    order,
    lowest,
    projected,
    starts,
    qkv,
    attended,
    mixed,
    log_total,
    value_t,
    summed,
    top,
    total,
):
    cols = heads * HEAD
    seq = projected.shape[0]
    tile = 2 * block

    @pl.loop(0, seq // block)
    def _(p):
        at = pl.ds(pl.multiple_of(p * block, block), block)
        rows = projected[pl.ds(pl.multiple_of(order[p] * block, block), block)]
        qkv[at] = rows
        value_t[:, at] = transposed(rows[:, 2 * cols :])

    @pl.loop(0, seq // tile)
    def _(i):
        at = pl.ds(pl.multiple_of(i * tile, tile), tile)
        query_t = head_stack(transposed(qkv[at, :cols]), heads)
        first_keys = starts[:, at]
        top[...] = jnp.full(top.shape, MASKED_SCORE, jnp.float32)
        total[...] = jnp.zeros_like(total)
        summed[...] = jnp.zeros_like(summed)

        def step(j, diagonal):
            keys_at = pl.ds(pl.multiple_of(j * tile, tile), tile)
            scores = jnp.dot(
                qkv[keys_at, cols : 2 * cols], query_t, preferred_element_type=jnp.float32
            )
            scores += pair_bias(j, tile, heads, first_keys, diagonal)
            old_top = top[...]
            new_top = jnp.maximum(old_top, jnp.max(scores, 0, keepdims=True))
            exps = jnp.exp(scores - new_top)
            fade = jnp.exp(old_top - new_top)
            total[...] = total[...] * fade + jnp.sum(exps, 0, keepdims=True)
            top[...] = new_top
            low = exps.astype(jnp.bfloat16)
            for h in range(heads):
                own = slice(h * tile, (h + 1) * tile)
                features = slice(h * HEAD, (h + 1) * HEAD)
                summed[features] = summed[features] * fade[:, own] + jnp.dot(
                    value_t[features, keys_at], low[:, own], preferred_element_type=jnp.float32
                )

        @pl.loop(lowest[i], i)
        def _(j):
            step(j, False)

        step(i, True)

        log_total[i] = top[...] + jnp.log(total[...])
        scale = 1.0 / total[...]
        for h in range(heads):
            features = slice(h * HEAD, (h + 1) * HEAD)
            summed[features] = summed[features] * scale[:, h * tile : (h + 1) * tile]
        rows = jnp.transpose(summed[...])
        attended[at] = rows
        for part in range(2):
            place = pl.ds(pl.multiple_of(order[2 * i + part] * block, block), block)
            mixed[place] = rows[part * block : (part + 1) * block].astype(jnp.bfloat16)


def attend(projected, order, lowest, starts, heads):
    seq, wide = projected.shape
    cols = wide // 3
    block = seq // order.shape[0]
    tile = 2 * block
    vmem = pl.BlockSpec(memory_space=pltpu.VMEM)
    smem = pl.BlockSpec(memory_space=pltpu.SMEM)
    return pl.pallas_call(
        functools.partial(attend_kernel, block, heads),
        in_specs=[smem, smem] + [vmem] * 2,
        out_specs=[vmem] * 4,
        out_shape=[
            jax.ShapeDtypeStruct((seq, wide), jnp.bfloat16),
            jax.ShapeDtypeStruct((seq, cols), jnp.float32),
            jax.ShapeDtypeStruct((seq, cols), jnp.bfloat16),
            jax.ShapeDtypeStruct((seq // tile, 1, heads * tile), jnp.float32),
        ],
        scratch_shapes=[
            pltpu.VMEM((cols, seq), jnp.bfloat16),
            pltpu.VMEM((cols, tile), jnp.float32),
            pltpu.VMEM((1, heads * tile), jnp.float32),
            pltpu.VMEM((1, heads * tile), jnp.float32),
        ],
        compiler_params=pltpu.CompilerParams(vmem_limit_bytes=48 << 20),
        cost_estimate=pl.CostEstimate(
            flops=4 * seq * seq * cols, bytes_accessed=12 * seq * cols, transcendentals=0
        ),
    )(order, lowest, projected, starts)


def attend_back_run(
    block,
    heads,
    order,
    places,
    qkv,
    grad_mixed,
    attended,
    log_total,
    starts,
    cosine,
    sine_low,
    sine_high,
    normed_t,
    out,
    sums,
    grad_weights,
    normed_buf,
    load_sem,
    key_t,
    grad_key,
    grad_value,
    grad_query,
    query_sum,
):
    cols = heads * HEAD
    seq = qkv.shape[0]
    tile = 2 * block
    chunk = normed_buf.shape[1]
    chunks = normed_t.shape[0] // chunk

    def load(i):
        at = pl.ds(pl.multiple_of(i * chunk, chunk), chunk)
        return pltpu.make_async_copy(normed_t.at[at], normed_buf.at[i % 2], load_sem.at[i % 2])

    load(0).start()

    @pl.loop(0, seq // block)
    def _(p):
        at = pl.ds(pl.multiple_of(p * block, block), block)
        key_t[:, at] = transposed(qkv[at, cols : 2 * cols])
        grad_key[p] = jnp.zeros((block, cols), jnp.float32)
        grad_value[p] = jnp.zeros((block, cols), jnp.float32)

    yield
    for i in reversed(range(seq // tile)):
        at = pl.ds(i * tile, tile)
        query = qkv[at, :cols]
        grad = jnp.concatenate(
            [
                grad_mixed[order[2 * i + part]]
                for part in range(2)
            ],
            0,
        )
        query_t = head_stack(transposed(query), heads)
        query_rows = row_stack(query, heads)
        grad_t = head_stack(transposed(grad), heads)
        grads = row_stack(grad, heads)
        products = jnp.transpose(grad.astype(jnp.float32) * attended[at])
        delta = jnp.concatenate(
            [
                jnp.sum(products[h * HEAD : (h + 1) * HEAD], 0, keepdims=True)
                for h in range(heads)
            ],
            1,
        )
        logs = log_total[i]
        first_keys = starts[:, at]
        query_sum[...] = jnp.zeros_like(query_sum)

        def step(j, diagonal):
            keys_at = pl.ds(pl.multiple_of(j * tile, tile), tile)
            scores = jnp.dot(
                qkv[keys_at, cols : 2 * cols], query_t, preferred_element_type=jnp.float32
            )
            scores += pair_bias(j, tile, heads, first_keys, diagonal)
            weights = jnp.exp(scores - logs)
            grad_soft = jnp.dot(
                qkv[keys_at, 2 * cols :], grad_t, preferred_element_type=jnp.float32
            )
            pair = pl.ds(2 * j, 2)
            grad_value[pair] += jnp.dot(
                weights.astype(jnp.bfloat16), grads, preferred_element_type=jnp.float32
            ).reshape(2, block, cols)
            grad_scores = (weights * (grad_soft - delta)).astype(jnp.bfloat16)
            grad_key[pair] += jnp.dot(
                grad_scores, query_rows, preferred_element_type=jnp.float32
            ).reshape(2, block, cols)
            for h in range(heads):
                features = slice(h * HEAD, (h + 1) * HEAD)
                query_sum[features] += jnp.dot(
                    key_t[features, keys_at],
                    grad_scores[:, h * tile : (h + 1) * tile],
                    preferred_element_type=jnp.float32,
                )

        if i > 0:

            @pl.loop(0, i)
            def _(j):
                step(j, False)

        step(i, True)
        grad_query[2 * i : 2 * i + 2] = (
            jnp.transpose(query_sum[...]) * HEAD ** (-0.5)
        ).reshape(2, block, cols)
        yield
    sums[...] = jnp.zeros_like(sums)

    @pl.loop(0, seq // block)
    def _(d):
        at = pl.ds(pl.multiple_of(d * block, block), block)
        place = places[d]
        tables = (cosine[at], -sine_low[at], -sine_high[at])
        for k, rows in enumerate(
            (
                turn(grad_query[place], *tables, cols),
                turn(grad_key[place], *tables, cols),
                grad_value[place],
            )
        ):
            columns = slice(k * cols, (k + 1) * cols)
            low = rows.astype(jnp.bfloat16)
            out[at, columns] = low
            sums[:, columns] += jnp.sum(low.astype(jnp.float32), 0, keepdims=True)

    @pl.loop(0, chunks)
    def _(i):
        @pl.when(i < chunks - 1)
        def _():
            load(i + 1).start()

        load(i).wait()
        at = pl.ds(pl.multiple_of(i * chunk, chunk), chunk)
        grad_weights[at] = jnp.dot(
            normed_buf[i % 2], out[...], preferred_element_type=jnp.float32
        ).astype(jnp.bfloat16)


def attend_back_op(
    qkv, grad_mixed, attended, log_total, order, places, starts, tables, normed_t, heads
):
    seq, wide = qkv.shape
    cols = wide // 3
    block = seq // order.shape[0]
    tile = 2 * block
    low = jnp.bfloat16
    return dict(
        run=functools.partial(attend_back_run, block, heads),
        inputs=[order, places, qkv, grad_mixed, attended, log_total, starts, *tables, normed_t],
        in_spaces=[pltpu.SMEM] * 2 + [pltpu.VMEM] * 8 + [pl.ANY],
        outs=[
            jax.ShapeDtypeStruct((seq, wide), low),
            jax.ShapeDtypeStruct((1, wide), jnp.float32),
            jax.ShapeDtypeStruct((normed_t.shape[0], wide), low),
        ],
        out_spaces=[pltpu.VMEM] * 3,
        scratch=[
            pltpu.VMEM((2, 256, seq), low),
            pltpu.SemaphoreType.DMA((2,)),
            pltpu.VMEM((cols, seq), low),
            pltpu.VMEM((seq // block, block, cols), jnp.float32),
            pltpu.VMEM((seq // block, block, cols), jnp.float32),
            pltpu.VMEM((seq // block, block, cols), jnp.float32),
            pltpu.VMEM((cols, tile), jnp.float32),
        ],
        moved=20 * seq * cols,
    )


def tables_run(cosines, sines, cosine, sine_low, sine_high):
    half_rot = ROT // 2
    step = 256
    yield

    @pl.loop(0, cosine.shape[0] // step)
    def _(i):
        at = pl.ds(pl.multiple_of(i * step, step), step)
        cos_rows, sin_rows = jnp.transpose(cosines[:, at]), jnp.transpose(sines[:, at])
        lane = lax.broadcasted_iota(jnp.int32, (step, 128), 1) % HEAD
        cos_wide = jnp.ones((step, 128), jnp.float32)
        sin_wide = jnp.zeros((step, 128), jnp.float32)
        for k in range(half_rot):
            own = (lane == k) | (lane == k + half_rot)
            cos_wide = jnp.where(own, cos_rows[:, k : k + 1], cos_wide)
            sin_wide = jnp.where(own, sin_rows[:, k : k + 1], sin_wide)
        cosine[at] = cos_wide
        sine_low[at] = jnp.where(lane < half_rot, -sin_wide, 0.0)
        sine_high[at] = jnp.where(lane >= half_rot, sin_wide, 0.0)


def tables_op(places):
    turns = jnp.arange(ROT // 2, dtype=jnp.int32)[:, None]
    freq = ROTARY_BASE ** (-turns.astype(jnp.float32) * 2.0 / ROT)
    angles = places.astype(jnp.float32)[None, :] * freq
    return dict(
        run=tables_run,
        inputs=[jnp.cos(angles), jnp.sin(angles)],
        in_space=pltpu.VMEM,
        outs=[jax.ShapeDtypeStruct((places.size, 128), jnp.float32)] * 3,
        out_space=pltpu.VMEM,
        scratch=[],
        moved=1024 * places.size,
    )


def place_order(block_pairs, axis_size):
    device_blocks = jnp.stack([block_pairs, 2 * axis_size - 1 - block_pairs], 1).reshape(-1)
    places = jnp.arange(2 * axis_size, dtype=jnp.int32)
    return jnp.sum(
        jnp.where(device_blocks[None, :] == places[:, None], places[None, :], 0), 1
    ).astype(jnp.int32)


def document_starts(docs):
    first = jnp.sum((docs < 1).astype(jnp.int32))
    second = jnp.sum((docs < 2).astype(jnp.int32))
    return jnp.where(docs == 0, 0, jnp.where(docs == 1, first, second))


def inner(left_side, right_side):
    return lax.dot_general(
        left_side, right_side, (((0,), (0,)), ((), ())), preferred_element_type=jnp.float32
    )


def times_transposed(left_side, right_side):
    return lax.dot_general(
        left_side, right_side, (((1,), (1,)), ((), ())), preferred_element_type=jnp.float32
    )


def times(left_side, right_side):
    return jnp.dot(left_side, right_side, preferred_element_type=jnp.float32)


def after(value, *earlier):
    return lax.optimization_barrier((value,) + earlier)[0]


def body(
    tokens,
    doc_ids,
    block_pairs,
    ln1_gain,
    ln1_bias,
    w_qkv,
    b_qkv,
    w_out,
    ln2_gain,
    ln2_bias,
    w_gate,
    w_up,
    w_down,
    cotangent,
):
    rows_here = tokens.shape[1]
    width = tokens.shape[2]
    head_count = width // HEAD
    ctx_size = lax.axis_size("ctx")
    fsdp_size = lax.axis_size("fsdp")
    seq_rows = rows_here * ctx_size
    position = lax.axis_index("ctx")
    heads_here = head_count // ctx_size
    cols = width // ctx_size
    shard_rows = w_qkv.shape[0]
    hidden_shard = w_down.shape[0]
    strip = hidden_shard // ctx_size

    tile = 2 * (rows_here // 2)
    order = place_order(block_pairs, ctx_size)
    starts = document_starts(doc_ids[0])
    lowest = starts[::tile] // tile
    starts = starts[None]
    device_blocks = jnp.stack([block_pairs, 2 * ctx_size - 1 - block_pairs], 1).reshape(-1, 1)
    half_rows = rows_here // 2
    places = device_blocks * half_rows + jnp.arange(half_rows, dtype=jnp.int32)[None, :]

    def strips(w, count, size):
        stride = w.shape[1] // count
        return [
            lax.dynamic_slice_in_dim(w, i * stride + position * size, size, 1)
            for i in range(count)
        ]

    qkv_strip = jnp.concatenate(strips(w_qkv, 3, cols) + strips(w_out, 1, cols), 1)
    hidden_here = fsdp_size * strip
    main = hidden_here // 128 * 128
    fused = ctx_size == 8 and hidden_here - main == 64 and rows_here == 256
    gate_strip = jnp.concatenate(strips(w_gate, fsdp_size, strip), 1)
    up_strip = jnp.concatenate(strips(w_up, fsdp_size, strip), 1)
    both_strip = jnp.concatenate(
        [gate_strip[:, :main], up_strip[:, :main], gate_strip[:, main:], up_strip[:, main:]], 1
    )
    down_strip = lax.dynamic_slice_in_dim(w_down, position * strip, strip, 0)
    out_piece = shard_rows // ctx_size
    qkv_here = lax.all_gather(qkv_strip, "fsdp", axis=0, tiled=True)
    both_here = lax.all_gather(both_strip, "fsdp", axis=0, tiled=True)
    down_here = lax.all_gather(down_strip, "fsdp", axis=0, tiled=True)

    small = jnp.concatenate([ln1_gain, ln1_bias, ln2_gain, ln2_bias, b_qkv])
    small_rows = -(-small.size // 2048) * 16
    small = jnp.pad(small, (0, small_rows * 128 - small.size)).reshape(small_rows, 128)
    grad_out = cotangent[0]
    gather_grads = gather_op(grad_out, ctx_size)
    if fused:
        gather_grads = gather_op(grad_out, ctx_size, row_half, tile_put, relative=True)
    *tables, small, tokens_all, grad_out_all = plane(
        ctx_size,
        1,
        tables_op(places.reshape(-1)),
        z_gather_op(small, fsdp_size),
        gather_op(tokens[0], ctx_size),
        gather_grads,
    )
    small = small.reshape(fsdp_size, small_rows * 128).astype(jnp.float32)
    gain_one, shift_one, gain_two, shift_two = (
        small[:, i * shard_rows : (i + 1) * shard_rows].reshape(1, width) for i in range(4)
    )
    bias_full = small[:, 4 * shard_rows : 4 * shard_rows + b_qkv.size]
    bias_full = bias_full.reshape(3, ctx_size, cols)
    bias_here = lax.dynamic_index_in_dim(bias_full, position, 1, keepdims=False)
    bias_here = bias_here.reshape(1, 3 * cols)
    out_full, projected, normed_t = plane(
        ctx_size,
        2,
        gather_op(
            qkv_here,
            ctx_size,
            functools.partial(last_strip, cols),
            functools.partial(column_strip, cols=cols),
            (width, width),
            pace=4,
        ),
        project_op(tokens_all, qkv_here, gain_one, shift_one, bias_here, tables),
    )
    tokens_in = tokens[0].astype(jnp.float32)
    unit_one, inverse_one = norm_rows(tokens_in, gain_one, shift_one)[1:]
    qkv_rows, attended, mixed_here, log_total = attend(
        projected.reshape(seq_rows, 3 * cols), order, lowest, starts, heads_here
    )
    mixed_here = mixed_here.reshape(ctx_size, rows_here, cols)
    mixed_rows, residual, normed_two_low = join_rows(
        mixed_here, out_full, tokens[0], gain_two, shift_two, 12
    )

    def blocks(rows):
        return rows.astype(jnp.bfloat16).reshape(ctx_size, rows_here, width)

    if fused:
        normed_two_t, both_value, hidden, grad_down_w = forward_mlp(
            normed_two_low, both_here, grad_out_all, hidden_here, 3
        )
        grad_normed_two, grad_both_w, layer_part = backward_mlp(
            grad_out_all, both_value, both_here, down_here, normed_two_t, hidden, 4
        )
    else:
        grad_out_all = grad_out_all.reshape(seq_rows, width)
        normed_two_all = plane(ctx_size, 3, gather_op(normed_two_low, ctx_size))
        normed_two_all = normed_two_all.reshape(seq_rows, width)
        both_value = times(normed_two_all, both_here)
        gate_value = jnp.concatenate(
            [both_value[:, :main], both_value[:, 2 * main : main + hidden_here]], 1
        )
        up_value = jnp.concatenate(
            [both_value[:, main : 2 * main], both_value[:, main + hidden_here :]], 1
        )
        sigmoid_gate = jax.nn.sigmoid(gate_value)
        silu_gate = gate_value * sigmoid_gate
        hidden = (silu_gate * up_value).astype(jnp.bfloat16)

        grad_down_w = inner(hidden, grad_out_all).astype(jnp.bfloat16)
        grad_hidden = times_transposed(after(grad_out_all, grad_down_w), down_here)
        grad_gate = grad_hidden * up_value * sigmoid_gate * (1.0 + gate_value * (1.0 - sigmoid_gate))
        grad_up = grad_hidden * silu_gate
        grad_both = jnp.concatenate(
            [grad_gate[:, :main], grad_up[:, :main], grad_gate[:, main:], grad_up[:, main:]], 1
        ).astype(jnp.bfloat16)
        grad_both_w = inner(normed_two_all, grad_both).astype(jnp.bfloat16)
        grad_normed_two = plane(
            ctx_size,
            4,
            scatter_op(blocks(times_transposed(after(grad_both, grad_both_w), both_here)), ctx_size),
        )
    grad_residual, grad_branch, norm_two_sums, grad_mixed = part_rows(
        grad_normed_two, residual, grad_out, gain_two, out_full, ctx_size, 5
    )

    def reduced(grad):
        return lax.psum_scatter(
            grad.astype(jnp.bfloat16), "fsdp", scatter_dimension=0, tiled=True
        )

    grad_down_w, grad_both_w = reduced(grad_down_w), reduced(grad_both_w)
    attend_op = attend_back_op(
        qkv_rows,
        grad_mixed.reshape(2 * ctx_size, half_rows, cols),
        attended,
        log_total,
        order,
        places[:, 0] // half_rows,
        starts,
        tables,
        normed_t,
        heads_here,
    )
    down_op = gather_op(grad_down_w, ctx_size, column_half, stacked_columns, pace=2)
    if fused:
        mixed_t = jnp.transpose(
            mixed_rows.reshape(rows_here, fsdp_size, ctx_size, out_piece), (2, 1, 3, 0)
        ).reshape(ctx_size, fsdp_size * out_piece, rows_here)
        out_op = produce_op(
            product_of_columns,
            rows_here,
            width,
            mixed_t,
            grad_branch,
            batch=2,
            late=5,
            kind=jnp.bfloat16,
        )
    else:
        mixed_blocks = jnp.transpose(
            mixed_rows.reshape(rows_here, fsdp_size, ctx_size, out_piece), (0, 2, 1, 3)
        ).reshape(rows_here, width)
        out_op = scatter_op(
            inner(mixed_blocks, grad_branch)
            .astype(jnp.bfloat16)
            .reshape(ctx_size, fsdp_size * out_piece, width),
            ctx_size,
        )
    if fused:
        grad_down_w, grad_out_w, grad_projected, grad_bias, grad_qkv_w = plane(
            ctx_size, 6, down_op, out_op, attend_op
        )
    else:
        grad_projected, grad_bias, grad_qkv_w = plane(ctx_size, 6, attend_op)
        grad_down_w, grad_out_w = plane(ctx_size, 7, down_op, out_op)
        layer_part = plane(ctx_size, 10, scatter_op(blocks(times(hidden, down_here)), ctx_size))
    if fused:
        grad_both_w, grad_tokens, norm_one_sums = plane(
            ctx_size,
            8,
            gather_op(grad_both_w, ctx_size, pace=3),
            norm_produce_op(
                product_of_rows,
                grad_projected.reshape(ctx_size, rows_here, 3 * cols),
                qkv_here,
                tokens[0],
                grad_residual,
                gain_one,
            ),
        )
    else:
        grad_both_w, grad_normed = plane_groups(
            ctx_size,
            8,
            gather_op(grad_both_w, ctx_size),
            scatter_op(
                blocks(times_transposed(grad_projected, qkv_here[:, : 3 * cols])), ctx_size
            ),
        )
        grad_tokens = grad_residual + norm_back(grad_normed, unit_one, inverse_one, gain_one)
        norm_one_sums = jnp.stack([jnp.sum(grad_normed * unit_one, 0), jnp.sum(grad_normed, 0)])
    layer_out = residual + layer_part
    grad_qkv_w = reduced(grad_qkv_w)
    grad_out_w = reduced(grad_out_w)

    norm_sums = jnp.concatenate([norm_one_sums, norm_two_sums])
    norm_sums = jnp.transpose(norm_sums.reshape(4, fsdp_size, shard_rows), (1, 0, 2)).reshape(
        fsdp_size, 1, 4 * shard_rows
    )
    bias_sums = lax.dynamic_update_slice(
        jnp.zeros((3, ctx_size, cols), jnp.float32),
        grad_bias.reshape(3, 1, cols),
        (0, position, 0),
    ).reshape(fsdp_size, 1, 3 * width // fsdp_size)
    sums = jnp.concatenate(
        [
            jnp.pad(rows, ((0, 0), (0, extra), (0, width - rows.shape[2])))
            for rows, extra in ((norm_sums, 0), (bias_sums, 6))
        ],
        1,
    )
    grad_qkv_w, grad_out_w, sums = plane(
        ctx_size,
        13,
        gather_op(grad_qkv_w, ctx_size, pace=2),
        gather_op(grad_out_w, ctx_size, column_half, stacked_columns, pace=2),
        z_sum_gather_op(sums, fsdp_size, ctx_size),
    )
    sums = jnp.sum(sums, 0)
    norm_sums = sums[0, : 4 * shard_rows].reshape(4, shard_rows)
    bias_sums = sums[1, : b_qkv.shape[0]]
    grad_out_w = unpack_rows(grad_out_w, out_piece)
    grad_gate_w, grad_up_w = unpack_both(grad_both_w, fsdp_size)
    float32 = jnp.float32
    return (
        layer_out.astype(jnp.bfloat16)[None],
        grad_tokens[None],
        norm_sums[0],
        norm_sums[1],
        unpack_columns(grad_qkv_w, 3),
        bias_sums,
        grad_out_w,
        norm_sums[2],
        norm_sums[3],
        grad_gate_w,
        grad_up_w,
        unpack_rows(grad_down_w, strip),
    )


def solution(mesh):
    placed = (
        P("fsdp", "ctx", None),
        P("fsdp", None),
        P(),
        P("fsdp"),
        P("fsdp"),
        P("fsdp", None),
        P("fsdp"),
        P("fsdp", None),
        P("fsdp"),
        P("fsdp"),
        P("fsdp", None),
        P("fsdp", None),
        P("fsdp", None),
        P("fsdp", "ctx", None),
    )
    return jax.shard_map(
        body,
        mesh=mesh,
        in_specs=placed,
        out_specs=(
            P("fsdp", "ctx", None),
            P("fsdp", "ctx", None),
            P("fsdp"),
            P("fsdp"),
            P("fsdp", None),
            P("fsdp"),
            P("fsdp", None),
            P("fsdp"),
            P("fsdp"),
            P("fsdp", None),
            P("fsdp", None),
            P("fsdp", None),
        ),
        check_vma=False,
    )
```
